32 devices in a mesh: seg: 4 (over y, x), slab: 8 (over z, core).
Axes of the slice: x: 2, y: 2, z: 4, core: 2. Of those that a mesh axis runs over, the one named last changes fastest.
Arguments:
- states: float32 [4, 4, 256, 64, 128], P('seg', None, 'slab'), may hold values from -6 to 6
- viscosity: float32 [256, 64, 128], P('slab'), may hold values from 0.2 to 2
- inverse: float32 [4, 256, 256], replicated, may hold values from -0.375 to 0.375
Outputs:
- residual: float32 [4, 4, 256, 64, 128], P('seg', None, 'slab')
- gradient: float32 [4, 4, 256, 64, 128], P('seg', None, 'slab')
The draws below stay inside these ranges and needn't reach their ends.
All inputs are finite; a program needn't handle non-finite values.
Results may differ from the reference program's by a relative error of at most 0.000075.
Values sent between devices are 32-bit elements; how exact they have to be, the bound alone decides.
No kernel may reach another device: no remote copies, remote signals or barrier semaphores. Data moves between devices by JAX's collectives and lax.ppermute only.
A program may use at most 128 MiB of HBM per device.

```python
import math
import jax
import jax.numpy as jnp
from jax import lax

NZ = 256
NY = 64
NX = 128
SEGS = 4


def level_of(key, dims, cuts, smallest, high):
    gain, own = 1.0, jax.random.fold_in(key, 6)
    for position, blocks in cuts:
        heights = jnp.exp(jax.random.uniform(jax.random.fold_in(own, position), (blocks,), jnp.float32, smallest / len(cuts), high / len(cuts)))
        gain = gain * jnp.repeat(heights, dims[position] // blocks).reshape([-1 if axis == position else 1 for axis in range(len(dims))])
    return gain


def scatter_about(own_key, extent, deviation, reach, split=(), held_as=jnp.bfloat16):
    gain = level_of(own_key, extent, split, -0.22, 0.18) if split else 1.0
    drawn = jax.random.normal(own_key, extent, jnp.float32) * deviation * gain
    return jnp.minimum(jnp.maximum(drawn, -reach), reach).astype(held_as)


def setup_inputs(seed: int = 0) -> dict:
    seeds = jax.random.split(jax.random.key(seed), 4)
    return {
        "states": scatter_about(seeds[0], (SEGS, 4, NZ, NY, NX), 1.0, 6.0, ((0, 4), (2, 8)), jnp.float32),
        "viscosity": jnp.clip(jnp.exp(math.log(2.0) - 2.3025851 * jax.random.uniform(seeds[1], (NZ, NY, NX), jnp.float32) ** level_of(seeds[1], (NZ, NY, NX), ((0, 8),), -0.2, 0.2)), 0.2, 2.0),
        "inverse": scatter_about(seeds[2], (4, NZ, NZ), NZ ** -0.5, 0.375, (), jnp.float32),
    }


time_step = 0.1
buoyancy = 1.0


def face_values(viscosity):
    viscous = viscosity[None]
    along_x = 0.5 * (viscous + jnp.roll(viscous, -1, axis=3))
    back_x = jnp.roll(along_x, 1, axis=3)
    along_y = 0.5 * (viscous + jnp.roll(viscous, -1, axis=2))
    back_y = 0.5 * (viscous + jnp.roll(viscous, 1, axis=2))
    return along_x, back_x, along_y, back_y


def horizontal(field_now, face_visc):
    along_x, back_x, along_y, back_y = face_visc
    north_side = jnp.roll(field_now, -1, axis=2)
    south_side = jnp.roll(field_now, 1, axis=2)
    east_side = jnp.roll(field_now, -1, axis=3)
    west_side = jnp.roll(field_now, 1, axis=3)
    return (along_x * (east_side - field_now) - back_x * (field_now - west_side)
            + along_y * (north_side - field_now) - back_y * (field_now - south_side))


def vertical(field_now):
    padded = jnp.pad(field_now, ((0, 0), (1, 1), (0, 0), (0, 0)))
    return padded[:, 2:] - padded[:, :-2]


def apply_columns(matrices, field_now):
    return jnp.einsum("fzk,fkyx->fzyx", matrices, field_now, precision=lax.Precision.HIGHEST)


def forcing(state_now):
    zero_plane = jnp.zeros_like(state_now[0])
    return jnp.stack([zero_plane, zero_plane, state_now[3], state_now[2]])


def advance(state_now, face_visc, matrices):
    slopes = vertical(state_now)
    explicit = state_now + time_step * (horizontal(state_now, face_visc) - state_now[2] * slopes + buoyancy * forcing(state_now))
    return apply_columns(matrices, explicit), slopes


def retreat(state_now, slopes, cotangent, face_visc, transposed):
    pulled = apply_columns(transposed, cotangent)
    scaled = time_step * pulled
    zero_plane = jnp.zeros_like(scaled[0])
    coupling = buoyancy * scaled[3] - jnp.sum(scaled * slopes, axis=0)
    coupled_terms = jnp.stack([zero_plane, zero_plane, coupling, buoyancy * scaled[2]])
    return pulled + horizontal(scaled, face_visc) + vertical(state_now[2] * scaled) + coupled_terms


def reference(states, viscosity, inverse):
    face_visc = face_values(viscosity)
    transposed = jnp.swapaxes(inverse, 1, 2)
    targets = jnp.roll(states, -1, axis=0)

    def forward_segment(pair):
        start_state, target = pair
        first_state = advance(start_state, face_visc, inverse)[0]
        second_state = advance(first_state, face_visc, inverse)[0]
        return second_state - target

    residual = lax.map(forward_segment, (states, targets))
    priors = jnp.roll(residual, 1, axis=0)

    def backward_segment(triple):
        start_state, residual_now, prior = triple
        first_state, slopes_start = advance(start_state, face_visc, inverse)
        slopes_first = vertical(first_state)
        carried = retreat(first_state, slopes_first, residual_now, face_visc, transposed)
        return retreat(start_state, slopes_start, carried, face_visc, transposed) - prior

    gradient = lax.map(backward_segment, (states, residual, priors))
    return residual, gradient
```

```python
import functools

import jax
import jax.numpy as jnp
from jax import lax
from jax.experimental import pallas as pl
from jax.experimental.pallas import tpu as pltpu
from jax.sharding import PartitionSpec as P

time_step = 0.1
vmem_bytes = 56 * 1024 * 1024
f32, bf16 = jnp.float32, jnp.bfloat16
U, V, W, T = range(4)
fields = 4


def whole():
    return pl.BlockSpec(memory_space=pltpu.VMEM)


def anywhere():
    return pl.BlockSpec(memory_space=pl.ANY)


def params():
    return pltpu.CompilerParams(vmem_limit_bytes=vmem_bytes)


def cost(flops, moved):
    return pl.CostEstimate(flops=flops, bytes_accessed=moved, transcendentals=0)


def east(value):
    return pltpu.roll(value, value.shape[1] - 1, 1)


def west(value):
    return pltpu.roll(value, 1, 1)


def slope(value, before, after):
    count = value.shape[0]
    row = lax.broadcasted_iota(jnp.int32, value.shape, 0)
    above = jnp.where(row == count - 1, after, pltpu.roll(value, count - 1, 0))
    below = jnp.where(row == 0, before, pltpu.roll(value, 1, 0))
    return above - below


def parts_of(value):
    high = value.astype(bf16)
    return high, (value - high.astype(f32)).astype(bf16)


def product(matrix_high, matrix_low, high, low):
    dot = functools.partial(jnp.dot, preferred_element_type=f32)
    return dot(matrix_high, high) + (dot(matrix_high, low) + dot(matrix_low, high))


def to_rows_kernel(x_ref, o_ref):
    depth, rows, _ = x_ref.shape
    for z in range(depth):
        o_ref[pl.ds(z, rows, stride=depth), :] = x_ref[z]


def to_rows(states, field):
    _, depth, rows, width = states.shape
    return pl.pallas_call(
        to_rows_kernel,
        grid=(1,),
        in_specs=[pl.BlockSpec((None, depth, rows, width), lambda i: (field, 0, 0, 0))],
        out_specs=pl.BlockSpec((rows * depth, width), lambda i: (0, 0)),
        out_shape=jax.ShapeDtypeStruct((rows * depth, width), f32),
        compiler_params=params(),
        cost_estimate=cost(0, 8 * rows * depth * width),
        name="to_rows",
    )(states)


def visc_rows_kernel(depth, rows, block, share, own_ref, x_ref, o_ref, send_ref):
    for z in range(depth):
        o_ref[pl.ds(z, rows, stride=depth), :] = x_ref[z]
    own = own_ref[0]
    for target in range(rows // block):
        for i in range(share):
            row = lax.rem(target * block - 2 + share * own + i + rows, rows)
            send_ref[target, i] = o_ref[pl.ds(pl.multiple_of(row * depth, depth), depth), :]


def visc_rows(viscosity, slabs, share):
    depth, rows, width = viscosity.shape
    own = jnp.full((1,), lax.axis_index("seg"), jnp.int32)
    return pl.pallas_call(
        functools.partial(visc_rows_kernel, depth, rows, rows // slabs, share),
        in_specs=[pl.BlockSpec(memory_space=pltpu.SMEM), whole()],
        out_specs=(whole(), whole()),
        out_shape=(
            jax.ShapeDtypeStruct((rows * depth, width), f32),
            jax.ShapeDtypeStruct((slabs, share, depth, width), f32),
        ),
        compiler_params=params(),
        cost_estimate=cost(0, 8 * rows * depth * width),
        name="visc_rows",
    )(own, viscosity)


def to_planes_kernel(*refs):
    o_ref = refs[-1]
    _, depth, rows, _ = o_ref.shape
    for f in range(fields):
        for z in range(depth):
            o_ref[f, z] = refs[f][pl.ds(z, rows, stride=depth), :]


def to_planes(parts, depth):
    total, width = parts[0].shape
    return pl.pallas_call(
        to_planes_kernel,
        in_specs=[whole()] * fields,
        out_specs=whole(),
        out_shape=jax.ShapeDtypeStruct((fields, depth, total // depth, width), f32),
        compiler_params=params(),
        cost_estimate=cost(0, 8 * fields * total * width),
        name="to_planes",
    )(*parts)


def advance_rows(state, visc, shift, mat_high, mat_low, carry, high, low, count, finish):
    slabs, _, depth, width = state.shape[1:]
    edge = jnp.zeros((1, width), f32)
    for p in range(slabs):
        along_y = 0.5 * (visc[p, shift] + visc[p, shift + 1])
        for f in range(fields):
            carry[f, p] = along_y * (state[f, p, 1] - state[f, p, 0])

    def pair(k, _):
        for half in range(2):
            j = 2 * k + half + 1
            for p in range(slabs):
                here = visc[p, j + shift]
                along_x = 0.5 * (here + east(here))
                along_y = 0.5 * (here + visc[p, j + shift + 1])
                speed = state[W, p, j]
                for f in range(fields):
                    value = state[f, p, j]
                    flux_x = along_x * (east(value) - value)
                    flux_y = along_y * (state[f, p, j + 1] - value)
                    spread = flux_x - west(flux_x) + (flux_y - carry[f, p])
                    carry[f, p] = flux_y
                    before = state[f, p - 1, j, depth - 1 : depth] if p > 0 else edge
                    after = state[f, p + 1, j, 0:1] if p < slabs - 1 else edge
                    rate = spread - speed * slope(value, before, after)
                    if f == W:
                        rate = rate + state[T, p, j]
                    if f == T:
                        rate = rate + speed
                    a, b = parts_of(value + time_step * rate)
                    high[f, p * depth : (p + 1) * depth, half * width : (half + 1) * width] = a
                    low[f, p * depth : (p + 1) * depth, half * width : (half + 1) * width] = b
        for f in range(fields):
            out = product(mat_high[f], mat_low[f], high[f], low[f])
            for half in range(2):
                piece = out[:, half * width : (half + 1) * width]
                finish(f, 2 * k + half, piece.reshape(slabs, depth, width))
        return 0

    lax.fori_loop(0, count // 2, pair, 0)


def first_kernel(share, *refs):
    mains, lows, highs = refs[0:4], refs[4:8], refs[8:12]
    visc_in, mat_high, mat_low, first, visc, state, carry, high, low, sem = refs[12:]
    block = mains[0].shape[1]
    copies = []
    for s in range(visc_in.shape[0]):
        copies.append((visc_in.at[s], visc.at[:, pl.ds(share * s, share)]))
    for f in range(fields):
        copies.append((lows[f], state.at[f, :, pl.ds(0, 2)]))
        copies.append((mains[f], state.at[f, :, pl.ds(2, block)]))
        copies.append((highs[f], state.at[f, :, pl.ds(block + 2, 2)]))
    copies = [
        pltpu.make_async_copy(source, target, sem.at[i])
        for i, (source, target) in enumerate(copies)
    ]
    for copy in copies:
        copy.start()
    for copy in copies:
        copy.wait()

    def finish(f, row, piece):
        first[f, :, row] = piece

    advance_rows(
        state, visc, 0, mat_high, mat_low, carry, high, low, first.shape[2], finish
    )


def first_step(mains, lows, highs, visc_in, mat_high, mat_low):
    slabs, block, depth, width = mains[0].shape
    segs, _, share = visc_in.shape[:3]
    order = slabs * depth
    volume = fields * (block + 2) * order * width
    return pl.pallas_call(
        functools.partial(first_kernel, share),
        in_specs=[anywhere()] * 13 + [whole()] * 2,
        out_specs=(whole(), whole()),
        out_shape=(
            jax.ShapeDtypeStruct((fields, slabs, block + 2, depth, width), f32),
            jax.ShapeDtypeStruct((slabs, segs * share, depth, width), f32),
        ),
        scratch_shapes=[
            pltpu.VMEM((fields, slabs, block + 4, depth, width), f32),
            pltpu.VMEM((fields, slabs, depth, width), f32),
            pltpu.VMEM((fields, order, 2 * width), bf16),
            pltpu.VMEM((fields, order, 2 * width), bf16),
            pltpu.SemaphoreType.DMA((segs + 12,)),
        ],
        compiler_params=params(),
        cost_estimate=cost(6 * order * volume, 12 * volume),
        name="first_step",
    )(*mains, *lows, *highs, visc_in, mat_high, mat_low)


def second_kernel(*refs):
    first, visc, mat_high, mat_low = refs[0:4]
    targets, outs = refs[4:8], refs[8:12]
    low_edge, high_edge, carry, high, low = refs[12:]
    block = outs[0].shape[1]

    def finish(f, row, piece):
        outs[f][:, row] = piece - targets[f][:, row]

    advance_rows(first, visc, 1, mat_high, mat_low, carry, high, low, block, finish)
    for f in range(fields):
        low_edge[f] = outs[f][:, 0]
        high_edge[f] = outs[f][:, block - 1]


def second_step(first, visc, mat_high, mat_low, targets):
    slabs, block, depth, width = targets[0].shape
    order = slabs * depth
    volume = fields * block * order * width
    one = jax.ShapeDtypeStruct(targets[0].shape, f32)
    edge = jax.ShapeDtypeStruct((fields, slabs, depth, width), f32)
    out = pl.pallas_call(
        second_kernel,
        in_specs=[whole()] * 8,
        out_specs=(whole(),) * 6,
        out_shape=(one,) * 4 + (edge,) * 2,
        scratch_shapes=[
            pltpu.VMEM((fields, slabs, depth, width), f32),
            pltpu.VMEM((fields, order, 2 * width), bf16),
            pltpu.VMEM((fields, order, 2 * width), bf16),
        ],
        compiler_params=params(),
        cost_estimate=cost(6 * order * volume, 12 * volume),
        name="second_step",
    )(first, visc, mat_high, mat_low, *targets)
    return out[:4], out[4], out[5]


def adjoint_kernel(*refs):
    parts = refs[0:4]
    low_edge, high_edge, first, visc, mat_high, mat_low = refs[4:10]
    outs = refs[10:14]
    cot, pulled, carry, high, low, sem = refs[14:]
    slabs, block, depth, width = outs[0].shape
    copies = []
    for f in range(fields):
        copies.append((low_edge.at[f], cot.at[f, :, 0]))
        copies.append((parts[f], cot.at[f, :, pl.ds(1, block)]))
        copies.append((high_edge.at[f], cot.at[f, :, block + 1]))
    copies = [
        pltpu.make_async_copy(source, target, sem.at[i])
        for i, (source, target) in enumerate(copies)
    ]
    for copy in copies:
        copy.start()
    for copy in copies:
        copy.wait()

    def pull(k, _):
        for f in range(fields):
            pair = [cot[f, :, 2 * k + half].reshape(slabs * depth, width) for half in range(2)]
            a, b = parts_of(jnp.concatenate(pair, axis=1))
            out = product(mat_high[f], mat_low[f], a, b)
            for half in range(2):
                piece = out[:, half * width : (half + 1) * width]
                pulled[f, :, 2 * k + half] = piece.reshape(slabs, depth, width)
        return 0

    lax.fori_loop(0, (block + 2) // 2, pull, 0)
    edge = jnp.zeros((1, width), f32)
    for p in range(slabs):
        along_y = 0.5 * (visc[p, 1] + visc[p, 2])
        for f in range(fields):
            carry[f, p] = along_y * (pulled[f, p, 1] - pulled[f, p, 0])

    def rows(k, _):
        for half in range(2):
            j = 2 * k + half + 1
            for p in range(slabs):
                here = visc[p, j + 1]
                along_x = 0.5 * (here + east(here))
                along_y = 0.5 * (here + visc[p, j + 2])
                speed = first[W, p, j]
                speed_before = first[W, p - 1, j, depth - 1 : depth] if p > 0 else edge
                speed_after = first[W, p + 1, j, 0:1] if p < slabs - 1 else edge
                coupling = pulled[T, p, j]
                for f in (U, V, T, W):
                    value = pulled[f, p, j]
                    flux_x = along_x * (east(value) - value)
                    flux_y = along_y * (pulled[f, p, j + 1] - value)
                    rate = flux_x - west(flux_x) + (flux_y - carry[f, p])
                    carry[f, p] = flux_y
                    before, after = edge, edge
                    q_before, q_after = edge, edge
                    if p > 0:
                        before = speed_before * pulled[f, p - 1, j, depth - 1 : depth]
                        q_before = first[f, p - 1, j, depth - 1 : depth]
                    if p < slabs - 1:
                        after = speed_after * pulled[f, p + 1, j, 0:1]
                        q_after = first[f, p + 1, j, 0:1]
                    rate = rate + slope(speed * value, before, after)
                    coupling = coupling - value * slope(first[f, p, j], q_before, q_after)
                    if f == T:
                        rate = rate + pulled[W, p, j]
                    if f == W:
                        rate = rate + coupling
                    a, b = parts_of(value + time_step * rate)
                    high[f, p * depth : (p + 1) * depth, half * width : (half + 1) * width] = a
                    low[f, p * depth : (p + 1) * depth, half * width : (half + 1) * width] = b
        for f in range(fields):
            out = product(mat_high[f], mat_low[f], high[f], low[f])
            for half in range(2):
                piece = out[:, half * width : (half + 1) * width]
                outs[f][:, 2 * k + half] = piece.reshape(slabs, depth, width)
        return 0

    lax.fori_loop(0, block // 2, rows, 0)


def adjoint_step(parts, low_edge, high_edge, first, visc, mat_high, mat_low):
    slabs, block, depth, width = parts[0].shape
    order = slabs * depth
    volume = fields * (block + 1) * order * width
    return pl.pallas_call(
        adjoint_kernel,
        in_specs=[anywhere()] * 6 + [whole()] * 4,
        out_specs=(whole(),) * 4,
        out_shape=(jax.ShapeDtypeStruct(parts[0].shape, f32),) * 4,
        scratch_shapes=[
            pltpu.VMEM((fields, slabs, block + 2, depth, width), f32),
            pltpu.VMEM((fields, slabs, block + 2, depth, width), f32),
            pltpu.VMEM((fields, slabs, depth, width), f32),
            pltpu.VMEM((fields, order, 2 * width), bf16),
            pltpu.VMEM((fields, order, 2 * width), bf16),
            pltpu.SemaphoreType.DMA((12,)),
        ],
        compiler_params=params(),
        cost_estimate=cost(12 * order * volume, 16 * volume),
        name="adjoint_step",
    )(*parts, low_edge, high_edge, first, visc, mat_high, mat_low)


def last_kernel(*refs):
    pulled, state, prior = refs[0:4], refs[4:8], refs[8:12]
    visc, pulled_before, pulled_after, state_before, state_after, out, carry = refs[12:]
    depth = out.shape[0] // fields // pulled_before.shape[1]
    rows = pulled_before.shape[1]

    def row_of(ref, y):
        return ref[pl.ds(pl.multiple_of(y * depth, depth), depth), :]

    along_y = 0.5 * (row_of(visc, rows - 1) + row_of(visc, 0))
    for f in range(fields):
        carry[f] = along_y * (row_of(pulled[f], 0) - row_of(pulled[f], rows - 1))

    def row(y, _):
        north = lax.rem(y + 1, rows)
        here = row_of(visc, y)
        along_x = 0.5 * (here + east(here))
        along_y = 0.5 * (here + row_of(visc, north))
        speed = row_of(state[W], y)
        one = pl.ds(y, 1)
        coupling = row_of(pulled[T], y)
        for f in (U, V, T, W):
            value = row_of(pulled[f], y)
            flux_x = along_x * (east(value) - value)
            flux_y = along_y * (row_of(pulled[f], north) - value)
            rate = flux_x - west(flux_x) + (flux_y - carry[f])
            carry[f] = flux_y
            before = state_before[W, one] * pulled_before[f, one]
            after = state_after[W, one] * pulled_after[f, one]
            rate = rate + slope(speed * value, before, after)
            q_slope = slope(row_of(state[f], y), state_before[f, one], state_after[f, one])
            coupling = coupling - value * q_slope
            if f == T:
                rate = rate + row_of(pulled[W], y)
            if f == W:
                rate = rate + coupling
            result = value + time_step * rate - row_of(prior[f], y)
            out[pl.ds(f * depth * rows + y, depth, stride=rows), :] = result
        return 0

    lax.fori_loop(0, rows, row, 0)


def last_step(pulled, state, prior, visc, edges, depth):
    total, width = visc.shape
    return pl.pallas_call(
        last_kernel,
        in_specs=[whole()] * 17,
        out_specs=whole(),
        out_shape=jax.ShapeDtypeStruct((fields * total, width), f32),
        scratch_shapes=[pltpu.VMEM((fields, depth, width), f32)],
        compiler_params=params(),
        cost_estimate=cost(30 * fields * total * width, 20 * fields * total * width),
        name="last_step",
    )(*pulled, *state, *prior, visc, *edges)


def exchange(value):
    return lax.all_to_all(value, "slab", split_axis=0, concat_axis=0, tiled=True)


def around(value, axis, steps):
    count = lax.axis_size(axis)
    return lax.ppermute(value, axis, [(i, (i + steps) % count) for i in range(count)])


def up_and_down(first_plane, last_plane):
    count = lax.axis_size("slab")
    forward = [(i, i + 1) for i in range(count - 1)]
    backward = [(target, source) for source, target in forward]
    return lax.ppermute(last_plane, "slab", forward), lax.ppermute(first_plane, "slab", backward)


def local(states, viscosity, inverse):
    start = states[0]
    _, depth, rows, width = start.shape
    slabs, segs = lax.axis_size("slab"), lax.axis_size("seg")
    block = rows // slabs
    share = -(-(block + 4) // segs)
    columns = (slabs, block, depth, width)

    visc, visc_send = visc_rows(viscosity, slabs, share)
    visc_in = lax.all_gather(exchange(visc_send), "seg", axis=0)
    state = [to_rows(start, f) for f in range(fields)]
    state_edges = up_and_down(start[:, 0], start[:, depth - 1])

    high = lax.reduce_precision(inverse, 8, 7)
    mat_high, mat_low = high.astype(bf16), (inverse - high).astype(bf16)
    adj_high, adj_low = jnp.swapaxes(mat_high, 1, 2), jnp.swapaxes(mat_low, 1, 2)

    mains = [exchange(part.reshape(columns)) for part in state]
    lows = [around(part[:, block - 2 :], "slab", 1) for part in mains]
    highs = [around(part[:, :2], "slab", -1) for part in mains]
    targets = [around(part, "seg", -1) for part in mains]

    first, frame = first_step(mains, lows, highs, visc_in, mat_high, mat_low)
    residual, low_edge, high_edge = second_step(first, frame, mat_high, mat_low, targets)
    before = around(high_edge, "slab", 1)
    after = around(low_edge, "slab", -1)
    residual_rows = [exchange(part).reshape(rows * depth, width) for part in residual]
    priors = [around(part, "seg", 1) for part in residual_rows]
    residual_out = to_planes(residual_rows, depth)

    pulled = adjoint_step(residual, before, after, first, frame, adj_high, adj_low)
    pulled = [exchange(part).reshape(rows, depth, width) for part in pulled]
    pulled_edges = up_and_down(
        jnp.stack([part[:, 0] for part in pulled]), jnp.stack([part[:, depth - 1] for part in pulled])
    )
    gradient = last_step(
        [part.reshape(rows * depth, width) for part in pulled],
        state,
        priors,
        visc,
        (*pulled_edges, *state_edges),
        depth,
    )
    return (residual_out[None], gradient.reshape(1, fields, depth, rows, width))


def solution(mesh):
    in_specs = (P("seg", None, "slab", None, None), P("slab", None, None), P())
    out_specs = (P("seg", None, "slab", None, None), P("seg", None, "slab", None, None))
    return jax.shard_map(local, mesh=mesh, in_specs=in_specs, out_specs=out_specs, check_vma=False)
```

```python
import functools

import jax
import jax.numpy as jnp
from jax import lax
from jax.experimental import pallas as pl
from jax.experimental.pallas import tpu as pltpu
from jax.sharding import PartitionSpec as P

time_step = 0.1
vmem_bytes = 56 * 1024 * 1024
f32, bf16 = jnp.float32, jnp.bfloat16
U, V, W, T = range(4)
fields = 4
pad = 8
tall = 32


def whole():
    return pl.BlockSpec(memory_space=pltpu.VMEM)


def anywhere():
    return pl.BlockSpec(memory_space=pl.ANY)


def scalars():
    return pl.BlockSpec(memory_space=pltpu.SMEM)


def vmem(*shape):
    return pltpu.VMEM(shape, f32)


def dmas(count):
    return pltpu.SemaphoreType.DMA((count,))


def call(kernel, ins, outs, scratch, flops, name, kind=f32):
    moved = sum(4 * x.size for x, _ in ins)
    return pl.pallas_call(
        kernel,
        in_specs=[spec for _, spec in ins],
        out_specs=tuple(spec for _, spec in outs),
        out_shape=tuple(jax.ShapeDtypeStruct(shape, kind) for shape, _ in outs),
        scratch_shapes=scratch,
        compiler_params=pltpu.CompilerParams(vmem_limit_bytes=vmem_bytes),
        cost_estimate=pl.CostEstimate(flops=flops, bytes_accessed=moved, transcendentals=0),
        name=name,
    )(*[x for x, _ in ins])


def start_all(pairs, sem):
    copies = [
        pltpu.make_async_copy(source, target, sem.at[i])
        for i, (source, target) in enumerate(pairs)
    ]
    for copy in copies:
        copy.start()
    return copies


def wait_all(copies):
    for copy in copies:
        copy.wait()


def east(value):
    return pltpu.roll(value, value.shape[1] - 1, 1)


def west(value):
    return pltpu.roll(value, 1, 1)


def parts_of(value):
    high = value.astype(bf16)
    return high, (value - high.astype(f32)).astype(bf16)


def product(matrix_high, matrix_low, high, low):
    dot = functools.partial(jnp.dot, preferred_element_type=f32)
    return dot(matrix_high, high) + (dot(matrix_high, low) + dot(matrix_low, high))


def split_kernel(x_ref, high, low, adj_high, adj_low):
    for f in range(fields):
        high[f], low[f] = parts_of(x_ref[f])
        adj_high[f], adj_low[f] = parts_of(x_ref[f].T)


def split(inverse):
    return call(
        split_kernel,
        [(inverse, whole())],
        [(inverse.shape, whole())] * 4,
        [],
        0,
        "split",
        bf16,
    )


def chunks_kernel(own, x_ref, visc_in, send, visc, edges, planes, held, extra, flat, sem):
    slabs, block = held.shape[1:3]
    rows, depth, _ = visc.shape
    share = extra.shape[1]
    visc_copy = pltpu.make_async_copy(visc_in, flat, sem.at[2 * fields])
    visc_copy.start()
    copies = start_all([(x_ref.at[f], planes.at[f]) for f in range(fields)], sem)
    visc_copy.wait()
    for y in range(rows):
        visc[y] = flat[pl.ds(y, depth, stride=rows), :]
    for p in range(slabs):
        for i in range(share):
            row = lax.rem(p * block - 2 + share * own[0] + i + rows, rows)
            extra[p, i] = visc[row]
    leaving = [
        pltpu.make_async_copy(extra, send.at[:, pl.ds(fields * block, share)], sem.at[2 * fields])
    ]
    leaving[0].start()
    for f in range(fields):
        copies[f].wait()
        for y in range(rows):
            held[f, y // block, y % block] = planes[f, pl.ds(y, depth, stride=rows), :]
        leaving.append(
            pltpu.make_async_copy(
                held.at[f], send.at[:, pl.ds(f * block, block)], sem.at[fields + f]
            )
        )
        leaving[-1].start()
        edges[0, f] = planes[f, pl.ds(0, rows), :]
        edges[1, f] = planes[f, pl.ds((depth - 1) * rows, rows), :]
    wait_all(leaving)


def to_chunks(states, viscosity, slabs, share):
    _, depth, rows, width = states.shape
    block = rows // slabs
    own = jnp.full((1,), lax.axis_index("seg"), jnp.int32)
    return call(
        chunks_kernel,
        [
            (own, scalars()),
            (states.reshape(fields, -1, width), anywhere()),
            (viscosity.reshape(-1, width), anywhere()),
        ],
        [
            ((slabs, fields * block + share, depth, width), anywhere()),
            ((rows, depth, width), whole()),
            ((2, fields, rows, width), whole()),
        ],
        [
            vmem(fields, depth * rows, width),
            vmem(fields, slabs, block, depth, width),
            vmem(slabs, share, depth, width),
            vmem(depth * rows, width),
            dmas(2 * fields + 1),
        ],
        0,
        "to_chunks",
    )


def planes_kernel(half, other, target, _, o_ref, held, sem):
    slabs, _, block, depth, _ = half.shape
    rows = slabs * block
    pairs = []
    for p in range(slabs):
        place = pl.ds(p * block, block)
        pairs.append((half.at[p], held.at[pl.ds(0, 2), place]))
        pairs.append((other.at[p], held.at[pl.ds(2, 2), place]))
    wait_all(start_all(pairs, sem))

    def row(y, _):
        for f in range(fields):
            where = pl.ds(f * depth * rows + y, depth, stride=rows)
            o_ref[where, :] = held[f, y] - target[where, :]
        return 0

    lax.fori_loop(0, rows, row, 0, unroll=4)


def residual_planes(halves, target, later):
    slabs, _, block, depth, width = halves[0].shape
    return call(
        planes_kernel,
        [(halves[0], anywhere()), (halves[1], anywhere())]
        + [(target.reshape(-1, width), whole()), (later, anywhere())],
        [((fields * depth * slabs * block, width), whole())],
        [vmem(fields, slabs * block, depth, width), dmas(2 * slabs)],
        0,
        "residual_planes",
    )[0]


def clear_pads(ref):
    edge = jnp.zeros(ref.shape[1:2] + (pad, ref.shape[3]), f32)
    for f in range(fields):
        ref[f, :, 0:pad] = edge
        ref[f, :, ref.shape[2] - pad :] = edge


def first_fluxes(state, visc, shift, carry):
    order = visc.shape[1]
    for z in range(0, order, tall):
        here, pads = pl.ds(z, tall), pl.ds(z + pad, tall)
        along_y = 0.5 * (visc[shift, here] + visc[shift + 1, here])
        for f in range(fields):
            carry[f, here] = along_y * (state[f, 1, pads] - state[f, 0, pads])


def spread_of(state, f, j, value, here, pads, along_x, along_y, carry):
    flux_x = along_x * (east(value) - value)
    flux_y = along_y * (state[f, j + 1, pads] - value)
    spread = flux_x - west(flux_x) + (flux_y - carry[f, here])
    carry[f, here] = flux_y
    return spread


def advance_rows(state, visc, shift, mat_high, mat_low, carry, high, low, count, finish):
    order, width = visc.shape[1:]
    first_fluxes(state, visc, shift, carry)

    def pair(k, _):
        for half in range(2):
            j = 2 * k + half + 1
            side = slice(half * width, (half + 1) * width)
            for z in range(0, order, tall):
                here, pads = pl.ds(z, tall), pl.ds(z + pad, tall)
                above, below = pl.ds(z + pad + 1, tall), pl.ds(z + pad - 1, tall)
                own = visc[j + shift, here]
                along_x = 0.5 * (own + east(own))
                along_y = 0.5 * (own + visc[j + shift + 1, here])
                speed = state[W, j, pads]
                for f in range(fields):
                    value = state[f, j, pads]
                    rate = spread_of(state, f, j, value, here, pads, along_x, along_y, carry)
                    rate = rate - speed * (state[f, j, above] - state[f, j, below])
                    if f == W:
                        rate = rate + state[T, j, pads]
                    if f == T:
                        rate = rate + speed
                    high[f, here, side], low[f, here, side] = parts_of(value + time_step * rate)
        for f in range(fields):
            out = product(mat_high[f], mat_low[f], high[f], low[f])
            finish(f, 2 * k, out[:, :width])
            finish(f, 2 * k + 1, out[:, width:])
        return 0

    lax.fori_loop(0, count // 2, pair, 0)


def step_scratch(order, width):
    return [
        vmem(fields, order, width),
        pltpu.VMEM((fields, order, 2 * width), bf16),
        pltpu.VMEM((fields, order, 2 * width), bf16),
    ]


def first_kernel(chunks, low_in, high_in, visc_in, mat_high, mat_low, first, visc, *scratch):
    state, carry, high, low, sem = scratch
    slabs, _, _, depth, _ = low_in.shape
    segs, _, share = visc_in.shape[:3]
    block = first.shape[1] - 2
    order = visc.shape[1]
    pairs = []
    for p in range(slabs):
        planes, padded = pl.ds(p * depth, depth), pl.ds(p * depth + pad, depth)
        for f in range(fields):
            source = chunks.at[p, pl.ds(f * block, block)]
            pairs.append((source, state.at[f, pl.ds(2, block), padded]))
        pairs.append((low_in.at[p], state.at[:, pl.ds(0, 2), padded]))
        pairs.append((high_in.at[p], state.at[:, pl.ds(block + 2, 2), padded]))
        for s in range(segs):
            pairs.append((visc_in.at[s, p], visc.at[pl.ds(share * s, share), planes]))
    copies = start_all(pairs, sem)
    clear_pads(state)
    clear_pads(first)
    wait_all(copies)

    def finish(f, row, piece):
        first[f, row, pl.ds(pad, order)] = piece

    advance_rows(state, visc, 0, mat_high, mat_low, carry, high, low, block + 2, finish)


def first_step(chunks, low_in, high_in, visc_in, mat_high, mat_low):
    slabs, _, depth, width = chunks.shape
    segs, _, share = visc_in.shape[:3]
    block = (chunks.shape[1] - share) // fields
    order = slabs * depth
    volume = fields * (block + 2) * order * width
    return call(
        first_kernel,
        [(x, anywhere()) for x in (chunks, low_in, high_in, visc_in)]
        + [(mat_high, whole()), (mat_low, whole())],
        [
            ((fields, block + 2, order + 2 * pad, width), whole()),
            ((segs * share, order, width), whole()),
        ],
        [vmem(fields, block + 4, order + 2 * pad, width)]
        + step_scratch(order, width)
        + [dmas(slabs * (fields + 2 + segs))],
        6 * order * volume,
        "first_step",
    )


def second_kernel(first, visc, mat_high, mat_low, half, other, carry, high, low, held, sem):
    slabs, _, block, depth, _ = half.shape

    def finish(f, row, piece):
        held[f, row] = piece

    advance_rows(first, visc, 1, mat_high, mat_low, carry, high, low, block, finish)
    pairs = []
    for p in range(slabs):
        planes = pl.ds(p * depth, depth)
        pairs.append((held.at[pl.ds(0, 2), :, planes], half.at[p]))
        pairs.append((held.at[pl.ds(2, 2), :, planes], other.at[p]))
    wait_all(start_all(pairs, sem))


def second_step(first, visc, mat_high, mat_low, slabs):
    _, block, _, width = first.shape
    block, order = block - 2, visc.shape[1]
    return call(
        second_kernel,
        [(x, whole()) for x in (first, visc, mat_high, mat_low)],
        [((slabs, 2, block, order // slabs, width), anywhere())] * 2,
        step_scratch(order, width) + [vmem(fields, block, order, width), dmas(2 * slabs)],
        6 * order * fields * block * order * width,
        "second_step",
    )


def outer_kernel(chunks, _, low_rows, high_rows, visc, sem):
    share = visc.shape[1]
    block = (chunks.shape[1] - share) // fields
    pairs = []
    for f in range(fields):
        pairs.append((chunks.at[:, pl.ds((f + 1) * block - 2, 2)], high_rows.at[:, f]))
        pairs.append((chunks.at[:, pl.ds(f * block, 2)], low_rows.at[:, f]))
    pairs.append((chunks.at[:, pl.ds(fields * block, share)], visc))
    wait_all(start_all(pairs, sem))


def outer_rows(chunks, share, later):
    slabs, _, depth, width = chunks.shape
    rows = ((slabs, fields, 2, depth, width), anywhere())
    return call(
        outer_kernel,
        [(chunks, anywhere()), (later, anywhere())],
        [rows, rows, ((slabs, share, depth, width), anywhere())],
        [dmas(2 * fields + 1)],
        0,
        "outer_rows",
    )


def edge_kernel(half, other, target, _, low_edge, high_edge, ours, theirs, sem):
    block = half.shape[2]
    pairs = []
    for side, row in ((0, 0), (1, block - 1)):
        for f in range(fields):
            source = (half, other)[f // 2]
            pairs.append((source.at[:, f % 2, row], ours.at[side, f]))
            pairs.append((target.at[:, f * block + row], theirs.at[side, f]))
    wait_all(start_all(pairs, sem))
    for f in range(fields):
        low_edge[:, f] = ours[0, f] - theirs[0, f]
        high_edge[:, f] = ours[1, f] - theirs[1, f]


def edge_rows(halves, target, later):
    slabs, _, _, depth, width = halves[0].shape
    edge = ((slabs, fields, depth, width), whole())
    both = vmem(2, fields, slabs, depth, width)
    return call(
        edge_kernel,
        [(x, anywhere()) for x in (*halves, target, later)],
        [edge, edge],
        [both, both, dmas(4 * fields)],
        0,
        "edge_rows",
    )


def adjoint_kernel(half, other, target, low_edge, high_edge, *refs):
    first, visc, mat_high, mat_low = refs[:4]
    out, cot, less, pulled, ends, carry, high, low, sem = refs[4:]
    slabs, _, block, depth, width = half.shape
    order = slabs * depth
    main = pl.ds(1, block)
    pairs = []
    for p in range(slabs):
        planes = pl.ds(p * depth, depth)
        pairs.append((half.at[p], cot.at[pl.ds(0, 2), main, planes]))
        pairs.append((other.at[p], cot.at[pl.ds(2, 2), main, planes]))
        for f in range(fields):
            source = target.at[p, pl.ds(f * block, block)]
            pairs.append((source, less.at[f, main, planes]))
        pairs.append((low_edge.at[p], cot.at[:, 0, planes]))
        pairs.append((high_edge.at[p], cot.at[:, block + 1, planes]))
    copies = start_all(pairs, sem)
    clear_pads(pulled)
    for f in range(fields):
        less[f, 0] = jnp.zeros((order, width), f32)
        less[f, block + 1] = jnp.zeros((order, width), f32)
    wait_all(copies)

    def pull(k, _):
        for f in range(fields):
            pair = [cot[f, 2 * k + i] - less[f, 2 * k + i] for i in range(2)]
            pair = jnp.concatenate(pair, axis=1)
            out = product(mat_high[f], mat_low[f], *parts_of(pair))
            pulled[f, 2 * k, pl.ds(pad, order)] = out[:, :width]
            pulled[f, 2 * k + 1, pl.ds(pad, order)] = out[:, width:]
        return 0

    lax.fori_loop(0, (block + 2) // 2, pull, 0)
    first_fluxes(pulled, visc, 1, carry)

    def rows(k, _):
        for half in range(2):
            j = 2 * k + half + 1
            side = slice(half * width, (half + 1) * width)
            for z in range(0, order, tall):
                here, pads = pl.ds(z, tall), pl.ds(z + pad, tall)
                above, below = pl.ds(z + pad + 1, tall), pl.ds(z + pad - 1, tall)
                own = visc[j + 1, here]
                along_x = 0.5 * (own + east(own))
                along_y = 0.5 * (own + visc[j + 2, here])
                speed_above, speed_below = first[W, j, above], first[W, j, below]
                coupling = pulled[T, j, pads]
                for f in (U, V, T, W):
                    value = pulled[f, j, pads]
                    rate = spread_of(pulled, f, j, value, here, pads, along_x, along_y, carry)
                    up, down = pulled[f, j, above], pulled[f, j, below]
                    rate = rate + (speed_above * up - speed_below * down)
                    if f == W:
                        slope = speed_above - speed_below
                    else:
                        slope = first[f, j, above] - first[f, j, below]
                    coupling = coupling - value * slope
                    if f == T:
                        rate = rate + pulled[W, j, pads]
                    if f == W:
                        rate = rate + coupling
                    high[f, here, side], low[f, here, side] = parts_of(value + time_step * rate)
        for f in range(fields):
            out = product(mat_high[f], mat_low[f], high[f], low[f])
            cot[f, 2 * k + 1] = out[:, :width]
            cot[f, 2 * k + 2] = out[:, width:]
        return 0

    lax.fori_loop(0, block // 2, rows, 0)
    pairs = []
    for p in range(slabs):
        for f in range(fields):
            source = cot.at[f, main, pl.ds(p * depth, depth)]
            pairs.append((source, out.at[p, pl.ds(f * block, block)]))
    copies = start_all(pairs, sem)
    for p in range(slabs):
        for f in range(fields):
            for y in range(block):
                for side, z in ((0, p * depth - 1), (1, (p + 1) * depth)):
                    to = slice(f * block + y, f * block + y + 1)
                    if 0 <= z < order:
                        ends[p, side, to] = cot[f, y + 1, z : z + 1]
                    else:
                        ends[p, side, to] = jnp.zeros((1, width), f32)
    ends_copy = pltpu.make_async_copy(
        ends, out.at[:, pl.ds(fields * block, 2)], sem.at[len(pairs)]
    )
    ends_copy.start()
    wait_all(copies)
    ends_copy.wait()


def adjoint_step(halves, target, low_edge, high_edge, first, visc, mat_high, mat_low):
    slabs, _, block, depth, width = halves[0].shape
    order = slabs * depth
    volume = fields * (block + 1) * order * width
    return call(
        adjoint_kernel,
        [(x, anywhere()) for x in (*halves, target, low_edge, high_edge)]
        + [(x, whole()) for x in (first, visc, mat_high, mat_low)],
        [((slabs, fields * block + 2, depth, width), anywhere())],
        [
            vmem(fields, block + 2, order, width),
            vmem(fields, block + 2, order, width),
            vmem(fields, block + 2, order + 2 * pad, width),
            vmem(slabs, 2, depth, width),
        ]
        + step_scratch(order, width)
        + [dmas(slabs * (fields + 4))],
        12 * order * volume,
        "adjoint_step",
    )[0]


def last_kernel(visc, edges_below, edges_above, prior, chunks, states, out, *scratch):
    pulled, state, ends, carry, sem = scratch
    slabs = chunks.shape[0]
    rows, depth, width = visc.shape
    block = rows // slabs
    pairs = []
    for p in range(slabs):
        for f in range(fields):
            source, place = pl.ds(f * block, block), pl.ds(p * block, block)
            pairs.append((chunks.at[p, source], pulled.at[f, place, pl.ds(pad, depth)]))
            pairs.append((states.at[p, source], state.at[f, place, pl.ds(pad, depth)]))
    pairs.append((chunks.at[:, pl.ds(fields * block, 2)], ends))
    copies = start_all(pairs, sem)
    first, last = slice(pad - 1, pad), slice(pad + depth, pad + depth + 1)
    for f in range(fields):
        for y in range(rows):
            state[f, y, first] = edges_below[f, y : y + 1]
            state[f, y, last] = edges_above[f, y : y + 1]
    wait_all(copies)
    for f in range(fields):
        for y in range(rows):
            row = f * block + y % block
            pulled[f, y, first] = ends[y // block, 0, row : row + 1]
            pulled[f, y, last] = ends[y // block, 1, row : row + 1]
    here = pl.ds(pad, depth)
    above, below = pl.ds(pad + 1, depth), pl.ds(pad - 1, depth)
    along_y = 0.5 * (visc[rows - 1] + visc[0])
    for f in range(fields):
        carry[f] = along_y * (pulled[f, 0, here] - pulled[f, rows - 1, here])

    def row(y, _):
        north = lax.rem(y + 1, rows)
        own = visc[y]
        along_x = 0.5 * (own + east(own))
        along_y = 0.5 * (own + visc[north])
        speed_above, speed_below = state[W, y, above], state[W, y, below]
        coupling = pulled[T, y, here]
        for f in (U, V, T, W):
            value = pulled[f, y, here]
            flux_x = along_x * (east(value) - value)
            flux_y = along_y * (pulled[f, north, here] - value)
            rate = flux_x - west(flux_x) + (flux_y - carry[f])
            carry[f] = flux_y
            up, down = pulled[f, y, above], pulled[f, y, below]
            rate = rate + (speed_above * up - speed_below * down)
            if f == W:
                slope = speed_above - speed_below
            else:
                slope = state[f, y, above] - state[f, y, below]
            coupling = coupling - value * slope
            if f == T:
                rate = rate + pulled[W, y, here]
            if f == W:
                rate = rate + coupling
            where = pl.ds(f * depth * rows + y, depth, stride=rows)
            out[where, :] = value + time_step * rate - prior[where, :]
        return 0

    lax.fori_loop(0, rows, row, 0, unroll=4)


def last_step(visc, below, above, prior, chunks, states):
    rows, depth, width = visc.shape
    slabs = chunks.shape[0]
    return call(
        last_kernel,
        [(x, whole()) for x in (visc, below, above, prior)]
        + [(chunks, anywhere()), (states, anywhere())],
        [((fields * depth * rows, width), whole())],
        [
            vmem(fields, rows, depth + 2 * pad, width),
            vmem(fields, rows, depth + 2 * pad, width),
            vmem(slabs, 2, depth, width),
            vmem(fields, depth, width),
            dmas(2 * fields * slabs + 1),
        ],
        30 * fields * rows * depth * width,
        "last_step",
    )[0]


def exchange(chunks):
    return lax.all_to_all(chunks, "slab", split_axis=0, concat_axis=0, tiled=True)


def around(value, axis, steps):
    count = lax.axis_size(axis)
    return lax.ppermute(value, axis, [(i, (i + steps) % count) for i in range(count)])


def local(states, viscosity, inverse):
    start = states[0]
    _, depth, rows, width = start.shape
    slabs, segs = lax.axis_size("slab"), lax.axis_size("seg")
    block = rows // slabs
    share = -(-(block + 4) // segs)

    send, visc, ends = to_chunks(start, viscosity, slabs, share)
    target_planes = around(start, "seg", -1)
    chunks = exchange(send)
    forward = [(i, i + 1) for i in range(slabs - 1)]
    below = lax.ppermute(ends[1], "slab", forward)
    above = lax.ppermute(ends[0], "slab", [(i, j) for j, i in forward])
    mat_high, mat_low, adj_high, adj_low = split(inverse)

    low_rows, high_rows, visc_rows = outer_rows(chunks, share, target_planes)
    low_in = around(high_rows, "slab", 1)
    high_in = around(low_rows, "slab", -1)
    visc_in = lax.all_gather(visc_rows, "seg", axis=0)
    target = around(chunks, "seg", -1)

    first, frame = first_step(chunks, low_in, high_in, visc_in, mat_high, mat_low)
    halves = second_step(first, frame, mat_high, mat_low, slabs)
    half = exchange(halves[0])
    low_edge, high_edge = edge_rows(halves, target, half)
    low_edge, high_edge = around(high_edge, "slab", 1), around(low_edge, "slab", -1)
    pulled = adjoint_step(halves, target, low_edge, high_edge, first, frame, adj_high, adj_low)
    other = exchange(halves[1])
    residual = residual_planes((half, other), target_planes, pulled)
    prior = around(residual, "seg", 1)
    gradient = last_step(visc, below, above, prior, exchange(pulled), send)
    shape = (1, fields, depth, rows, width)
    return (residual.reshape(shape), gradient.reshape(shape))


def solution(mesh):
    in_specs = (P("seg", None, "slab", None, None), P("slab", None, None), P())
    out_specs = (P("seg", None, "slab", None, None), P("seg", None, "slab", None, None))
    return jax.shard_map(local, mesh=mesh, in_specs=in_specs, out_specs=out_specs, check_vma=False)
```

```python
import functools

import jax
import jax.numpy as jnp
from jax import lax
from jax.experimental import pallas as pl
from jax.experimental.pallas import tpu as pltpu
from jax.sharding import PartitionSpec as P

time_step = 0.1
vmem_bytes = 56 * 1024 * 1024
f32, bf16 = jnp.float32, jnp.bfloat16
U, V, W, T = range(4)
fields = 4
pad = 8
tall = 32


def whole():
    return pl.BlockSpec(memory_space=pltpu.VMEM)


def anywhere():
    return pl.BlockSpec(memory_space=pl.ANY)


def scalars():
    return pl.BlockSpec(memory_space=pltpu.SMEM)


def vmem(*shape):
    return pltpu.VMEM(shape, f32)


def dmas(count):
    return pltpu.SemaphoreType.DMA((count,))


def call(kernel, ins, outs, scratch, flops, name, kind=f32):
    moved = sum(4 * x.size for x, _ in ins)
    return pl.pallas_call(
        kernel,
        in_specs=[spec for _, spec in ins],
        out_specs=tuple(spec for _, spec in outs),
        out_shape=tuple(jax.ShapeDtypeStruct(shape, kind) for shape, _ in outs),
        scratch_shapes=scratch,
        compiler_params=pltpu.CompilerParams(vmem_limit_bytes=vmem_bytes),
        cost_estimate=pl.CostEstimate(flops=flops, bytes_accessed=moved, transcendentals=0),
        name=name,
    )(*[x for x, _ in ins])


def start_all(pairs, sem):
    copies = [
        pltpu.make_async_copy(source, target, sem.at[i])
        for i, (source, target) in enumerate(pairs)
    ]
    for copy in copies:
        copy.start()
    return copies


def wait_all(copies):
    for copy in copies:
        copy.wait()


def spans(parts):
    start = 0
    for part in parts:
        yield part, pl.ds(start, part.shape[1])
        start += part.shape[1]


def east(value):
    return pltpu.roll(value, value.shape[1] - 1, 1)


def west(value):
    return pltpu.roll(value, 1, 1)


def parts_of(value):
    high = value.astype(bf16)
    return high, (value - high.astype(f32)).astype(bf16)


def product(matrix_high, matrix_low, high, low):
    dot = functools.partial(jnp.dot, preferred_element_type=f32)
    return dot(matrix_high, high) + (dot(matrix_high, low) + dot(matrix_low, high))


def split_kernel(x_ref, high, low, adj_high, adj_low):
    for f in range(fields):
        high[f], low[f] = parts_of(x_ref[f])
        adj_high[f], adj_low[f] = parts_of(x_ref[f].T)


def split(inverse):
    return call(
        split_kernel,
        [(inverse, whole())],
        [(inverse.shape, whole())] * 4,
        [],
        0,
        "split",
        bf16,
    )


def visc_kernel(own, x_ref, visc, send):
    slabs, share = send.shape[:2]
    rows, depth, _ = visc.shape
    block = rows // slabs
    for y in range(rows):
        visc[y] = x_ref[pl.ds(y, depth, stride=rows), :]
    for p in range(slabs):
        for i in range(share):
            send[p, i] = visc[lax.rem(p * block - 2 + share * own[0] + i + rows, rows)]


def visc_chunks(viscosity, slabs, share):
    depth, rows, width = viscosity.shape
    own = jnp.full((1,), lax.axis_index("seg"), jnp.int32)
    return call(
        visc_kernel,
        [(own, scalars()), (viscosity.reshape(-1, width), whole())],
        [((rows, depth, width), whole()), ((slabs, share, depth, width), whole())],
        [],
        0,
        "visc_chunks",
    )


def chunks_kernel(start, x_ref, _, send, edges, planes, held, sem):
    count, slabs, block, depth, _ = held.shape
    rows = slabs * block
    copies = start_all([(x_ref.at[start + f], planes.at[f]) for f in range(count)], sem)
    ends = [
        pltpu.make_async_copy(x_ref.at[:, pl.ds(z * rows, rows)], edges.at[i], sem.at[count + i])
        for i, z in enumerate((0, depth - 1))
    ]
    for copy in ends:
        copy.start()
    leaving = []
    for f in range(count):
        copies[f].wait()
        for y in range(rows):
            held[f, y // block, y % block] = planes[f, pl.ds(y, depth, stride=rows), :]
        copy = pltpu.make_async_copy(held.at[f], send.at[:, f], sem.at[f])
        copy.start()
        leaving.append(copy)
    wait_all(leaving + ends)


def to_chunks(states, slabs, start, count, later):
    _, depth, rows, width = states.shape
    block = rows // slabs
    return call(
        functools.partial(chunks_kernel, start),
        [(states.reshape(fields, -1, width), anywhere()), (later, anywhere())],
        [
            ((slabs, count, block, depth, width), anywhere()),
            ((2, fields, rows, width), whole()),
        ],
        [
            vmem(count, depth * rows, width),
            vmem(count, slabs, block, depth, width),
            dmas(count + 2),
        ],
        0,
        "to_chunks",
    )


def planes_kernel(half, other, target, _, o_ref, again, held, sem):
    slabs, _, block, depth, _ = half.shape
    rows = slabs * block
    pairs = []
    for p in range(slabs):
        place = pl.ds(p * block, block)
        pairs.append((half.at[p], held.at[pl.ds(0, 2), place]))
        pairs.append((other.at[p], held.at[pl.ds(2, 2), place]))
    wait_all(start_all(pairs, sem))

    def row(y, _):
        for f in range(fields):
            where = pl.ds(f * depth * rows + y, depth, stride=rows)
            o_ref[where, :] = held[f, y] - target[where, :]
        return 0

    places = [held.at[pl.ds(2, 2), pl.ds(p * block, block)] for p in range(slabs)]
    copies = start_all([(places[p], again.at[p]) for p in range(slabs)], sem)
    lax.fori_loop(0, rows, row, 0, unroll=4)
    wait_all(copies)


def residual_planes(halves, target, later):
    slabs, _, block, depth, width = halves[0].shape
    return call(
        planes_kernel,
        [(halves[0], anywhere()), (halves[1], anywhere())]
        + [(target.reshape(-1, width), whole()), (later, anywhere())],
        [
            ((fields * depth * slabs * block, width), whole()),
            (halves[1].shape, anywhere()),
        ],
        [vmem(fields, slabs * block, depth, width), dmas(2 * slabs)],
        0,
        "residual_planes",
    )


def clear_pads(ref):
    edge = jnp.zeros(ref.shape[1:2] + (pad, ref.shape[3]), f32)
    for f in range(fields):
        ref[f, :, 0:pad] = edge
        ref[f, :, ref.shape[2] - pad :] = edge


def first_fluxes(state, visc, shift, carry):
    order = visc.shape[1]
    for z in range(0, order, tall):
        here, pads = pl.ds(z, tall), pl.ds(z + pad, tall)
        along_y = 0.5 * (visc[shift, here] + visc[shift + 1, here])
        for f in range(fields):
            carry[f, here] = along_y * (state[f, 1, pads] - state[f, 0, pads])


def spread_of(state, f, j, value, here, pads, along_x, along_y, carry):
    flux_x = along_x * (east(value) - value)
    flux_y = along_y * (state[f, j + 1, pads] - value)
    spread = flux_x - west(flux_x) + (flux_y - carry[f, here])
    carry[f, here] = flux_y
    return spread


def advance_rows(state, visc, shift, mat_high, mat_low, carry, high, low, count, finish):
    order, width = visc.shape[1:]
    first_fluxes(state, visc, shift, carry)

    def pair(k, _):
        for half in range(2):
            j = 2 * k + half + 1
            side = slice(half * width, (half + 1) * width)
            for z in range(0, order, tall):
                here, pads = pl.ds(z, tall), pl.ds(z + pad, tall)
                above, below = pl.ds(z + pad + 1, tall), pl.ds(z + pad - 1, tall)
                own = visc[j + shift, here]
                along_x = 0.5 * (own + east(own))
                along_y = 0.5 * (own + visc[j + shift + 1, here])
                speed = state[W, j, pads]
                for f in range(fields):
                    value = state[f, j, pads]
                    rate = spread_of(state, f, j, value, here, pads, along_x, along_y, carry)
                    rate = rate - speed * (state[f, j, above] - state[f, j, below])
                    if f == W:
                        rate = rate + state[T, j, pads]
                    if f == T:
                        rate = rate + speed
                    high[f, here, side], low[f, here, side] = parts_of(value + time_step * rate)
        for f in range(fields):
            out = product(mat_high[f], mat_low[f], high[f], low[f])
            finish(f, 2 * k, out[:, :width])
            finish(f, 2 * k + 1, out[:, width:])
        return 0

    lax.fori_loop(0, count // 2, pair, 0)


def step_scratch(order, width):
    return [
        vmem(fields, order, width),
        pltpu.VMEM((fields, order, 2 * width), bf16),
        pltpu.VMEM((fields, order, 2 * width), bf16),
    ]


def first_kernel(*refs):
    visc_in, mat_high, mat_low, first, visc, state, carry, high, low, sem = refs[-10:]
    halves, low_in, high_in = refs[0:2], refs[2:4], refs[4:6]
    slabs, _, block, depth, _ = halves[0].shape
    segs, _, share = visc_in.shape[:3]
    order = visc.shape[1]
    pairs = []
    for p in range(slabs):
        planes, padded = pl.ds(p * depth, depth), pl.ds(p * depth + pad, depth)
        for row, count, parts in ((0, 2, low_in), (2, block, halves), (block + 2, 2, high_in)):
            for part, span in spans(parts):
                pairs.append((part.at[p], state.at[span, pl.ds(row, count), padded]))
        for s in range(segs):
            pairs.append((visc_in.at[s, p], visc.at[pl.ds(share * s, share), planes]))
    copies = start_all(pairs, sem)
    clear_pads(state)
    clear_pads(first)
    wait_all(copies)

    def finish(f, row, piece):
        first[f, row, pl.ds(pad, order)] = piece

    advance_rows(state, visc, 0, mat_high, mat_low, carry, high, low, block + 2, finish)


def first_step(halves, low_in, high_in, later, visc_in, mat_high, mat_low):
    slabs, _, block, depth, width = halves[0].shape
    segs, _, share = visc_in.shape[:3]
    order = slabs * depth
    volume = fields * (block + 2) * order * width
    return call(
        first_kernel,
        [(x, anywhere()) for x in (*halves, *low_in, *high_in, later, visc_in)]
        + [(mat_high, whole()), (mat_low, whole())],
        [
            ((fields, block + 2, order + 2 * pad, width), whole()),
            ((segs * share, order, width), whole()),
        ],
        [vmem(fields, block + 4, order + 2 * pad, width)]
        + step_scratch(order, width)
        + [dmas(slabs * (6 + segs))],
        6 * order * volume,
        "first_step",
    )


def second_kernel(first, visc, mat_high, mat_low, _, half, other, carry, high, low, held, sem):
    slabs, _, block, depth, _ = half.shape

    def finish(f, row, piece):
        held[f, row] = piece

    advance_rows(first, visc, 1, mat_high, mat_low, carry, high, low, block, finish)
    pairs = []
    for p in range(slabs):
        planes = pl.ds(p * depth, depth)
        pairs.append((held.at[pl.ds(0, 2), :, planes], half.at[p]))
        pairs.append((held.at[pl.ds(2, 2), :, planes], other.at[p]))
    wait_all(start_all(pairs, sem))


def second_step(first, visc, mat_high, mat_low, slabs, later):
    _, block, _, width = first.shape
    block, order = block - 2, visc.shape[1]
    return call(
        second_kernel,
        [(x, whole()) for x in (first, visc, mat_high, mat_low)] + [(later, anywhere())],
        [((slabs, 2, block, order // slabs, width), anywhere())] * 2,
        step_scratch(order, width) + [vmem(fields, block, order, width), dmas(2 * slabs)],
        6 * order * fields * block * order * width,
        "second_step",
    )


def outer_kernel(chunks, _, low_rows, high_rows, sem):
    block = chunks.shape[2]
    low, high = chunks.at[:, :, pl.ds(0, 2)], chunks.at[:, :, pl.ds(block - 2, 2)]
    wait_all(start_all([(high, high_rows), (low, low_rows)], sem))


def outer_rows(chunks, later):
    slabs, _, _, depth, width = chunks.shape
    rows = ((slabs, chunks.shape[1], 2, depth, width), whole())
    return call(
        outer_kernel,
        [(chunks, anywhere()), (later, anywhere())],
        [rows, rows],
        [dmas(2)],
        0,
        "outer_rows",
    )


def edge_kernel(*refs):
    half, other, *targets, _, low_edge, high_edge, ours, theirs, sem = refs
    block = half.shape[2]
    pairs = []
    for side, row in ((0, 0), (1, block - 1)):
        for source, span in spans((half, other)):
            pairs.append((source.at[:, :, row], ours.at[side, :, span]))
        for source, span in spans(targets):
            pairs.append((source.at[:, :, row], theirs.at[side, :, span]))
    wait_all(start_all(pairs, sem))
    low_edge[...] = ours[0] - theirs[0]
    high_edge[...] = ours[1] - theirs[1]


def edge_rows(halves, targets, later):
    slabs, _, _, depth, width = halves[0].shape
    edge = ((slabs, fields, depth, width), whole())
    both = vmem(2, slabs, fields, depth, width)
    return call(
        edge_kernel,
        [(x, anywhere()) for x in (*halves, *targets, later)],
        [edge, edge],
        [both, both, dmas(4 * fields)],
        0,
        "edge_rows",
    )


def adjoint_kernel(*refs):
    half, other, *targets, low_edge, high_edge = refs[:-13]
    first, visc, mat_high, mat_low = refs[-13:-9]
    out, cot, less, pulled, ends, carry, high, low, sem = refs[-9:]
    slabs, _, block, depth, width = half.shape
    order = slabs * depth
    main = pl.ds(1, block)
    pairs = []
    for p in range(slabs):
        planes = pl.ds(p * depth, depth)
        for source, span in spans((half, other)):
            pairs.append((source.at[p], cot.at[span, main, planes]))
        for source, span in spans(targets):
            pairs.append((source.at[p], less.at[span, main, planes]))
        pairs.append((low_edge.at[p], cot.at[:, 0, planes]))
        pairs.append((high_edge.at[p], cot.at[:, block + 1, planes]))
    copies = start_all(pairs, sem)
    clear_pads(pulled)
    for f in range(fields):
        less[f, 0] = jnp.zeros((order, width), f32)
        less[f, block + 1] = jnp.zeros((order, width), f32)
    wait_all(copies)

    def pull(k, _):
        for f in range(fields):
            pair = [cot[f, 2 * k + i] - less[f, 2 * k + i] for i in range(2)]
            pair = jnp.concatenate(pair, axis=1)
            out = product(mat_high[f], mat_low[f], *parts_of(pair))
            pulled[f, 2 * k, pl.ds(pad, order)] = out[:, :width]
            pulled[f, 2 * k + 1, pl.ds(pad, order)] = out[:, width:]
        return 0

    lax.fori_loop(0, (block + 2) // 2, pull, 0)
    first_fluxes(pulled, visc, 1, carry)

    def rows(k, _):
        for half in range(2):
            j = 2 * k + half + 1
            side = slice(half * width, (half + 1) * width)
            for z in range(0, order, tall):
                here, pads = pl.ds(z, tall), pl.ds(z + pad, tall)
                above, below = pl.ds(z + pad + 1, tall), pl.ds(z + pad - 1, tall)
                own = visc[j + 1, here]
                along_x = 0.5 * (own + east(own))
                along_y = 0.5 * (own + visc[j + 2, here])
                speed_above, speed_below = first[W, j, above], first[W, j, below]
                coupling = pulled[T, j, pads]
                for f in (U, V, T, W):
                    value = pulled[f, j, pads]
                    rate = spread_of(pulled, f, j, value, here, pads, along_x, along_y, carry)
                    up, down = pulled[f, j, above], pulled[f, j, below]
                    rate = rate + (speed_above * up - speed_below * down)
                    if f == W:
                        slope = speed_above - speed_below
                    else:
                        slope = first[f, j, above] - first[f, j, below]
                    coupling = coupling - value * slope
                    if f == T:
                        rate = rate + pulled[W, j, pads]
                    if f == W:
                        rate = rate + coupling
                    high[f, here, side], low[f, here, side] = parts_of(value + time_step * rate)
        for f in range(fields):
            out = product(mat_high[f], mat_low[f], high[f], low[f])
            cot[f, 2 * k + 1] = out[:, :width]
            cot[f, 2 * k + 2] = out[:, width:]
        return 0

    lax.fori_loop(0, block // 2, rows, 0)
    pairs = []
    for p in range(slabs):
        for f in range(fields):
            source = cot.at[f, main, pl.ds(p * depth, depth)]
            pairs.append((source, out.at[p, pl.ds(f * block, block)]))
    copies = start_all(pairs, sem)
    for p in range(slabs):
        for f in range(fields):
            for y in range(block):
                for side, z in ((0, p * depth - 1), (1, (p + 1) * depth)):
                    to = slice(f * block + y, f * block + y + 1)
                    if 0 <= z < order:
                        ends[p, side, to] = cot[f, y + 1, z : z + 1]
                    else:
                        ends[p, side, to] = jnp.zeros((1, width), f32)
    ends_copy = pltpu.make_async_copy(
        ends, out.at[:, pl.ds(fields * block, 2)], sem.at[len(pairs)]
    )
    ends_copy.start()
    wait_all(copies)
    ends_copy.wait()


def adjoint_step(halves, targets, low_edge, high_edge, first, visc, mat_high, mat_low):
    slabs, _, block, depth, width = halves[0].shape
    order = slabs * depth
    volume = fields * (block + 1) * order * width
    return call(
        adjoint_kernel,
        [(x, anywhere()) for x in (*halves, *targets, low_edge, high_edge)]
        + [(x, whole()) for x in (first, visc, mat_high, mat_low)],
        [((slabs, fields * block + 2, depth, width), anywhere())],
        [
            vmem(fields, block + 2, order, width),
            vmem(fields, block + 2, order, width),
            vmem(fields, block + 2, order + 2 * pad, width),
            vmem(slabs, 2, depth, width),
        ]
        + step_scratch(order, width)
        + [dmas(slabs * (fields + 6))],
        12 * order * volume,
        "adjoint_step",
    )[0]


def last_kernel(*refs):
    visc, edges_below, edges_above, chunks, *states, half, other, out = refs[:9]
    pulled, state, prior, planes, coupling, ends, carry, sem = refs[9:]
    slabs = chunks.shape[0]
    rows, depth, width = visc.shape
    block = rows // slabs
    main = pl.ds(pad, depth)
    above, below = pl.ds(pad + 1, depth), pl.ds(pad - 1, depth)
    first, last = slice(pad - 1, pad), slice(pad + depth, pad + depth + 1)

    def arrive(f, which):
        pairs = []
        for p in range(slabs):
            place, rest = pl.ds(p * block, block), pl.ds(f * block, block)
            if which == "pulled":
                pairs.append((chunks.at[p, rest], pulled.at[f, place, main]))
            if which == "state":
                pairs.append((states[f // 2].at[p, f % 2], state.at[f, place, main]))
            if which == "prior":
                pairs.append(((half, other)[f // 2].at[p, f % 2], prior.at[f, place]))
        return [pltpu.make_async_copy(a, b, sem.at[f, which_of[which]]) for a, b in pairs]

    which_of = {"pulled": 0, "state": 1, "prior": 2}
    ends_copy = pltpu.make_async_copy(
        chunks.at[:, pl.ds(fields * block, 2)], ends, sem.at[fields, 0]
    )
    copies = {}
    for f, which in [(W, "state"), (U, "pulled"), (U, "state"), (U, "prior")] + [
        (f, which) for f in (V, T, W) for which in which_of if (f, which) != (W, "state")
    ]:
        copies[f, which] = arrive(f, which)
        for copy in copies[f, which]:
            copy.start()
        if (f, which) == (U, "pulled"):
            ends_copy.start()
    for f in range(fields):
        for y in range(rows):
            state[f, y, first] = edges_below[f, y : y + 1]
            state[f, y, last] = edges_above[f, y : y + 1]
    ends_copy.wait()
    for f in range(fields):
        for y in range(rows):
            row = f * block + y % block
            pulled[f, y, first] = ends[y // block, 0, row : row + 1]
            pulled[f, y, last] = ends[y // block, 1, row : row + 1]
    wait_all(copies[W, "state"])
    leaving = []
    for f in (U, V, T, W):
        for which in which_of:
            if (f, which) != (W, "state"):
                wait_all(copies[f, which])
        if f == T:
            wait_all(copies[W, "pulled"])
            copies[W, "pulled"] = []
        along_y = 0.5 * (visc[rows - 1] + visc[0])
        carry[...] = along_y * (pulled[f, 0, main] - pulled[f, rows - 1, main])

        def row(y, _):
            north = lax.rem(y + 1, rows)
            own = visc[y]
            along_x = 0.5 * (own + east(own))
            along_y = 0.5 * (own + visc[north])
            value = pulled[f, y, main]
            flux_x = along_x * (east(value) - value)
            flux_y = along_y * (pulled[f, north, main] - value)
            rate = flux_x - west(flux_x) + (flux_y - carry[...])
            carry[...] = flux_y
            flow = state[W, y, above] * pulled[f, y, above]
            rate = rate + (flow - state[W, y, below] * pulled[f, y, below])
            lost = value * (state[f, y, above] - state[f, y, below])
            if f == U:
                coupling[y] = lost
            elif f == V:
                coupling[y] = coupling[y] + lost
            elif f == T:
                coupling[y] = value - (coupling[y] + lost)
                rate = rate + pulled[W, y, main]
            else:
                rate = rate + (coupling[y] - lost)
            result = value + time_step * rate - (prior[f, y] - state[f, y, main])
            planes[f, pl.ds(y, depth, stride=rows), :] = result
            return 0

        lax.fori_loop(0, rows, row, 0, unroll=8)
        copy = pltpu.make_async_copy(planes.at[f], out.at[f], sem.at[fields, 1 + f])
        copy.start()
        leaving.append(copy)
    wait_all(leaving)


def last_step(visc, below, above, chunks, states, priors):
    rows, depth, width = visc.shape
    slabs = chunks.shape[0]
    return call(
        last_kernel,
        [(x, whole()) for x in (visc, below, above)]
        + [(x, anywhere()) for x in (chunks, *states, *priors)],
        [((fields, depth * rows, width), anywhere())],
        [
            vmem(fields, rows, depth + 2 * pad, width),
            vmem(fields, rows, depth + 2 * pad, width),
            vmem(fields, rows, depth, width),
            vmem(fields, depth * rows, width),
            vmem(rows, depth, width),
            vmem(slabs, 2, depth, width),
            vmem(depth, width),
            pltpu.SemaphoreType.DMA((fields + 1, fields + 1)),
        ],
        30 * fields * rows * depth * width,
        "last_step",
    )[0]


def exchange(chunks):
    return lax.all_to_all(chunks, "slab", split_axis=0, concat_axis=0, tiled=True)


def around(value, axis, steps):
    count = lax.axis_size(axis)
    return lax.ppermute(value, axis, [(i, (i + steps) % count) for i in range(count)])


def local(states, viscosity, inverse):
    start = states[0]
    _, depth, rows, width = start.shape
    slabs, segs = lax.axis_size("slab"), lax.axis_size("seg")
    share = -(-(rows // slabs + 4) // segs)

    visc, visc_send = visc_chunks(viscosity, slabs, share)
    visc_share = exchange(visc_send)
    visc_in = lax.all_gather(visc_share, "seg", axis=0)
    target_planes = around(start, "seg", -1)
    send_half, _ = to_chunks(start, slabs, 0, 2, visc_send)
    main_half = exchange(send_half)
    send_other, ends = to_chunks(start, slabs, 2, 2, visc_share)
    main_other = exchange(send_other)
    forward = [(i, i + 1) for i in range(slabs - 1)]
    below = lax.ppermute(ends[1], "slab", forward)
    above = lax.ppermute(ends[0], "slab", [(i, j) for j, i in forward])
    mat_high, mat_low, adj_high, adj_low = split(inverse)

    main = (main_half, main_other)
    low_in, high_in, later = [], [], visc_share
    for part in main:
        low_rows, high_rows = outer_rows(part, later)
        low_in.append(around(high_rows, "slab", 1))
        high_in.append(around(low_rows, "slab", -1))
        later = low_in[0]
    target = [around(part, "seg", -1) for part in main]

    first, frame = first_step(
        main, low_in, high_in, target_planes, visc_in, mat_high, mat_low
    )
    halves = second_step(first, frame, mat_high, mat_low, slabs, target[0])
    half = exchange(halves[0])
    low_edge, high_edge = edge_rows(halves, target, half)
    low_edge, high_edge = around(high_edge, "slab", 1), around(low_edge, "slab", -1)
    pulled = adjoint_step(halves, target, low_edge, high_edge, first, frame, adj_high, adj_low)
    residual, other = residual_planes((half, exchange(halves[1])), target_planes, pulled)
    priors = [around(part, "seg", 1) for part in (half, other)]
    gradient = last_step(visc, below, above, exchange(pulled), (send_half, send_other), priors)
    shape = (1, fields, depth, rows, width)
    return (residual.reshape(shape), gradient.reshape(shape))


def solution(mesh):
    in_specs = (P("seg", None, "slab", None, None), P("slab", None, None), P())
    out_specs = (P("seg", None, "slab", None, None), P("seg", None, "slab", None, None))
    return jax.shard_map(local, mesh=mesh, in_specs=in_specs, out_specs=out_specs, check_vma=False)
```

```python
import functools

import jax
import jax.numpy as jnp
from jax import lax
from jax.experimental import pallas as pl
from jax.experimental.pallas import tpu as pltpu
from jax.sharding import PartitionSpec as P

time_step = 0.1
vmem_bytes = 56 * 1024 * 1024
f32, bf16 = jnp.float32, jnp.bfloat16
U, V, W, T = range(4)
fields = 4
pad = 8
tall = 32


def whole():
    return pl.BlockSpec(memory_space=pltpu.VMEM)


def anywhere():
    return pl.BlockSpec(memory_space=pl.ANY)


def scalars():
    return pl.BlockSpec(memory_space=pltpu.SMEM)


def vmem(*shape):
    return pltpu.VMEM(shape, f32)


def dmas(count):
    return pltpu.SemaphoreType.DMA((count,))


def call(kernel, ins, outs, scratch, flops, name, kind=f32):
    moved = sum(4 * x.size for x, _ in ins)
    return pl.pallas_call(
        kernel,
        in_specs=[spec for _, spec in ins],
        out_specs=tuple(spec for _, spec in outs),
        out_shape=tuple(jax.ShapeDtypeStruct(shape, kind) for shape, _ in outs),
        scratch_shapes=scratch,
        compiler_params=pltpu.CompilerParams(vmem_limit_bytes=vmem_bytes),
        cost_estimate=pl.CostEstimate(flops=flops, bytes_accessed=moved, transcendentals=0),
        name=name,
    )(*[x for x, _ in ins])


def start_all(pairs, sem):
    copies = [
        pltpu.make_async_copy(source, target, sem.at[i])
        for i, (source, target) in enumerate(pairs)
    ]
    for copy in copies:
        copy.start()
    return copies


def wait_all(copies):
    for copy in copies:
        copy.wait()


def spans(parts):
    start = 0
    for part in parts:
        yield part, pl.ds(start, part.shape[1])
        start += part.shape[1]


def east(value):
    return pltpu.roll(value, value.shape[1] - 1, 1)


def west(value):
    return pltpu.roll(value, 1, 1)


def parts_of(value):
    high = value.astype(bf16)
    return high, (value - high.astype(f32)).astype(bf16)


def product(matrix_high, matrix_low, high, low):
    dot = functools.partial(jnp.dot, preferred_element_type=f32)
    return dot(matrix_high, high) + (dot(matrix_high, low) + dot(matrix_low, high))


def split_kernel(x_ref, high, low, adj_high, adj_low):
    for f in range(fields):
        high[f], low[f] = parts_of(x_ref[f])
        adj_high[f], adj_low[f] = parts_of(x_ref[f].T)


def split(inverse):
    return call(
        split_kernel,
        [(inverse, whole())],
        [(inverse.shape, whole())] * 4,
        [],
        0,
        "split",
        bf16,
    )


def visc_kernel(own, x_ref, visc, send):
    slabs, share = send.shape[:2]
    rows, depth, _ = visc.shape
    block = rows // slabs
    for y in range(rows):
        visc[y] = x_ref[pl.ds(y, depth, stride=rows), :]
    for p in range(slabs):
        for i in range(share):
            send[p, i] = visc[lax.rem(p * block - 2 + share * own[0] + i + rows, rows)]


def visc_chunks(viscosity, slabs, share):
    depth, rows, width = viscosity.shape
    own = jnp.full((1,), lax.axis_index("seg"), jnp.int32)
    return call(
        visc_kernel,
        [(own, scalars()), (viscosity.reshape(-1, width), whole())],
        [((rows, depth, width), whole()), ((slabs, share, depth, width), whole())],
        [],
        0,
        "visc_chunks",
    )


def chunks_kernel(start, x_ref, _, send, edges, planes, held, sem):
    count, slabs, block, depth, _ = held.shape
    rows = slabs * block
    copies = start_all([(x_ref.at[start + f], planes.at[f]) for f in range(count)], sem)
    ends = [
        pltpu.make_async_copy(x_ref.at[:, pl.ds(z * rows, rows)], edges.at[i], sem.at[count + i])
        for i, z in enumerate((0, depth - 1))
    ]
    for copy in ends:
        copy.start()
    leaving = []
    for f in range(count):
        copies[f].wait()
        for y in range(rows):
            held[f, y // block, y % block] = planes[f, pl.ds(y, depth, stride=rows), :]
        copy = pltpu.make_async_copy(held.at[f], send.at[:, f], sem.at[f])
        copy.start()
        leaving.append(copy)
    wait_all(leaving + ends)


def to_chunks(states, slabs, start, count, later):
    _, depth, rows, width = states.shape
    block = rows // slabs
    return call(
        functools.partial(chunks_kernel, start),
        [(states.reshape(fields, -1, width), anywhere()), (later, anywhere())],
        [
            ((slabs, count, block, depth, width), anywhere()),
            ((2, fields, rows, width), whole()),
        ],
        [
            vmem(count, depth * rows, width),
            vmem(count, slabs, block, depth, width),
            dmas(count + 2),
        ],
        0,
        "to_chunks",
    )


def planes_kernel(half, other, _, o_ref, again, held, sem):
    slabs, _, block, depth, _ = half.shape
    rows = slabs * block
    pairs = []
    for p in range(slabs):
        place = pl.ds(p * block, block)
        pairs.append((half.at[p], held.at[pl.ds(0, 2), place]))
        pairs.append((other.at[p], held.at[pl.ds(2, 2), place]))
    wait_all(start_all(pairs, sem))
    places = [held.at[pl.ds(2, 2), pl.ds(p * block, block)] for p in range(slabs)]
    copies = start_all([(places[p], again.at[p]) for p in range(slabs)], sem)

    def row(y, _):
        for f in range(fields):
            o_ref[pl.ds(f * depth * rows + y, depth, stride=rows), :] = held[f, y]
        return 0

    lax.fori_loop(0, rows, row, 0, unroll=4)
    wait_all(copies)


def to_planes(halves, later):
    slabs, _, block, depth, width = halves[0].shape
    return call(
        planes_kernel,
        [(x, anywhere()) for x in (*halves, later)],
        [
            ((fields * depth * slabs * block, width), whole()),
            (halves[1].shape, anywhere()),
        ],
        [vmem(fields, slabs * block, depth, width), dmas(2 * slabs)],
        0,
        "to_planes",
    )


def clear_pads(ref):
    edge = jnp.zeros(ref.shape[1:2] + (pad, ref.shape[3]), f32)
    for f in range(fields):
        ref[f, :, 0:pad] = edge
        ref[f, :, ref.shape[2] - pad :] = edge


def first_fluxes(state, visc, shift, carry, some=range(fields)):
    order = visc.shape[1]
    for z in range(0, order, tall):
        here, pads = pl.ds(z, tall), pl.ds(z + pad, tall)
        along_y = 0.5 * (visc[shift, here] + visc[shift + 1, here])
        for f in some:
            carry[f, here] = along_y * (state[f, 1, pads] - state[f, 0, pads])


def spread_of(state, f, j, value, here, pads, along_x, along_y, carry):
    flux_x = along_x * (east(value) - value)
    flux_y = along_y * (state[f, j + 1, pads] - value)
    spread = flux_x - west(flux_x) + (flux_y - carry[f, here])
    carry[f, here] = flux_y
    return spread


def advance_rows(state, visc, shift, mats, scratch, count, finish, some=range(fields)):
    mat_high, mat_low, carry, high, low = *mats, *scratch
    order, width = visc.shape[1:]
    first_fluxes(state, visc, shift, carry, some)

    def pair(k, _):
        for half in range(2):
            j = 2 * k + half + 1
            side = slice(half * width, (half + 1) * width)
            for z in range(0, order, tall):
                here, pads = pl.ds(z, tall), pl.ds(z + pad, tall)
                above, below = pl.ds(z + pad + 1, tall), pl.ds(z + pad - 1, tall)
                own = visc[j + shift, here]
                along_x = 0.5 * (own + east(own))
                along_y = 0.5 * (own + visc[j + shift + 1, here])
                speed = state[W, j, pads]
                for f in some:
                    value = state[f, j, pads]
                    rate = spread_of(state, f, j, value, here, pads, along_x, along_y, carry)
                    rate = rate - speed * (state[f, j, above] - state[f, j, below])
                    if f == W:
                        rate = rate + state[T, j, pads]
                    if f == T:
                        rate = rate + speed
                    high[f, here, side], low[f, here, side] = parts_of(value + time_step * rate)
        for f in some:
            out = product(mat_high[f], mat_low[f], high[f], low[f])
            finish(f, 2 * k, out[:, :width])
            finish(f, 2 * k + 1, out[:, width:])
        return 0

    lax.fori_loop(0, count // 2, pair, 0)


def step_scratch(order, width):
    return [
        vmem(fields, order, width),
        pltpu.VMEM((fields, order, 2 * width), bf16),
        pltpu.VMEM((fields, order, 2 * width), bf16),
    ]


def first_kernel(*refs):
    visc_in, mat_high, mat_low, first, visc, state, carry, high, low, sem = refs[-10:]
    halves, low_in, high_in = refs[0:2], refs[2:4], refs[4:6]
    slabs, _, block, depth, _ = halves[0].shape
    segs, _, share = visc_in.shape[:3]
    order = visc.shape[1]
    pairs = []
    for p in range(slabs):
        planes, padded = pl.ds(p * depth, depth), pl.ds(p * depth + pad, depth)
        for row, count, parts in ((0, 2, low_in), (2, block, halves), (block + 2, 2, high_in)):
            for part, span in spans(parts):
                pairs.append((part.at[p], state.at[span, pl.ds(row, count), padded]))
        for s in range(segs):
            pairs.append((visc_in.at[s, p], visc.at[pl.ds(share * s, share), planes]))
    copies = start_all(pairs, sem)
    clear_pads(state)
    clear_pads(first)
    wait_all(copies)

    def finish(f, row, piece):
        first[f, row, pl.ds(pad, order)] = piece

    scratch = (carry, high, low)
    advance_rows(state, visc, 0, (mat_high, mat_low), scratch, block + 2, finish)


def first_step(halves, low_in, high_in, visc_in, mat_high, mat_low):
    slabs, _, block, depth, width = halves[0].shape
    segs, _, share = visc_in.shape[:3]
    order = slabs * depth
    volume = fields * (block + 2) * order * width
    return call(
        first_kernel,
        [(x, anywhere()) for x in (*halves, *low_in, *high_in, visc_in)]
        + [(mat_high, whole()), (mat_low, whole())],
        [
            ((fields, block + 2, order + 2 * pad, width), whole()),
            ((segs * share, order, width), whole()),
        ],
        [vmem(fields, block + 4, order + 2 * pad, width)]
        + step_scratch(order, width)
        + [dmas(slabs * (6 + segs))],
        6 * order * volume,
        "first_step",
    )


def second_kernel(some, first, visc, mat_high, mat_low, target, out, low_edge, high_edge, *rest):
    state, *scratch, held, sem = rest
    slabs, _, block, depth, _ = out.shape
    needed = pl.ds(min(some), 3) if W not in some else pl.ds(W, 2)
    places = [held.at[:, :, pl.ds(p * depth, depth)] for p in range(slabs)]
    pairs = [(target.at[p], places[p]) for p in range(slabs)]
    pairs.append((first.at[needed], state.at[needed]))
    wait_all(start_all(pairs, sem))

    def finish(f, row, piece):
        held[f - some[0], row] = piece - held[f - some[0], row]

    advance_rows(state, visc, 1, (mat_high, mat_low), scratch, block, finish, some)
    copies = start_all([(places[p], out.at[p]) for p in range(slabs)], sem)
    low_edge[...] = held[:, 0]
    high_edge[...] = held[:, block - 1]
    wait_all(copies)


def second_step(first, visc, mat_high, mat_low, some, target):
    width, order = visc.shape[2], visc.shape[1]
    slabs, _, block, _, _ = target.shape
    return call(
        functools.partial(second_kernel, some),
        [(first, anywhere())]
        + [(x, whole()) for x in (visc, mat_high, mat_low)]
        + [(target, anywhere())],
        [(target.shape, anywhere())] + [((2, order, width), whole())] * 2,
        [vmem(*first.shape)]
        + step_scratch(order, width)
        + [vmem(2, block, order, width), dmas(slabs + 1)],
        6 * order * 2 * block * order * width,
        "second_step",
    )


def outer_kernel(chunks, _, low_rows, high_rows, again, sem):
    block = chunks.shape[2]
    wait_all(start_all([(chunks, again)], sem))
    low_rows[...] = again[:, :, 0:2]
    high_rows[...] = again[:, :, block - 2 :]


def outer_rows(chunks, later):
    slabs, count, _, depth, width = chunks.shape
    rows = ((slabs, count, 2, depth, width), whole())
    return call(
        outer_kernel,
        [(chunks, anywhere()), (later, anywhere())],
        [rows, rows, (chunks.shape, whole())],
        [dmas(1)],
        0,
        "outer_rows",
    )


def adjoint_kernel(*refs):
    halves, low_edges, high_edges = refs[0:2], refs[2:4], refs[4:6]
    first, visc, mat_high, mat_low = refs[6:10]
    out, cot, pulled, ends, carry, high, low, sem = refs[10:]
    slabs, _, block, depth, width = halves[0].shape
    order = slabs * depth
    main = pl.ds(1, block)
    pairs = []
    for source, span in spans(halves):
        for p in range(slabs):
            pairs.append((source.at[p], cot.at[span, main, pl.ds(p * depth, depth)]))
    for i in range(2):
        pairs.append((low_edges[i], cot.at[pl.ds(2 * i, 2), 0]))
        pairs.append((high_edges[i], cot.at[pl.ds(2 * i, 2), block + 1]))
    copies = start_all(pairs, sem)
    clear_pads(pulled)
    wait_all(copies)

    def pull(k, _):
        for f in range(fields):
            pair = jnp.concatenate([cot[f, 2 * k], cot[f, 2 * k + 1]], axis=1)
            out = product(mat_high[f], mat_low[f], *parts_of(pair))
            pulled[f, 2 * k, pl.ds(pad, order)] = out[:, :width]
            pulled[f, 2 * k + 1, pl.ds(pad, order)] = out[:, width:]
        return 0

    lax.fori_loop(0, (block + 2) // 2, pull, 0)
    first_fluxes(pulled, visc, 1, carry)

    def rows(k, _):
        for half in range(2):
            j = 2 * k + half + 1
            side = slice(half * width, (half + 1) * width)
            for z in range(0, order, tall):
                here, pads = pl.ds(z, tall), pl.ds(z + pad, tall)
                above, below = pl.ds(z + pad + 1, tall), pl.ds(z + pad - 1, tall)
                own = visc[j + 1, here]
                along_x = 0.5 * (own + east(own))
                along_y = 0.5 * (own + visc[j + 2, here])
                speed_above, speed_below = first[W, j, above], first[W, j, below]
                coupling = pulled[T, j, pads]
                for f in (U, V, T, W):
                    value = pulled[f, j, pads]
                    rate = spread_of(pulled, f, j, value, here, pads, along_x, along_y, carry)
                    up, down = pulled[f, j, above], pulled[f, j, below]
                    rate = rate + (speed_above * up - speed_below * down)
                    if f == W:
                        slope = speed_above - speed_below
                    else:
                        slope = first[f, j, above] - first[f, j, below]
                    coupling = coupling - value * slope
                    if f == T:
                        rate = rate + pulled[W, j, pads]
                    if f == W:
                        rate = rate + coupling
                    high[f, here, side], low[f, here, side] = parts_of(value + time_step * rate)
        for f in range(fields):
            out = product(mat_high[f], mat_low[f], high[f], low[f])
            cot[f, 2 * k + 1] = out[:, :width]
            cot[f, 2 * k + 2] = out[:, width:]
        return 0

    lax.fori_loop(0, block // 2, rows, 0)
    pairs = []
    for p in range(slabs):
        for f in range(fields):
            source = cot.at[f, main, pl.ds(p * depth, depth)]
            pairs.append((source, out.at[p, pl.ds(f * block, block)]))
    copies = start_all(pairs, sem)
    for p in range(slabs):
        for f in range(fields):
            for y in range(block):
                for side, z in ((0, p * depth - 1), (1, (p + 1) * depth)):
                    to = slice(f * block + y, f * block + y + 1)
                    if 0 <= z < order:
                        ends[p, side, to] = cot[f, y + 1, z : z + 1]
                    else:
                        ends[p, side, to] = jnp.zeros((1, width), f32)
    ends_copy = pltpu.make_async_copy(
        ends, out.at[:, pl.ds(fields * block, 2)], sem.at[len(pairs)]
    )
    ends_copy.start()
    wait_all(copies)
    ends_copy.wait()


def adjoint_step(halves, low_edges, high_edges, first, visc, mat_high, mat_low):
    slabs, _, block, depth, width = halves[0].shape
    order = slabs * depth
    volume = fields * (block + 1) * order * width
    return call(
        adjoint_kernel,
        [(x, anywhere()) for x in (*halves, *low_edges, *high_edges)]
        + [(x, whole()) for x in (first, visc, mat_high, mat_low)],
        [((slabs, fields * block + 2, depth, width), anywhere())],
        [
            vmem(fields, block + 2, order, width),
            vmem(fields, block + 2, order + 2 * pad, width),
            vmem(slabs, 2, depth, width),
        ]
        + step_scratch(order, width)
        + [dmas(slabs * fields + 1)],
        12 * order * volume,
        "adjoint_step",
    )[0]


def last_kernel(*refs):
    visc, edges_below, edges_above, chunks, *states, half, other, out = refs[:9]
    pulled, state, prior, planes, coupling, ends, carry, sem = refs[9:]
    slabs = chunks.shape[0]
    rows, depth, width = visc.shape
    block = rows // slabs
    main = pl.ds(pad, depth)
    above, below = pl.ds(pad + 1, depth), pl.ds(pad - 1, depth)
    first, last = slice(pad - 1, pad), slice(pad + depth, pad + depth + 1)

    def arrive(f, which):
        pairs = []
        for p in range(slabs):
            place, rest = pl.ds(p * block, block), pl.ds(f * block, block)
            if which == "pulled":
                pairs.append((chunks.at[p, rest], pulled.at[f, place, main]))
            if which == "state":
                pairs.append((states[f // 2].at[p, f % 2], state.at[f, place, main]))
            if which == "prior":
                pairs.append(((half, other)[f // 2].at[p, f % 2], prior.at[f, place]))
        return [pltpu.make_async_copy(a, b, sem.at[f, which_of[which]]) for a, b in pairs]

    which_of = {"pulled": 0, "state": 1, "prior": 2}
    ends_copy = pltpu.make_async_copy(
        chunks.at[:, pl.ds(fields * block, 2)], ends, sem.at[fields, 0]
    )
    copies = {}
    for f, which in [(W, "state"), (U, "pulled"), (U, "state"), (U, "prior")] + [
        (f, which) for f in (V, T, W) for which in which_of if (f, which) != (W, "state")
    ]:
        copies[f, which] = arrive(f, which)
        for copy in copies[f, which]:
            copy.start()
        if (f, which) == (U, "pulled"):
            ends_copy.start()
    for f in range(fields):
        for y in range(rows):
            state[f, y, first] = edges_below[f, y : y + 1]
            state[f, y, last] = edges_above[f, y : y + 1]
    ends_copy.wait()
    for f in range(fields):
        for y in range(rows):
            row = f * block + y % block
            pulled[f, y, first] = ends[y // block, 0, row : row + 1]
            pulled[f, y, last] = ends[y // block, 1, row : row + 1]
    wait_all(copies[W, "state"])
    leaving = []
    for f in (U, V, T, W):
        for which in which_of:
            if (f, which) != (W, "state"):
                wait_all(copies[f, which])
        if f == T:
            wait_all(copies[W, "pulled"])
            copies[W, "pulled"] = []
        along_y = 0.5 * (visc[rows - 1] + visc[0])
        carry[...] = along_y * (pulled[f, 0, main] - pulled[f, rows - 1, main])

        def row(y, _):
            north = lax.rem(y + 1, rows)
            own = visc[y]
            along_x = 0.5 * (own + east(own))
            along_y = 0.5 * (own + visc[north])
            value = pulled[f, y, main]
            flux_x = along_x * (east(value) - value)
            flux_y = along_y * (pulled[f, north, main] - value)
            rate = flux_x - west(flux_x) + (flux_y - carry[...])
            carry[...] = flux_y
            flow = state[W, y, above] * pulled[f, y, above]
            rate = rate + (flow - state[W, y, below] * pulled[f, y, below])
            lost = value * (state[f, y, above] - state[f, y, below])
            if f == U:
                coupling[y] = lost
            elif f == V:
                coupling[y] = coupling[y] + lost
            elif f == T:
                coupling[y] = value - (coupling[y] + lost)
                rate = rate + pulled[W, y, main]
            else:
                rate = rate + (coupling[y] - lost)
            result = value + time_step * rate - prior[f, y]
            planes[f, pl.ds(y, depth, stride=rows), :] = result
            return 0

        lax.fori_loop(0, rows, row, 0, unroll=8)
        copy = pltpu.make_async_copy(planes.at[f], out.at[f], sem.at[fields, 1 + f])
        copy.start()
        leaving.append(copy)
    wait_all(leaving)


def last_step(visc, below, above, chunks, states, priors):
    rows, depth, width = visc.shape
    slabs = chunks.shape[0]
    return call(
        last_kernel,
        [(x, whole()) for x in (visc, below, above)]
        + [(x, anywhere()) for x in (chunks, *states, *priors)],
        [((fields, depth * rows, width), anywhere())],
        [
            vmem(fields, rows, depth + 2 * pad, width),
            vmem(fields, rows, depth + 2 * pad, width),
            vmem(fields, rows, depth, width),
            vmem(fields, depth * rows, width),
            vmem(rows, depth, width),
            vmem(slabs, 2, depth, width),
            vmem(depth, width),
            pltpu.SemaphoreType.DMA((fields + 1, fields + 1)),
        ],
        30 * fields * rows * depth * width,
        "last_step",
    )[0]


def exchange(chunks):
    return lax.all_to_all(chunks, "slab", split_axis=0, concat_axis=0, tiled=True)


def around(value, axis, steps):
    count = lax.axis_size(axis)
    return lax.ppermute(value, axis, [(i, (i + steps) % count) for i in range(count)])


def local(states, viscosity, inverse):
    start = states[0]
    _, depth, rows, width = start.shape
    slabs, segs = lax.axis_size("slab"), lax.axis_size("seg")
    share = -(-(rows // slabs + 4) // segs)

    visc, visc_send = visc_chunks(viscosity, slabs, share)
    visc_share = exchange(visc_send)
    visc_in = lax.all_gather(visc_share, "seg", axis=0)
    send_half, _ = to_chunks(start, slabs, 0, 2, visc_send)
    main_half = exchange(send_half)
    send_other, ends = to_chunks(start, slabs, 2, 2, visc_share)
    main_other = exchange(send_other)
    forward = [(i, i + 1) for i in range(slabs - 1)]
    below = lax.ppermute(ends[1], "slab", forward)
    above = lax.ppermute(ends[0], "slab", [(i, j) for j, i in forward])
    mat_high, mat_low, adj_high, adj_low = split(inverse)

    main = (main_half, main_other)
    low_in, high_in, target, later = [], [], [], visc_in
    for part in main:
        low_rows, high_rows, again = outer_rows(part, later)
        low_in.append(around(high_rows, "slab", 1))
        high_in.append(around(low_rows, "slab", -1))
        target.append(around(again, "seg", -1))
        later = low_in[0]

    first, frame = first_step(main, low_in, high_in, visc_in, mat_high, mat_low)
    residual, low_edges, high_edges = [], [], []
    for some, part in zip(((U, V), (W, T)), target):
        out, low_edge, high_edge = second_step(first, frame, mat_high, mat_low, some, part)
        residual.append(out)
        low_edges.append(around(high_edge, "slab", 1))
        high_edges.append(around(low_edge, "slab", -1))
    half = exchange(residual[0])
    pulled = adjoint_step(residual, low_edges, high_edges, first, frame, adj_high, adj_low)
    planes, other = to_planes((half, exchange(residual[1])), pulled)
    priors = [around(part, "seg", 1) for part in (half, other)]
    gradient = last_step(visc, below, above, exchange(pulled), (send_half, send_other), priors)
    shape = (1, fields, depth, rows, width)
    return (planes.reshape(shape), gradient.reshape(shape))


def solution(mesh):
    in_specs = (P("seg", None, "slab", None, None), P("slab", None, None), P())
    out_specs = (P("seg", None, "slab", None, None), P("seg", None, "slab", None, None))
    return jax.shard_map(local, mesh=mesh, in_specs=in_specs, out_specs=out_specs, check_vma=False)
```

```python
import functools

import jax
import jax.numpy as jnp
from jax import lax
from jax.experimental import pallas as pl
from jax.experimental.pallas import tpu as pltpu
from jax.sharding import PartitionSpec as P

time_step = 0.1
vmem_bytes = 56 * 1024 * 1024
f32, bf16 = jnp.float32, jnp.bfloat16
fields = 4
W, T, U, V = range(4)
outside = (2, 3, 0, 1)
pad = 8
tall = 32


def whole():
    return pl.BlockSpec(memory_space=pltpu.VMEM)


def anywhere():
    return pl.BlockSpec(memory_space=pl.ANY)


def scalars():
    return pl.BlockSpec(memory_space=pltpu.SMEM)


def vmem(*shape):
    return pltpu.VMEM(shape, f32)


def dmas(count):
    return pltpu.SemaphoreType.DMA((count,))


def call(kernel, ins, outs, scratch, flops, name, kind=f32):
    moved = sum(4 * x.size for x, _ in ins)
    return pl.pallas_call(
        kernel,
        in_specs=[spec for _, spec in ins],
        out_specs=tuple(spec for _, spec in outs),
        out_shape=tuple(jax.ShapeDtypeStruct(shape, kind) for shape, _ in outs),
        scratch_shapes=scratch,
        compiler_params=pltpu.CompilerParams(vmem_limit_bytes=vmem_bytes),
        cost_estimate=pl.CostEstimate(flops=flops, bytes_accessed=moved, transcendentals=0),
        name=name,
    )(*[x for x, _ in ins])


def start_all(pairs, sem):
    copies = [
        pltpu.make_async_copy(source, target, sem.at[i])
        for i, (source, target) in enumerate(pairs)
    ]
    for copy in copies:
        copy.start()
    return copies


def wait_all(copies):
    for copy in copies:
        copy.wait()


def spans(parts):
    start = 0
    for part in parts:
        yield part, pl.ds(start, part.shape[1])
        start += part.shape[1]


def east(value):
    return pltpu.roll(value, value.shape[1] - 1, 1)


def west(value):
    return pltpu.roll(value, 1, 1)


def parts_of(value):
    high = value.astype(bf16)
    return high, (value - high.astype(f32)).astype(bf16)


def product(matrix_high, matrix_low, high, low):
    dot = functools.partial(jnp.dot, preferred_element_type=f32)
    return dot(matrix_high, high) + (dot(matrix_high, low) + dot(matrix_low, high))


def split_kernel(x_ref, high, low, adj_high, adj_low):
    for f in range(fields):
        high[f], low[f] = parts_of(x_ref[outside[f]])
        adj_high[f], adj_low[f] = parts_of(x_ref[outside[f]].T)


def split(inverse):
    return call(
        split_kernel,
        [(inverse, whole())],
        [(inverse.shape, whole())] * 4,
        [],
        0,
        "split",
        bf16,
    )


def visc_kernel(own, x_ref, visc, send):
    slabs, share = send.shape[:2]
    rows, depth, _ = visc.shape
    block = rows // slabs
    for y in range(rows):
        visc[y] = x_ref[pl.ds(y, depth, stride=rows), :]
    for p in range(slabs):
        for i in range(share):
            send[p, i] = visc[lax.rem(p * block - 2 + share * own[0] + i + rows, rows)]


def visc_chunks(viscosity, slabs, share):
    depth, rows, width = viscosity.shape
    own = jnp.full((1,), lax.axis_index("seg"), jnp.int32)
    return call(
        visc_kernel,
        [(own, scalars()), (viscosity.reshape(-1, width), whole())],
        [((rows, depth, width), whole()), ((slabs, share, depth, width), whole())],
        [],
        0,
        "visc_chunks",
    )


def chunks_kernel(start, x_ref, _, send, edges, planes, held, sem):
    count, slabs, block, depth, _ = held.shape
    rows = slabs * block
    copies = start_all([(x_ref.at[start + f], planes.at[f]) for f in range(count)], sem)
    ends = [
        pltpu.make_async_copy(x_ref.at[:, pl.ds(z * rows, rows)], edges.at[i], sem.at[count + i])
        for i, z in enumerate((0, depth - 1))
    ]
    for copy in ends:
        copy.start()
    leaving = []
    for f in range(count):
        copies[f].wait()
        for y in range(rows):
            held[f, y // block, y % block] = planes[f, pl.ds(y, depth, stride=rows), :]
        copy = pltpu.make_async_copy(held.at[f], send.at[:, f], sem.at[f])
        copy.start()
        leaving.append(copy)
    wait_all(leaving + ends)


def to_chunks(states, slabs, start, count, later):
    _, depth, rows, width = states.shape
    block = rows // slabs
    return call(
        functools.partial(chunks_kernel, start),
        [(states.reshape(fields, -1, width), anywhere()), (later, anywhere())],
        [
            ((slabs, count, block, depth, width), anywhere()),
            ((2, fields, rows, width), whole()),
        ],
        [
            vmem(count, depth * rows, width),
            vmem(count, slabs, block, depth, width),
            dmas(count + 2),
        ],
        0,
        "to_chunks",
    )


def planes_kernel(half, other, _, o_ref, again, held, sem):
    slabs, _, block, depth, _ = half.shape
    rows = slabs * block
    pairs = []
    for p in range(slabs):
        place = pl.ds(p * block, block)
        pairs.append((half.at[p], held.at[pl.ds(0, 2), place]))
        pairs.append((other.at[p], held.at[pl.ds(2, 2), place]))
    wait_all(start_all(pairs, sem))
    places = [held.at[pl.ds(2, 2), pl.ds(p * block, block)] for p in range(slabs)]
    copies = start_all([(places[p], again.at[p]) for p in range(slabs)], sem)

    def row(y, _):
        for f in range(fields):
            where = pl.ds(outside[f] * depth * rows + y, depth, stride=rows)
            o_ref[where, :] = held[f, y]
        return 0

    lax.fori_loop(0, rows, row, 0, unroll=4)
    wait_all(copies)


def to_planes(halves, later):
    slabs, _, block, depth, width = halves[0].shape
    return call(
        planes_kernel,
        [(x, anywhere()) for x in (*halves, later)],
        [
            ((fields * depth * slabs * block, width), whole()),
            (halves[1].shape, anywhere()),
        ],
        [vmem(fields, slabs * block, depth, width), dmas(2 * slabs)],
        0,
        "to_planes",
    )


def clear_pads(ref):
    edge = jnp.zeros(ref.shape[1:2] + (pad, ref.shape[3]), f32)
    for f in range(ref.shape[0]):
        ref[f, :, 0:pad] = edge
        ref[f, :, ref.shape[2] - pad :] = edge


def first_fluxes(state, visc, shift, carry):
    order = visc.shape[1]
    for z in range(0, order, tall):
        here, pads = pl.ds(z, tall), pl.ds(z + pad, tall)
        along_y = 0.5 * (visc[shift, here] + visc[shift + 1, here])
        for f in range(state.shape[0]):
            carry[f, here] = along_y * (state[f, 1, pads] - state[f, 0, pads])


def spread_of(state, f, j, value, here, pads, along_x, along_y, carry):
    flux_x = along_x * (east(value) - value)
    flux_y = along_y * (state[f, j + 1, pads] - value)
    spread = flux_x - west(flux_x) + (flux_y - carry[f, here])
    carry[f, here] = flux_y
    return spread


def advance_rows(state, speeds, visc, shift, mats, base, scratch, count, finish):
    mat_high, mat_low, carry, high, low = *mats, *scratch
    order, width = visc.shape[1:]
    first_fluxes(state, visc, shift, carry)

    def pair(k, _):
        for half in range(2):
            j = 2 * k + half + 1
            side = slice(half * width, (half + 1) * width)
            for z in range(0, order, tall):
                here, pads = pl.ds(z, tall), pl.ds(z + pad, tall)
                above, below = pl.ds(z + pad + 1, tall), pl.ds(z + pad - 1, tall)
                own = visc[j + shift, here]
                along_x = 0.5 * (own + east(own))
                along_y = 0.5 * (own + visc[j + shift + 1, here])
                speed = speeds[j, pads]
                for f in range(2):
                    value = state[f, j, pads]
                    rate = spread_of(state, f, j, value, here, pads, along_x, along_y, carry)
                    rate = rate - speed * (state[f, j, above] - state[f, j, below])
                    if base == W:
                        rate = rate + state[1 - f, j, pads]
                    high[f, here, side], low[f, here, side] = parts_of(value + time_step * rate)
        for f in range(2):
            out = product(mat_high[base + f], mat_low[base + f], high[f], low[f])
            finish(f, 2 * k, out[:, :width])
            finish(f, 2 * k + 1, out[:, width:])
        return 0

    lax.fori_loop(0, count // 2, pair, 0)


def step_scratch(order, width, count):
    return [
        vmem(count, order, width),
        pltpu.VMEM((count, order, 2 * width), bf16),
        pltpu.VMEM((count, order, 2 * width), bf16),
    ]


def rows_of(low_in, main, high_in, p, target):
    _, _, block, depth, _ = main.shape
    padded = pl.ds(p * depth + pad, depth)
    for row, count, part in ((0, 2, low_in), (2, block, main), (block + 2, 2, high_in)):
        yield part, target.at[:, pl.ds(row, count), padded]


def first_finish(first, order):
    def finish(f, row, piece):
        first[f, row, pl.ds(pad, order)] = piece

    return finish


def first_kernel(low_in, main, high_in, visc_in, mat_high, mat_low, first, visc, *scratch):
    state, *scratch, sem = scratch
    slabs, _, block, depth, _ = main.shape
    segs, _, share = visc_in.shape[:3]
    pairs = []
    for p in range(slabs):
        pairs += [(a.at[p], b) for a, b in rows_of(low_in, main, high_in, p, state)]
        planes = pl.ds(p * depth, depth)
        for i in range(segs):
            pairs.append((visc_in.at[i, p], visc.at[pl.ds(share * i, share), planes]))
    copies = start_all(pairs, sem)
    clear_pads(state)
    clear_pads(first)
    wait_all(copies)
    mats, finish = (mat_high, mat_low), first_finish(first, slabs * depth)
    advance_rows(state, state.at[W], visc, 0, mats, W, scratch, block + 2, finish)


def first_step(low_in, main, high_in, visc_in, mat_high, mat_low):
    slabs, _, block, depth, width = main.shape
    segs, _, share = visc_in.shape[:3]
    order = slabs * depth
    volume = 2 * (block + 2) * order * width
    return call(
        first_kernel,
        [(x, anywhere()) for x in (low_in, main, high_in, visc_in)]
        + [(mat_high, whole()), (mat_low, whole())],
        [
            ((2, block + 2, order + 2 * pad, width), whole()),
            ((segs * share, order, width), whole()),
        ],
        [vmem(2, block + 4, order + 2 * pad, width)]
        + step_scratch(order, width, 2)
        + [dmas(slabs * (3 + segs))],
        6 * order * volume,
        "first_step",
    )


def carried_kernel(*refs):
    low_in, main, high_in, low_w, main_w, high_w, _, _, visc, mat_high, mat_low = refs[:11]
    first, state, speeds, *scratch, sem = refs[11:]
    slabs, _, block, depth, _ = main.shape
    pairs = []
    for p in range(slabs):
        pairs += [(a.at[p], b) for a, b in rows_of(low_in, main, high_in, p, state)]
        w_rows = rows_of(low_w, main_w, high_w, p, speeds)
        pairs += [(a.at[p, pl.ds(W, 1)], b) for a, b in w_rows]
    copies = start_all(pairs, sem)
    clear_pads(state)
    clear_pads(first)
    wait_all(copies)
    mats, finish = (mat_high, mat_low), first_finish(first, slabs * depth)
    advance_rows(state, speeds.at[0], visc, 0, mats, U, scratch, block + 2, finish)


def carried_step(own, with_w, later, visc, mat_high, mat_low):
    slabs, _, block, depth, width = own[1].shape
    order = slabs * depth
    volume = 2 * (block + 2) * order * width
    return call(
        carried_kernel,
        [(x, anywhere()) for x in (*own, *with_w, *later)]
        + [(x, whole()) for x in (visc, mat_high, mat_low)],
        [((2, block + 2, order + 2 * pad, width), whole())],
        [
            vmem(2, block + 4, order + 2 * pad, width),
            vmem(1, block + 4, order + 2 * pad, width),
        ]
        + step_scratch(order, width, 2)
        + [dmas(6 * slabs)],
        6 * order * volume,
        "carried_step",
    )[0]


def second_kernel(base, first, with_w, visc, mat_high, mat_low, *refs):
    targets, (out, low_edge, high_edge, state, speeds) = refs[:-10], refs[-10:-5]
    *scratch, held, sem = refs[-5:]
    slabs, _, block, depth, _ = out.shape
    places = [held.at[:, :, pl.ds(p * depth, depth)] for p in range(slabs)]
    pairs = [(first, state)] + ([(with_w.at[W], speeds)] if base != W else [])
    for target, span in spans(targets):
        for p in range(slabs):
            pairs.append((target.at[p], held.at[span, :, pl.ds(p * depth, depth)]))
    wait_all(start_all(pairs, sem))

    def finish(f, row, piece):
        held[f, row] = piece - held[f, row]

    mats, speeds = (mat_high, mat_low), state.at[W] if base == W else speeds
    advance_rows(state, speeds, visc, 1, mats, base, scratch, block, finish)
    copies = start_all([(places[p], out.at[p]) for p in range(slabs)], sem)
    low_edge[...] = held[:, 0]
    high_edge[...] = held[:, block - 1]
    wait_all(copies)


def second_step(first, with_w, visc, mat_high, mat_low, base, targets):
    width, order = visc.shape[2], visc.shape[1]
    slabs, _, block, depth, _ = targets[0].shape
    return call(
        functools.partial(second_kernel, base),
        [(first, anywhere()), (with_w, anywhere())]
        + [(x, whole()) for x in (visc, mat_high, mat_low)]
        + [(x, anywhere()) for x in targets],
        [((slabs, 2, block, depth, width), anywhere())] + [((2, order, width), whole())] * 2,
        [vmem(*first.shape), vmem(*first.shape[1:])]
        + step_scratch(order, width, 2)
        + [vmem(2, block, order, width), dmas(2 * slabs + 2)],
        6 * order * 2 * block * order * width,
        "second_step",
    )


def after_kernel(x_ref, *refs):
    o_ref, sem = refs[-2:]
    wait_all(start_all([(x_ref, o_ref)], sem))


def after(value, later):
    return call(
        after_kernel,
        [(x, anywhere()) for x in (value, *later)],
        [(value.shape, whole())],
        [dmas(1)],
        0,
        "after",
    )[0]


def outer_kernel(chunks, _, low_rows, high_rows, *refs):
    *again, sem = refs
    block = chunks.shape[2]
    pairs = [(chunks.at[:, span], part) for part, span in spans(again)]
    wait_all(start_all(pairs, sem))
    for part, span in spans(again):
        low_rows[:, span] = part[:, :, 0:2]
        high_rows[:, span] = part[:, :, block - 2 :]


def outer_rows(chunks, later, pieces):
    slabs, count, block, depth, width = chunks.shape
    rows = ((slabs, count, 2, depth, width), whole())
    again = ((slabs, count // pieces, block, depth, width), whole())
    return call(
        outer_kernel,
        [(chunks, anywhere()), (later, anywhere())],
        [rows, rows] + [again] * pieces,
        [dmas(pieces)],
        0,
        "outer_rows",
    )


def adjoint_kernel(*refs):
    halves, low_edges, high_edges = refs[0:2], refs[2:4], refs[4:6]
    firsts, (visc, mat_high, mat_low) = refs[6:8], refs[8:11]
    out, cot, pulled, ends, carry, high, low, sem = refs[11:]
    slabs, _, block, depth, width = halves[0].shape
    order = slabs * depth
    main = pl.ds(1, block)
    pairs = []
    for source, span in spans(halves):
        for p in range(slabs):
            pairs.append((source.at[p], cot.at[span, main, pl.ds(p * depth, depth)]))
    for i in range(2):
        pairs.append((low_edges[i], cot.at[pl.ds(2 * i, 2), 0]))
        pairs.append((high_edges[i], cot.at[pl.ds(2 * i, 2), block + 1]))
    copies = start_all(pairs, sem)
    clear_pads(pulled)
    wait_all(copies)

    def pull(k, _):
        for f in range(fields):
            pair = jnp.concatenate([cot[f, 2 * k], cot[f, 2 * k + 1]], axis=1)
            out = product(mat_high[f], mat_low[f], *parts_of(pair))
            pulled[f, 2 * k, pl.ds(pad, order)] = out[:, :width]
            pulled[f, 2 * k + 1, pl.ds(pad, order)] = out[:, width:]
        return 0

    lax.fori_loop(0, (block + 2) // 2, pull, 0)
    first_fluxes(pulled, visc, 1, carry)

    def rows(k, _):
        for half in range(2):
            j = 2 * k + half + 1
            side = slice(half * width, (half + 1) * width)
            for z in range(0, order, tall):
                here, pads = pl.ds(z, tall), pl.ds(z + pad, tall)
                above, below = pl.ds(z + pad + 1, tall), pl.ds(z + pad - 1, tall)
                own = visc[j + 1, here]
                along_x = 0.5 * (own + east(own))
                along_y = 0.5 * (own + visc[j + 2, here])
                speed_above, speed_below = firsts[0][W, j, above], firsts[0][W, j, below]
                coupling = pulled[T, j, pads]
                for f in (U, V, T, W):
                    value = pulled[f, j, pads]
                    rate = spread_of(pulled, f, j, value, here, pads, along_x, along_y, carry)
                    up, down = pulled[f, j, above], pulled[f, j, below]
                    rate = rate + (speed_above * up - speed_below * down)
                    if f == W:
                        slope = speed_above - speed_below
                    else:
                        ref, i = firsts[f // 2], f % 2
                        slope = ref[i, j, above] - ref[i, j, below]
                    coupling = coupling - value * slope
                    if f == T:
                        rate = rate + pulled[W, j, pads]
                    if f == W:
                        rate = rate + coupling
                    high[f, here, side], low[f, here, side] = parts_of(value + time_step * rate)
        for f in range(fields):
            out = product(mat_high[f], mat_low[f], high[f], low[f])
            cot[f, 2 * k + 1] = out[:, :width]
            cot[f, 2 * k + 2] = out[:, width:]
        return 0

    lax.fori_loop(0, block // 2, rows, 0)
    pairs = []
    for p in range(slabs):
        for f in range(fields):
            source = cot.at[f, main, pl.ds(p * depth, depth)]
            pairs.append((source, out.at[p, pl.ds(f * block, block)]))
    copies = start_all(pairs, sem)
    for p in range(slabs):
        for f in range(fields):
            for y in range(block):
                for side, z in ((0, p * depth - 1), (1, (p + 1) * depth)):
                    to = slice(f * block + y, f * block + y + 1)
                    if 0 <= z < order:
                        ends[p, side, to] = cot[f, y + 1, z : z + 1]
                    else:
                        ends[p, side, to] = jnp.zeros((1, width), f32)
    ends_copy = pltpu.make_async_copy(
        ends, out.at[:, pl.ds(fields * block, 2)], sem.at[len(pairs)]
    )
    ends_copy.start()
    wait_all(copies)
    ends_copy.wait()


def adjoint_step(halves, low_edges, high_edges, firsts, visc, mat_high, mat_low):
    slabs, _, block, depth, width = halves[0].shape
    order = slabs * depth
    volume = fields * (block + 1) * order * width
    return call(
        adjoint_kernel,
        [(x, anywhere()) for x in (*halves, *low_edges, *high_edges)]
        + [(x, whole()) for x in (*firsts, visc, mat_high, mat_low)],
        [((slabs, fields * block + 2, depth, width), anywhere())],
        [
            vmem(fields, block + 2, order, width),
            vmem(fields, block + 2, order + 2 * pad, width),
            vmem(slabs, 2, depth, width),
        ]
        + step_scratch(order, width, fields)
        + [dmas(slabs * fields + 1)],
        12 * order * volume,
        "adjoint_step",
    )[0]


def last_kernel(*refs):
    visc, edges_below, edges_above, chunks, *states, half, other, out = refs[:9]
    pulled, state, prior, planes, coupling, ends, carry, sem = refs[9:]
    slabs = chunks.shape[0]
    rows, depth, width = visc.shape
    block = rows // slabs
    main = pl.ds(pad, depth)
    above, below = pl.ds(pad + 1, depth), pl.ds(pad - 1, depth)
    first, last = slice(pad - 1, pad), slice(pad + depth, pad + depth + 1)

    def arrive(f, which):
        pairs = []
        for p in range(slabs):
            place, rest = pl.ds(p * block, block), pl.ds(f * block, block)
            if which == "pulled":
                pairs.append((chunks.at[p, rest], pulled.at[f, place, main]))
            if which == "state":
                pairs.append((states[f // 2].at[p, f % 2], state.at[f, place, main]))
            if which == "prior":
                pairs.append(((half, other)[f // 2].at[p, f % 2], prior.at[f, place]))
        return [pltpu.make_async_copy(a, b, sem.at[f, which_of[which]]) for a, b in pairs]

    which_of = {"pulled": 0, "state": 1, "prior": 2}
    ends_copy = pltpu.make_async_copy(
        chunks.at[:, pl.ds(fields * block, 2)], ends, sem.at[fields, 0]
    )
    copies = {}
    for f, which in [(W, "state"), (U, "pulled"), (U, "state"), (U, "prior")] + [
        (f, which) for f in (V, T, W) for which in which_of if (f, which) != (W, "state")
    ]:
        copies[f, which] = arrive(f, which)
        for copy in copies[f, which]:
            copy.start()
        if (f, which) == (U, "pulled"):
            ends_copy.start()
    for f in range(fields):
        for y in range(rows):
            state[f, y, first] = edges_below[outside[f], y : y + 1]
            state[f, y, last] = edges_above[outside[f], y : y + 1]
    ends_copy.wait()
    for f in range(fields):
        for y in range(rows):
            row = f * block + y % block
            pulled[f, y, first] = ends[y // block, 0, row : row + 1]
            pulled[f, y, last] = ends[y // block, 1, row : row + 1]
    wait_all(copies[W, "state"])
    leaving = []
    for f in (U, V, T, W):
        for which in which_of:
            if (f, which) != (W, "state"):
                wait_all(copies[f, which])
        if f == T:
            wait_all(copies[W, "pulled"])
            copies[W, "pulled"] = []
        along_y = 0.5 * (visc[rows - 1] + visc[0])
        carry[...] = along_y * (pulled[f, 0, main] - pulled[f, rows - 1, main])

        def row(y, _):
            north = lax.rem(y + 1, rows)
            own = visc[y]
            along_x = 0.5 * (own + east(own))
            along_y = 0.5 * (own + visc[north])
            value = pulled[f, y, main]
            flux_x = along_x * (east(value) - value)
            flux_y = along_y * (pulled[f, north, main] - value)
            rate = flux_x - west(flux_x) + (flux_y - carry[...])
            carry[...] = flux_y
            flow = state[W, y, above] * pulled[f, y, above]
            rate = rate + (flow - state[W, y, below] * pulled[f, y, below])
            lost = value * (state[f, y, above] - state[f, y, below])
            if f == U:
                coupling[y] = lost
            elif f == V:
                coupling[y] = coupling[y] + lost
            elif f == T:
                coupling[y] = value - (coupling[y] + lost)
                rate = rate + pulled[W, y, main]
            else:
                rate = rate + (coupling[y] - lost)
            result = value + time_step * rate - prior[f, y]
            planes[f, pl.ds(y, depth, stride=rows), :] = result
            return 0

        lax.fori_loop(0, rows, row, 0, unroll=8)
        copy = pltpu.make_async_copy(planes.at[f], out.at[outside[f]], sem.at[fields, 1 + f])
        copy.start()
        leaving.append(copy)
    wait_all(leaving)


def last_step(visc, below, above, chunks, states, priors):
    rows, depth, width = visc.shape
    slabs = chunks.shape[0]
    return call(
        last_kernel,
        [(x, whole()) for x in (visc, below, above)]
        + [(x, anywhere()) for x in (chunks, *states, *priors)],
        [((fields, depth * rows, width), anywhere())],
        [
            vmem(fields, rows, depth + 2 * pad, width),
            vmem(fields, rows, depth + 2 * pad, width),
            vmem(fields, rows, depth, width),
            vmem(fields, depth * rows, width),
            vmem(rows, depth, width),
            vmem(slabs, 2, depth, width),
            vmem(depth, width),
            pltpu.SemaphoreType.DMA((fields + 1, fields + 1)),
        ],
        30 * fields * rows * depth * width,
        "last_step",
    )[0]


def exchange(chunks):
    return lax.all_to_all(chunks, "slab", split_axis=0, concat_axis=0, tiled=True)


def around(value, axis, steps):
    count = lax.axis_size(axis)
    return lax.ppermute(value, axis, [(i, (i + steps) % count) for i in range(count)])


def local(states, viscosity, inverse):
    start = states[0]
    _, depth, rows, width = start.shape
    slabs, segs = lax.axis_size("slab"), lax.axis_size("seg")
    share = -(-(rows // slabs + 4) // segs)

    visc, visc_send = visc_chunks(viscosity, slabs, share)
    visc_share = exchange(visc_send)
    visc_in = lax.all_gather(visc_share, "seg", axis=0)
    send_half, _ = to_chunks(start, slabs, outside[W], 2, visc_send)
    main_half = exchange(send_half)
    send_other, ends = to_chunks(start, slabs, outside[U], 2, visc_share)
    main_other = exchange(send_other)
    forward = [(i, i + 1) for i in range(slabs - 1)]
    below = lax.ppermute(ends[1], "slab", forward)
    above = lax.ppermute(ends[0], "slab", [(i, j) for j, i in forward])
    mat_high, mat_low, adj_high, adj_low = split(inverse)

    own, targets, later = [], [], visc_in
    for part, pieces in ((main_half, 1), (main_other, 2)):
        low_rows, high_rows, *again = outer_rows(part, later, pieces)
        low_in = around(high_rows, "slab", 1)
        own.append((low_in, part, around(low_rows, "slab", -1)))
        targets.append([around(piece, "seg", -1) for piece in again])
        later = low_in

    mats = mat_high, mat_low
    first_half, frame = first_step(*own[0], visc_in, *mats)
    out, low_edge, high_edge = second_step(first_half, first_half, frame, *mats, W, targets[0])
    first_other = carried_step(own[1], own[0], (targets[1][0], out), frame, *mats)
    other, *more = second_step(first_other, first_half, frame, *mats, U, targets[1])
    low_edges = [around(edge, "slab", 1) for edge in (high_edge, more[1])]
    high_edges = [around(edge, "slab", -1) for edge in (low_edge, more[0])]
    half = exchange(out)
    residual = (out, after(other, (*low_edges, *high_edges, half)))
    firsts = (first_half, first_other)
    pulled = adjoint_step(residual, low_edges, high_edges, firsts, frame, adj_high, adj_low)
    planes, other = to_planes((half, exchange(residual[1])), pulled)
    priors = [around(part, "seg", 1) for part in (half, other)]
    gradient = last_step(visc, below, above, exchange(pulled), (send_half, send_other), priors)
    shape = (1, fields, depth, rows, width)
    return (planes.reshape(shape), gradient.reshape(shape))


def solution(mesh):
    in_specs = (P("seg", None, "slab", None, None), P("slab", None, None), P())
    out_specs = (P("seg", None, "slab", None, None), P("seg", None, "slab", None, None))
    return jax.shard_map(local, mesh=mesh, in_specs=in_specs, out_specs=out_specs, check_vma=False)
```

```python
import functools

import jax
import jax.numpy as jnp
from jax import lax
from jax.experimental import pallas as pl
from jax.experimental.pallas import tpu as pltpu
from jax.sharding import PartitionSpec as P

time_step = 0.1
vmem_bytes = 56 * 1024 * 1024
f32, bf16 = jnp.float32, jnp.bfloat16
fields = 4
W, T, U, V = range(4)
outside = (2, 3, 0, 1)
pad = 8
tall = 32


def whole():
    return pl.BlockSpec(memory_space=pltpu.VMEM)


def anywhere():
    return pl.BlockSpec(memory_space=pl.ANY)


def scalars():
    return pl.BlockSpec(memory_space=pltpu.SMEM)


def vmem(*shape):
    return pltpu.VMEM(shape, f32)


def dmas(count):
    return pltpu.SemaphoreType.DMA((count,))


def call(kernel, ins, outs, scratch, flops, name, kind=f32):
    moved = sum(4 * x.size for x, _ in ins)
    return pl.pallas_call(
        kernel,
        in_specs=[spec for _, spec in ins],
        out_specs=tuple(spec for _, spec in outs),
        out_shape=tuple(jax.ShapeDtypeStruct(shape, kind) for shape, _ in outs),
        scratch_shapes=scratch,
        compiler_params=pltpu.CompilerParams(vmem_limit_bytes=vmem_bytes),
        cost_estimate=pl.CostEstimate(flops=flops, bytes_accessed=moved, transcendentals=0),
        name=name,
    )(*[x for x, _ in ins])


def start_all(pairs, sem):
    copies = [
        pltpu.make_async_copy(source, target, sem.at[i])
        for i, (source, target) in enumerate(pairs)
    ]
    for copy in copies:
        copy.start()
    return copies


def wait_all(copies):
    for copy in copies:
        copy.wait()


def spans(parts):
    start = 0
    for part in parts:
        yield part, pl.ds(start, part.shape[1])
        start += part.shape[1]


def east(value):
    return pltpu.roll(value, value.shape[1] - 1, 1)


def west(value):
    return pltpu.roll(value, 1, 1)


def parts_of(value):
    high = value.astype(bf16)
    return high, (value - high.astype(f32)).astype(bf16)


def product(matrix_high, matrix_low, high, low):
    dot = functools.partial(jnp.dot, preferred_element_type=f32)
    return dot(matrix_high, high) + (dot(matrix_high, low) + dot(matrix_low, high))


def split_kernel(x_ref, high, low, adj_high, adj_low):
    for f in range(fields):
        high[f], low[f] = parts_of(x_ref[outside[f]])
        adj_high[f], adj_low[f] = parts_of(x_ref[outside[f]].T)


def split(inverse):
    return call(
        split_kernel,
        [(inverse, whole())],
        [(inverse.shape, whole())] * 4,
        [],
        0,
        "split",
        bf16,
    )


def visc_kernel(own, x_ref, visc, send):
    slabs, share = send.shape[:2]
    rows, depth, _ = visc.shape
    block = rows // slabs
    for y in range(rows):
        visc[y] = x_ref[pl.ds(y, depth, stride=rows), :]
    for p in range(slabs):
        for i in range(share):
            send[p, i] = visc[lax.rem(p * block - 2 + share * own[0] + i + rows, rows)]


def visc_chunks(own, viscosity, slabs, share):
    depth, rows, width = viscosity.shape
    return call(
        visc_kernel,
        [(own, scalars()), (viscosity.reshape(-1, width), whole())],
        [((rows, depth, width), whole()), ((slabs, share, depth, width), whole())],
        [],
        0,
        "visc_chunks",
    )


def chunks_kernel(start, x_ref, *refs):
    send, edges, planes, held, sem = refs[-5:]
    count, slabs, block, depth, _ = held.shape
    rows = slabs * block
    copies = start_all([(x_ref.at[start + f], planes.at[f]) for f in range(count)], sem)
    ends = [
        pltpu.make_async_copy(x_ref.at[:, pl.ds(z * rows, rows)], edges.at[i], sem.at[count + i])
        for i, z in enumerate((0, depth - 1))
    ]
    for copy in ends:
        copy.start()
    leaving = []
    for f in range(count):
        copies[f].wait()
        for y in range(rows):
            held[f, y // block, y % block] = planes[f, pl.ds(y, depth, stride=rows), :]
        copy = pltpu.make_async_copy(held.at[f], send.at[:, f], sem.at[f])
        copy.start()
        leaving.append(copy)
    wait_all(leaving + ends)


def to_chunks(states, slabs, start, count, later):
    _, depth, rows, width = states.shape
    block = rows // slabs
    return call(
        functools.partial(chunks_kernel, start),
        [(states.reshape(fields, -1, width), anywhere())]
        + [(x, anywhere()) for x in later],
        [
            ((slabs, count, block, depth, width), anywhere()),
            ((2, fields, rows, width), whole()),
        ],
        [
            vmem(count, depth * rows, width),
            vmem(count, slabs, block, depth, width),
            dmas(count + 2),
        ],
        0,
        "to_chunks",
    )


def planes_kernel(half, other, _, o_ref, again, held, sem):
    slabs, _, block, depth, _ = half.shape
    rows = slabs * block
    pairs = []
    for p in range(slabs):
        place = pl.ds(p * block, block)
        pairs.append((half.at[p], held.at[pl.ds(0, 2), place]))
        pairs.append((other.at[p], held.at[pl.ds(2, 2), place]))
    wait_all(start_all(pairs, sem))
    places = [held.at[pl.ds(2, 2), pl.ds(p * block, block)] for p in range(slabs)]
    copies = start_all([(places[p], again.at[p]) for p in range(slabs)], sem)

    def row(y, _):
        for f in range(fields):
            where = pl.ds(outside[f] * depth * rows + y, depth, stride=rows)
            o_ref[where, :] = held[f, y]
        return 0

    lax.fori_loop(0, rows, row, 0, unroll=4)
    wait_all(copies)


def to_planes(halves, later):
    slabs, _, block, depth, width = halves[0].shape
    return call(
        planes_kernel,
        [(x, anywhere()) for x in (*halves, later)],
        [
            ((fields * depth * slabs * block, width), whole()),
            (halves[1].shape, anywhere()),
        ],
        [vmem(fields, slabs * block, depth, width), dmas(2 * slabs)],
        0,
        "to_planes",
    )


def clear_pads(ref):
    edge = jnp.zeros(ref.shape[1:2] + (pad, ref.shape[3]), f32)
    for f in range(ref.shape[0]):
        ref[f, :, 0:pad] = edge
        ref[f, :, ref.shape[2] - pad :] = edge


def first_fluxes(state, visc, shift, carry):
    order = visc.shape[1]
    for z in range(0, order, tall):
        here, pads = pl.ds(z, tall), pl.ds(z + pad, tall)
        along_y = 0.5 * (visc[shift, here] + visc[shift + 1, here])
        for f in range(state.shape[0]):
            carry[f, here] = along_y * (state[f, 1, pads] - state[f, 0, pads])


def spread_of(state, f, j, value, here, pads, along_x, along_y, carry):
    flux_x = along_x * (east(value) - value)
    flux_y = along_y * (state[f, j + 1, pads] - value)
    spread = flux_x - west(flux_x) + (flux_y - carry[f, here])
    carry[f, here] = flux_y
    return spread


def advance_rows(state, speeds, visc, shift, mats, base, scratch, count, finish):
    mat_high, mat_low, carry, high, low = *mats, *scratch
    order, width = visc.shape[1:]
    first_fluxes(state, visc, shift, carry)

    def pair(k, _):
        for half in range(2):
            j = 2 * k + half + 1
            side = slice(half * width, (half + 1) * width)
            for z in range(0, order, tall):
                here, pads = pl.ds(z, tall), pl.ds(z + pad, tall)
                above, below = pl.ds(z + pad + 1, tall), pl.ds(z + pad - 1, tall)
                own = visc[j + shift, here]
                along_x = 0.5 * (own + east(own))
                along_y = 0.5 * (own + visc[j + shift + 1, here])
                speed = speeds[j, pads]
                for f in range(2):
                    value = state[f, j, pads]
                    rate = spread_of(state, f, j, value, here, pads, along_x, along_y, carry)
                    rate = rate - speed * (state[f, j, above] - state[f, j, below])
                    if base == W:
                        rate = rate + state[1 - f, j, pads]
                    high[f, here, side], low[f, here, side] = parts_of(value + time_step * rate)
        for f in range(2):
            out = product(mat_high[base + f], mat_low[base + f], high[f], low[f])
            finish(f, 2 * k, out[:, :width])
            finish(f, 2 * k + 1, out[:, width:])
        return 0

    lax.fori_loop(0, count // 2, pair, 0)


def step_scratch(order, width, count):
    return [
        vmem(count, order, width),
        pltpu.VMEM((count, order, 2 * width), bf16),
        pltpu.VMEM((count, order, 2 * width), bf16),
    ]


def rows_of(low_in, main, high_in, p, target):
    _, _, block, depth, _ = main.shape
    padded = pl.ds(p * depth + pad, depth)
    for row, count, part in ((0, 2, low_in), (2, block, main), (block + 2, 2, high_in)):
        yield part, target.at[:, pl.ds(row, count), padded]


def first_finish(first, order):
    def finish(f, row, piece):
        first[f, row, pl.ds(pad, order)] = piece

    return finish


def first_kernel(segs, own, low_in, main, high_in, _, mat_high, mat_low, *refs):
    visc_in, (first, visc, state, *scratch, sem) = refs[:segs], refs[segs:]
    slabs, _, block, depth, _ = main.shape
    share = visc_in[0].shape[1]
    pairs = []
    for p in range(slabs):
        pairs += [(a.at[p], b) for a, b in rows_of(low_in, main, high_in, p, state)]
        planes = pl.ds(p * depth, depth)
        for i in range(segs):
            start = lax.rem(own[0] + i, segs) * share
            pairs.append((visc_in[i].at[p], visc.at[pl.ds(start, share), planes]))
    copies = start_all(pairs, sem)
    clear_pads(state)
    clear_pads(first)
    wait_all(copies)
    mats, finish = (mat_high, mat_low), first_finish(first, slabs * depth)
    advance_rows(state, state.at[W], visc, 0, mats, W, scratch, block + 2, finish)


def first_step(own, low_in, main, high_in, later, visc_in, mat_high, mat_low):
    slabs, _, block, depth, width = main.shape
    segs, share = len(visc_in), visc_in[0].shape[1]
    order = slabs * depth
    volume = 2 * (block + 2) * order * width
    return call(
        functools.partial(first_kernel, segs),
        [(own, scalars())]
        + [(x, anywhere()) for x in (low_in, main, high_in, later)]
        + [(mat_high, whole()), (mat_low, whole())]
        + [(x, anywhere()) for x in visc_in],
        [
            ((2, block + 2, order + 2 * pad, width), whole()),
            ((segs * share, order, width), whole()),
        ],
        [vmem(2, block + 4, order + 2 * pad, width)]
        + step_scratch(order, width, 2)
        + [dmas(slabs * (3 + segs))],
        6 * order * volume,
        "first_step",
    )


def carried_kernel(*refs):
    low_in, main, high_in, low_w, main_w, high_w, _, _, visc, mat_high, mat_low = refs[:11]
    first, state, speeds, *scratch, sem = refs[11:]
    slabs, _, block, depth, _ = main.shape
    pairs = []
    for p in range(slabs):
        pairs += [(a.at[p], b) for a, b in rows_of(low_in, main, high_in, p, state)]
        w_rows = rows_of(low_w, main_w, high_w, p, speeds)
        pairs += [(a.at[p, pl.ds(W, 1)], b) for a, b in w_rows]
    copies = start_all(pairs, sem)
    clear_pads(state)
    clear_pads(first)
    wait_all(copies)
    mats, finish = (mat_high, mat_low), first_finish(first, slabs * depth)
    advance_rows(state, speeds.at[0], visc, 0, mats, U, scratch, block + 2, finish)


def carried_step(own, with_w, later, visc, mat_high, mat_low):
    slabs, _, block, depth, width = own[1].shape
    order = slabs * depth
    volume = 2 * (block + 2) * order * width
    return call(
        carried_kernel,
        [(x, anywhere()) for x in (*own, *with_w, *later)]
        + [(x, whole()) for x in (visc, mat_high, mat_low)],
        [((2, block + 2, order + 2 * pad, width), whole())],
        [
            vmem(2, block + 4, order + 2 * pad, width),
            vmem(1, block + 4, order + 2 * pad, width),
        ]
        + step_scratch(order, width, 2)
        + [dmas(6 * slabs)],
        6 * order * volume,
        "carried_step",
    )[0]


def second_kernel(base, first, with_w, visc, mat_high, mat_low, *refs):
    targets, (_, _, out, low_edge, high_edge, state, speeds) = refs[:-12], refs[-12:-5]
    *scratch, held, sem = refs[-5:]
    slabs, _, block, depth, _ = out.shape
    places = [held.at[:, :, pl.ds(p * depth, depth)] for p in range(slabs)]
    pairs = [(first, state)] + ([(with_w.at[W], speeds)] if base != W else [])
    for target, span in spans(targets):
        for p in range(slabs):
            pairs.append((target.at[p], held.at[span, :, pl.ds(p * depth, depth)]))
    wait_all(start_all(pairs, sem))

    def finish(f, row, piece):
        held[f, row] = piece - held[f, row]

    mats, speeds = (mat_high, mat_low), state.at[W] if base == W else speeds
    advance_rows(state, speeds, visc, 1, mats, base, scratch, block, finish)
    copies = start_all([(places[p], out.at[p]) for p in range(slabs)], sem)
    low_edge[...] = held[:, 0]
    high_edge[...] = held[:, block - 1]
    wait_all(copies)


def second_step(first, with_w, visc, mat_high, mat_low, base, targets, later):
    width, order = visc.shape[2], visc.shape[1]
    slabs, _, block, depth, _ = targets[0].shape
    return call(
        functools.partial(second_kernel, base),
        [(first, anywhere()), (with_w, anywhere())]
        + [(x, whole()) for x in (visc, mat_high, mat_low)]
        + [(x, anywhere()) for x in (*targets, *later)],
        [((slabs, 2, block, depth, width), anywhere())] + [((2, order, width), whole())] * 2,
        [vmem(*first.shape), vmem(*first.shape[1:])]
        + step_scratch(order, width, 2)
        + [vmem(2, block, order, width), dmas(2 * slabs + 2)],
        6 * order * 2 * block * order * width,
        "second_step",
    )


def after_kernel(x_ref, *refs):
    o_ref, sem = refs[-2:]
    wait_all(start_all([(x_ref, o_ref)], sem))


def after(value, later):
    return call(
        after_kernel,
        [(x, anywhere()) for x in (value, *later)],
        [(value.shape, whole())],
        [dmas(1)],
        0,
        "after",
    )[0]


def outer_kernel(chunks, _, low_rows, high_rows, *refs):
    *again, sem = refs
    block = chunks.shape[2]
    pairs = [(chunks.at[:, span], part) for part, span in spans(again)]
    wait_all(start_all(pairs, sem))
    for part, span in spans(again):
        low_rows[:, span] = part[:, :, 0:2]
        high_rows[:, span] = part[:, :, block - 2 :]


def outer_rows(chunks, later, pieces):
    slabs, count, block, depth, width = chunks.shape
    rows = ((slabs, count, 2, depth, width), whole())
    again = ((slabs, count // pieces, block, depth, width), whole())
    return call(
        outer_kernel,
        [(chunks, anywhere()), (later, anywhere())],
        [rows, rows] + [again] * pieces,
        [dmas(pieces)],
        0,
        "outer_rows",
    )


def adjoint_kernel(*refs):
    halves, low_edges, high_edges = refs[0:2], refs[2:4], refs[4:6]
    firsts, (visc, mat_high, mat_low) = refs[6:8], refs[8:11]
    out, cot, pulled, ends, carry, high, low, sem = refs[11:]
    slabs, _, block, depth, width = halves[0].shape
    order = slabs * depth
    main = pl.ds(1, block)
    pairs = []
    for source, span in spans(halves):
        for p in range(slabs):
            pairs.append((source.at[p], cot.at[span, main, pl.ds(p * depth, depth)]))
    for i in range(2):
        pairs.append((low_edges[i], cot.at[pl.ds(2 * i, 2), 0]))
        pairs.append((high_edges[i], cot.at[pl.ds(2 * i, 2), block + 1]))
    copies = start_all(pairs, sem)
    clear_pads(pulled)
    wait_all(copies)

    def pull(k, _):
        for f in range(fields):
            pair = jnp.concatenate([cot[f, 2 * k], cot[f, 2 * k + 1]], axis=1)
            out = product(mat_high[f], mat_low[f], *parts_of(pair))
            pulled[f, 2 * k, pl.ds(pad, order)] = out[:, :width]
            pulled[f, 2 * k + 1, pl.ds(pad, order)] = out[:, width:]
        return 0

    lax.fori_loop(0, (block + 2) // 2, pull, 0)
    first_fluxes(pulled, visc, 1, carry)

    def rows(k, _):
        for half in range(2):
            j = 2 * k + half + 1
            side = slice(half * width, (half + 1) * width)
            for z in range(0, order, tall):
                here, pads = pl.ds(z, tall), pl.ds(z + pad, tall)
                above, below = pl.ds(z + pad + 1, tall), pl.ds(z + pad - 1, tall)
                own = visc[j + 1, here]
                along_x = 0.5 * (own + east(own))
                along_y = 0.5 * (own + visc[j + 2, here])
                speed_above, speed_below = firsts[0][W, j, above], firsts[0][W, j, below]
                coupling = pulled[T, j, pads]
                for f in (U, V, T, W):
                    value = pulled[f, j, pads]
                    rate = spread_of(pulled, f, j, value, here, pads, along_x, along_y, carry)
                    up, down = pulled[f, j, above], pulled[f, j, below]
                    rate = rate + (speed_above * up - speed_below * down)
                    if f == W:
                        slope = speed_above - speed_below
                    else:
                        ref, i = firsts[f // 2], f % 2
                        slope = ref[i, j, above] - ref[i, j, below]
                    coupling = coupling - value * slope
                    if f == T:
                        rate = rate + pulled[W, j, pads]
                    if f == W:
                        rate = rate + coupling
                    high[f, here, side], low[f, here, side] = parts_of(value + time_step * rate)
        for f in range(fields):
            out = product(mat_high[f], mat_low[f], high[f], low[f])
            cot[f, 2 * k + 1] = out[:, :width]
            cot[f, 2 * k + 2] = out[:, width:]
        return 0

    lax.fori_loop(0, block // 2, rows, 0)
    pairs = []
    for p in range(slabs):
        for f in range(fields):
            source = cot.at[f, main, pl.ds(p * depth, depth)]
            pairs.append((source, out.at[p, pl.ds(f * block, block)]))
    copies = start_all(pairs, sem)
    for p in range(slabs):
        for f in range(fields):
            for y in range(block):
                for side, z in ((0, p * depth - 1), (1, (p + 1) * depth)):
                    to = slice(f * block + y, f * block + y + 1)
                    if 0 <= z < order:
                        ends[p, side, to] = cot[f, y + 1, z : z + 1]
                    else:
                        ends[p, side, to] = jnp.zeros((1, width), f32)
    ends_copy = pltpu.make_async_copy(
        ends, out.at[:, pl.ds(fields * block, 2)], sem.at[len(pairs)]
    )
    ends_copy.start()
    wait_all(copies)
    ends_copy.wait()


def adjoint_step(halves, low_edges, high_edges, firsts, visc, mat_high, mat_low):
    slabs, _, block, depth, width = halves[0].shape
    order = slabs * depth
    volume = fields * (block + 1) * order * width
    return call(
        adjoint_kernel,
        [(x, anywhere()) for x in (*halves, *low_edges, *high_edges)]
        + [(x, whole()) for x in (*firsts, visc, mat_high, mat_low)],
        [((slabs, fields * block + 2, depth, width), anywhere())],
        [
            vmem(fields, block + 2, order, width),
            vmem(fields, block + 2, order + 2 * pad, width),
            vmem(slabs, 2, depth, width),
        ]
        + step_scratch(order, width, fields)
        + [dmas(slabs * fields + 1)],
        12 * order * volume,
        "adjoint_step",
    )[0]


def last_kernel(*refs):
    visc, edges_below, edges_above, chunks, *states, half, other, out = refs[:9]
    pulled, state, prior, planes, coupling, ends, carry, sem = refs[9:]
    slabs = chunks.shape[0]
    rows, depth, width = visc.shape
    block = rows // slabs
    main = pl.ds(pad, depth)
    above, below = pl.ds(pad + 1, depth), pl.ds(pad - 1, depth)
    first, last = slice(pad - 1, pad), slice(pad + depth, pad + depth + 1)

    def arrive(f, which):
        pairs = []
        for p in range(slabs):
            place, rest = pl.ds(p * block, block), pl.ds(f * block, block)
            if which == "pulled":
                pairs.append((chunks.at[p, rest], pulled.at[f, place, main]))
            if which == "state":
                pairs.append((states[f // 2].at[p, f % 2], state.at[f, place, main]))
            if which == "prior":
                pairs.append(((half, other)[f // 2].at[p, f % 2], prior.at[f, place]))
        return [pltpu.make_async_copy(a, b, sem.at[f, which_of[which]]) for a, b in pairs]

    which_of = {"pulled": 0, "state": 1, "prior": 2}
    ends_copy = pltpu.make_async_copy(
        chunks.at[:, pl.ds(fields * block, 2)], ends, sem.at[fields, 0]
    )
    copies = {}
    for f, which in [(W, "state"), (U, "pulled"), (U, "state"), (U, "prior")] + [
        (f, which) for f in (V, T, W) for which in which_of if (f, which) != (W, "state")
    ]:
        copies[f, which] = arrive(f, which)
        for copy in copies[f, which]:
            copy.start()
        if (f, which) == (U, "pulled"):
            ends_copy.start()
    for f in range(fields):
        for y in range(rows):
            state[f, y, first] = edges_below[outside[f], y : y + 1]
            state[f, y, last] = edges_above[outside[f], y : y + 1]
    ends_copy.wait()
    for f in range(fields):
        for y in range(rows):
            row = f * block + y % block
            pulled[f, y, first] = ends[y // block, 0, row : row + 1]
            pulled[f, y, last] = ends[y // block, 1, row : row + 1]
    wait_all(copies[W, "state"])
    leaving = []
    for f in (U, V, T, W):
        for which in which_of:
            if (f, which) != (W, "state"):
                wait_all(copies[f, which])
        if f == T:
            wait_all(copies[W, "pulled"])
            copies[W, "pulled"] = []
        along_y = 0.5 * (visc[rows - 1] + visc[0])
        carry[...] = along_y * (pulled[f, 0, main] - pulled[f, rows - 1, main])

        def row(y, _):
            north = lax.rem(y + 1, rows)
            own = visc[y]
            along_x = 0.5 * (own + east(own))
            along_y = 0.5 * (own + visc[north])
            value = pulled[f, y, main]
            flux_x = along_x * (east(value) - value)
            flux_y = along_y * (pulled[f, north, main] - value)
            rate = flux_x - west(flux_x) + (flux_y - carry[...])
            carry[...] = flux_y
            flow = state[W, y, above] * pulled[f, y, above]
            rate = rate + (flow - state[W, y, below] * pulled[f, y, below])
            lost = value * (state[f, y, above] - state[f, y, below])
            if f == U:
                coupling[y] = lost
            elif f == V:
                coupling[y] = coupling[y] + lost
            elif f == T:
                coupling[y] = value - (coupling[y] + lost)
                rate = rate + pulled[W, y, main]
            else:
                rate = rate + (coupling[y] - lost)
            result = value + time_step * rate - prior[f, y]
            planes[f, pl.ds(y, depth, stride=rows), :] = result
            return 0

        lax.fori_loop(0, rows, row, 0, unroll=8)
        copy = pltpu.make_async_copy(planes.at[f], out.at[outside[f]], sem.at[fields, 1 + f])
        copy.start()
        leaving.append(copy)
    wait_all(leaving)


def last_step(visc, below, above, chunks, states, priors):
    rows, depth, width = visc.shape
    slabs = chunks.shape[0]
    return call(
        last_kernel,
        [(x, whole()) for x in (visc, below, above)]
        + [(x, anywhere()) for x in (chunks, *states, *priors)],
        [((fields, depth * rows, width), anywhere())],
        [
            vmem(fields, rows, depth + 2 * pad, width),
            vmem(fields, rows, depth + 2 * pad, width),
            vmem(fields, rows, depth, width),
            vmem(fields, depth * rows, width),
            vmem(rows, depth, width),
            vmem(slabs, 2, depth, width),
            vmem(depth, width),
            pltpu.SemaphoreType.DMA((fields + 1, fields + 1)),
        ],
        30 * fields * rows * depth * width,
        "last_step",
    )[0]


def exchange(chunks):
    return lax.all_to_all(chunks, "slab", split_axis=0, concat_axis=0, tiled=True)


def around(value, axis, steps):
    count = lax.axis_size(axis)
    return lax.ppermute(value, axis, [(i, (i + steps) % count) for i in range(count)])


def local(states, viscosity, inverse):
    start = states[0]
    _, depth, rows, width = start.shape
    slabs, segs = lax.axis_size("slab"), lax.axis_size("seg")
    share = -(-(rows // slabs + 4) // segs)

    own_seg = jnp.full((1,), lax.axis_index("seg"), jnp.int32)
    visc, visc_send = visc_chunks(own_seg, viscosity, slabs, share)
    visc_share = exchange(visc_send)
    visc_in = [visc_share] + [around(visc_share, "seg", -i) for i in range(1, segs)]
    send_half, _ = to_chunks(start, slabs, outside[W], 2, [visc_send])
    main_half = exchange(send_half)
    send_other, ends = to_chunks(start, slabs, outside[U], 2, visc_in)
    main_other = exchange(send_other)
    forward = [(i, i + 1) for i in range(slabs - 1)]
    below = lax.ppermute(ends[1], "slab", forward)
    above = lax.ppermute(ends[0], "slab", [(i, j) for j, i in forward])
    mat_high, mat_low, adj_high, adj_low = split(inverse)

    own, outer, targets, later = [], [], [], visc_share
    for part, pieces in ((main_half, 1), (main_other, 2)):
        low_rows, high_rows, *again = outer_rows(part, later, pieces)
        low_in = around(high_rows, "slab", 1)
        own.append((low_in, part, around(low_rows, "slab", -1)))
        outer.append(low_rows)
        targets.append([around(piece, "seg", -1) for piece in again])
        later = low_in

    mats = mat_high, mat_low
    first_half, frame = first_step(own_seg, *own[0], outer[1], visc_in, *mats)
    later = (own[1][0], own[1][2])
    out, low_edge, high_edge = second_step(
        first_half, first_half, frame, *mats, W, targets[0], later
    )
    first_other = carried_step(own[1], own[0], (targets[1][0], out), frame, *mats)
    other, *more = second_step(
        first_other, first_half, frame, *mats, U, targets[1], (out, out)
    )
    low_edges = [around(edge, "slab", 1) for edge in (high_edge, more[1])]
    high_edges = [around(edge, "slab", -1) for edge in (low_edge, more[0])]
    half = exchange(out)
    residual = (out, after(other, (*low_edges, *high_edges, half)))
    firsts = (first_half, first_other)
    pulled = adjoint_step(residual, low_edges, high_edges, firsts, frame, adj_high, adj_low)
    planes, other = to_planes((half, exchange(residual[1])), pulled)
    priors = [around(part, "seg", 1) for part in (half, other)]
    gradient = last_step(visc, below, above, exchange(pulled), (send_half, send_other), priors)
    shape = (1, fields, depth, rows, width)
    return (planes.reshape(shape), gradient.reshape(shape))


def solution(mesh):
    in_specs = (P("seg", None, "slab", None, None), P("slab", None, None), P())
    out_specs = (P("seg", None, "slab", None, None), P("seg", None, "slab", None, None))
    return jax.shard_map(local, mesh=mesh, in_specs=in_specs, out_specs=out_specs, check_vma=False)
```

```python
import functools

import jax
import jax.numpy as jnp
from jax import lax
from jax.experimental import pallas as pl
from jax.experimental.pallas import tpu as pltpu
from jax.sharding import PartitionSpec as P

time_step = 0.1
vmem_bytes = 56 * 1024 * 1024
f32, bf16 = jnp.float32, jnp.bfloat16
fields = 4
W, T, U, V = range(4)
outside = (2, 3, 0, 1)
pad = 8
tall = 32


def whole():
    return pl.BlockSpec(memory_space=pltpu.VMEM)


def anywhere():
    return pl.BlockSpec(memory_space=pl.ANY)


def scalars():
    return pl.BlockSpec(memory_space=pltpu.SMEM)


def vmem(*shape):
    return pltpu.VMEM(shape, f32)


def dmas(count):
    return pltpu.SemaphoreType.DMA((count,))


def call(kernel, ins, outs, scratch, flops, name, kind=f32):
    moved = sum(4 * x.size for x, _ in ins)
    return pl.pallas_call(
        kernel,
        in_specs=[spec for _, spec in ins],
        out_specs=tuple(spec for _, spec in outs),
        out_shape=tuple(jax.ShapeDtypeStruct(shape, kind) for shape, _ in outs),
        scratch_shapes=scratch,
        compiler_params=pltpu.CompilerParams(vmem_limit_bytes=vmem_bytes),
        cost_estimate=pl.CostEstimate(flops=flops, bytes_accessed=moved, transcendentals=0),
        name=name,
    )(*[x for x, _ in ins])


def start_all(pairs, sem):
    copies = [
        pltpu.make_async_copy(source, target, sem.at[i])
        for i, (source, target) in enumerate(pairs)
    ]
    for copy in copies:
        copy.start()
    return copies


def wait_all(copies):
    for copy in copies:
        copy.wait()


def spans(parts, axis=1):
    start = 0
    for part in parts:
        yield part, pl.ds(start, part.shape[axis])
        start += part.shape[axis]


def east(value):
    return pltpu.roll(value, value.shape[1] - 1, 1)


def west(value):
    return pltpu.roll(value, 1, 1)


def parts_of(value):
    high = value.astype(bf16)
    return high, (value - high.astype(f32)).astype(bf16)


def product(matrix_high, matrix_low, high, low):
    dot = functools.partial(jnp.dot, preferred_element_type=f32)
    return dot(matrix_high, high) + (dot(matrix_high, low) + dot(matrix_low, high))


def split_kernel(x_ref, high, low, adj_high, adj_low):
    for f in range(fields):
        high[f], low[f] = parts_of(x_ref[outside[f]])
        adj_high[f], adj_low[f] = parts_of(x_ref[outside[f]].T)


def split(inverse):
    return call(
        split_kernel,
        [(inverse, whole())],
        [(inverse.shape, whole())] * 4,
        [],
        0,
        "split",
        bf16,
    )


def visc_kernel(own, x_ref, visc, send):
    slabs, share = send.shape[:2]
    rows, depth, _ = visc.shape
    block = rows // slabs
    for y in range(rows):
        visc[y] = x_ref[pl.ds(y, depth, stride=rows), :]
    for p in range(slabs):
        for i in range(share):
            send[p, i] = visc[lax.rem(p * block - 2 + share * own[0] + i + rows, rows)]


def visc_chunks(own, viscosity, slabs, share):
    depth, rows, width = viscosity.shape
    return call(
        visc_kernel,
        [(own, scalars()), (viscosity.reshape(-1, width), whole())],
        [((rows, depth, width), whole()), ((slabs, share, depth, width), whole())],
        [],
        0,
        "visc_chunks",
    )


def chunks_kernel(start, x_ref, *refs):
    send, edges, planes, held, sem = refs[-5:]
    count, slabs, block, depth, _ = held.shape
    rows = slabs * block
    copies = start_all([(x_ref.at[start + f], planes.at[f]) for f in range(count)], sem)
    ends = [
        pltpu.make_async_copy(x_ref.at[:, pl.ds(z * rows, rows)], edges.at[i], sem.at[count + i])
        for i, z in enumerate((0, depth - 1))
    ]
    for copy in ends:
        copy.start()
    leaving = []
    for f in range(count):
        copies[f].wait()
        for y in range(rows):
            held[f, y // block, y % block] = planes[f, pl.ds(y, depth, stride=rows), :]
        copy = pltpu.make_async_copy(held.at[f], send.at[:, f], sem.at[f])
        copy.start()
        leaving.append(copy)
    wait_all(leaving + ends)


def to_chunks(states, slabs, start, count, later):
    _, depth, rows, width = states.shape
    block = rows // slabs
    return call(
        functools.partial(chunks_kernel, start),
        [(states.reshape(fields, -1, width), anywhere())]
        + [(x, anywhere()) for x in later],
        [
            ((slabs, count, block, depth, width), anywhere()),
            ((2, fields, rows, width), whole()),
        ],
        [
            vmem(count, depth * rows, width),
            vmem(count, slabs, block, depth, width),
            dmas(count + 2),
        ],
        0,
        "to_chunks",
    )


def planes_kernel(half, other, _, o_ref, again, held, sem):
    slabs, _, block, depth, _ = half.shape
    rows = slabs * block
    pairs = []
    for p in range(slabs):
        place = pl.ds(p * block, block)
        pairs.append((half.at[p], held.at[pl.ds(0, 2), place]))
        pairs.append((other.at[p], held.at[pl.ds(2, 2), place]))
    wait_all(start_all(pairs, sem))
    places = [held.at[pl.ds(2, 2), pl.ds(p * block, block)] for p in range(slabs)]
    copies = start_all([(places[p], again.at[p]) for p in range(slabs)], sem)

    def row(y, _):
        for f in range(fields):
            where = pl.ds(outside[f] * depth * rows + y, depth, stride=rows)
            o_ref[where, :] = held[f, y]
        return 0

    lax.fori_loop(0, rows, row, 0, unroll=4)
    wait_all(copies)


def to_planes(halves, later):
    slabs, _, block, depth, width = halves[0].shape
    return call(
        planes_kernel,
        [(x, anywhere()) for x in (*halves, later)],
        [
            ((fields * depth * slabs * block, width), whole()),
            (halves[1].shape, anywhere()),
        ],
        [vmem(fields, slabs * block, depth, width), dmas(2 * slabs)],
        0,
        "to_planes",
    )


def clear_pads(ref):
    edge = jnp.zeros(ref.shape[1:2] + (pad, ref.shape[3]), f32)
    for f in range(ref.shape[0]):
        ref[f, :, 0:pad] = edge
        ref[f, :, ref.shape[2] - pad :] = edge


def first_fluxes(state, visc, shift, carry):
    order = visc.shape[1]
    for z in range(0, order, tall):
        here, pads = pl.ds(z, tall), pl.ds(z + pad, tall)
        along_y = 0.5 * (visc[shift, here] + visc[shift + 1, here])
        for f in range(state.shape[0]):
            carry[f, here] = along_y * (state[f, 1, pads] - state[f, 0, pads])


def spread_of(state, f, j, value, here, pads, along_x, along_y, carry):
    flux_x = along_x * (east(value) - value)
    flux_y = along_y * (state[f, j + 1, pads] - value)
    spread = flux_x - west(flux_x) + (flux_y - carry[f, here])
    carry[f, here] = flux_y
    return spread


def advance_rows(state, speeds, visc, shift, mats, base, scratch, count, finish):
    mat_high, mat_low, carry, high, low = *mats, *scratch
    order, width = visc.shape[1:]
    first_fluxes(state, visc, shift, carry)

    def pair(k, _):
        for half in range(2):
            j = 2 * k + half + 1
            side = slice(half * width, (half + 1) * width)
            for z in range(0, order, tall):
                here, pads = pl.ds(z, tall), pl.ds(z + pad, tall)
                above, below = pl.ds(z + pad + 1, tall), pl.ds(z + pad - 1, tall)
                own = visc[j + shift, here]
                along_x = 0.5 * (own + east(own))
                along_y = 0.5 * (own + visc[j + shift + 1, here])
                speed = speeds[j, pads]
                for f in range(2):
                    value = state[f, j, pads]
                    rate = spread_of(state, f, j, value, here, pads, along_x, along_y, carry)
                    rate = rate - speed * (state[f, j, above] - state[f, j, below])
                    if base == W:
                        rate = rate + state[1 - f, j, pads]
                    high[f, here, side], low[f, here, side] = parts_of(value + time_step * rate)
        for f in range(2):
            out = product(mat_high[base + f], mat_low[base + f], high[f], low[f])
            finish(f, 2 * k, out[:, :width])
            finish(f, 2 * k + 1, out[:, width:])
        return 0

    lax.fori_loop(0, count // 2, pair, 0)


def step_scratch(order, width, count):
    return [
        vmem(count, order, width),
        pltpu.VMEM((count, order, 2 * width), bf16),
        pltpu.VMEM((count, order, 2 * width), bf16),
    ]


def rows_of(low_in, main, high_in, p, target):
    _, _, block, depth, _ = main.shape
    padded = pl.ds(p * depth + pad, depth)
    for row, count, part in ((0, 2, low_in), (2, block, main), (block + 2, 2, high_in)):
        yield part, target.at[:, pl.ds(row, count), padded]


def first_finish(first, order):
    def finish(f, row, piece):
        first[f, row, pl.ds(pad, order)] = piece

    return finish


def first_kernel(segs, own, low_in, main, high_in, _, mat_high, mat_low, *refs):
    visc_in, (first, visc, state, *scratch, sem) = refs[:segs], refs[segs:]
    slabs, _, block, depth, _ = main.shape
    share = visc_in[0].shape[1]
    pairs = []
    for p in range(slabs):
        pairs += [(a.at[p], b) for a, b in rows_of(low_in, main, high_in, p, state)]
        planes = pl.ds(p * depth, depth)
        for i in range(segs):
            start = lax.rem(own[0] + i, segs) * share
            pairs.append((visc_in[i].at[p], visc.at[pl.ds(start, share), planes]))
    copies = start_all(pairs, sem)
    clear_pads(state)
    clear_pads(first)
    wait_all(copies)
    mats, finish = (mat_high, mat_low), first_finish(first, slabs * depth)
    advance_rows(state, state.at[W], visc, 0, mats, W, scratch, block + 2, finish)


def first_step(own, low_in, main, high_in, later, visc_in, mat_high, mat_low):
    slabs, _, block, depth, width = main.shape
    segs, share = len(visc_in), visc_in[0].shape[1]
    order = slabs * depth
    volume = 2 * (block + 2) * order * width
    return call(
        functools.partial(first_kernel, segs),
        [(own, scalars())]
        + [(x, anywhere()) for x in (low_in, main, high_in, later)]
        + [(mat_high, whole()), (mat_low, whole())]
        + [(x, anywhere()) for x in visc_in],
        [
            ((2, block + 2, order + 2 * pad, width), whole()),
            ((segs * share, order, width), whole()),
        ],
        [vmem(2, block + 4, order + 2 * pad, width)]
        + step_scratch(order, width, 2)
        + [dmas(slabs * (3 + segs))],
        6 * order * volume,
        "first_step",
    )


def carried_kernel(*refs):
    low_in, main, high_in, low_w, main_w, high_w, _, _, visc, mat_high, mat_low = refs[:11]
    first, state, speeds, *scratch, sem = refs[11:]
    slabs, _, block, depth, _ = main.shape
    pairs = []
    for p in range(slabs):
        pairs += [(a.at[p], b) for a, b in rows_of(low_in, main, high_in, p, state)]
        w_rows = rows_of(low_w, main_w, high_w, p, speeds)
        pairs += [(a.at[p, pl.ds(W, 1)], b) for a, b in w_rows]
    copies = start_all(pairs, sem)
    clear_pads(state)
    clear_pads(first)
    wait_all(copies)
    mats, finish = (mat_high, mat_low), first_finish(first, slabs * depth)
    advance_rows(state, speeds.at[0], visc, 0, mats, U, scratch, block + 2, finish)


def carried_step(own, with_w, later, visc, mat_high, mat_low):
    slabs, _, block, depth, width = own[1].shape
    order = slabs * depth
    volume = 2 * (block + 2) * order * width
    return call(
        carried_kernel,
        [(x, anywhere()) for x in (*own, *with_w, *later)]
        + [(x, whole()) for x in (visc, mat_high, mat_low)],
        [((2, block + 2, order + 2 * pad, width), whole())],
        [
            vmem(2, block + 4, order + 2 * pad, width),
            vmem(1, block + 4, order + 2 * pad, width),
        ]
        + step_scratch(order, width, 2)
        + [dmas(6 * slabs)],
        6 * order * volume,
        "carried_step",
    )[0]


def second_kernel(base, first, with_w, visc, mat_high, mat_low, *refs):
    targets, (out, low_edge, high_edge, state, speeds) = refs[:-13], refs[-10:-5]
    *scratch, held, sem = refs[-5:]
    slabs, _, block, depth, _ = out.shape
    places = [held.at[:, :, pl.ds(p * depth, depth)] for p in range(slabs)]
    pairs = [(first, state)] + ([(with_w.at[W], speeds)] if base != W else [])
    for target, span in spans(targets, 2):
        for p in range(slabs):
            pairs.append((target.at[p], held.at[:, span, pl.ds(p * depth, depth)]))
    wait_all(start_all(pairs, sem))

    def finish(f, row, piece):
        held[f, row] = piece - held[f, row]

    mats, speeds = (mat_high, mat_low), state.at[W] if base == W else speeds
    advance_rows(state, speeds, visc, 1, mats, base, scratch, block, finish)
    copies = start_all([(places[p], out.at[p]) for p in range(slabs)], sem)
    low_edge[...] = held[:, 0]
    high_edge[...] = held[:, block - 1]
    wait_all(copies)


def second_step(first, with_w, visc, mat_high, mat_low, base, targets, later):
    width, order = visc.shape[2], visc.shape[1]
    slabs, _, _, depth, _ = targets[0].shape
    block = sum(target.shape[2] for target in targets)
    return call(
        functools.partial(second_kernel, base),
        [(first, anywhere()), (with_w, anywhere())]
        + [(x, whole()) for x in (visc, mat_high, mat_low)]
        + [(x, anywhere()) for x in (*targets, *later)],
        [((slabs, 2, block, depth, width), anywhere())] + [((2, order, width), whole())] * 2,
        [vmem(*first.shape), vmem(*first.shape[1:])]
        + step_scratch(order, width, 2)
        + [vmem(2, block, order, width), dmas(2 * slabs + 2)],
        6 * order * 2 * block * order * width,
        "second_step",
    )


def after_kernel(x_ref, *refs):
    o_ref, sem = refs[-2:]
    wait_all(start_all([(x_ref, o_ref)], sem))


def after(value, later):
    return call(
        after_kernel,
        [(x, anywhere()) for x in (value, *later)],
        [(value.shape, whole())],
        [dmas(1)],
        0,
        "after",
    )[0]


def outer_kernel(chunks, _, low_rows, high_rows, *refs):
    *again, sem = refs
    block = chunks.shape[2]
    low, high = chunks.at[:, :, pl.ds(0, 2)], chunks.at[:, :, pl.ds(block - 2, 2)]
    pairs = [(low, low_rows), (high, high_rows)]
    pairs += [(chunks.at[:, :, span], part) for part, span in spans(again, 2)]
    wait_all(start_all(pairs, sem))


def outer_rows(chunks, later, pieces):
    slabs, count, _, depth, width = chunks.shape
    rows = [((slabs, count, size, depth, width), whole()) for size in (2, 2, *pieces)]
    return call(
        outer_kernel,
        [(chunks, anywhere()), (later, anywhere())],
        rows,
        [dmas(len(rows))],
        0,
        "outer_rows",
    )


def adjoint_kernel(*refs):
    halves, low_edges, high_edges = refs[0:2], refs[2:4], refs[4:6]
    firsts, (visc, mat_high, mat_low) = refs[6:8], refs[8:11]
    out, cot, pulled, ends, carry, high, low, sem = refs[11:]
    slabs, _, block, depth, width = halves[0].shape
    order = slabs * depth
    main = pl.ds(1, block)
    pairs = []
    for source, span in spans(halves):
        for p in range(slabs):
            pairs.append((source.at[p], cot.at[span, main, pl.ds(p * depth, depth)]))
    for i in range(2):
        pairs.append((low_edges[i], cot.at[pl.ds(2 * i, 2), 0]))
        pairs.append((high_edges[i], cot.at[pl.ds(2 * i, 2), block + 1]))
    copies = start_all(pairs, sem)
    clear_pads(pulled)
    wait_all(copies)

    def pull(k, _):
        for f in range(fields):
            pair = jnp.concatenate([cot[f, 2 * k], cot[f, 2 * k + 1]], axis=1)
            out = product(mat_high[f], mat_low[f], *parts_of(pair))
            pulled[f, 2 * k, pl.ds(pad, order)] = out[:, :width]
            pulled[f, 2 * k + 1, pl.ds(pad, order)] = out[:, width:]
        return 0

    lax.fori_loop(0, (block + 2) // 2, pull, 0)
    first_fluxes(pulled, visc, 1, carry)

    def rows(k, _):
        for half in range(2):
            j = 2 * k + half + 1
            side = slice(half * width, (half + 1) * width)
            for z in range(0, order, tall):
                here, pads = pl.ds(z, tall), pl.ds(z + pad, tall)
                above, below = pl.ds(z + pad + 1, tall), pl.ds(z + pad - 1, tall)
                own = visc[j + 1, here]
                along_x = 0.5 * (own + east(own))
                along_y = 0.5 * (own + visc[j + 2, here])
                speed_above, speed_below = firsts[0][W, j, above], firsts[0][W, j, below]
                coupling = pulled[T, j, pads]
                for f in (U, V, T, W):
                    value = pulled[f, j, pads]
                    rate = spread_of(pulled, f, j, value, here, pads, along_x, along_y, carry)
                    up, down = pulled[f, j, above], pulled[f, j, below]
                    rate = rate + (speed_above * up - speed_below * down)
                    if f == W:
                        slope = speed_above - speed_below
                    else:
                        ref, i = firsts[f // 2], f % 2
                        slope = ref[i, j, above] - ref[i, j, below]
                    coupling = coupling - value * slope
                    if f == T:
                        rate = rate + pulled[W, j, pads]
                    if f == W:
                        rate = rate + coupling
                    high[f, here, side], low[f, here, side] = parts_of(value + time_step * rate)
        for f in range(fields):
            out = product(mat_high[f], mat_low[f], high[f], low[f])
            cot[f, 2 * k + 1] = out[:, :width]
            cot[f, 2 * k + 2] = out[:, width:]
        return 0

    lax.fori_loop(0, block // 2, rows, 0)
    pairs = []
    for p in range(slabs):
        for f in range(fields):
            source = cot.at[f, main, pl.ds(p * depth, depth)]
            pairs.append((source, out.at[p, pl.ds(f * block, block)]))
    copies = start_all(pairs, sem)
    for p in range(slabs):
        for f in range(fields):
            for y in range(block):
                for side, z in ((0, p * depth - 1), (1, (p + 1) * depth)):
                    to = slice(f * block + y, f * block + y + 1)
                    if 0 <= z < order:
                        ends[p, side, to] = cot[f, y + 1, z : z + 1]
                    else:
                        ends[p, side, to] = jnp.zeros((1, width), f32)
    ends_copy = pltpu.make_async_copy(
        ends, out.at[:, pl.ds(fields * block, 2)], sem.at[len(pairs)]
    )
    ends_copy.start()
    wait_all(copies)
    ends_copy.wait()


def adjoint_step(halves, low_edges, high_edges, firsts, visc, mat_high, mat_low):
    slabs, _, block, depth, width = halves[0].shape
    order = slabs * depth
    volume = fields * (block + 1) * order * width
    return call(
        adjoint_kernel,
        [(x, anywhere()) for x in (*halves, *low_edges, *high_edges)]
        + [(x, whole()) for x in (*firsts, visc, mat_high, mat_low)],
        [((slabs, fields * block + 2, depth, width), anywhere())],
        [
            vmem(fields, block + 2, order, width),
            vmem(fields, block + 2, order + 2 * pad, width),
            vmem(slabs, 2, depth, width),
        ]
        + step_scratch(order, width, fields)
        + [dmas(slabs * fields + 1)],
        12 * order * volume,
        "adjoint_step",
    )[0]


def last_kernel(*refs):
    visc, edges_below, edges_above, chunks, *states, half, other, out = refs[:9]
    pulled, state, prior, planes, coupling, ends, carry, sem = refs[9:]
    slabs = chunks.shape[0]
    rows, depth, width = visc.shape
    block = rows // slabs
    main = pl.ds(pad, depth)
    above, below = pl.ds(pad + 1, depth), pl.ds(pad - 1, depth)
    first, last = slice(pad - 1, pad), slice(pad + depth, pad + depth + 1)

    def arrive(f, which):
        pairs = []
        for p in range(slabs):
            place, rest = pl.ds(p * block, block), pl.ds(f * block, block)
            if which == "pulled":
                pairs.append((chunks.at[p, rest], pulled.at[f, place, main]))
            if which == "state":
                pairs.append((states[f // 2].at[p, f % 2], state.at[f, place, main]))
            if which == "prior":
                pairs.append(((half, other)[f // 2].at[p, f % 2], prior.at[f, place]))
        return [pltpu.make_async_copy(a, b, sem.at[f, which_of[which]]) for a, b in pairs]

    which_of = {"pulled": 0, "state": 1, "prior": 2}
    ends_copy = pltpu.make_async_copy(
        chunks.at[:, pl.ds(fields * block, 2)], ends, sem.at[fields, 0]
    )
    copies = {}
    for f, which in [(W, "state"), (U, "pulled"), (U, "state"), (U, "prior")] + [
        (f, which) for f in (V, T, W) for which in which_of if (f, which) != (W, "state")
    ]:
        copies[f, which] = arrive(f, which)
        for copy in copies[f, which]:
            copy.start()
        if (f, which) == (U, "pulled"):
            ends_copy.start()
    for f in range(fields):
        for y in range(rows):
            state[f, y, first] = edges_below[outside[f], y : y + 1]
            state[f, y, last] = edges_above[outside[f], y : y + 1]
    ends_copy.wait()
    for f in range(fields):
        for y in range(rows):
            row = f * block + y % block
            pulled[f, y, first] = ends[y // block, 0, row : row + 1]
            pulled[f, y, last] = ends[y // block, 1, row : row + 1]
    wait_all(copies[W, "state"])
    leaving = []
    for f in (U, V, T, W):
        for which in which_of:
            if (f, which) != (W, "state"):
                wait_all(copies[f, which])
        if f == T:
            wait_all(copies[W, "pulled"])
            copies[W, "pulled"] = []
        along_y = 0.5 * (visc[rows - 1] + visc[0])
        carry[...] = along_y * (pulled[f, 0, main] - pulled[f, rows - 1, main])

        def row(y, _):
            north = lax.rem(y + 1, rows)
            own = visc[y]
            along_x = 0.5 * (own + east(own))
            along_y = 0.5 * (own + visc[north])
            value = pulled[f, y, main]
            flux_x = along_x * (east(value) - value)
            flux_y = along_y * (pulled[f, north, main] - value)
            rate = flux_x - west(flux_x) + (flux_y - carry[...])
            carry[...] = flux_y
            flow = state[W, y, above] * pulled[f, y, above]
            rate = rate + (flow - state[W, y, below] * pulled[f, y, below])
            lost = value * (state[f, y, above] - state[f, y, below])
            if f == U:
                coupling[y] = lost
            elif f == V:
                coupling[y] = coupling[y] + lost
            elif f == T:
                coupling[y] = value - (coupling[y] + lost)
                rate = rate + pulled[W, y, main]
            else:
                rate = rate + (coupling[y] - lost)
            result = value + time_step * rate - prior[f, y]
            planes[f, pl.ds(y, depth, stride=rows), :] = result
            return 0

        lax.fori_loop(0, rows, row, 0, unroll=8)
        copy = pltpu.make_async_copy(planes.at[f], out.at[outside[f]], sem.at[fields, 1 + f])
        copy.start()
        leaving.append(copy)
    wait_all(leaving)


def last_step(visc, below, above, chunks, states, priors):
    rows, depth, width = visc.shape
    slabs = chunks.shape[0]
    return call(
        last_kernel,
        [(x, whole()) for x in (visc, below, above)]
        + [(x, anywhere()) for x in (chunks, *states, *priors)],
        [((fields, depth * rows, width), anywhere())],
        [
            vmem(fields, rows, depth + 2 * pad, width),
            vmem(fields, rows, depth + 2 * pad, width),
            vmem(fields, rows, depth, width),
            vmem(fields, depth * rows, width),
            vmem(rows, depth, width),
            vmem(slabs, 2, depth, width),
            vmem(depth, width),
            pltpu.SemaphoreType.DMA((fields + 1, fields + 1)),
        ],
        30 * fields * rows * depth * width,
        "last_step",
    )[0]


def exchange(chunks):
    return lax.all_to_all(chunks, "slab", split_axis=0, concat_axis=0, tiled=True)


def around(value, axis, steps):
    count = lax.axis_size(axis)
    return lax.ppermute(value, axis, [(i, (i + steps) % count) for i in range(count)])


def local(states, viscosity, inverse):
    start = states[0]
    _, depth, rows, width = start.shape
    slabs, segs = lax.axis_size("slab"), lax.axis_size("seg")
    block = rows // slabs
    share = -(-(block + 4) // segs)

    own_seg = jnp.full((1,), lax.axis_index("seg"), jnp.int32)
    visc, visc_send = visc_chunks(own_seg, viscosity, slabs, share)
    visc_share = exchange(visc_send)
    visc_in = [visc_share] + [around(visc_share, "seg", -i) for i in range(1, segs)]
    send_half, _ = to_chunks(start, slabs, outside[W], 2, [visc_send])
    main_half = exchange(send_half)
    mat_high, mat_low, adj_high, adj_low = split(inverse)
    send_other, ends = to_chunks(start, slabs, outside[U], 2, [*visc_in, mat_high])
    main_other = exchange(send_other)
    forward = [(i, i + 1) for i in range(slabs - 1)]
    below = lax.ppermute(ends[1], "slab", forward)
    above = lax.ppermute(ends[0], "slab", [(i, j) for j, i in forward])

    own, outer, targets, later = [], [], [], visc_share
    few = max(1, 3 * block // 8)
    for part, pieces in ((main_half, (block,)), (main_other, (few, block - few))):
        low_rows, high_rows, *again = outer_rows(part, later, pieces)
        low_in = around(high_rows, "slab", 1)
        own.append((low_in, part, around(low_rows, "slab", -1)))
        outer.append(low_rows)
        targets.append([around(piece, "seg", -1) for piece in again])
        later = low_in

    mats = mat_high, mat_low
    first_half, frame = first_step(own_seg, *own[0], outer[1], visc_in, *mats)
    later = (own[1][0], own[1][2], targets[1][0])
    out, low_edge, high_edge = second_step(
        first_half, first_half, frame, *mats, W, targets[0], later
    )
    first_other = carried_step(own[1], own[0], (out, out), frame, *mats)
    other, *more = second_step(
        first_other, first_half, frame, *mats, U, targets[1], (out, out, out)
    )
    low_edges = [around(edge, "slab", 1) for edge in (high_edge, more[1])]
    high_edges = [around(edge, "slab", -1) for edge in (low_edge, more[0])]
    half = exchange(out)
    residual = (out, after(other, (*low_edges, *high_edges, half)))
    firsts = (first_half, first_other)
    pulled = adjoint_step(residual, low_edges, high_edges, firsts, frame, adj_high, adj_low)
    planes, other = to_planes((half, exchange(residual[1])), pulled)
    priors = [around(part, "seg", 1) for part in (half, other)]
    gradient = last_step(visc, below, above, exchange(pulled), (send_half, send_other), priors)
    shape = (1, fields, depth, rows, width)
    return (planes.reshape(shape), gradient.reshape(shape))


def solution(mesh):
    in_specs = (P("seg", None, "slab", None, None), P("slab", None, None), P())
    out_specs = (P("seg", None, "slab", None, None), P("seg", None, "slab", None, None))
    return jax.shard_map(local, mesh=mesh, in_specs=in_specs, out_specs=out_specs, check_vma=False)
```

```python
import functools

import jax
import jax.numpy as jnp
from jax import lax
from jax.experimental import pallas as pl
from jax.experimental.pallas import tpu as pltpu
from jax.sharding import PartitionSpec as P

time_step = 0.1
vmem_bytes = 56 * 1024 * 1024
f32, bf16 = jnp.float32, jnp.bfloat16
fields = 4
W, T, U, V = range(4)
outside = (2, 3, 0, 1)
pad = 8
tall = 32


def whole():
    return pl.BlockSpec(memory_space=pltpu.VMEM)


def anywhere():
    return pl.BlockSpec(memory_space=pl.ANY)


def scalars():
    return pl.BlockSpec(memory_space=pltpu.SMEM)


def vmem(*shape):
    return pltpu.VMEM(shape, f32)


def dmas(count):
    return pltpu.SemaphoreType.DMA((count,))


def call(kernel, ins, outs, scratch, flops, name, kind=f32, aliases=None):
    moved = sum(4 * x.size for x, _ in ins)
    return pl.pallas_call(
        kernel,
        in_specs=[spec for _, spec in ins],
        out_specs=tuple(spec for _, spec in outs),
        out_shape=tuple(jax.ShapeDtypeStruct(shape, kind) for shape, _ in outs),
        scratch_shapes=scratch,
        input_output_aliases=aliases or {},
        compiler_params=pltpu.CompilerParams(vmem_limit_bytes=vmem_bytes),
        cost_estimate=pl.CostEstimate(flops=flops, bytes_accessed=moved, transcendentals=0),
        name=name,
    )(*[x for x, _ in ins])


def start_all(pairs, sem):
    copies = [
        pltpu.make_async_copy(source, target, sem.at[i])
        for i, (source, target) in enumerate(pairs)
    ]
    for copy in copies:
        copy.start()
    return copies


def wait_all(copies):
    for copy in copies:
        copy.wait()


def spans(parts, axis=1):
    start = 0
    for part in parts:
        yield part, pl.ds(start, part.shape[axis])
        start += part.shape[axis]


def east(value):
    return pltpu.roll(value, value.shape[1] - 1, 1)


def west(value):
    return pltpu.roll(value, 1, 1)


def parts_of(value):
    high = value.astype(bf16)
    return high, (value - high.astype(f32)).astype(bf16)


def product(matrix_high, matrix_low, high, low):
    dot = functools.partial(jnp.dot, preferred_element_type=f32)
    return dot(matrix_high, high) + (dot(matrix_high, low) + dot(matrix_low, high))


def split_kernel(x_ref, high, low, adj_high, adj_low):
    for f in range(fields):
        high[f], low[f] = parts_of(x_ref[outside[f]])
        adj_high[f], adj_low[f] = parts_of(x_ref[outside[f]].T)


def split(inverse):
    return call(
        split_kernel,
        [(inverse, whole())],
        [(inverse.shape, whole())] * 4,
        [],
        0,
        "split",
        bf16,
    )


def visc_kernel(own, x_ref, visc, send):
    slabs, share = send.shape[:2]
    rows, depth, _ = visc.shape
    block = rows // slabs
    for y in range(rows):
        visc[y] = x_ref[pl.ds(y, depth, stride=rows), :]
    for p in range(slabs):
        for i in range(share):
            send[p, i] = visc[lax.rem(p * block - 2 + share * own[0] + i + rows, rows)]


def visc_chunks(own, viscosity, slabs, share):
    depth, rows, width = viscosity.shape
    return call(
        visc_kernel,
        [(own, scalars()), (viscosity.reshape(-1, width), whole())],
        [((rows, depth, width), whole()), ((slabs, share, depth, width), whole())],
        [],
        0,
        "visc_chunks",
    )


def frame_kernel(own, *refs):
    *shares, frame, sem = refs
    slabs, share, depth, _ = shares[0].shape
    pairs = []
    for i, part in enumerate(shares):
        start = lax.rem(own[0] + i, len(shares)) * share
        for p in range(slabs):
            pairs.append((part.at[p], frame.at[pl.ds(start, share), pl.ds(p * depth, depth)]))
    wait_all(start_all(pairs, sem))


def to_frame(own, shares):
    slabs, share, depth, width = shares[0].shape
    return call(
        frame_kernel,
        [(own, scalars())] + [(x, anywhere()) for x in shares],
        [((len(shares) * share, slabs * depth, width), whole())],
        [dmas(len(shares) * slabs)],
        0,
        "to_frame",
    )[0]


def chunks_kernel(start, x_ref, *refs):
    send, edges, planes, held, sem = refs[-5:]
    count, slabs, block, depth, _ = held.shape
    rows = slabs * block
    copies = start_all([(x_ref.at[start + f], planes.at[f]) for f in range(count)], sem)
    ends = [
        pltpu.make_async_copy(x_ref.at[:, pl.ds(z * rows, rows)], edges.at[i], sem.at[count + i])
        for i, z in enumerate((0, depth - 1))
    ]
    for copy in ends:
        copy.start()
    leaving = []
    for f in range(count):
        copies[f].wait()
        for y in range(rows):
            held[f, y // block, y % block] = planes[f, pl.ds(y, depth, stride=rows), :]
        copy = pltpu.make_async_copy(held.at[f], send.at[:, f], sem.at[f])
        copy.start()
        leaving.append(copy)
    wait_all(leaving + ends)


def to_chunks(states, slabs, start, count, later):
    _, depth, rows, width = states.shape
    block = rows // slabs
    return call(
        functools.partial(chunks_kernel, start),
        [(states.reshape(fields, -1, width), anywhere())]
        + [(x, anywhere()) for x in later],
        [
            ((slabs, count, block, depth, width), anywhere()),
            ((2, fields, rows, width), whole()),
        ],
        [
            vmem(count, depth * rows, width),
            vmem(count, slabs, block, depth, width),
            dmas(count + 2),
        ],
        0,
        "to_chunks",
    )


def planes_kernel(half, other, _, o_ref, again, held, sem):
    slabs, _, block, depth, _ = half.shape
    rows = slabs * block
    pairs = []
    for p in range(slabs):
        place = pl.ds(p * block, block)
        pairs.append((half.at[p], held.at[pl.ds(0, 2), place]))
        pairs.append((other.at[p], held.at[pl.ds(2, 2), place]))
    wait_all(start_all(pairs, sem))
    places = [held.at[pl.ds(2, 2), pl.ds(p * block, block)] for p in range(slabs)]
    copies = start_all([(places[p], again.at[p]) for p in range(slabs)], sem)

    def row(y, _):
        for f in range(fields):
            where = pl.ds(outside[f] * depth * rows + y, depth, stride=rows)
            o_ref[where, :] = held[f, y]
        return 0

    lax.fori_loop(0, rows, row, 0, unroll=4)
    wait_all(copies)


def to_planes(halves, later):
    slabs, _, block, depth, width = halves[0].shape
    return call(
        planes_kernel,
        [(x, anywhere()) for x in (*halves, later)],
        [
            ((fields * depth * slabs * block, width), whole()),
            (halves[1].shape, anywhere()),
        ],
        [vmem(fields, slabs * block, depth, width), dmas(2 * slabs)],
        0,
        "to_planes",
    )


def clear_pads(ref):
    edge = jnp.zeros(ref.shape[1:2] + (pad, ref.shape[3]), f32)
    for f in range(ref.shape[0]):
        ref[f, :, 0:pad] = edge
        ref[f, :, ref.shape[2] - pad :] = edge


def first_fluxes(state, visc, shift, carry):
    order = visc.shape[1]
    for z in range(0, order, tall):
        here, pads = pl.ds(z, tall), pl.ds(z + pad, tall)
        along_y = 0.5 * (visc[shift, here] + visc[shift + 1, here])
        for f in range(state.shape[0]):
            carry[f, here] = along_y * (state[f, 1, pads] - state[f, 0, pads])


def spread_of(state, f, j, value, here, pads, along_x, along_y, carry):
    flux_x = along_x * (east(value) - value)
    flux_y = along_y * (state[f, j + 1, pads] - value)
    spread = flux_x - west(flux_x) + (flux_y - carry[f, here])
    carry[f, here] = flux_y
    return spread


def advance_rows(state, speeds, shift, coupled, scratch, count, finish):
    visc, mat_high, mat_low, carry, high, low = scratch
    order, width = visc.shape[1:]
    first_fluxes(state, visc, shift, carry)

    def pair(k, _):
        for half in range(2):
            j = 2 * k + half + 1
            side = slice(half * width, (half + 1) * width)
            for z in range(0, order, tall):
                here, pads = pl.ds(z, tall), pl.ds(z + pad, tall)
                above, below = pl.ds(z + pad + 1, tall), pl.ds(z + pad - 1, tall)
                own = visc[j + shift, here]
                along_x = 0.5 * (own + east(own))
                along_y = 0.5 * (own + visc[j + shift + 1, here])
                speed = speeds[j, pads]
                for f in range(2):
                    value = state[f, j, pads]
                    rate = spread_of(state, f, j, value, here, pads, along_x, along_y, carry)
                    rate = rate - speed * (state[f, j, above] - state[f, j, below])
                    if coupled:
                        rate = rate + state[1 - f, j, pads]
                    high[f, here, side], low[f, here, side] = parts_of(value + time_step * rate)
        for f in range(2):
            out = product(mat_high[f], mat_low[f], high[f], low[f])
            finish(f, 2 * k, out[:, :width])
            finish(f, 2 * k + 1, out[:, width:])
        return 0

    lax.fori_loop(0, count // 2, pair, 0)


def step_scratch(order, width, count):
    return [
        vmem(count, order, width),
        pltpu.VMEM((count, order, 2 * width), bf16),
        pltpu.VMEM((count, order, 2 * width), bf16),
    ]


def two_scratch(frame):
    _, order, width = frame.shape
    matrix = pltpu.VMEM((2, order, order), bf16)
    return [vmem(*frame.shape), matrix, matrix] + step_scratch(order, width, 2)


def constants(base, sources, scratch):
    frame, mat_high, mat_low = sources
    two = pl.ds(base, 2)
    return [(frame, scratch[0]), (mat_high.at[two], scratch[1]), (mat_low.at[two], scratch[2])]


def rows_of(low_in, main, high_in, p, target):
    _, _, block, depth, _ = main.shape
    padded = pl.ds(p * depth + pad, depth)
    for row, count, part in ((0, 2, low_in), (2, block, main), (block + 2, 2, high_in)):
        yield part, target.at[:, pl.ds(row, count), padded]


def first_finish(first, order):
    def finish(f, row, piece):
        first[f, row, pl.ds(pad, order)] = piece

    return finish


def first_kernel(low_in, main, high_in, _, *refs):
    sources, (first, state, *scratch, sem) = refs[:3], refs[3:]
    slabs, _, block, depth, _ = main.shape
    pairs = constants(W, sources, scratch)
    for p in range(slabs):
        pairs += [(a.at[p], b) for a, b in rows_of(low_in, main, high_in, p, state)]
    copies = start_all(pairs, sem)
    clear_pads(state)
    clear_pads(first)
    wait_all(copies)
    finish = first_finish(first, slabs * depth)
    advance_rows(state, state.at[W], 0, True, scratch, block + 2, finish)


def first_step(low_in, main, high_in, later, frame, mat_high, mat_low):
    slabs, _, block, depth, width = main.shape
    order = slabs * depth
    volume = 2 * (block + 2) * order * width
    return call(
        first_kernel,
        [(x, anywhere()) for x in (low_in, main, high_in, later, frame, mat_high, mat_low)],
        [((2, block + 2, order + 2 * pad, width), whole())],
        [vmem(2, block + 4, order + 2 * pad, width)]
        + two_scratch(frame)
        + [dmas(3 * slabs + 3)],
        6 * order * volume,
        "first_step",
    )[0]


def carried_kernel(*refs):
    low_in, main, high_in, low_w, main_w, high_w, _ = refs[:7]
    sources, (first, state, speeds, *scratch, sem) = refs[7:10], refs[10:]
    slabs, _, block, depth, _ = main.shape
    pairs = constants(U, sources, scratch)
    for p in range(slabs):
        pairs += [(a.at[p], b) for a, b in rows_of(low_in, main, high_in, p, state)]
        w_rows = rows_of(low_w, main_w, high_w, p, speeds)
        pairs += [(a.at[p, pl.ds(W, 1)], b) for a, b in w_rows]
    copies = start_all(pairs, sem)
    clear_pads(state)
    clear_pads(first)
    wait_all(copies)
    finish = first_finish(first, slabs * depth)
    advance_rows(state, speeds.at[0], 0, False, scratch, block + 2, finish)


def carried_step(own, with_w, later, frame, mat_high, mat_low):
    slabs, _, block, depth, width = own[1].shape
    order = slabs * depth
    volume = 2 * (block + 2) * order * width
    return call(
        carried_kernel,
        [(x, anywhere()) for x in (*own, *with_w, later, frame, mat_high, mat_low)],
        [((2, block + 2, order + 2 * pad, width), whole())],
        [
            vmem(2, block + 4, order + 2 * pad, width),
            vmem(1, block + 4, order + 2 * pad, width),
        ]
        + two_scratch(frame)
        + [dmas(6 * slabs + 3)],
        6 * order * volume,
        "carried_step",
    )[0]


def second_kernel(base, count, first, with_w, *refs):
    sources, targets = refs[:3], refs[3 : 3 + count]
    out, low_edge, high_edge, state, speeds, *scratch, held, sem = refs[-13:]
    slabs, _, block, depth, _ = out.shape
    places = [held.at[:, :, pl.ds(p * depth, depth)] for p in range(slabs)]
    pairs = constants(base, sources, scratch) + [(first, state)]
    if base != W:
        pairs.append((with_w.at[W], speeds))
    for target, span in spans(targets, 2):
        for p in range(slabs):
            pairs.append((target.at[p], held.at[:, span, pl.ds(p * depth, depth)]))
    wait_all(start_all(pairs, sem))

    def finish(f, row, piece):
        held[f, row] = piece - held[f, row]

    speeds = state.at[W] if base == W else speeds
    advance_rows(state, speeds, 1, base == W, scratch, block, finish)
    copies = start_all([(places[p], out.at[p]) for p in range(slabs)], sem)
    low_edge[...] = held[:, 0]
    high_edge[...] = held[:, block - 1]
    wait_all(copies)


def second_step(first, with_w, frame, mat_high, mat_low, base, targets, later):
    _, order, width = frame.shape
    slabs, _, _, depth, _ = targets[0].shape
    block = sum(target.shape[2] for target in targets)
    operands = (first, with_w, frame, mat_high, mat_low, *targets, *later)
    return call(
        functools.partial(second_kernel, base, len(targets)),
        [(x, anywhere()) for x in operands],
        [((slabs, 2, block, depth, width), anywhere())] + [((2, order, width), whole())] * 2,
        [vmem(*first.shape), vmem(*first.shape[1:])]
        + two_scratch(frame)
        + [vmem(2, block, order, width), dmas(2 * slabs + 5)],
        6 * order * 2 * block * order * width,
        "second_step",
    )


def after_kernel(*refs):
    del refs


def after(value, later):
    return call(
        after_kernel,
        [(x, anywhere()) for x in (value, *later)],
        [(value.shape, anywhere())],
        [],
        0,
        "after",
        aliases={0: 0},
    )[0]


def outer_kernel(chunks, _before, _after, low_rows, high_rows, *refs):
    *again, sem = refs
    block = chunks.shape[2]
    low, high = chunks.at[:, :, pl.ds(0, 2)], chunks.at[:, :, pl.ds(block - 2, 2)]
    pairs = [(low, low_rows), (high, high_rows)]
    pairs += [(chunks.at[:, :, span], part) for part, span in spans(again, 2)]
    wait_all(start_all(pairs, sem))


def outer_rows(chunks, later, pieces):
    slabs, count, _, depth, width = chunks.shape
    rows = [((slabs, count, size, depth, width), whole()) for size in (2, 2, *pieces)]
    return call(
        outer_kernel,
        [(chunks, anywhere())] + [(x, anywhere()) for x in later],
        rows,
        [dmas(len(rows))],
        0,
        "outer_rows",
    )


def adjoint_kernel(*refs):
    halves, low_edges, high_edges = refs[0:2], refs[2:4], refs[4:6]
    firsts, (visc, mat_high, mat_low) = refs[6:8], refs[8:11]
    out, cot, pulled, ends, carry, high, low, sem = refs[11:]
    slabs, _, block, depth, width = halves[0].shape
    order = slabs * depth
    main = pl.ds(1, block)
    pairs = []
    for source, span in spans(halves):
        for p in range(slabs):
            pairs.append((source.at[p], cot.at[span, main, pl.ds(p * depth, depth)]))
    for i in range(2):
        pairs.append((low_edges[i], cot.at[pl.ds(2 * i, 2), 0]))
        pairs.append((high_edges[i], cot.at[pl.ds(2 * i, 2), block + 1]))
    copies = start_all(pairs, sem)
    clear_pads(pulled)
    wait_all(copies)

    def pull(k, _):
        for f in range(fields):
            pair = jnp.concatenate([cot[f, 2 * k], cot[f, 2 * k + 1]], axis=1)
            out = product(mat_high[f], mat_low[f], *parts_of(pair))
            pulled[f, 2 * k, pl.ds(pad, order)] = out[:, :width]
            pulled[f, 2 * k + 1, pl.ds(pad, order)] = out[:, width:]
        return 0

    lax.fori_loop(0, (block + 2) // 2, pull, 0)
    first_fluxes(pulled, visc, 1, carry)

    def rows(k, _):
        for half in range(2):
            j = 2 * k + half + 1
            side = slice(half * width, (half + 1) * width)
            for z in range(0, order, tall):
                here, pads = pl.ds(z, tall), pl.ds(z + pad, tall)
                above, below = pl.ds(z + pad + 1, tall), pl.ds(z + pad - 1, tall)
                own = visc[j + 1, here]
                along_x = 0.5 * (own + east(own))
                along_y = 0.5 * (own + visc[j + 2, here])
                speed_above, speed_below = firsts[0][W, j, above], firsts[0][W, j, below]
                coupling = pulled[T, j, pads]
                for f in (U, V, T, W):
                    value = pulled[f, j, pads]
                    rate = spread_of(pulled, f, j, value, here, pads, along_x, along_y, carry)
                    up, down = pulled[f, j, above], pulled[f, j, below]
                    rate = rate + (speed_above * up - speed_below * down)
                    if f == W:
                        slope = speed_above - speed_below
                    else:
                        ref, i = firsts[f // 2], f % 2
                        slope = ref[i, j, above] - ref[i, j, below]
                    coupling = coupling - value * slope
                    if f == T:
                        rate = rate + pulled[W, j, pads]
                    if f == W:
                        rate = rate + coupling
                    high[f, here, side], low[f, here, side] = parts_of(value + time_step * rate)
        for f in range(fields):
            out = product(mat_high[f], mat_low[f], high[f], low[f])
            cot[f, 2 * k + 1] = out[:, :width]
            cot[f, 2 * k + 2] = out[:, width:]
        return 0

    lax.fori_loop(0, block // 2, rows, 0)
    pairs = []
    for p in range(slabs):
        for f in range(fields):
            source = cot.at[f, main, pl.ds(p * depth, depth)]
            pairs.append((source, out.at[p, pl.ds(f * block, block)]))
    copies = start_all(pairs, sem)
    for p in range(slabs):
        for f in range(fields):
            for y in range(block):
                for side, z in ((0, p * depth - 1), (1, (p + 1) * depth)):
                    to = slice(f * block + y, f * block + y + 1)
                    if 0 <= z < order:
                        ends[p, side, to] = cot[f, y + 1, z : z + 1]
                    else:
                        ends[p, side, to] = jnp.zeros((1, width), f32)
    ends_copy = pltpu.make_async_copy(
        ends, out.at[:, pl.ds(fields * block, 2)], sem.at[len(pairs)]
    )
    ends_copy.start()
    wait_all(copies)
    ends_copy.wait()


def adjoint_step(halves, low_edges, high_edges, firsts, visc, mat_high, mat_low):
    slabs, _, block, depth, width = halves[0].shape
    order = slabs * depth
    volume = fields * (block + 1) * order * width
    return call(
        adjoint_kernel,
        [(x, anywhere()) for x in (*halves, *low_edges, *high_edges)]
        + [(x, whole()) for x in (*firsts, visc, mat_high, mat_low)],
        [((slabs, fields * block + 2, depth, width), anywhere())],
        [
            vmem(fields, block + 2, order, width),
            vmem(fields, block + 2, order + 2 * pad, width),
            vmem(slabs, 2, depth, width),
        ]
        + step_scratch(order, width, fields)
        + [dmas(slabs * fields + 1)],
        12 * order * volume,
        "adjoint_step",
    )[0]


def last_kernel(*refs):
    visc_in, edges_below, edges_above, chunks, *states, half, other, out = refs[:9]
    pulled, state, prior, planes, coupling, ends, visc, sem = refs[9:]
    slabs = chunks.shape[0]
    visc_copy = pltpu.make_async_copy(visc_in, visc, sem.at[fields, fields + 1])
    visc_copy.start()
    rows, depth, width = visc.shape
    block = rows // slabs
    main = pl.ds(pad, depth)
    above, below = pl.ds(pad + 1, depth), pl.ds(pad - 1, depth)
    first, last = slice(pad - 1, pad), slice(pad + depth, pad + depth + 1)

    def arrive(f, which):
        pairs = []
        for p in range(slabs):
            place, rest = pl.ds(p * block, block), pl.ds(f * block, block)
            if which == "pulled":
                pairs.append((chunks.at[p, rest], pulled.at[f, place, main]))
            if which == "state":
                pairs.append((states[f // 2].at[p, f % 2], state.at[f, place, main]))
            if which == "prior":
                pairs.append(((half, other)[f // 2].at[p, f % 2], prior.at[f, place]))
        return [pltpu.make_async_copy(a, b, sem.at[f, which_of[which]]) for a, b in pairs]

    which_of = {"pulled": 0, "state": 1, "prior": 2}
    ends_copy = pltpu.make_async_copy(
        chunks.at[:, pl.ds(fields * block, 2)], ends, sem.at[fields, 0]
    )
    copies = {}
    for f, which in [(W, "state"), (U, "pulled"), (U, "state"), (U, "prior")] + [
        (f, which) for f in (V, T, W) for which in which_of if (f, which) != (W, "state")
    ]:
        copies[f, which] = arrive(f, which)
        for copy in copies[f, which]:
            copy.start()
        if (f, which) == (U, "pulled"):
            ends_copy.start()
    for f in range(fields):
        for y in range(rows):
            state[f, y, first] = edges_below[outside[f], y : y + 1]
            state[f, y, last] = edges_above[outside[f], y : y + 1]
    ends_copy.wait()
    for f in range(fields):
        for y in range(rows):
            row = f * block + y % block
            pulled[f, y, first] = ends[y // block, 0, row : row + 1]
            pulled[f, y, last] = ends[y // block, 1, row : row + 1]
    visc_copy.wait()
    wait_all(copies[W, "state"])
    leaving = []
    for f in (U, V, T, W):
        for which in which_of:
            if (f, which) != (W, "state"):
                wait_all(copies[f, which])
        if f == T:
            wait_all(copies[W, "pulled"])
            copies[W, "pulled"] = []
        along_y = 0.5 * (visc[rows - 1] + visc[0])
        south = along_y * (pulled[f, 0, main] - pulled[f, rows - 1, main])

        def row(y, south):
            north = lax.rem(y + 1, rows)
            own = visc[y]
            along_x = 0.5 * (own + east(own))
            along_y = 0.5 * (own + visc[north])
            value = pulled[f, y, main]
            flux_x = along_x * (east(value) - value)
            flux_y = along_y * (pulled[f, north, main] - value)
            rate = flux_x - west(flux_x) + (flux_y - south)
            flow = state[W, y, above] * pulled[f, y, above]
            rate = rate + (flow - state[W, y, below] * pulled[f, y, below])
            lost = value * (state[f, y, above] - state[f, y, below])
            if f == U:
                coupling[y] = lost
            elif f == V:
                coupling[y] = coupling[y] + lost
            elif f == T:
                coupling[y] = value - (coupling[y] + lost)
                rate = rate + pulled[W, y, main]
            else:
                rate = rate + (coupling[y] - lost)
            result = value + time_step * rate - prior[f, y]
            planes[f, pl.ds(y, depth, stride=rows), :] = result
            return flux_y

        lax.fori_loop(0, rows, row, south, unroll=8)
        copy = pltpu.make_async_copy(planes.at[f], out.at[outside[f]], sem.at[fields, 1 + f])
        copy.start()
        leaving.append(copy)
    wait_all(leaving)


def last_step(visc, below, above, chunks, states, priors):
    rows, depth, width = visc.shape
    slabs = chunks.shape[0]
    return call(
        last_kernel,
        [(visc, anywhere()), (below, whole()), (above, whole())]
        + [(x, anywhere()) for x in (chunks, *states, *priors)],
        [((fields, depth * rows, width), anywhere())],
        [
            vmem(fields, rows, depth + 2 * pad, width),
            vmem(fields, rows, depth + 2 * pad, width),
            vmem(fields, rows, depth, width),
            vmem(fields, depth * rows, width),
            vmem(rows, depth, width),
            vmem(slabs, 2, depth, width),
            vmem(rows, depth, width),
            pltpu.SemaphoreType.DMA((fields + 1, fields + 2)),
        ],
        30 * fields * rows * depth * width,
        "last_step",
    )[0]


def exchange(chunks):
    return lax.all_to_all(chunks, "slab", split_axis=0, concat_axis=0, tiled=True)


def around(value, axis, steps):
    count = lax.axis_size(axis)
    return lax.ppermute(value, axis, [(i, (i + steps) % count) for i in range(count)])


def local(states, viscosity, inverse):
    start = states[0]
    _, depth, rows, width = start.shape
    slabs, segs = lax.axis_size("slab"), lax.axis_size("seg")
    block = rows // slabs
    share = -(-(block + 4) // segs)

    own_seg = jnp.full((1,), lax.axis_index("seg"), jnp.int32)
    visc, visc_send = visc_chunks(own_seg, viscosity, slabs, share)
    visc_share = exchange(visc_send)
    visc_in = [visc_share] + [around(visc_share, "seg", -i) for i in range(1, segs)]
    send_half, _ = to_chunks(start, slabs, outside[W], 2, [visc_send])
    main_half = exchange(send_half)
    mat_high, mat_low, adj_high, adj_low = split(inverse)
    frame = to_frame(own_seg, visc_in)
    send_other, ends = to_chunks(start, slabs, outside[U], 2, [frame, mat_high])
    main_other = exchange(send_other)
    forward = [(i, i + 1) for i in range(slabs - 1)]
    below = lax.ppermute(ends[1], "slab", forward)
    above = lax.ppermute(ends[0], "slab", [(i, j) for j, i in forward])

    own, outer, targets, later = [], [], [], (visc_share, visc_share)
    few = max(1, 3 * block // 8)
    for part, pieces in ((main_half, (block,)), (main_other, (few, block - few))):
        low_rows, high_rows, *again = outer_rows(part, later, pieces)
        low_in = around(high_rows, "slab", 1)
        high_in = around(low_rows, "slab", -1)
        own.append((low_in, part, high_in))
        outer.append(low_rows)
        targets.append([around(piece, "seg", -1) for piece in again])
        later = (low_in, high_in)

    mats = mat_high, mat_low
    first_half = first_step(*own[0], outer[1], frame, *mats)
    later = (own[1][0], own[1][2], targets[1][0])
    out, low_edge, high_edge = second_step(
        first_half, first_half, frame, *mats, W, targets[0], later
    )
    first_other = carried_step(own[1], own[0], out, frame, *mats)
    other, *more = second_step(
        first_other, first_half, frame, *mats, U, targets[1], (out,)
    )
    low_edges = [around(edge, "slab", 1) for edge in (high_edge, more[1])]
    high_edges = [around(edge, "slab", -1) for edge in (low_edge, more[0])]
    half = exchange(out)
    residual = (out, after(other, (*low_edges, *high_edges, half)))
    firsts = (first_half, first_other)
    pulled = adjoint_step(residual, low_edges, high_edges, firsts, frame, adj_high, adj_low)
    planes, other = to_planes((half, exchange(residual[1])), pulled)
    priors = [around(part, "seg", 1) for part in (half, other)]
    gradient = last_step(visc, below, above, exchange(pulled), (send_half, send_other), priors)
    shape = (1, fields, depth, rows, width)
    return (planes.reshape(shape), gradient.reshape(shape))


def solution(mesh):
    in_specs = (P("seg", None, "slab", None, None), P("slab", None, None), P())
    out_specs = (P("seg", None, "slab", None, None), P("seg", None, "slab", None, None))
    return jax.shard_map(local, mesh=mesh, in_specs=in_specs, out_specs=out_specs, check_vma=False)
```

```python
import functools

import jax
import jax.numpy as jnp
from jax import lax
from jax.experimental import pallas as pl
from jax.experimental.pallas import tpu as pltpu
from jax.sharding import PartitionSpec as P

time_step = 0.1
vmem_bytes = 56 * 1024 * 1024
f32, bf16 = jnp.float32, jnp.bfloat16
fields = 4
W, T, U, V = range(4)
outside = (2, 3, 0, 1)
pad = 8
tall = 32


def whole():
    return pl.BlockSpec(memory_space=pltpu.VMEM)


def anywhere():
    return pl.BlockSpec(memory_space=pl.ANY)


def scalars():
    return pl.BlockSpec(memory_space=pltpu.SMEM)


def vmem(*shape):
    return pltpu.VMEM(shape, f32)


def dmas(count):
    return pltpu.SemaphoreType.DMA((count,))


def call(kernel, ins, outs, scratch, flops, name, kind=f32, aliases=None):
    moved = sum(4 * x.size for x, _ in ins)
    return pl.pallas_call(
        kernel,
        in_specs=[spec for _, spec in ins],
        out_specs=tuple(spec for _, spec in outs),
        out_shape=tuple(jax.ShapeDtypeStruct(shape, kind) for shape, _ in outs),
        scratch_shapes=scratch,
        input_output_aliases=aliases or {},
        compiler_params=pltpu.CompilerParams(vmem_limit_bytes=vmem_bytes),
        cost_estimate=pl.CostEstimate(flops=flops, bytes_accessed=moved, transcendentals=0),
        name=name,
    )(*[x for x, _ in ins])


def start_all(pairs, sem):
    copies = [
        pltpu.make_async_copy(source, target, sem.at[i])
        for i, (source, target) in enumerate(pairs)
    ]
    for copy in copies:
        copy.start()
    return copies


def wait_all(copies):
    for copy in copies:
        copy.wait()


def spans(parts, axis=1):
    start = 0
    for part in parts:
        yield part, pl.ds(start, part.shape[axis])
        start += part.shape[axis]


def east(value):
    return pltpu.roll(value, value.shape[1] - 1, 1)


def west(value):
    return pltpu.roll(value, 1, 1)


def parts_of(value):
    high = value.astype(bf16)
    return high, (value - high.astype(f32)).astype(bf16)


def product(matrix_high, matrix_low, high, low):
    dot = functools.partial(jnp.dot, preferred_element_type=f32)
    return dot(matrix_high, high) + (dot(matrix_high, low) + dot(matrix_low, high))


def split_kernel(x_ref, high, low, adj_high, adj_low):
    for f in range(fields):
        high[f], low[f] = parts_of(x_ref[outside[f]])
        adj_high[f], adj_low[f] = parts_of(x_ref[outside[f]].T)


def split(inverse):
    return call(
        split_kernel,
        [(inverse, whole())],
        [(inverse.shape, whole())] * 4,
        [],
        0,
        "split",
        bf16,
    )


def visc_kernel(own, x_ref, visc, send):
    slabs, share = send.shape[:2]
    rows, depth, _ = visc.shape
    block = rows // slabs
    for y in range(rows):
        visc[y] = x_ref[pl.ds(y, depth, stride=rows), :]
    for p in range(slabs):
        for i in range(share):
            send[p, i] = visc[lax.rem(p * block - 2 + share * own[0] + i + rows, rows)]


def visc_chunks(own, viscosity, slabs, share):
    depth, rows, width = viscosity.shape
    return call(
        visc_kernel,
        [(own, scalars()), (viscosity.reshape(-1, width), whole())],
        [((rows, depth, width), whole()), ((slabs, share, depth, width), whole())],
        [],
        0,
        "visc_chunks",
    )


def frame_kernel(own, *refs):
    *shares, frame, sem = refs
    slabs, share, depth, _ = shares[0].shape
    pairs = []
    for i, part in enumerate(shares):
        start = lax.rem(own[0] + i, len(shares)) * share
        for p in range(slabs):
            pairs.append((part.at[p], frame.at[pl.ds(start, share), pl.ds(p * depth, depth)]))
    wait_all(start_all(pairs, sem))


def to_frame(own, shares):
    slabs, share, depth, width = shares[0].shape
    return call(
        frame_kernel,
        [(own, scalars())] + [(x, anywhere()) for x in shares],
        [((len(shares) * share, slabs * depth, width), whole())],
        [dmas(len(shares) * slabs)],
        0,
        "to_frame",
    )[0]


def chunks_kernel(start, x_ref, *refs):
    send, edges, planes, held, sem = refs[-5:]
    count, slabs, block, depth, _ = held.shape
    rows = slabs * block
    copies = start_all([(x_ref.at[start + f], planes.at[f]) for f in range(count)], sem)
    ends = [
        pltpu.make_async_copy(x_ref.at[:, pl.ds(z * rows, rows)], edges.at[i], sem.at[count + i])
        for i, z in enumerate((0, depth - 1))
    ]
    for copy in ends:
        copy.start()
    leaving = []
    for f in range(count):
        copies[f].wait()
        for y in range(rows):
            held[f, y // block, y % block] = planes[f, pl.ds(y, depth, stride=rows), :]
        copy = pltpu.make_async_copy(held.at[f], send.at[:, f], sem.at[f])
        copy.start()
        leaving.append(copy)
    wait_all(leaving + ends)


def to_chunks(states, slabs, start, count, later):
    _, depth, rows, width = states.shape
    block = rows // slabs
    return call(
        functools.partial(chunks_kernel, start),
        [(states.reshape(fields, -1, width), anywhere())]
        + [(x, anywhere()) for x in later],
        [
            ((slabs, count, block, depth, width), anywhere()),
            ((2, fields, rows, width), whole()),
        ],
        [
            vmem(count, depth * rows, width),
            vmem(count, slabs, block, depth, width),
            dmas(count + 2),
        ],
        0,
        "to_chunks",
    )


def planes_kernel(half, other, _, o_ref, again, held, sem):
    slabs, _, block, depth, _ = half.shape
    rows = slabs * block
    pairs = []
    for p in range(slabs):
        place = pl.ds(p * block, block)
        pairs.append((half.at[p], held.at[pl.ds(0, 2), place]))
        pairs.append((other.at[p], held.at[pl.ds(2, 2), place]))
    wait_all(start_all(pairs, sem))
    places = [held.at[pl.ds(2, 2), pl.ds(p * block, block)] for p in range(slabs)]
    copies = start_all([(places[p], again.at[p]) for p in range(slabs)], sem)

    def row(y, _):
        for f in range(fields):
            where = pl.ds(outside[f] * depth * rows + y, depth, stride=rows)
            o_ref[where, :] = held[f, y]
        return 0

    lax.fori_loop(0, rows, row, 0, unroll=4)
    wait_all(copies)


def to_planes(halves, later):
    slabs, _, block, depth, width = halves[0].shape
    return call(
        planes_kernel,
        [(x, anywhere()) for x in (*halves, later)],
        [
            ((fields * depth * slabs * block, width), whole()),
            (halves[1].shape, anywhere()),
        ],
        [vmem(fields, slabs * block, depth, width), dmas(2 * slabs)],
        0,
        "to_planes",
    )


def clear_pads(ref):
    edge = jnp.zeros(ref.shape[1:2] + (pad, ref.shape[3]), f32)
    for f in range(ref.shape[0]):
        ref[f, :, 0:pad] = edge
        ref[f, :, ref.shape[2] - pad :] = edge


def first_fluxes(state, visc, shift, carry):
    order = visc.shape[1]
    for z in range(0, order, tall):
        here, pads = pl.ds(z, tall), pl.ds(z + pad, tall)
        along_y = 0.5 * (visc[shift, here] + visc[shift + 1, here])
        for f in range(state.shape[0]):
            carry[f, here] = along_y * (state[f, 1, pads] - state[f, 0, pads])


def spread_of(state, f, j, value, here, pads, along_x, along_y, carry):
    flux_x = along_x * (east(value) - value)
    flux_y = along_y * (state[f, j + 1, pads] - value)
    spread = flux_x - west(flux_x) + (flux_y - carry[f, here])
    carry[f, here] = flux_y
    return spread


def advance_rows(state, speeds, shift, coupled, scratch, count, finish):
    visc, mat_high, mat_low, carry, high, low = scratch
    order, width = visc.shape[1:]
    first_fluxes(state, visc, shift, carry)

    def pair(k, _):
        for half in range(2):
            j = 2 * k + half + 1
            side = slice(half * width, (half + 1) * width)
            for z in range(0, order, tall):
                here, pads = pl.ds(z, tall), pl.ds(z + pad, tall)
                above, below = pl.ds(z + pad + 1, tall), pl.ds(z + pad - 1, tall)
                own = visc[j + shift, here]
                along_x = 0.5 * (own + east(own))
                along_y = 0.5 * (own + visc[j + shift + 1, here])
                speed = speeds[j, pads]
                for f in range(2):
                    value = state[f, j, pads]
                    rate = spread_of(state, f, j, value, here, pads, along_x, along_y, carry)
                    rate = rate - speed * (state[f, j, above] - state[f, j, below])
                    if coupled:
                        rate = rate + state[1 - f, j, pads]
                    high[f, here, side], low[f, here, side] = parts_of(value + time_step * rate)
        for f in range(2):
            out = product(mat_high[f], mat_low[f], high[f], low[f])
            finish(f, 2 * k, out[:, :width])
            finish(f, 2 * k + 1, out[:, width:])
        return 0

    lax.fori_loop(0, count // 2, pair, 0)


def step_scratch(order, width, count):
    return [
        vmem(count, order, width),
        pltpu.VMEM((count, order, 2 * width), bf16),
        pltpu.VMEM((count, order, 2 * width), bf16),
    ]


def two_scratch(frame):
    _, order, width = frame.shape
    matrix = pltpu.VMEM((2, order, order), bf16)
    return [vmem(*frame.shape), matrix, matrix] + step_scratch(order, width, 2)


def constants(base, sources, scratch):
    frame, mat_high, mat_low = sources
    two = pl.ds(base, 2)
    return [(frame, scratch[0]), (mat_high.at[two], scratch[1]), (mat_low.at[two], scratch[2])]


def rows_of(low_in, main, high_in, p, target):
    _, _, block, depth, _ = main.shape
    padded = pl.ds(p * depth + pad, depth)
    for row, count, part in ((0, 2, low_in), (2, block, main), (block + 2, 2, high_in)):
        yield part, target.at[:, pl.ds(row, count), padded]


def first_finish(first, order):
    def finish(f, row, piece):
        first[f, row, pl.ds(pad, order)] = piece

    return finish


def first_kernel(low_in, main, high_in, _, *refs):
    sources, (first, state, *scratch, sem) = refs[:3], refs[3:]
    slabs, _, block, depth, _ = main.shape
    pairs = constants(W, sources, scratch)
    for p in range(slabs):
        pairs += [(a.at[p], b) for a, b in rows_of(low_in, main, high_in, p, state)]
    copies = start_all(pairs, sem)
    clear_pads(state)
    clear_pads(first)
    wait_all(copies)
    finish = first_finish(first, slabs * depth)
    advance_rows(state, state.at[W], 0, True, scratch, block + 2, finish)


def first_step(low_in, main, high_in, later, frame, mat_high, mat_low):
    slabs, _, block, depth, width = main.shape
    order = slabs * depth
    volume = 2 * (block + 2) * order * width
    return call(
        first_kernel,
        [(x, anywhere()) for x in (low_in, main, high_in, later, frame, mat_high, mat_low)],
        [((2, block + 2, order + 2 * pad, width), whole())],
        [vmem(2, block + 4, order + 2 * pad, width)]
        + two_scratch(frame)
        + [dmas(3 * slabs + 3)],
        6 * order * volume,
        "first_step",
    )[0]


def carried_kernel(*refs):
    low_in, main, high_in, low_w, main_w, high_w, _ = refs[:7]
    sources, (first, state, speeds, *scratch, sem) = refs[7:10], refs[10:]
    slabs, _, block, depth, _ = main.shape
    pairs = constants(U, sources, scratch)
    for p in range(slabs):
        pairs += [(a.at[p], b) for a, b in rows_of(low_in, main, high_in, p, state)]
        w_rows = rows_of(low_w, main_w, high_w, p, speeds)
        pairs += [(a.at[p, pl.ds(W, 1)], b) for a, b in w_rows]
    copies = start_all(pairs, sem)
    clear_pads(state)
    clear_pads(first)
    wait_all(copies)
    finish = first_finish(first, slabs * depth)
    advance_rows(state, speeds.at[0], 0, False, scratch, block + 2, finish)


def carried_step(own, with_w, later, frame, mat_high, mat_low):
    slabs, _, block, depth, width = own[1].shape
    order = slabs * depth
    volume = 2 * (block + 2) * order * width
    return call(
        carried_kernel,
        [(x, anywhere()) for x in (*own, *with_w, later, frame, mat_high, mat_low)],
        [((2, block + 2, order + 2 * pad, width), whole())],
        [
            vmem(2, block + 4, order + 2 * pad, width),
            vmem(1, block + 4, order + 2 * pad, width),
        ]
        + two_scratch(frame)
        + [dmas(6 * slabs + 3)],
        6 * order * volume,
        "carried_step",
    )[0]


def second_kernel(base, count, first, with_w, *refs):
    sources, targets = refs[:3], refs[3 : 3 + count]
    out, low_edge, high_edge, state, speeds, *scratch, held, sem = refs[-13:]
    slabs, _, block, depth, _ = out.shape
    places = [held.at[:, :, pl.ds(p * depth, depth)] for p in range(slabs)]
    pairs = constants(base, sources, scratch) + [(first, state)]
    if base != W:
        pairs.append((with_w.at[W], speeds))
    for target, span in spans(targets, 2):
        for p in range(slabs):
            pairs.append((target.at[p], held.at[:, span, pl.ds(p * depth, depth)]))
    wait_all(start_all(pairs, sem))

    def finish(f, row, piece):
        held[f, row] = piece - held[f, row]

    speeds = state.at[W] if base == W else speeds
    advance_rows(state, speeds, 1, base == W, scratch, block, finish)
    copies = start_all([(places[p], out.at[p]) for p in range(slabs)], sem)
    low_edge[...] = held[:, 0]
    high_edge[...] = held[:, block - 1]
    wait_all(copies)


def second_step(first, with_w, frame, mat_high, mat_low, base, targets, later):
    _, order, width = frame.shape
    slabs, _, _, depth, _ = targets[0].shape
    block = sum(target.shape[2] for target in targets)
    operands = (first, with_w, frame, mat_high, mat_low, *targets, *later)
    return call(
        functools.partial(second_kernel, base, len(targets)),
        [(x, anywhere()) for x in operands],
        [((slabs, 2, block, depth, width), anywhere())] + [((2, order, width), whole())] * 2,
        [vmem(*first.shape), vmem(*first.shape[1:])]
        + two_scratch(frame)
        + [vmem(2, block, order, width), dmas(2 * slabs + 5)],
        6 * order * 2 * block * order * width,
        "second_step",
    )


def after_kernel(*refs):
    del refs


def after(value, later):
    return call(
        after_kernel,
        [(x, anywhere()) for x in (value, *later)],
        [(value.shape, anywhere())],
        [],
        0,
        "after",
        aliases={0: 0},
    )[0]


def outer_kernel(chunks, _before, _after, low_rows, high_rows, *refs):
    *again, sem = refs
    block = chunks.shape[2]
    low, high = chunks.at[:, :, pl.ds(0, 2)], chunks.at[:, :, pl.ds(block - 2, 2)]
    pairs = [(low, low_rows), (high, high_rows)]
    pairs += [(chunks.at[:, :, span], part) for part, span in spans(again, 2)]
    wait_all(start_all(pairs, sem))


def outer_rows(chunks, later, pieces):
    slabs, count, _, depth, width = chunks.shape
    rows = [((slabs, count, size, depth, width), whole()) for size in (2, 2, *pieces)]
    return call(
        outer_kernel,
        [(chunks, anywhere())] + [(x, anywhere()) for x in later],
        rows,
        [dmas(len(rows))],
        0,
        "outer_rows",
    )


def adjoint_kernel(*refs):
    halves, low_edges, high_edges = refs[0:2], refs[2:4], refs[4:6]
    firsts, (visc, mat_high, mat_low) = refs[6:8], refs[8:11]
    out, cot, pulled, ends, carry, high, low, sem = refs[11:]
    slabs, _, block, depth, width = halves[0].shape
    order = slabs * depth
    main = pl.ds(1, block)
    pairs = []
    for source, span in spans(halves):
        for p in range(slabs):
            pairs.append((source.at[p], cot.at[span, main, pl.ds(p * depth, depth)]))
    for i in range(2):
        pairs.append((low_edges[i], cot.at[pl.ds(2 * i, 2), 0]))
        pairs.append((high_edges[i], cot.at[pl.ds(2 * i, 2), block + 1]))
    copies = start_all(pairs, sem)
    clear_pads(pulled)
    wait_all(copies)

    def pull(k, _):
        for f in range(fields):
            pair = jnp.concatenate([cot[f, 2 * k], cot[f, 2 * k + 1]], axis=1)
            out = product(mat_high[f], mat_low[f], *parts_of(pair))
            pulled[f, 2 * k, pl.ds(pad, order)] = out[:, :width]
            pulled[f, 2 * k + 1, pl.ds(pad, order)] = out[:, width:]
        return 0

    lax.fori_loop(0, (block + 2) // 2, pull, 0)
    first_fluxes(pulled, visc, 1, carry)

    def rows(k, _):
        for half in range(2):
            j = 2 * k + half + 1
            side = slice(half * width, (half + 1) * width)
            for z in range(0, order, tall):
                here, pads = pl.ds(z, tall), pl.ds(z + pad, tall)
                above, below = pl.ds(z + pad + 1, tall), pl.ds(z + pad - 1, tall)
                own = visc[j + 1, here]
                along_x = 0.5 * (own + east(own))
                along_y = 0.5 * (own + visc[j + 2, here])
                speed_above, speed_below = firsts[0][W, j, above], firsts[0][W, j, below]
                coupling = pulled[T, j, pads]
                for f in (U, V, T, W):
                    value = pulled[f, j, pads]
                    rate = spread_of(pulled, f, j, value, here, pads, along_x, along_y, carry)
                    up, down = pulled[f, j, above], pulled[f, j, below]
                    rate = rate + (speed_above * up - speed_below * down)
                    if f == W:
                        slope = speed_above - speed_below
                    else:
                        ref, i = firsts[f // 2], f % 2
                        slope = ref[i, j, above] - ref[i, j, below]
                    coupling = coupling - value * slope
                    if f == T:
                        rate = rate + pulled[W, j, pads]
                    if f == W:
                        rate = rate + coupling
                    high[f, here, side], low[f, here, side] = parts_of(value + time_step * rate)
        for f in range(fields):
            out = product(mat_high[f], mat_low[f], high[f], low[f])
            cot[f, 2 * k + 1] = out[:, :width]
            cot[f, 2 * k + 2] = out[:, width:]
        return 0

    lax.fori_loop(0, block // 2, rows, 0)
    pairs = []
    for p in range(slabs):
        for f in range(fields):
            source = cot.at[f, main, pl.ds(p * depth, depth)]
            pairs.append((source, out.at[p, pl.ds(f * block, block)]))
    copies = start_all(pairs, sem)
    for p in range(slabs):
        for f in range(fields):
            for y in range(block):
                for side, z in ((0, p * depth - 1), (1, (p + 1) * depth)):
                    to = slice(f * block + y, f * block + y + 1)
                    if 0 <= z < order:
                        ends[p, side, to] = cot[f, y + 1, z : z + 1]
                    else:
                        ends[p, side, to] = jnp.zeros((1, width), f32)
    ends_copy = pltpu.make_async_copy(
        ends, out.at[:, pl.ds(fields * block, 2)], sem.at[len(pairs)]
    )
    ends_copy.start()
    wait_all(copies)
    ends_copy.wait()


def adjoint_step(halves, low_edges, high_edges, firsts, visc, mat_high, mat_low):
    slabs, _, block, depth, width = halves[0].shape
    order = slabs * depth
    volume = fields * (block + 1) * order * width
    return call(
        adjoint_kernel,
        [(x, anywhere()) for x in (*halves, *low_edges, *high_edges)]
        + [(x, whole()) for x in (*firsts, visc, mat_high, mat_low)],
        [((slabs, fields * block + 2, depth, width), anywhere())],
        [
            vmem(fields, block + 2, order, width),
            vmem(fields, block + 2, order + 2 * pad, width),
            vmem(slabs, 2, depth, width),
        ]
        + step_scratch(order, width, fields)
        + [dmas(slabs * fields + 1)],
        12 * order * volume,
        "adjoint_step",
    )[0]


def last_kernel(*refs):
    visc_in, edges_below, edges_above, chunks, *states, half, other, out = refs[:9]
    pulled, state, prior, planes, coupling, ends, visc, sem = refs[9:]
    slabs, block, depth, width = visc.shape
    rows, step = slabs * block, pulled.shape[3]
    main = pl.ds(pad, depth)
    above, below = pl.ds(pad + 1, depth), pl.ds(pad - 1, depth)

    def copy(source, target, which):
        return pltpu.make_async_copy(source, target, sem.at[which])

    arrive = {"visc": copy(visc_in, visc, 0)}
    arrive["ends"] = copy(chunks.at[:, pl.ds(fields * block, 2)], ends, 1)
    for f in range(fields):
        source = chunks.at[:, pl.ds(f * block, block)]
        arrive["pulled", f] = copy(source, pulled.at[f, :, :, main], 2 + f)
        source = states[f // 2].at[:, f % 2]
        arrive["state", f] = copy(source, state.at[f, :, :, main], 2 + fields + f)
        source = (half, other)[f // 2].at[:, f % 2]
        arrive["prior", f] = copy(source, prior.at[f], 2 + 2 * fields + f)
    order = ["visc", "ends", ("state", W)]
    order += [(which, f) for f in (U, V, T, W) for which in ("pulled", "state", "prior")]
    for which in dict.fromkeys(order):
        arrive[which].start()

    def ready(*which):
        for name in which:
            if name in arrive:
                arrive.pop(name).wait()

    flat = (fields * rows * step, width)
    state_rows, pulled_rows = state.reshape(flat), pulled.reshape(flat)
    first, last = pad - 1, pad + depth
    for f in range(fields):
        base = f * rows * step
        state_rows[pl.ds(base + first, rows, stride=step), :] = edges_below[outside[f]]
        state_rows[pl.ds(base + last, rows, stride=step), :] = edges_above[outside[f]]
    ready("visc", "ends")
    for f in range(fields):
        for p in range(slabs):
            base, part = (f * rows + p * block) * step, pl.ds(f * block, block)
            pulled_rows[pl.ds(base + first, block, stride=step), :] = ends[p, 0, part]
            pulled_rows[pl.ds(base + last, block, stride=step), :] = ends[p, 1, part]
    ready(("state", W))
    leaving = []
    for f in (U, V, T, W):
        ready(("pulled", f), ("state", f), ("prior", f))
        if f == T:
            ready(("pulled", W))
        along_y = 0.5 * (visc[slabs - 1, block - 1] + visc[0, 0])
        south = along_y * (pulled[f, 0, 0, main] - pulled[f, slabs - 1, block - 1, main])

        def group(p, south):
            after = lax.rem(p + 1, slabs)
            for i in range(block):
                n, m = (p, i + 1) if i + 1 < block else (after, 0)
                own = visc[p, i]
                along_x = 0.5 * (own + east(own))
                along_y = 0.5 * (own + visc[n, m])
                value = pulled[f, p, i, main]
                flux_x = along_x * (east(value) - value)
                flux_y = along_y * (pulled[f, n, m, main] - value)
                rate = flux_x - west(flux_x) + (flux_y - south)
                south = flux_y
                flow = state[W, p, i, above] * pulled[f, p, i, above]
                rate = rate + (flow - state[W, p, i, below] * pulled[f, p, i, below])
                lost = value * (state[f, p, i, above] - state[f, p, i, below])
                if f == U:
                    coupling[p, i] = lost
                elif f == V:
                    coupling[p, i] = coupling[p, i] + lost
                elif f == T:
                    coupling[p, i] = value - (coupling[p, i] + lost)
                    rate = rate + pulled[W, p, i, main]
                else:
                    rate = rate + (coupling[p, i] - lost)
                result = value + time_step * rate - prior[f, p, i]
                planes[f, pl.ds(p * block + i, depth, stride=rows), :] = result
            return south

        lax.fori_loop(0, slabs, group, south)
        leave = copy(planes.at[f], out.at[outside[f]], 2 + f)
        leave.start()
        leaving.append(leave)
    wait_all(leaving)


def last_step(visc, below, above, chunks, states, priors):
    rows, depth, width = visc.shape
    slabs = chunks.shape[0]
    block = rows // slabs
    padded = vmem(fields, slabs, block, depth + 2 * pad, width)
    one = (slabs, block, depth, width)
    return call(
        last_kernel,
        [(visc.reshape(one), anywhere()), (below, whole()), (above, whole())]
        + [(x, anywhere()) for x in (chunks, *states, *priors)],
        [((fields, depth * rows, width), anywhere())],
        [
            padded,
            padded,
            vmem(fields, *one),
            vmem(fields, depth * rows, width),
            vmem(*one),
            vmem(slabs, 2, depth, width),
            vmem(*one),
            dmas(2 + 3 * fields),
        ],
        30 * fields * rows * depth * width,
        "last_step",
    )[0]


def exchange(chunks):
    return lax.all_to_all(chunks, "slab", split_axis=0, concat_axis=0, tiled=True)


def around(value, axis, steps):
    count = lax.axis_size(axis)
    return lax.ppermute(value, axis, [(i, (i + steps) % count) for i in range(count)])


def local(states, viscosity, inverse):
    start = states[0]
    _, depth, rows, width = start.shape
    slabs, segs = lax.axis_size("slab"), lax.axis_size("seg")
    block = rows // slabs
    share = -(-(block + 4) // segs)

    own_seg = jnp.full((1,), lax.axis_index("seg"), jnp.int32)
    visc, visc_send = visc_chunks(own_seg, viscosity, slabs, share)
    visc_share = exchange(visc_send)
    visc_in = [visc_share] + [around(visc_share, "seg", -i) for i in range(1, segs)]
    send_half, _ = to_chunks(start, slabs, outside[W], 2, [visc_send])
    main_half = exchange(send_half)
    mat_high, mat_low, adj_high, adj_low = split(inverse)
    frame = to_frame(own_seg, visc_in)
    send_other, ends = to_chunks(start, slabs, outside[U], 2, [frame, mat_high])
    main_other = exchange(send_other)
    forward = [(i, i + 1) for i in range(slabs - 1)]
    below = lax.ppermute(ends[1], "slab", forward)
    above = lax.ppermute(ends[0], "slab", [(i, j) for j, i in forward])

    own, outer, targets, later = [], [], [], (visc_share, visc_share)
    few = max(1, 3 * block // 8)
    for part, pieces in ((main_half, (block,)), (main_other, (few, block - few))):
        low_rows, high_rows, *again = outer_rows(part, later, pieces)
        low_in = around(high_rows, "slab", 1)
        high_in = around(low_rows, "slab", -1)
        own.append((low_in, part, high_in))
        outer.append(low_rows)
        targets.append([around(piece, "seg", -1) for piece in again])
        later = (low_in, high_in)

    mats = mat_high, mat_low
    first_half = first_step(*own[0], outer[1], frame, *mats)
    out, low_edge, high_edge = second_step(
        first_half, first_half, frame, *mats, W, targets[0], ()
    )
    out = after(out, (own[1][0], own[1][2], targets[1][0]))
    first_other = carried_step(own[1], own[0], out, frame, *mats)
    other, *more = second_step(
        first_other, first_half, frame, *mats, U, targets[1], (out,)
    )
    low_edges = [around(edge, "slab", 1) for edge in (high_edge, more[1])]
    high_edges = [around(edge, "slab", -1) for edge in (low_edge, more[0])]
    half = exchange(out)
    residual = (out, after(other, (*low_edges, *high_edges, half)))
    firsts = (first_half, first_other)
    pulled = adjoint_step(residual, low_edges, high_edges, firsts, frame, adj_high, adj_low)
    planes, other = to_planes((half, exchange(residual[1])), pulled)
    priors = [around(part, "seg", 1) for part in (half, other)]
    gradient = last_step(visc, below, above, exchange(pulled), (send_half, send_other), priors)
    shape = (1, fields, depth, rows, width)
    return (planes.reshape(shape), gradient.reshape(shape))


def solution(mesh):
    in_specs = (P("seg", None, "slab", None, None), P("slab", None, None), P())
    out_specs = (P("seg", None, "slab", None, None), P("seg", None, "slab", None, None))
    return jax.shard_map(local, mesh=mesh, in_specs=in_specs, out_specs=out_specs, check_vma=False)
```

```python
import functools

import jax
import jax.numpy as jnp
from jax import lax
from jax.experimental import pallas as pl
from jax.experimental.pallas import tpu as pltpu
from jax.sharding import PartitionSpec as P

time_step = 0.1
vmem_bytes = 56 * 1024 * 1024
f32, bf16 = jnp.float32, jnp.bfloat16
fields = 4
W, T, U, V = range(4)
outside = (2, 3, 0, 1)
pad = 8
tall = 32


def whole():
    return pl.BlockSpec(memory_space=pltpu.VMEM)


def anywhere():
    return pl.BlockSpec(memory_space=pl.ANY)


def scalars():
    return pl.BlockSpec(memory_space=pltpu.SMEM)


def vmem(*shape):
    return pltpu.VMEM(shape, f32)


def dmas(count):
    return pltpu.SemaphoreType.DMA((count,))


def call(kernel, ins, outs, scratch, flops, name, kind=f32, aliases=None):
    moved = sum(4 * x.size for x, _ in ins)
    return pl.pallas_call(
        kernel,
        in_specs=[spec for _, spec in ins],
        out_specs=tuple(spec for _, spec in outs),
        out_shape=tuple(jax.ShapeDtypeStruct(shape, kind) for shape, _ in outs),
        scratch_shapes=scratch,
        input_output_aliases=aliases or {},
        compiler_params=pltpu.CompilerParams(vmem_limit_bytes=vmem_bytes),
        cost_estimate=pl.CostEstimate(flops=flops, bytes_accessed=moved, transcendentals=0),
        name=name,
    )(*[x for x, _ in ins])


def start_all(pairs, sem):
    copies = [
        pltpu.make_async_copy(source, target, sem.at[i])
        for i, (source, target) in enumerate(pairs)
    ]
    for copy in copies:
        copy.start()
    return copies


def wait_all(copies):
    for copy in copies:
        copy.wait()


def spans(parts, axis=1):
    start = 0
    for part in parts:
        yield part, pl.ds(start, part.shape[axis])
        start += part.shape[axis]


def east(value):
    return pltpu.roll(value, value.shape[1] - 1, 1)


def west(value):
    return pltpu.roll(value, 1, 1)


def parts_of(value):
    high = value.astype(bf16)
    return high, (value - high.astype(f32)).astype(bf16)


def product(matrix_high, matrix_low, high, low):
    dot = functools.partial(jnp.dot, preferred_element_type=f32)
    return dot(matrix_high, high) + (dot(matrix_high, low) + dot(matrix_low, high))


def split_kernel(x_ref, high, low, adj_high, adj_low):
    for f in range(fields):
        high[f], low[f] = parts_of(x_ref[outside[f]])
        adj_high[f], adj_low[f] = parts_of(x_ref[outside[f]].T)


def split(inverse):
    return call(
        split_kernel,
        [(inverse, whole())],
        [(inverse.shape, whole())] * 4,
        [],
        0,
        "split",
        bf16,
    )


def first_chunks_kernel(own, x_ref, visc_in, send, visc, planes, held, extra, flat, sem):
    count, slabs, block, depth, _ = held.shape
    rows, share = slabs * block, extra.shape[1]
    visc_copy = pltpu.make_async_copy(visc_in, flat, sem.at[count])
    visc_copy.start()
    copies = start_all([(x_ref.at[outside[W] + f], planes.at[f]) for f in range(count)], sem)
    visc_copy.wait()
    for y in range(rows):
        visc[y] = flat[pl.ds(y, depth, stride=rows), :]
    for p in range(slabs):
        for i in range(share):
            row = lax.rem(p * block - 2 + share * own[0] + i + rows, rows)
            extra[p, i] = visc[row]
    places = [send.at[:, pl.ds(f * block, block)] for f in range(count)]
    leaving = [
        pltpu.make_async_copy(extra, send.at[:, pl.ds(count * block, share)], sem.at[count])
    ]
    leaving[0].start()
    for f in range(count):
        copies[f].wait()
        for y in range(rows):
            held[f, y // block, y % block] = planes[f, pl.ds(y, depth, stride=rows), :]
        leaving.append(pltpu.make_async_copy(held.at[f], places[f], sem.at[f]))
        leaving[-1].start()
    wait_all(leaving)


def to_first_chunks(own, states, viscosity, slabs, share):
    _, depth, rows, width = states.shape
    block = rows // slabs
    return call(
        first_chunks_kernel,
        [
            (own, scalars()),
            (states.reshape(fields, -1, width), anywhere()),
            (viscosity.reshape(-1, width), anywhere()),
        ],
        [
            ((slabs, 2 * block + share, depth, width), anywhere()),
            ((rows, depth, width), whole()),
        ],
        [
            vmem(2, depth * rows, width),
            vmem(2, slabs, block, depth, width),
            vmem(slabs, share, depth, width),
            vmem(depth * rows, width),
            dmas(3),
        ],
        0,
        "to_first_chunks",
    )


def unpack_kernel(chunks, _, low_rows, high_rows, main, visc, sem):
    block, share = main.shape[2], visc.shape[1]
    pairs = [(chunks.at[:, pl.ds(2 * block, share)], visc)]
    for f in range(2):
        start = f * block
        pairs.append((chunks.at[:, pl.ds(start, 2)], low_rows.at[:, f]))
        pairs.append((chunks.at[:, pl.ds(start + block - 2, 2)], high_rows.at[:, f]))
        pairs.append((chunks.at[:, pl.ds(start, block)], main.at[:, f]))
    wait_all(start_all(pairs, sem))


def unpack(chunks, block, later):
    slabs, total, depth, width = chunks.shape
    sizes = [(2, 2), (2, 2), (2, block), (total - 2 * block,)]
    return call(
        unpack_kernel,
        [(chunks, anywhere()), (later, anywhere())],
        [((slabs, *size, depth, width), whole()) for size in sizes],
        [dmas(7)],
        0,
        "unpack",
    )


def frame_kernel(own, *refs):
    *shares, frame, sem = refs
    slabs, share, depth, _ = shares[0].shape
    pairs = []
    for i, part in enumerate(shares):
        start = lax.rem(own[0] + i, len(shares)) * share
        for p in range(slabs):
            pairs.append((part.at[p], frame.at[pl.ds(start, share), pl.ds(p * depth, depth)]))
    wait_all(start_all(pairs, sem))


def to_frame(own, shares):
    slabs, share, depth, width = shares[0].shape
    return call(
        frame_kernel,
        [(own, scalars())] + [(x, anywhere()) for x in shares],
        [((len(shares) * share, slabs * depth, width), whole())],
        [dmas(len(shares) * slabs)],
        0,
        "to_frame",
    )[0]


def chunks_kernel(start, x_ref, *refs):
    send, edges, planes, held, sem = refs[-5:]
    count, slabs, block, depth, _ = held.shape
    rows = slabs * block
    copies = start_all([(x_ref.at[start + f], planes.at[f]) for f in range(count)], sem)
    ends = [
        pltpu.make_async_copy(x_ref.at[:, pl.ds(z * rows, rows)], edges.at[i], sem.at[count + i])
        for i, z in enumerate((0, depth - 1))
    ]
    for copy in ends:
        copy.start()
    leaving = []
    for f in range(count):
        copies[f].wait()
        for y in range(rows):
            held[f, y // block, y % block] = planes[f, pl.ds(y, depth, stride=rows), :]
        copy = pltpu.make_async_copy(held.at[f], send.at[:, f], sem.at[f])
        copy.start()
        leaving.append(copy)
    wait_all(leaving + ends)


def to_chunks(states, slabs, start, count, later):
    _, depth, rows, width = states.shape
    block = rows // slabs
    return call(
        functools.partial(chunks_kernel, start),
        [(states.reshape(fields, -1, width), anywhere())]
        + [(x, anywhere()) for x in later],
        [
            ((slabs, count, block, depth, width), anywhere()),
            ((2, fields, rows, width), whole()),
        ],
        [
            vmem(count, depth * rows, width),
            vmem(count, slabs, block, depth, width),
            dmas(count + 2),
        ],
        0,
        "to_chunks",
    )


def planes_kernel(half, other, _, o_ref, again, held, sem):
    slabs, _, block, depth, _ = half.shape
    rows = slabs * block
    pairs = []
    for p in range(slabs):
        place = pl.ds(p * block, block)
        pairs.append((half.at[p], held.at[pl.ds(0, 2), place]))
        pairs.append((other.at[p], held.at[pl.ds(2, 2), place]))
    wait_all(start_all(pairs, sem))
    places = [held.at[pl.ds(2, 2), pl.ds(p * block, block)] for p in range(slabs)]
    copies = start_all([(places[p], again.at[p]) for p in range(slabs)], sem)

    def row(y, _):
        for f in range(fields):
            where = pl.ds(outside[f] * depth * rows + y, depth, stride=rows)
            o_ref[where, :] = held[f, y]
        return 0

    lax.fori_loop(0, rows, row, 0, unroll=4)
    wait_all(copies)


def to_planes(halves, later):
    slabs, _, block, depth, width = halves[0].shape
    return call(
        planes_kernel,
        [(x, anywhere()) for x in (*halves, later)],
        [
            ((fields * depth * slabs * block, width), whole()),
            (halves[1].shape, anywhere()),
        ],
        [vmem(fields, slabs * block, depth, width), dmas(2 * slabs)],
        0,
        "to_planes",
    )


def clear_pads(ref):
    edge = jnp.zeros(ref.shape[1:2] + (pad, ref.shape[3]), f32)
    for f in range(ref.shape[0]):
        ref[f, :, 0:pad] = edge
        ref[f, :, ref.shape[2] - pad :] = edge


def first_fluxes(state, visc, shift, carry):
    order = visc.shape[1]
    for z in range(0, order, tall):
        here, pads = pl.ds(z, tall), pl.ds(z + pad, tall)
        along_y = 0.5 * (visc[shift, here] + visc[shift + 1, here])
        for f in range(state.shape[0]):
            carry[f, here] = along_y * (state[f, 1, pads] - state[f, 0, pads])


def spread_of(state, f, j, value, here, pads, along_x, along_y, carry):
    flux_x = along_x * (east(value) - value)
    flux_y = along_y * (state[f, j + 1, pads] - value)
    spread = flux_x - west(flux_x) + (flux_y - carry[f, here])
    carry[f, here] = flux_y
    return spread


def advance_rows(state, speeds, shift, coupled, scratch, count, finish):
    visc, mat_high, mat_low, carry, high, low = scratch
    order, width = visc.shape[1:]
    first_fluxes(state, visc, shift, carry)

    def pair(k, _):
        for half in range(2):
            j = 2 * k + half + 1
            side = slice(half * width, (half + 1) * width)
            for z in range(0, order, tall):
                here, pads = pl.ds(z, tall), pl.ds(z + pad, tall)
                above, below = pl.ds(z + pad + 1, tall), pl.ds(z + pad - 1, tall)
                own = visc[j + shift, here]
                along_x = 0.5 * (own + east(own))
                along_y = 0.5 * (own + visc[j + shift + 1, here])
                speed = speeds[j, pads]
                for f in range(2):
                    value = state[f, j, pads]
                    rate = spread_of(state, f, j, value, here, pads, along_x, along_y, carry)
                    rate = rate - speed * (state[f, j, above] - state[f, j, below])
                    if coupled:
                        rate = rate + state[1 - f, j, pads]
                    high[f, here, side], low[f, here, side] = parts_of(value + time_step * rate)
        for f in range(2):
            out = product(mat_high[f], mat_low[f], high[f], low[f])
            finish(f, 2 * k, out[:, :width])
            finish(f, 2 * k + 1, out[:, width:])
        return 0

    lax.fori_loop(0, count // 2, pair, 0)


def step_scratch(order, width, count):
    return [
        vmem(count, order, width),
        pltpu.VMEM((count, order, 2 * width), bf16),
        pltpu.VMEM((count, order, 2 * width), bf16),
    ]


def two_scratch(frame):
    _, order, width = frame.shape
    matrix = pltpu.VMEM((2, order, order), bf16)
    return [vmem(*frame.shape), matrix, matrix] + step_scratch(order, width, 2)


def constants(base, sources, scratch):
    frame, mat_high, mat_low = sources
    two = pl.ds(base, 2)
    return [(frame, scratch[0]), (mat_high.at[two], scratch[1]), (mat_low.at[two], scratch[2])]


def rows_of(low_in, main, high_in, p, target):
    _, _, block, depth, _ = main.shape
    padded = pl.ds(p * depth + pad, depth)
    for row, count, part in ((0, 2, low_in), (2, block, main), (block + 2, 2, high_in)):
        yield part, target.at[:, pl.ds(row, count), padded]


def first_finish(first, order):
    def finish(f, row, piece):
        first[f, row, pl.ds(pad, order)] = piece

    return finish


def first_kernel(low_in, main, high_in, _, *refs):
    sources, (first, state, *scratch, sem) = refs[:3], refs[3:]
    slabs, _, block, depth, _ = main.shape
    pairs = constants(W, sources, scratch)
    for p in range(slabs):
        pairs += [(a.at[p], b) for a, b in rows_of(low_in, main, high_in, p, state)]
    copies = start_all(pairs, sem)
    clear_pads(state)
    clear_pads(first)
    wait_all(copies)
    finish = first_finish(first, slabs * depth)
    advance_rows(state, state.at[W], 0, True, scratch, block + 2, finish)


def first_step(low_in, main, high_in, later, frame, mat_high, mat_low):
    slabs, _, block, depth, width = main.shape
    order = slabs * depth
    volume = 2 * (block + 2) * order * width
    return call(
        first_kernel,
        [(x, anywhere()) for x in (low_in, main, high_in, later, frame, mat_high, mat_low)],
        [((2, block + 2, order + 2 * pad, width), whole())],
        [vmem(2, block + 4, order + 2 * pad, width)]
        + two_scratch(frame)
        + [dmas(3 * slabs + 3)],
        6 * order * volume,
        "first_step",
    )[0]


def carried_kernel(*refs):
    low_in, main, high_in, low_w, main_w, high_w, _ = refs[:7]
    sources, (first, state, speeds, *scratch, sem) = refs[7:10], refs[10:]
    slabs, _, block, depth, _ = main.shape
    pairs = constants(U, sources, scratch)
    for p in range(slabs):
        pairs += [(a.at[p], b) for a, b in rows_of(low_in, main, high_in, p, state)]
        w_rows = rows_of(low_w, main_w, high_w, p, speeds)
        pairs += [(a.at[p, pl.ds(W, 1)], b) for a, b in w_rows]
    copies = start_all(pairs, sem)
    clear_pads(state)
    clear_pads(first)
    wait_all(copies)
    finish = first_finish(first, slabs * depth)
    advance_rows(state, speeds.at[0], 0, False, scratch, block + 2, finish)


def carried_step(own, with_w, later, frame, mat_high, mat_low):
    slabs, _, block, depth, width = own[1].shape
    order = slabs * depth
    volume = 2 * (block + 2) * order * width
    return call(
        carried_kernel,
        [(x, anywhere()) for x in (*own, *with_w, later, frame, mat_high, mat_low)],
        [((2, block + 2, order + 2 * pad, width), whole())],
        [
            vmem(2, block + 4, order + 2 * pad, width),
            vmem(1, block + 4, order + 2 * pad, width),
        ]
        + two_scratch(frame)
        + [dmas(6 * slabs + 3)],
        6 * order * volume,
        "carried_step",
    )[0]


def second_kernel(base, count, first, with_w, *refs):
    sources, targets = refs[:3], refs[3 : 3 + count]
    out, low_edge, high_edge, state, speeds, *scratch, held, sem = refs[-13:]
    slabs, _, block, depth, _ = out.shape
    places = [held.at[:, :, pl.ds(p * depth, depth)] for p in range(slabs)]
    pairs = constants(base, sources, scratch) + [(first, state)]
    if base != W:
        pairs.append((with_w.at[W], speeds))
    for target, span in spans(targets, 2):
        for p in range(slabs):
            pairs.append((target.at[p], held.at[:, span, pl.ds(p * depth, depth)]))
    wait_all(start_all(pairs, sem))

    def finish(f, row, piece):
        held[f, row] = piece - held[f, row]

    speeds = state.at[W] if base == W else speeds
    advance_rows(state, speeds, 1, base == W, scratch, block, finish)
    copies = start_all([(places[p], out.at[p]) for p in range(slabs)], sem)
    low_edge[...] = held[:, 0]
    high_edge[...] = held[:, block - 1]
    wait_all(copies)


def second_step(first, with_w, frame, mat_high, mat_low, base, targets, later):
    _, order, width = frame.shape
    slabs, _, _, depth, _ = targets[0].shape
    block = sum(target.shape[2] for target in targets)
    operands = (first, with_w, frame, mat_high, mat_low, *targets, *later)
    return call(
        functools.partial(second_kernel, base, len(targets)),
        [(x, anywhere()) for x in operands],
        [((slabs, 2, block, depth, width), anywhere())] + [((2, order, width), whole())] * 2,
        [vmem(*first.shape), vmem(*first.shape[1:])]
        + two_scratch(frame)
        + [vmem(2, block, order, width), dmas(2 * slabs + 5)],
        6 * order * 2 * block * order * width,
        "second_step",
    )


def after_kernel(*refs):
    del refs


def after(value, later):
    return call(
        after_kernel,
        [(x, anywhere()) for x in (value, *later)],
        [(value.shape, anywhere())],
        [],
        0,
        "after",
        aliases={0: 0},
    )[0]


def outer_kernel(chunks, *refs):
    *outs, sem = refs[-3:]
    block = chunks.shape[2]
    low, high = chunks.at[:, :, pl.ds(0, 2)], chunks.at[:, :, pl.ds(block - 2, 2)]
    wait_all(start_all([(low, outs[0]), (high, outs[1])], sem))


def pieces_kernel(chunks, _, *refs):
    *outs, sem = refs
    wait_all(start_all([(chunks.at[:, :, span], part) for part, span in spans(outs, 2)], sem))


def row_parts(kernel, chunks, later, sizes, name):
    slabs, count, _, depth, width = chunks.shape
    return call(
        kernel,
        [(chunks, anywhere())] + [(x, anywhere()) for x in later],
        [((slabs, count, size, depth, width), whole()) for size in sizes],
        [dmas(len(sizes))],
        0,
        name,
    )


def adjoint_kernel(*refs):
    halves, low_edges, high_edges = refs[0:2], refs[2:4], refs[4:6]
    firsts, (visc, mat_high, mat_low) = refs[6:8], refs[8:11]
    out, cot, pulled, ends, carry, high, low, sem = refs[11:]
    slabs, _, block, depth, width = halves[0].shape
    order = slabs * depth
    main = pl.ds(1, block)
    pairs = []
    for source, span in spans(halves):
        for p in range(slabs):
            pairs.append((source.at[p], cot.at[span, main, pl.ds(p * depth, depth)]))
    for i in range(2):
        pairs.append((low_edges[i], cot.at[pl.ds(2 * i, 2), 0]))
        pairs.append((high_edges[i], cot.at[pl.ds(2 * i, 2), block + 1]))
    copies = start_all(pairs, sem)
    clear_pads(pulled)
    wait_all(copies)

    def pull(k, _):
        for f in range(fields):
            pair = jnp.concatenate([cot[f, 2 * k], cot[f, 2 * k + 1]], axis=1)
            out = product(mat_high[f], mat_low[f], *parts_of(pair))
            pulled[f, 2 * k, pl.ds(pad, order)] = out[:, :width]
            pulled[f, 2 * k + 1, pl.ds(pad, order)] = out[:, width:]
        return 0

    lax.fori_loop(0, (block + 2) // 2, pull, 0)
    first_fluxes(pulled, visc, 1, carry)

    def rows(k, _):
        for half in range(2):
            j = 2 * k + half + 1
            side = slice(half * width, (half + 1) * width)
            for z in range(0, order, tall):
                here, pads = pl.ds(z, tall), pl.ds(z + pad, tall)
                above, below = pl.ds(z + pad + 1, tall), pl.ds(z + pad - 1, tall)
                own = visc[j + 1, here]
                along_x = 0.5 * (own + east(own))
                along_y = 0.5 * (own + visc[j + 2, here])
                speed_above, speed_below = firsts[0][W, j, above], firsts[0][W, j, below]
                coupling = pulled[T, j, pads]
                for f in (U, V, T, W):
                    value = pulled[f, j, pads]
                    rate = spread_of(pulled, f, j, value, here, pads, along_x, along_y, carry)
                    up, down = pulled[f, j, above], pulled[f, j, below]
                    rate = rate + (speed_above * up - speed_below * down)
                    if f == W:
                        slope = speed_above - speed_below
                    else:
                        ref, i = firsts[f // 2], f % 2
                        slope = ref[i, j, above] - ref[i, j, below]
                    coupling = coupling - value * slope
                    if f == T:
                        rate = rate + pulled[W, j, pads]
                    if f == W:
                        rate = rate + coupling
                    high[f, here, side], low[f, here, side] = parts_of(value + time_step * rate)
        for f in range(fields):
            out = product(mat_high[f], mat_low[f], high[f], low[f])
            cot[f, 2 * k + 1] = out[:, :width]
            cot[f, 2 * k + 2] = out[:, width:]
        return 0

    lax.fori_loop(0, block // 2, rows, 0)
    pairs = []
    for p in range(slabs):
        for f in range(fields):
            source = cot.at[f, main, pl.ds(p * depth, depth)]
            pairs.append((source, out.at[p, pl.ds(f * block, block)]))
    copies = start_all(pairs, sem)
    for p in range(slabs):
        for f in range(fields):
            for y in range(block):
                for side, z in ((0, p * depth - 1), (1, (p + 1) * depth)):
                    to = slice(f * block + y, f * block + y + 1)
                    if 0 <= z < order:
                        ends[p, side, to] = cot[f, y + 1, z : z + 1]
                    else:
                        ends[p, side, to] = jnp.zeros((1, width), f32)
    ends_copy = pltpu.make_async_copy(
        ends, out.at[:, pl.ds(fields * block, 2)], sem.at[len(pairs)]
    )
    ends_copy.start()
    wait_all(copies)
    ends_copy.wait()


def adjoint_step(halves, low_edges, high_edges, firsts, visc, mat_high, mat_low):
    slabs, _, block, depth, width = halves[0].shape
    order = slabs * depth
    volume = fields * (block + 1) * order * width
    return call(
        adjoint_kernel,
        [(x, anywhere()) for x in (*halves, *low_edges, *high_edges)]
        + [(x, whole()) for x in (*firsts, visc, mat_high, mat_low)],
        [((slabs, fields * block + 2, depth, width), anywhere())],
        [
            vmem(fields, block + 2, order, width),
            vmem(fields, block + 2, order + 2 * pad, width),
            vmem(slabs, 2, depth, width),
        ]
        + step_scratch(order, width, fields)
        + [dmas(slabs * fields + 1)],
        12 * order * volume,
        "adjoint_step",
    )[0]


def last_kernel(*refs):
    visc_in, edges_below, edges_above, chunks, *states, half, other, out = refs[:9]
    pulled, state, prior, planes, coupling, ends, visc, sem = refs[9:]
    slabs, block, depth, width = visc.shape
    rows, step = slabs * block, pulled.shape[3]
    main = pl.ds(pad, depth)
    above, below = pl.ds(pad + 1, depth), pl.ds(pad - 1, depth)

    def copy(source, target, which):
        return pltpu.make_async_copy(source, target, sem.at[which])

    arrive = {"visc": copy(visc_in, visc, 0)}
    arrive["ends"] = copy(chunks.at[:, pl.ds(fields * block, 2)], ends, 1)
    for f in range(fields):
        source = chunks.at[:, pl.ds(f * block, block)]
        arrive["pulled", f] = copy(source, pulled.at[f, :, :, main], 2 + f)
        source = states[0].at[:, pl.ds(f * block, block)] if f < 2 else states[1].at[:, f - 2]
        arrive["state", f] = copy(source, state.at[f, :, :, main], 2 + fields + f)
        source = (half, other)[f // 2].at[:, f % 2]
        arrive["prior", f] = copy(source, prior.at[f], 2 + 2 * fields + f)
    order = ["visc", "ends", ("state", W)]
    order += [(which, f) for f in (U, V, T, W) for which in ("pulled", "state", "prior")]
    for which in dict.fromkeys(order):
        arrive[which].start()

    def ready(*which):
        for name in which:
            if name in arrive:
                arrive.pop(name).wait()

    flat = (fields * rows * step, width)
    state_rows, pulled_rows = state.reshape(flat), pulled.reshape(flat)
    first, last = pad - 1, pad + depth
    for f in range(fields):
        base = f * rows * step
        state_rows[pl.ds(base + first, rows, stride=step), :] = edges_below[outside[f]]
        state_rows[pl.ds(base + last, rows, stride=step), :] = edges_above[outside[f]]
    ready("visc", "ends")
    for f in range(fields):
        for p in range(slabs):
            base, part = (f * rows + p * block) * step, pl.ds(f * block, block)
            pulled_rows[pl.ds(base + first, block, stride=step), :] = ends[p, 0, part]
            pulled_rows[pl.ds(base + last, block, stride=step), :] = ends[p, 1, part]
    ready(("state", W))
    leaving = []
    for f in (U, V, T, W):
        ready(("pulled", f), ("state", f), ("prior", f))
        if f == T:
            ready(("pulled", W))
        along_y = 0.5 * (visc[slabs - 1, block - 1] + visc[0, 0])
        south = along_y * (pulled[f, 0, 0, main] - pulled[f, slabs - 1, block - 1, main])

        def group(p, south):
            after = lax.rem(p + 1, slabs)
            for i in range(block):
                n, m = (p, i + 1) if i + 1 < block else (after, 0)
                own = visc[p, i]
                along_x = 0.5 * (own + east(own))
                along_y = 0.5 * (own + visc[n, m])
                value = pulled[f, p, i, main]
                flux_x = along_x * (east(value) - value)
                flux_y = along_y * (pulled[f, n, m, main] - value)
                rate = flux_x - west(flux_x) + (flux_y - south)
                south = flux_y
                flow = state[W, p, i, above] * pulled[f, p, i, above]
                rate = rate + (flow - state[W, p, i, below] * pulled[f, p, i, below])
                lost = value * (state[f, p, i, above] - state[f, p, i, below])
                if f == U:
                    coupling[p, i] = lost
                elif f == V:
                    coupling[p, i] = coupling[p, i] + lost
                elif f == T:
                    coupling[p, i] = value - (coupling[p, i] + lost)
                    rate = rate + pulled[W, p, i, main]
                else:
                    rate = rate + (coupling[p, i] - lost)
                result = value + time_step * rate - prior[f, p, i]
                planes[f, pl.ds(p * block + i, depth, stride=rows), :] = result
            return south

        lax.fori_loop(0, slabs, group, south)
        leave = copy(planes.at[f], out.at[outside[f]], 2 + f)
        leave.start()
        leaving.append(leave)
    wait_all(leaving)


def last_step(visc, below, above, chunks, states, priors):
    rows, depth, width = visc.shape
    slabs = chunks.shape[0]
    block = rows // slabs
    padded = vmem(fields, slabs, block, depth + 2 * pad, width)
    one = (slabs, block, depth, width)
    return call(
        last_kernel,
        [(visc.reshape(one), anywhere()), (below, whole()), (above, whole())]
        + [(x, anywhere()) for x in (chunks, *states, *priors)],
        [((fields, depth * rows, width), anywhere())],
        [
            padded,
            padded,
            vmem(fields, *one),
            vmem(fields, depth * rows, width),
            vmem(*one),
            vmem(slabs, 2, depth, width),
            vmem(*one),
            dmas(2 + 3 * fields),
        ],
        30 * fields * rows * depth * width,
        "last_step",
    )[0]


def exchange(chunks):
    return lax.all_to_all(chunks, "slab", split_axis=0, concat_axis=0, tiled=True)


def around(value, axis, steps):
    count = lax.axis_size(axis)
    return lax.ppermute(value, axis, [(i, (i + steps) % count) for i in range(count)])


def local(states, viscosity, inverse):
    start = states[0]
    _, depth, rows, width = start.shape
    slabs, segs = lax.axis_size("slab"), lax.axis_size("seg")
    block = rows // slabs
    share = -(-(block + 4) // segs)

    own_seg = jnp.full((1,), lax.axis_index("seg"), jnp.int32)
    send_half, visc = to_first_chunks(own_seg, start, viscosity, slabs, share)
    packed = exchange(send_half)
    mat_high, mat_low, adj_high, adj_low = split(inverse)
    send_other, ends = to_chunks(start, slabs, outside[U], 2, [mat_high])
    main_other = exchange(send_other)
    forward = [(i, i + 1) for i in range(slabs - 1)]
    below = lax.ppermute(ends[1], "slab", forward)
    above = lax.ppermute(ends[0], "slab", [(i, j) for j, i in forward])

    low_rows, high_rows, main_half, visc_share = unpack(packed, block, send_other)
    visc_in = [visc_share] + [around(visc_share, "seg", -i) for i in range(1, segs)]
    low_in, high_in = around(high_rows, "slab", 1), around(low_rows, "slab", -1)
    frame = to_frame(own_seg, visc_in)
    main_half = after(main_half, (frame,))
    half_rows = (low_in, main_half, high_in)
    target = around(main_half, "seg", -1)

    sizes, few = (2, 2), max(1, block // 8)
    low_rows, high_rows = row_parts(
        outer_kernel, main_other, (low_in, high_in, frame), sizes, "outer_rows"
    )
    other_rows = (around(high_rows, "slab", 1), main_other, around(low_rows, "slab", -1))
    sizes = (few, block - few)
    parts = row_parts(pieces_kernel, main_other, (low_rows,), sizes, "pieces")
    targets = [around(part, "seg", -1) for part in parts]

    mats = mat_high, mat_low
    first_half = first_step(*half_rows, parts[0], frame, *mats)
    out, low_edge, high_edge = second_step(
        first_half, first_half, frame, *mats, W, (target,), ()
    )
    out = after(out, (other_rows[0], other_rows[2], targets[0]))
    first_other = carried_step(other_rows, half_rows, out, frame, *mats)
    other, *more = second_step(first_other, first_half, frame, *mats, U, targets, (out,))
    low_edges = [around(edge, "slab", 1) for edge in (high_edge, more[1])]
    high_edges = [around(edge, "slab", -1) for edge in (low_edge, more[0])]
    half = exchange(out)
    residual = (out, after(other, (*low_edges, *high_edges, half)))
    firsts = (first_half, first_other)
    pulled = adjoint_step(residual, low_edges, high_edges, firsts, frame, adj_high, adj_low)
    planes, other = to_planes((half, exchange(residual[1])), pulled)
    priors = [around(part, "seg", 1) for part in (half, other)]
    gradient = last_step(visc, below, above, exchange(pulled), (send_half, send_other), priors)
    shape = (1, fields, depth, rows, width)
    return (planes.reshape(shape), gradient.reshape(shape))


def solution(mesh):
    in_specs = (P("seg", None, "slab", None, None), P("slab", None, None), P())
    out_specs = (P("seg", None, "slab", None, None), P("seg", None, "slab", None, None))
    return jax.shard_map(local, mesh=mesh, in_specs=in_specs, out_specs=out_specs, check_vma=False)
```

```python
import functools
import math

import jax
import jax.numpy as jnp
from jax import lax
from jax.experimental import pallas as pl
from jax.experimental.pallas import tpu as pltpu
from jax.sharding import PartitionSpec as P

time_step = 0.1
mebibyte = 1024 * 1024
f32, bf16 = jnp.float32, jnp.bfloat16
fields = 4
W, T, U, V = range(4)
outside = (2, 3, 0, 1)
pad = 8
tall = 32


def whole():
    return pl.BlockSpec(memory_space=pltpu.VMEM)


def anywhere():
    return pl.BlockSpec(memory_space=pl.ANY)


def scalars():
    return pl.BlockSpec(memory_space=pltpu.SMEM)


def vmem(*shape):
    return pltpu.VMEM(shape, f32)


def dmas(count):
    return pltpu.SemaphoreType.DMA((count,))


def call(kernel, ins, outs, scratch, flops, name, kind=f32, aliases=None):
    moved = sum(4 * x.size for x, _ in ins)
    held = [(x.shape, x.dtype) for x, spec in ins if spec.memory_space == pltpu.VMEM]
    held += [(shape, kind) for shape, spec in outs if spec.memory_space == pltpu.VMEM]
    held += [(x.shape, x.dtype) for x in scratch if x.memory_space == pltpu.VMEM]
    needed = sum(math.prod(shape) * jnp.dtype(dtype).itemsize for shape, dtype in held)
    limit = min(56 * mebibyte, 6 * mebibyte + needed * 9 // 8)
    return pl.pallas_call(
        kernel,
        in_specs=[spec for _, spec in ins],
        out_specs=tuple(spec for _, spec in outs),
        out_shape=tuple(jax.ShapeDtypeStruct(shape, kind) for shape, _ in outs),
        scratch_shapes=scratch,
        input_output_aliases=aliases or {},
        compiler_params=pltpu.CompilerParams(vmem_limit_bytes=limit),
        cost_estimate=pl.CostEstimate(flops=flops, bytes_accessed=moved, transcendentals=0),
        name=name,
    )(*[x for x, _ in ins])


def start_all(pairs, sem):
    copies = [
        pltpu.make_async_copy(source, target, sem.at[i])
        for i, (source, target) in enumerate(pairs)
    ]
    for copy in copies:
        copy.start()
    return copies


def wait_all(copies):
    for copy in copies:
        copy.wait()


def spans(parts, axis=1):
    start = 0
    for part in parts:
        yield part, pl.ds(start, part.shape[axis])
        start += part.shape[axis]


def east(value):
    return pltpu.roll(value, value.shape[1] - 1, 1)


def west(value):
    return pltpu.roll(value, 1, 1)


def parts_of(value):
    high = value.astype(bf16)
    return high, (value - high.astype(f32)).astype(bf16)


def product(matrix_high, matrix_low, high, low):
    dot = functools.partial(jnp.dot, preferred_element_type=f32)
    return dot(matrix_high, high) + (dot(matrix_high, low) + dot(matrix_low, high))


def split_kernel(x_ref, high, low, adj_high, adj_low):
    for f in range(fields):
        high[f], low[f] = parts_of(x_ref[outside[f]])
        adj_high[f], adj_low[f] = parts_of(x_ref[outside[f]].T)


def split(inverse):
    return call(
        split_kernel,
        [(inverse, whole())],
        [(inverse.shape, whole())] * 4,
        [],
        0,
        "split",
        bf16,
    )


def first_chunks_kernel(own, x_ref, visc_in, send, visc, planes, held, extra, flat, sem):
    count, slabs, block, depth, _ = held.shape
    rows, share = slabs * block, extra.shape[1]
    visc_copy = pltpu.make_async_copy(visc_in, flat, sem.at[count])
    visc_copy.start()
    copies = start_all([(x_ref.at[outside[W] + f], planes.at[f]) for f in range(count)], sem)
    visc_copy.wait()
    for y in range(rows):
        visc[y] = flat[pl.ds(y, depth, stride=rows), :]
    for p in range(slabs):
        for i in range(share):
            row = lax.rem(p * block - 2 + share * own[0] + i + rows, rows)
            extra[p, i] = visc[row]
    places = [send.at[:, pl.ds(f * block, block)] for f in range(count)]
    leaving = [
        pltpu.make_async_copy(extra, send.at[:, pl.ds(count * block, share)], sem.at[count])
    ]
    leaving[0].start()
    for f in range(count):
        copies[f].wait()
        for y in range(rows):
            held[f, y // block, y % block] = planes[f, pl.ds(y, depth, stride=rows), :]
        leaving.append(pltpu.make_async_copy(held.at[f], places[f], sem.at[f]))
        leaving[-1].start()
    wait_all(leaving)


def to_first_chunks(own, states, viscosity, slabs, share):
    _, depth, rows, width = states.shape
    block = rows // slabs
    return call(
        first_chunks_kernel,
        [
            (own, scalars()),
            (states.reshape(fields, -1, width), anywhere()),
            (viscosity.reshape(-1, width), anywhere()),
        ],
        [
            ((slabs, 2 * block + share, depth, width), anywhere()),
            ((rows, depth, width), whole()),
        ],
        [
            vmem(2, depth * rows, width),
            vmem(2, slabs, block, depth, width),
            vmem(slabs, share, depth, width),
            vmem(depth * rows, width),
            dmas(3),
        ],
        0,
        "to_first_chunks",
    )


def unpack_kernel(chunks, _, low_rows, high_rows, main, visc, sem):
    block, share = main.shape[2], visc.shape[1]
    pairs = [(chunks.at[:, pl.ds(2 * block, share)], visc)]
    for f in range(2):
        start = f * block
        pairs.append((chunks.at[:, pl.ds(start, 2)], low_rows.at[:, f]))
        pairs.append((chunks.at[:, pl.ds(start + block - 2, 2)], high_rows.at[:, f]))
        pairs.append((chunks.at[:, pl.ds(start, block)], main.at[:, f]))
    wait_all(start_all(pairs, sem))


def unpack(chunks, block, later):
    slabs, total, depth, width = chunks.shape
    sizes = [(2, 2), (2, 2), (2, block), (total - 2 * block,)]
    return call(
        unpack_kernel,
        [(chunks, anywhere()), (later, anywhere())],
        [((slabs, *size, depth, width), whole()) for size in sizes],
        [dmas(7)],
        0,
        "unpack",
    )


def frame_kernel(own, *refs):
    *shares, frame, sem = refs
    slabs, share, depth, _ = shares[0].shape
    pairs = []
    for i, part in enumerate(shares):
        start = lax.rem(own[0] + i, len(shares)) * share
        for p in range(slabs):
            pairs.append((part.at[p], frame.at[pl.ds(start, share), pl.ds(p * depth, depth)]))
    wait_all(start_all(pairs, sem))


def to_frame(own, shares):
    slabs, share, depth, width = shares[0].shape
    return call(
        frame_kernel,
        [(own, scalars())] + [(x, anywhere()) for x in shares],
        [((len(shares) * share, slabs * depth, width), whole())],
        [dmas(len(shares) * slabs)],
        0,
        "to_frame",
    )[0]


def chunks_kernel(start, x_ref, *refs):
    send, edges, planes, held, sem = refs[-5:]
    count, slabs, block, depth, _ = held.shape
    rows = slabs * block
    copies = start_all([(x_ref.at[start + f], planes.at[f]) for f in range(count)], sem)
    ends = [
        pltpu.make_async_copy(x_ref.at[:, pl.ds(z * rows, rows)], edges.at[i], sem.at[count + i])
        for i, z in enumerate((0, depth - 1))
    ]
    for copy in ends:
        copy.start()
    leaving = []
    for f in range(count):
        copies[f].wait()
        for y in range(rows):
            held[f, y // block, y % block] = planes[f, pl.ds(y, depth, stride=rows), :]
        copy = pltpu.make_async_copy(held.at[f], send.at[:, f], sem.at[f])
        copy.start()
        leaving.append(copy)
    wait_all(leaving + ends)


def to_chunks(states, slabs, start, count, later):
    _, depth, rows, width = states.shape
    block = rows // slabs
    return call(
        functools.partial(chunks_kernel, start),
        [(states.reshape(fields, -1, width), anywhere())]
        + [(x, anywhere()) for x in later],
        [
            ((slabs, count, block, depth, width), anywhere()),
            ((2, fields, rows, width), whole()),
        ],
        [
            vmem(count, depth * rows, width),
            vmem(count, slabs, block, depth, width),
            dmas(count + 2),
        ],
        0,
        "to_chunks",
    )


def planes_kernel(half, other, _, o_ref, again, held, sem):
    slabs, _, block, depth, _ = half.shape
    rows = slabs * block
    pairs = []
    for p in range(slabs):
        place = pl.ds(p * block, block)
        pairs.append((half.at[p], held.at[pl.ds(0, 2), place]))
        pairs.append((other.at[p], held.at[pl.ds(2, 2), place]))
    wait_all(start_all(pairs, sem))
    places = [held.at[pl.ds(2, 2), pl.ds(p * block, block)] for p in range(slabs)]
    copies = start_all([(places[p], again.at[p]) for p in range(slabs)], sem)

    def row(y, _):
        for f in range(fields):
            where = pl.ds(outside[f] * depth * rows + y, depth, stride=rows)
            o_ref[where, :] = held[f, y]
        return 0

    lax.fori_loop(0, rows, row, 0, unroll=4)
    wait_all(copies)


def to_planes(halves, later):
    slabs, _, block, depth, width = halves[0].shape
    return call(
        planes_kernel,
        [(x, anywhere()) for x in (*halves, later)],
        [
            ((fields * depth * slabs * block, width), whole()),
            (halves[1].shape, anywhere()),
        ],
        [vmem(fields, slabs * block, depth, width), dmas(2 * slabs)],
        0,
        "to_planes",
    )


def clear_pads(ref):
    edge = jnp.zeros(ref.shape[1:2] + (pad, ref.shape[3]), f32)
    for f in range(ref.shape[0]):
        ref[f, :, 0:pad] = edge
        ref[f, :, ref.shape[2] - pad :] = edge


def first_fluxes(state, visc, shift, carry):
    order = visc.shape[1]
    for z in range(0, order, tall):
        here, pads = pl.ds(z, tall), pl.ds(z + pad, tall)
        along_y = 0.5 * (visc[shift, here] + visc[shift + 1, here])
        for f in range(state.shape[0]):
            carry[f, here] = along_y * (state[f, 1, pads] - state[f, 0, pads])


def spread_of(state, f, j, value, here, pads, along_x, along_y, carry):
    flux_x = along_x * (east(value) - value)
    flux_y = along_y * (state[f, j + 1, pads] - value)
    spread = flux_x - west(flux_x) + (flux_y - carry[f, here])
    carry[f, here] = flux_y
    return spread


def advance_rows(state, speeds, shift, coupled, scratch, count, finish):
    visc, mat_high, mat_low, carry, high, low = scratch
    order, width = visc.shape[1:]
    first_fluxes(state, visc, shift, carry)

    def pair(k, _):
        for half in range(2):
            j = 2 * k + half + 1
            side = slice(half * width, (half + 1) * width)
            for z in range(0, order, tall):
                here, pads = pl.ds(z, tall), pl.ds(z + pad, tall)
                above, below = pl.ds(z + pad + 1, tall), pl.ds(z + pad - 1, tall)
                own = visc[j + shift, here]
                along_x = 0.5 * (own + east(own))
                along_y = 0.5 * (own + visc[j + shift + 1, here])
                speed = speeds[j, pads]
                for f in range(2):
                    value = state[f, j, pads]
                    rate = spread_of(state, f, j, value, here, pads, along_x, along_y, carry)
                    rate = rate - speed * (state[f, j, above] - state[f, j, below])
                    if coupled:
                        rate = rate + state[1 - f, j, pads]
                    high[f, here, side], low[f, here, side] = parts_of(value + time_step * rate)
        for f in range(2):
            out = product(mat_high[f], mat_low[f], high[f], low[f])
            finish(f, 2 * k, out[:, :width])
            finish(f, 2 * k + 1, out[:, width:])
        return 0

    lax.fori_loop(0, count // 2, pair, 0)


def step_scratch(order, width, count):
    return [
        vmem(count, order, width),
        pltpu.VMEM((count, order, 2 * width), bf16),
        pltpu.VMEM((count, order, 2 * width), bf16),
    ]


def two_scratch(frame):
    _, order, width = frame.shape
    matrix = pltpu.VMEM((2, order, order), bf16)
    return [vmem(*frame.shape), matrix, matrix] + step_scratch(order, width, 2)


def constants(base, sources, scratch):
    frame, mat_high, mat_low = sources
    two = pl.ds(base, 2)
    return [(frame, scratch[0]), (mat_high.at[two], scratch[1]), (mat_low.at[two], scratch[2])]


def rows_of(low_in, main, high_in, p, target):
    _, _, block, depth, _ = main.shape
    padded = pl.ds(p * depth + pad, depth)
    for row, count, part in ((0, 2, low_in), (2, block, main), (block + 2, 2, high_in)):
        yield part, target.at[:, pl.ds(row, count), padded]


def first_finish(first, order):
    def finish(f, row, piece):
        first[f, row, pl.ds(pad, order)] = piece

    return finish


def first_kernel(low_in, main, high_in, _, *refs):
    sources, (first, state, *scratch, sem) = refs[:3], refs[3:]
    slabs, _, block, depth, _ = main.shape
    pairs = constants(W, sources, scratch)
    for p in range(slabs):
        pairs += [(a.at[p], b) for a, b in rows_of(low_in, main, high_in, p, state)]
    copies = start_all(pairs, sem)
    clear_pads(state)
    clear_pads(first)
    wait_all(copies)
    finish = first_finish(first, slabs * depth)
    advance_rows(state, state.at[W], 0, True, scratch, block + 2, finish)


def first_step(low_in, main, high_in, later, frame, mat_high, mat_low):
    slabs, _, block, depth, width = main.shape
    order = slabs * depth
    volume = 2 * (block + 2) * order * width
    return call(
        first_kernel,
        [(x, anywhere()) for x in (low_in, main, high_in, later, frame, mat_high, mat_low)],
        [((2, block + 2, order + 2 * pad, width), whole())],
        [vmem(2, block + 4, order + 2 * pad, width)]
        + two_scratch(frame)
        + [dmas(3 * slabs + 3)],
        6 * order * volume,
        "first_step",
    )[0]


def carried_kernel(*refs):
    low_in, main, high_in, low_w, main_w, high_w, _ = refs[:7]
    sources, (first, state, speeds, *scratch, sem) = refs[7:10], refs[10:]
    slabs, _, block, depth, _ = main.shape
    pairs = constants(U, sources, scratch)
    for p in range(slabs):
        pairs += [(a.at[p], b) for a, b in rows_of(low_in, main, high_in, p, state)]
        w_rows = rows_of(low_w, main_w, high_w, p, speeds)
        pairs += [(a.at[p, pl.ds(W, 1)], b) for a, b in w_rows]
    copies = start_all(pairs, sem)
    clear_pads(state)
    clear_pads(first)
    wait_all(copies)
    finish = first_finish(first, slabs * depth)
    advance_rows(state, speeds.at[0], 0, False, scratch, block + 2, finish)


def carried_step(own, with_w, later, frame, mat_high, mat_low):
    slabs, _, block, depth, width = own[1].shape
    order = slabs * depth
    volume = 2 * (block + 2) * order * width
    return call(
        carried_kernel,
        [(x, anywhere()) for x in (*own, *with_w, later, frame, mat_high, mat_low)],
        [((2, block + 2, order + 2 * pad, width), whole())],
        [
            vmem(2, block + 4, order + 2 * pad, width),
            vmem(1, block + 4, order + 2 * pad, width),
        ]
        + two_scratch(frame)
        + [dmas(6 * slabs + 3)],
        6 * order * volume,
        "carried_step",
    )[0]


def second_kernel(base, count, first, with_w, *refs):
    sources, targets = refs[:3], refs[3 : 3 + count]
    out, low_edge, high_edge, state, speeds, *scratch, held, sem = refs[-13:]
    slabs, _, block, depth, _ = out.shape
    places = [held.at[:, :, pl.ds(p * depth, depth)] for p in range(slabs)]
    pairs = constants(base, sources, scratch) + [(first, state)]
    if base != W:
        pairs.append((with_w.at[W], speeds))
    for target, span in spans(targets, 2):
        for p in range(slabs):
            pairs.append((target.at[p], held.at[:, span, pl.ds(p * depth, depth)]))
    wait_all(start_all(pairs, sem))

    def finish(f, row, piece):
        held[f, row] = piece - held[f, row]

    speeds = state.at[W] if base == W else speeds
    advance_rows(state, speeds, 1, base == W, scratch, block, finish)
    copies = start_all([(places[p], out.at[p]) for p in range(slabs)], sem)
    low_edge[...] = held[:, 0]
    high_edge[...] = held[:, block - 1]
    wait_all(copies)


def second_step(first, with_w, frame, mat_high, mat_low, base, targets, later):
    _, order, width = frame.shape
    slabs, _, _, depth, _ = targets[0].shape
    block = sum(target.shape[2] for target in targets)
    operands = (first, with_w, frame, mat_high, mat_low, *targets, *later)
    return call(
        functools.partial(second_kernel, base, len(targets)),
        [(x, anywhere()) for x in operands],
        [((slabs, 2, block, depth, width), anywhere())] + [((2, order, width), whole())] * 2,
        [vmem(*first.shape), vmem(*first.shape[1:])]
        + two_scratch(frame)
        + [vmem(2, block, order, width), dmas(2 * slabs + 5)],
        6 * order * 2 * block * order * width,
        "second_step",
    )


def after_kernel(*refs):
    del refs


def after(value, later):
    return call(
        after_kernel,
        [(x, anywhere()) for x in (value, *later)],
        [(value.shape, anywhere())],
        [],
        0,
        "after",
        aliases={0: 0},
    )[0]


def outer_kernel(chunks, *refs):
    *outs, sem = refs[-3:]
    block = chunks.shape[2]
    low, high = chunks.at[:, :, pl.ds(0, 2)], chunks.at[:, :, pl.ds(block - 2, 2)]
    wait_all(start_all([(low, outs[0]), (high, outs[1])], sem))


def pieces_kernel(chunks, _, *refs):
    *outs, sem = refs
    wait_all(start_all([(chunks.at[:, :, span], part) for part, span in spans(outs, 2)], sem))


def row_parts(kernel, chunks, later, sizes, name):
    slabs, count, _, depth, width = chunks.shape
    return call(
        kernel,
        [(chunks, anywhere())] + [(x, anywhere()) for x in later],
        [((slabs, count, size, depth, width), whole()) for size in sizes],
        [dmas(len(sizes))],
        0,
        name,
    )


def adjoint_kernel(*refs):
    halves, low_edges, high_edges = refs[0:2], refs[2:4], refs[4:6]
    firsts, (visc, mat_high, mat_low) = refs[6:8], refs[8:11]
    out, cot, pulled, ends, carry, high, low, sem = refs[11:]
    slabs, _, block, depth, width = halves[0].shape
    order = slabs * depth
    main = pl.ds(1, block)
    pairs = []
    for source, span in spans(halves):
        for p in range(slabs):
            pairs.append((source.at[p], cot.at[span, main, pl.ds(p * depth, depth)]))
    for i in range(2):
        pairs.append((low_edges[i], cot.at[pl.ds(2 * i, 2), 0]))
        pairs.append((high_edges[i], cot.at[pl.ds(2 * i, 2), block + 1]))
    copies = start_all(pairs, sem)
    clear_pads(pulled)
    wait_all(copies)

    def pull(k, _):
        for f in range(fields):
            pair = jnp.concatenate([cot[f, 2 * k], cot[f, 2 * k + 1]], axis=1)
            out = product(mat_high[f], mat_low[f], *parts_of(pair))
            pulled[f, 2 * k, pl.ds(pad, order)] = out[:, :width]
            pulled[f, 2 * k + 1, pl.ds(pad, order)] = out[:, width:]
        return 0

    lax.fori_loop(0, (block + 2) // 2, pull, 0)
    first_fluxes(pulled, visc, 1, carry)

    def rows(k, _):
        for half in range(2):
            j = 2 * k + half + 1
            side = slice(half * width, (half + 1) * width)
            for z in range(0, order, tall):
                here, pads = pl.ds(z, tall), pl.ds(z + pad, tall)
                above, below = pl.ds(z + pad + 1, tall), pl.ds(z + pad - 1, tall)
                own = visc[j + 1, here]
                along_x = 0.5 * (own + east(own))
                along_y = 0.5 * (own + visc[j + 2, here])
                speed_above, speed_below = firsts[0][W, j, above], firsts[0][W, j, below]
                coupling = pulled[T, j, pads]
                for f in (U, V, T, W):
                    value = pulled[f, j, pads]
                    rate = spread_of(pulled, f, j, value, here, pads, along_x, along_y, carry)
                    up, down = pulled[f, j, above], pulled[f, j, below]
                    rate = rate + (speed_above * up - speed_below * down)
                    if f == W:
                        slope = speed_above - speed_below
                    else:
                        ref, i = firsts[f // 2], f % 2
                        slope = ref[i, j, above] - ref[i, j, below]
                    coupling = coupling - value * slope
                    if f == T:
                        rate = rate + pulled[W, j, pads]
                    if f == W:
                        rate = rate + coupling
                    high[f, here, side], low[f, here, side] = parts_of(value + time_step * rate)
        for f in range(fields):
            out = product(mat_high[f], mat_low[f], high[f], low[f])
            cot[f, 2 * k + 1] = out[:, :width]
            cot[f, 2 * k + 2] = out[:, width:]
        return 0

    lax.fori_loop(0, block // 2, rows, 0)
    pairs = []
    for p in range(slabs):
        for f in range(fields):
            source = cot.at[f, main, pl.ds(p * depth, depth)]
            pairs.append((source, out.at[p, pl.ds(f * block, block)]))
    copies = start_all(pairs, sem)
    for p in range(slabs):
        for f in range(fields):
            for y in range(block):
                for side, z in ((0, p * depth - 1), (1, (p + 1) * depth)):
                    to = slice(f * block + y, f * block + y + 1)
                    if 0 <= z < order:
                        ends[p, side, to] = cot[f, y + 1, z : z + 1]
                    else:
                        ends[p, side, to] = jnp.zeros((1, width), f32)
    ends_copy = pltpu.make_async_copy(
        ends, out.at[:, pl.ds(fields * block, 2)], sem.at[len(pairs)]
    )
    ends_copy.start()
    wait_all(copies)
    ends_copy.wait()


def adjoint_step(halves, low_edges, high_edges, firsts, visc, mat_high, mat_low):
    slabs, _, block, depth, width = halves[0].shape
    order = slabs * depth
    volume = fields * (block + 1) * order * width
    return call(
        adjoint_kernel,
        [(x, anywhere()) for x in (*halves, *low_edges, *high_edges)]
        + [(x, whole()) for x in (*firsts, visc, mat_high, mat_low)],
        [((slabs, fields * block + 2, depth, width), anywhere())],
        [
            vmem(fields, block + 2, order, width),
            vmem(fields, block + 2, order + 2 * pad, width),
            vmem(slabs, 2, depth, width),
        ]
        + step_scratch(order, width, fields)
        + [dmas(slabs * fields + 1)],
        12 * order * volume,
        "adjoint_step",
    )[0]


def last_kernel(*refs):
    visc_in, edges_below, edges_above, chunks, *states, half, other, out = refs[:9]
    pulled, state, prior, planes, coupling, ends, visc, sem = refs[9:]
    slabs, block, depth, width = visc.shape
    rows, step = slabs * block, pulled.shape[3]
    main = pl.ds(pad, depth)
    above, below = pl.ds(pad + 1, depth), pl.ds(pad - 1, depth)

    def copy(source, target, which):
        return pltpu.make_async_copy(source, target, sem.at[which])

    arrive = {"visc": copy(visc_in, visc, 0)}
    arrive["ends"] = copy(chunks.at[:, pl.ds(fields * block, 2)], ends, 1)
    for f in range(fields):
        source = chunks.at[:, pl.ds(f * block, block)]
        arrive["pulled", f] = copy(source, pulled.at[f, :, :, main], 2 + f)
        source = states[0].at[:, pl.ds(f * block, block)] if f < 2 else states[1].at[:, f - 2]
        arrive["state", f] = copy(source, state.at[f, :, :, main], 2 + fields + f)
        source = (half, other)[f // 2].at[:, f % 2]
        arrive["prior", f] = copy(source, prior.at[f], 2 + 2 * fields + f)
    order = ["visc", "ends", ("state", W)]
    order += [(which, f) for f in (U, V, T, W) for which in ("pulled", "state", "prior")]
    for which in dict.fromkeys(order):
        arrive[which].start()

    def ready(*which):
        for name in which:
            if name in arrive:
                arrive.pop(name).wait()

    flat = (fields * rows * step, width)
    state_rows, pulled_rows = state.reshape(flat), pulled.reshape(flat)
    first, last = pad - 1, pad + depth
    for f in range(fields):
        base = f * rows * step
        state_rows[pl.ds(base + first, rows, stride=step), :] = edges_below[outside[f]]
        state_rows[pl.ds(base + last, rows, stride=step), :] = edges_above[outside[f]]
    ready("visc", "ends")
    for f in range(fields):
        for p in range(slabs):
            base, part = (f * rows + p * block) * step, pl.ds(f * block, block)
            pulled_rows[pl.ds(base + first, block, stride=step), :] = ends[p, 0, part]
            pulled_rows[pl.ds(base + last, block, stride=step), :] = ends[p, 1, part]
    ready(("state", W))
    leaving = []
    for f in (U, V, T, W):
        ready(("pulled", f), ("state", f), ("prior", f))
        if f == T:
            ready(("pulled", W))
        along_y = 0.5 * (visc[slabs - 1, block - 1] + visc[0, 0])
        south = along_y * (pulled[f, 0, 0, main] - pulled[f, slabs - 1, block - 1, main])

        def group(p, south):
            after = lax.rem(p + 1, slabs)
            for i in range(block):
                n, m = (p, i + 1) if i + 1 < block else (after, 0)
                own = visc[p, i]
                along_x = 0.5 * (own + east(own))
                along_y = 0.5 * (own + visc[n, m])
                value = pulled[f, p, i, main]
                flux_x = along_x * (east(value) - value)
                flux_y = along_y * (pulled[f, n, m, main] - value)
                rate = flux_x - west(flux_x) + (flux_y - south)
                south = flux_y
                flow = state[W, p, i, above] * pulled[f, p, i, above]
                rate = rate + (flow - state[W, p, i, below] * pulled[f, p, i, below])
                lost = value * (state[f, p, i, above] - state[f, p, i, below])
                if f == U:
                    coupling[p, i] = lost
                elif f == V:
                    coupling[p, i] = coupling[p, i] + lost
                elif f == T:
                    coupling[p, i] = value - (coupling[p, i] + lost)
                    rate = rate + pulled[W, p, i, main]
                else:
                    rate = rate + (coupling[p, i] - lost)
                result = value + time_step * rate - prior[f, p, i]
                planes[f, pl.ds(p * block + i, depth, stride=rows), :] = result
            return south

        lax.fori_loop(0, slabs, group, south)
        leave = copy(planes.at[f], out.at[outside[f]], 2 + f)
        leave.start()
        leaving.append(leave)
    wait_all(leaving)


def last_step(visc, below, above, chunks, states, priors):
    rows, depth, width = visc.shape
    slabs = chunks.shape[0]
    block = rows // slabs
    padded = vmem(fields, slabs, block, depth + 2 * pad, width)
    one = (slabs, block, depth, width)
    return call(
        last_kernel,
        [(visc.reshape(one), anywhere()), (below, whole()), (above, whole())]
        + [(x, anywhere()) for x in (chunks, *states, *priors)],
        [((fields, depth * rows, width), anywhere())],
        [
            padded,
            padded,
            vmem(fields, *one),
            vmem(fields, depth * rows, width),
            vmem(*one),
            vmem(slabs, 2, depth, width),
            vmem(*one),
            dmas(2 + 3 * fields),
        ],
        30 * fields * rows * depth * width,
        "last_step",
    )[0]


def exchange(chunks):
    return lax.all_to_all(chunks, "slab", split_axis=0, concat_axis=0, tiled=True)


def around(value, axis, steps):
    count = lax.axis_size(axis)
    return lax.ppermute(value, axis, [(i, (i + steps) % count) for i in range(count)])


def local(states, viscosity, inverse):
    start = states[0]
    _, depth, rows, width = start.shape
    slabs, segs = lax.axis_size("slab"), lax.axis_size("seg")
    block = rows // slabs
    share = -(-(block + 4) // segs)

    own_seg = jnp.full((1,), lax.axis_index("seg"), jnp.int32)
    send_half, visc = to_first_chunks(own_seg, start, viscosity, slabs, share)
    packed = exchange(send_half)
    mat_high, mat_low, adj_high, adj_low = split(inverse)
    send_other, ends = to_chunks(start, slabs, outside[U], 2, [mat_high])
    main_other = exchange(send_other)
    forward = [(i, i + 1) for i in range(slabs - 1)]
    below = lax.ppermute(ends[1], "slab", forward)
    above = lax.ppermute(ends[0], "slab", [(i, j) for j, i in forward])

    low_rows, high_rows, main_half, visc_share = unpack(packed, block, send_other)
    visc_in = [visc_share] + [around(visc_share, "seg", -i) for i in range(1, segs)]
    low_in, high_in = around(high_rows, "slab", 1), around(low_rows, "slab", -1)
    frame = to_frame(own_seg, visc_in)
    main_half = after(main_half, (frame,))
    half_rows = (low_in, main_half, high_in)
    target = around(main_half, "seg", -1)

    sizes, few = (2, 2), max(1, block // 4)
    low_rows, high_rows = row_parts(
        outer_kernel, main_other, (low_in, high_in, frame), sizes, "outer_rows"
    )
    other_rows = (around(high_rows, "slab", 1), main_other, around(low_rows, "slab", -1))
    mats = mat_high, mat_low
    sizes = (few, block - few)
    parts = row_parts(pieces_kernel, main_other, (low_rows,), sizes, "pieces")
    targets = [around(part, "seg", -1) for part in parts]
    first_half = first_step(*half_rows, parts[0], frame, *mats)
    out, low_edge, high_edge = second_step(
        first_half, first_half, frame, *mats, W, (target,), ()
    )
    out = after(out, (other_rows[0], other_rows[2], targets[0]))
    first_other = carried_step(other_rows, half_rows, out, frame, *mats)
    other, *more = second_step(first_other, first_half, frame, *mats, U, targets, (out,))
    low_edges = [around(edge, "slab", 1) for edge in (high_edge, more[1])]
    high_edges = [around(edge, "slab", -1) for edge in (low_edge, more[0])]
    half = exchange(out)
    residual = (out, after(other, (*low_edges, *high_edges, half)))
    firsts = (first_half, first_other)
    pulled = adjoint_step(residual, low_edges, high_edges, firsts, frame, adj_high, adj_low)
    planes, other = to_planes((half, exchange(residual[1])), pulled)
    priors = [around(part, "seg", 1) for part in (half, other)]
    gradient = last_step(visc, below, above, exchange(pulled), (send_half, send_other), priors)
    shape = (1, fields, depth, rows, width)
    return (planes.reshape(shape), gradient.reshape(shape))


def solution(mesh):
    in_specs = (P("seg", None, "slab", None, None), P("slab", None, None), P())
    out_specs = (P("seg", None, "slab", None, None), P("seg", None, "slab", None, None))
    return jax.shard_map(local, mesh=mesh, in_specs=in_specs, out_specs=out_specs, check_vma=False)
```

```python
import functools

import jax
import jax.numpy as jnp
from jax import lax
from jax.experimental import pallas as pl
from jax.experimental.pallas import tpu as pltpu
from jax.sharding import PartitionSpec as P

time_step = 0.1
vmem_bytes = 56 * 1024 * 1024
f32, bf16 = jnp.float32, jnp.bfloat16
fields = 4
W, T, U, V = range(4)
outside = (2, 3, 0, 1)
pad = 8
tall = 32


def whole():
    return pl.BlockSpec(memory_space=pltpu.VMEM)


def anywhere():
    return pl.BlockSpec(memory_space=pl.ANY)


def scalars():
    return pl.BlockSpec(memory_space=pltpu.SMEM)


def vmem(*shape):
    return pltpu.VMEM(shape, f32)


def dmas(count):
    return pltpu.SemaphoreType.DMA((count,))


def call(kernel, ins, outs, scratch, flops, name, kind=f32, aliases=None, limit=vmem_bytes):
    moved = sum(4 * x.size for x, _ in ins)
    return pl.pallas_call(
        kernel,
        in_specs=[spec for _, spec in ins],
        out_specs=tuple(spec for _, spec in outs),
        out_shape=tuple(jax.ShapeDtypeStruct(shape, kind) for shape, _ in outs),
        scratch_shapes=scratch,
        input_output_aliases=aliases or {},
        compiler_params=pltpu.CompilerParams(vmem_limit_bytes=limit),
        cost_estimate=pl.CostEstimate(flops=flops, bytes_accessed=moved, transcendentals=0),
        name=name,
    )(*[x for x, _ in ins])


def start_all(pairs, sem):
    copies = [
        pltpu.make_async_copy(source, target, sem.at[i])
        for i, (source, target) in enumerate(pairs)
    ]
    for copy in copies:
        copy.start()
    return copies


def wait_all(copies):
    for copy in copies:
        copy.wait()


def spans(parts, axis=1):
    start = 0
    for part in parts:
        yield part, pl.ds(start, part.shape[axis])
        start += part.shape[axis]


def east(value):
    return pltpu.roll(value, value.shape[1] - 1, 1)


def west(value):
    return pltpu.roll(value, 1, 1)


def parts_of(value):
    high = value.astype(bf16)
    return high, (value - high.astype(f32)).astype(bf16)


def product(matrix_high, matrix_low, high, low):
    dot = functools.partial(jnp.dot, preferred_element_type=f32)
    return dot(matrix_high, high) + (dot(matrix_high, low) + dot(matrix_low, high))


def split_kernel(x_ref, high, low, adj_high, adj_low):
    for f in range(fields):
        high[f], low[f] = parts_of(x_ref[outside[f]])
        adj_high[f], adj_low[f] = parts_of(x_ref[outside[f]].T)


def split(inverse):
    return call(
        split_kernel,
        [(inverse, whole())],
        [(inverse.shape, whole())] * 4,
        [],
        0,
        "split",
        bf16,
    )


def visc_kernel(own, x_ref, visc, send):
    slabs, share = send.shape[:2]
    rows, depth, _ = visc.shape
    block = rows // slabs
    for y in range(rows):
        visc[y] = x_ref[pl.ds(y, depth, stride=rows), :]
    for p in range(slabs):
        for i in range(share):
            send[p, i] = visc[lax.rem(p * block - 2 + share * own[0] + i + rows, rows)]


def visc_chunks(own, viscosity, slabs, share):
    depth, rows, width = viscosity.shape
    return call(
        visc_kernel,
        [(own, scalars()), (viscosity.reshape(-1, width), whole())],
        [((rows, depth, width), whole()), ((slabs, share, depth, width), whole())],
        [],
        0,
        "visc_chunks",
    )


def frame_kernel(own, *refs):
    *shares, frame, sem = refs
    slabs, share, depth, _ = shares[0].shape
    pairs = []
    for i, part in enumerate(shares):
        start = lax.rem(own[0] + i, len(shares)) * share
        for p in range(slabs):
            pairs.append((part.at[p], frame.at[pl.ds(start, share), pl.ds(p * depth, depth)]))
    wait_all(start_all(pairs, sem))


def to_frame(own, shares):
    slabs, share, depth, width = shares[0].shape
    return call(
        frame_kernel,
        [(own, scalars())] + [(x, anywhere()) for x in shares],
        [((len(shares) * share, slabs * depth, width), whole())],
        [dmas(len(shares) * slabs)],
        0,
        "to_frame",
    )[0]


def chunks_kernel(start, x_ref, *refs):
    send, edges, planes, held, sem = refs[-5:]
    count, slabs, block, depth, _ = held.shape
    rows = slabs * block
    copies = start_all([(x_ref.at[start + f], planes.at[f]) for f in range(count)], sem)
    ends = [
        pltpu.make_async_copy(x_ref.at[:, pl.ds(z * rows, rows)], edges.at[i], sem.at[count + i])
        for i, z in enumerate((0, depth - 1))
    ]
    for copy in ends:
        copy.start()
    leaving = []
    for f in range(count):
        copies[f].wait()
        for y in range(rows):
            held[f, y // block, y % block] = planes[f, pl.ds(y, depth, stride=rows), :]
        copy = pltpu.make_async_copy(held.at[f], send.at[:, f], sem.at[f])
        copy.start()
        leaving.append(copy)
    wait_all(leaving + ends)


def to_chunks(states, slabs, start, count, later):
    _, depth, rows, width = states.shape
    block = rows // slabs
    return call(
        functools.partial(chunks_kernel, start),
        [(states.reshape(fields, -1, width), anywhere())]
        + [(x, anywhere()) for x in later],
        [
            ((slabs, count, block, depth, width), anywhere()),
            ((2, fields, rows, width), whole()),
        ],
        [
            vmem(count, depth * rows, width),
            vmem(count, slabs, block, depth, width),
            dmas(count + 2),
        ],
        0,
        "to_chunks",
    )


def planes_kernel(half, other, _, o_ref, again, held, sem):
    slabs, _, block, depth, _ = half.shape
    rows = slabs * block
    pairs = []
    for p in range(slabs):
        place = pl.ds(p * block, block)
        pairs.append((half.at[p], held.at[pl.ds(0, 2), place]))
        pairs.append((other.at[p], held.at[pl.ds(2, 2), place]))
    wait_all(start_all(pairs, sem))
    places = [held.at[pl.ds(2, 2), pl.ds(p * block, block)] for p in range(slabs)]
    copies = start_all([(places[p], again.at[p]) for p in range(slabs)], sem)

    def row(y, _):
        for f in range(fields):
            where = pl.ds(outside[f] * depth * rows + y, depth, stride=rows)
            o_ref[where, :] = held[f, y]
        return 0

    lax.fori_loop(0, rows, row, 0, unroll=4)
    wait_all(copies)


def to_planes(halves, later):
    slabs, _, block, depth, width = halves[0].shape
    return call(
        planes_kernel,
        [(x, anywhere()) for x in (*halves, later)],
        [
            ((fields * depth * slabs * block, width), whole()),
            (halves[1].shape, anywhere()),
        ],
        [vmem(fields, slabs * block, depth, width), dmas(2 * slabs)],
        0,
        "to_planes",
    )


def clear_pads(ref):
    edge = jnp.zeros(ref.shape[1:2] + (pad, ref.shape[3]), f32)
    for f in range(ref.shape[0]):
        ref[f, :, 0:pad] = edge
        ref[f, :, ref.shape[2] - pad :] = edge


def first_fluxes(state, visc, shift, carry):
    order = visc.shape[1]
    for z in range(0, order, tall):
        here, pads = pl.ds(z, tall), pl.ds(z + pad, tall)
        along_y = 0.5 * (visc[shift, here] + visc[shift + 1, here])
        for f in range(state.shape[0]):
            carry[f, here] = along_y * (state[f, 1, pads] - state[f, 0, pads])


def spread_of(state, f, j, value, here, pads, along_x, along_y, carry):
    flux_x = along_x * (east(value) - value)
    flux_y = along_y * (state[f, j + 1, pads] - value)
    spread = flux_x - west(flux_x) + (flux_y - carry[f, here])
    carry[f, here] = flux_y
    return spread


def advance_rows(state, speeds, shift, coupled, scratch, count, finish):
    visc, mat_high, mat_low, carry, high, low = scratch
    order, width = visc.shape[1:]
    first_fluxes(state, visc, shift, carry)

    def pair(k, _):
        for half in range(2):
            j = 2 * k + half + 1
            side = slice(half * width, (half + 1) * width)
            for z in range(0, order, tall):
                here, pads = pl.ds(z, tall), pl.ds(z + pad, tall)
                above, below = pl.ds(z + pad + 1, tall), pl.ds(z + pad - 1, tall)
                own = visc[j + shift, here]
                along_x = 0.5 * (own + east(own))
                along_y = 0.5 * (own + visc[j + shift + 1, here])
                speed = speeds[j, pads]
                for f in range(2):
                    value = state[f, j, pads]
                    rate = spread_of(state, f, j, value, here, pads, along_x, along_y, carry)
                    rate = rate - speed * (state[f, j, above] - state[f, j, below])
                    if coupled:
                        rate = rate + state[1 - f, j, pads]
                    high[f, here, side], low[f, here, side] = parts_of(value + time_step * rate)
        for f in range(2):
            out = product(mat_high[f], mat_low[f], high[f], low[f])
            finish(f, 2 * k, out[:, :width])
            finish(f, 2 * k + 1, out[:, width:])
        return 0

    lax.fori_loop(0, count // 2, pair, 0)


def step_scratch(order, width, count):
    return [
        vmem(count, order, width),
        pltpu.VMEM((count, order, 2 * width), bf16),
        pltpu.VMEM((count, order, 2 * width), bf16),
    ]


def two_scratch(frame):
    _, order, width = frame.shape
    matrix = pltpu.VMEM((2, order, order), bf16)
    return [vmem(*frame.shape), matrix, matrix] + step_scratch(order, width, 2)


def constants(base, sources, scratch):
    frame, mat_high, mat_low = sources
    two = pl.ds(base, 2)
    return [(frame, scratch[0]), (mat_high.at[two], scratch[1]), (mat_low.at[two], scratch[2])]


def rows_of(low_in, main, high_in, p, target):
    _, _, block, depth, _ = main.shape
    padded = pl.ds(p * depth + pad, depth)
    for row, count, part in ((0, 2, low_in), (2, block, main), (block + 2, 2, high_in)):
        yield part, target.at[:, pl.ds(row, count), padded]


def first_finish(first, order):
    def finish(f, row, piece):
        first[f, row, pl.ds(pad, order)] = piece

    return finish


def first_kernel(low_in, main, high_in, _, *refs):
    sources, (first, state, *scratch, sem) = refs[:3], refs[3:]
    slabs, _, block, depth, _ = main.shape
    pairs = constants(W, sources, scratch)
    for p in range(slabs):
        pairs += [(a.at[p], b) for a, b in rows_of(low_in, main, high_in, p, state)]
    copies = start_all(pairs, sem)
    clear_pads(state)
    clear_pads(first)
    wait_all(copies)
    finish = first_finish(first, slabs * depth)
    advance_rows(state, state.at[W], 0, True, scratch, block + 2, finish)


def first_step(low_in, main, high_in, later, frame, mat_high, mat_low):
    slabs, _, block, depth, width = main.shape
    order = slabs * depth
    volume = 2 * (block + 2) * order * width
    return call(
        first_kernel,
        [(x, anywhere()) for x in (low_in, main, high_in, later, frame, mat_high, mat_low)],
        [((2, block + 2, order + 2 * pad, width), whole())],
        [vmem(2, block + 4, order + 2 * pad, width)]
        + two_scratch(frame)
        + [dmas(3 * slabs + 3)],
        6 * order * volume,
        "first_step",
    )[0]


def carried_kernel(*refs):
    low_in, main, high_in, low_w, main_w, high_w, _ = refs[:7]
    sources, (first, state, speeds, *scratch, sem) = refs[7:10], refs[10:]
    slabs, _, block, depth, _ = main.shape
    pairs = constants(U, sources, scratch)
    for p in range(slabs):
        pairs += [(a.at[p], b) for a, b in rows_of(low_in, main, high_in, p, state)]
        w_rows = rows_of(low_w, main_w, high_w, p, speeds)
        pairs += [(a.at[p, pl.ds(W, 1)], b) for a, b in w_rows]
    copies = start_all(pairs, sem)
    clear_pads(state)
    clear_pads(first)
    wait_all(copies)
    finish = first_finish(first, slabs * depth)
    advance_rows(state, speeds.at[0], 0, False, scratch, block + 2, finish)


def carried_step(own, with_w, later, frame, mat_high, mat_low):
    slabs, _, block, depth, width = own[1].shape
    order = slabs * depth
    volume = 2 * (block + 2) * order * width
    return call(
        carried_kernel,
        [(x, anywhere()) for x in (*own, *with_w, later, frame, mat_high, mat_low)],
        [((2, block + 2, order + 2 * pad, width), whole())],
        [
            vmem(2, block + 4, order + 2 * pad, width),
            vmem(1, block + 4, order + 2 * pad, width),
        ]
        + two_scratch(frame)
        + [dmas(6 * slabs + 3)],
        6 * order * volume,
        "carried_step",
    )[0]


def second_kernel(base, count, first, with_w, *refs):
    sources, targets = refs[:3], refs[3 : 3 + count]
    out, low_edge, high_edge, state, speeds, *scratch, held, sem = refs[-13:]
    slabs, _, block, depth, _ = out.shape
    places = [held.at[:, :, pl.ds(p * depth, depth)] for p in range(slabs)]
    pairs = constants(base, sources, scratch) + [(first, state)]
    if base != W:
        pairs.append((with_w.at[W], speeds))
    for target, span in spans(targets, 2):
        for p in range(slabs):
            pairs.append((target.at[p], held.at[:, span, pl.ds(p * depth, depth)]))
    wait_all(start_all(pairs, sem))

    def finish(f, row, piece):
        held[f, row] = piece - held[f, row]

    speeds = state.at[W] if base == W else speeds
    advance_rows(state, speeds, 1, base == W, scratch, block, finish)
    copies = start_all([(places[p], out.at[p]) for p in range(slabs)], sem)
    low_edge[...] = held[:, 0]
    high_edge[...] = held[:, block - 1]
    wait_all(copies)


def second_step(first, with_w, frame, mat_high, mat_low, base, targets, later):
    _, order, width = frame.shape
    slabs, _, _, depth, _ = targets[0].shape
    block = sum(target.shape[2] for target in targets)
    operands = (first, with_w, frame, mat_high, mat_low, *targets, *later)
    return call(
        functools.partial(second_kernel, base, len(targets)),
        [(x, anywhere()) for x in operands],
        [((slabs, 2, block, depth, width), anywhere())] + [((2, order, width), whole())] * 2,
        [vmem(*first.shape), vmem(*first.shape[1:])]
        + two_scratch(frame)
        + [vmem(2, block, order, width), dmas(2 * slabs + 5)],
        6 * order * 2 * block * order * width,
        "second_step",
    )


def after_kernel(*refs):
    del refs


def after(value, later):
    return call(
        after_kernel,
        [(x, anywhere()) for x in (value, *later)],
        [(value.shape, anywhere())],
        [],
        0,
        "after",
        aliases={0: 0},
    )[0]


def outer_kernel(chunks, *refs):
    *outs, sem = refs[-3:]
    block = chunks.shape[2]
    low, high = chunks.at[:, :, pl.ds(0, 2)], chunks.at[:, :, pl.ds(block - 2, 2)]
    wait_all(start_all([(low, outs[0]), (high, outs[1])], sem))


def pieces_kernel(chunks, _, *refs):
    *outs, sem = refs
    wait_all(start_all([(chunks.at[:, :, span], part) for part, span in spans(outs, 2)], sem))


def row_parts(kernel, chunks, later, sizes, name):
    slabs, count, _, depth, width = chunks.shape
    return call(
        kernel,
        [(chunks, anywhere())] + [(x, anywhere()) for x in later],
        [((slabs, count, size, depth, width), whole()) for size in sizes],
        [dmas(len(sizes))],
        0,
        name,
    )


def adjoint_kernel(*refs):
    halves, low_edges, high_edges = refs[0:2], refs[2:4], refs[4:6]
    firsts, (visc, mat_high, mat_low) = refs[6:8], refs[8:11]
    out, cot, pulled, ends, carry, high, low, sem = refs[11:]
    slabs, _, block, depth, width = halves[0].shape
    order = slabs * depth
    main = pl.ds(1, block)
    pairs = []
    for source, span in spans(halves):
        for p in range(slabs):
            pairs.append((source.at[p], cot.at[span, main, pl.ds(p * depth, depth)]))
    for i in range(2):
        pairs.append((low_edges[i], cot.at[pl.ds(2 * i, 2), 0]))
        pairs.append((high_edges[i], cot.at[pl.ds(2 * i, 2), block + 1]))
    copies = start_all(pairs, sem)
    clear_pads(pulled)
    wait_all(copies)

    def pull(k, _):
        for f in range(fields):
            pair = jnp.concatenate([cot[f, 2 * k], cot[f, 2 * k + 1]], axis=1)
            out = product(mat_high[f], mat_low[f], *parts_of(pair))
            pulled[f, 2 * k, pl.ds(pad, order)] = out[:, :width]
            pulled[f, 2 * k + 1, pl.ds(pad, order)] = out[:, width:]
        return 0

    lax.fori_loop(0, (block + 2) // 2, pull, 0)
    first_fluxes(pulled, visc, 1, carry)

    def rows(k, _):
        for half in range(2):
            j = 2 * k + half + 1
            side = slice(half * width, (half + 1) * width)
            for z in range(0, order, tall):
                here, pads = pl.ds(z, tall), pl.ds(z + pad, tall)
                above, below = pl.ds(z + pad + 1, tall), pl.ds(z + pad - 1, tall)
                own = visc[j + 1, here]
                along_x = 0.5 * (own + east(own))
                along_y = 0.5 * (own + visc[j + 2, here])
                speed_above, speed_below = firsts[0][W, j, above], firsts[0][W, j, below]
                coupling = pulled[T, j, pads]
                for f in (U, V, T, W):
                    value = pulled[f, j, pads]
                    rate = spread_of(pulled, f, j, value, here, pads, along_x, along_y, carry)
                    up, down = pulled[f, j, above], pulled[f, j, below]
                    rate = rate + (speed_above * up - speed_below * down)
                    if f == W:
                        slope = speed_above - speed_below
                    else:
                        ref, i = firsts[f // 2], f % 2
                        slope = ref[i, j, above] - ref[i, j, below]
                    coupling = coupling - value * slope
                    if f == T:
                        rate = rate + pulled[W, j, pads]
                    if f == W:
                        rate = rate + coupling
                    high[f, here, side], low[f, here, side] = parts_of(value + time_step * rate)
        for f in range(fields):
            out = product(mat_high[f], mat_low[f], high[f], low[f])
            cot[f, 2 * k + 1] = out[:, :width]
            cot[f, 2 * k + 2] = out[:, width:]
        return 0

    lax.fori_loop(0, block // 2, rows, 0)
    pairs = []
    for p in range(slabs):
        for f in range(fields):
            source = cot.at[f, main, pl.ds(p * depth, depth)]
            pairs.append((source, out.at[p, pl.ds(f * block, block)]))
    copies = start_all(pairs, sem)
    for p in range(slabs):
        for f in range(fields):
            for y in range(block):
                for side, z in ((0, p * depth - 1), (1, (p + 1) * depth)):
                    to = slice(f * block + y, f * block + y + 1)
                    if 0 <= z < order:
                        ends[p, side, to] = cot[f, y + 1, z : z + 1]
                    else:
                        ends[p, side, to] = jnp.zeros((1, width), f32)
    ends_copy = pltpu.make_async_copy(
        ends, out.at[:, pl.ds(fields * block, 2)], sem.at[len(pairs)]
    )
    ends_copy.start()
    wait_all(copies)
    ends_copy.wait()


def adjoint_step(halves, low_edges, high_edges, firsts, visc, mat_high, mat_low):
    slabs, _, block, depth, width = halves[0].shape
    order = slabs * depth
    volume = fields * (block + 1) * order * width
    return call(
        adjoint_kernel,
        [(x, anywhere()) for x in (*halves, *low_edges, *high_edges)]
        + [(x, whole()) for x in (*firsts, visc, mat_high, mat_low)],
        [((slabs, fields * block + 2, depth, width), anywhere())],
        [
            vmem(fields, block + 2, order, width),
            vmem(fields, block + 2, order + 2 * pad, width),
            vmem(slabs, 2, depth, width),
        ]
        + step_scratch(order, width, fields)
        + [dmas(slabs * fields + 1)],
        12 * order * volume,
        "adjoint_step",
    )[0]


def last_kernel(*refs):
    visc, edges_below, edges_above, *states, half, other, chunks, out = refs[:9]
    pulled, state, planes, coupling, ends, sem = refs[9:]
    slabs, block, depth, width = visc.shape
    rows, step = slabs * block, pulled.shape[3]
    main = pl.ds(pad, depth)
    above, below = pl.ds(pad + 1, depth), pl.ds(pad - 1, depth)

    def copy(source, target, which):
        return pltpu.make_async_copy(source, target, sem.at[which])

    arrive = {}
    arrive["ends"] = copy(chunks.at[:, pl.ds(fields * block, 2)], ends, 1)
    for f in range(fields):
        source = chunks.at[:, pl.ds(f * block, block)]
        arrive["pulled", f] = copy(source, pulled.at[f, :, :, main], 2 + f)
        source = states[f // 2].at[:, f % 2]
        arrive["state", f] = copy(source, state.at[f, :, :, main], 2 + fields + f)
    order = ["ends", ("state", W)]
    order += [(which, f) for f in (U, V, T, W) for which in ("pulled", "state")]
    for which in dict.fromkeys(order):
        arrive[which].start()

    def ready(*which):
        for name in which:
            if name in arrive:
                arrive.pop(name).wait()

    flat = (fields * rows * step, width)
    state_rows, pulled_rows = state.reshape(flat), pulled.reshape(flat)
    first, last = pad - 1, pad + depth
    for f in range(fields):
        base = f * rows * step
        state_rows[pl.ds(base + first, rows, stride=step), :] = edges_below[outside[f]]
        state_rows[pl.ds(base + last, rows, stride=step), :] = edges_above[outside[f]]
    ready("ends")
    for f in range(fields):
        for p in range(slabs):
            base, part = (f * rows + p * block) * step, pl.ds(f * block, block)
            pulled_rows[pl.ds(base + first, block, stride=step), :] = ends[p, 0, part]
            pulled_rows[pl.ds(base + last, block, stride=step), :] = ends[p, 1, part]
    ready(("state", W))
    leaving = []
    for f in (U, V, T, W):
        ready(("pulled", f), ("state", f))
        if f == T:
            ready(("pulled", W))
        along_y = 0.5 * (visc[slabs - 1, block - 1] + visc[0, 0])
        south = along_y * (pulled[f, 0, 0, main] - pulled[f, slabs - 1, block - 1, main])

        def group(p, south):
            after = lax.rem(p + 1, slabs)
            for i in range(block):
                n, m = (p, i + 1) if i + 1 < block else (after, 0)
                own = visc[p, i]
                along_x = 0.5 * (own + east(own))
                along_y = 0.5 * (own + visc[n, m])
                value = pulled[f, p, i, main]
                flux_x = along_x * (east(value) - value)
                flux_y = along_y * (pulled[f, n, m, main] - value)
                rate = flux_x - west(flux_x) + (flux_y - south)
                south = flux_y
                flow = state[W, p, i, above] * pulled[f, p, i, above]
                rate = rate + (flow - state[W, p, i, below] * pulled[f, p, i, below])
                lost = value * (state[f, p, i, above] - state[f, p, i, below])
                if f == U:
                    coupling[p, i] = lost
                elif f == V:
                    coupling[p, i] = coupling[p, i] + lost
                elif f == T:
                    coupling[p, i] = value - (coupling[p, i] + lost)
                    rate = rate + pulled[W, p, i, main]
                else:
                    rate = rate + (coupling[p, i] - lost)
                prior = (half, other)[f // 2]
                result = value + time_step * rate - prior[p, f % 2, i]
                planes[f, pl.ds(p * block + i, depth, stride=rows), :] = result
            return south

        lax.fori_loop(0, slabs, group, south)
        leave = copy(planes.at[f], out.at[outside[f]], 2 + f)
        leave.start()
        leaving.append(leave)
    wait_all(leaving)


def last_step(visc, below, above, chunks, states, priors):
    rows, depth, width = visc.shape
    slabs = chunks.shape[0]
    block = rows // slabs
    padded = vmem(fields, slabs, block, depth + 2 * pad, width)
    one = (slabs, block, depth, width)
    return call(
        last_kernel,
        [(x, whole()) for x in (visc.reshape(one), below, above, *states, *priors)]
        + [(chunks, anywhere())],
        [((fields, depth * rows, width), anywhere())],
        [
            padded,
            padded,
            vmem(fields, depth * rows, width),
            vmem(*one),
            vmem(slabs, 2, depth, width),
            dmas(2 + 2 * fields),
        ],
        30 * fields * rows * depth * width,
        "last_step",
        limit=36 * 1024 * 1024,
    )[0]


def exchange(chunks):
    return lax.all_to_all(chunks, "slab", split_axis=0, concat_axis=0, tiled=True)


def around(value, axis, steps):
    count = lax.axis_size(axis)
    return lax.ppermute(value, axis, [(i, (i + steps) % count) for i in range(count)])


def local(states, viscosity, inverse):
    start = states[0]
    _, depth, rows, width = start.shape
    slabs, segs = lax.axis_size("slab"), lax.axis_size("seg")
    block = rows // slabs
    share = -(-(block + 4) // segs)

    own_seg = jnp.full((1,), lax.axis_index("seg"), jnp.int32)
    visc, visc_send = visc_chunks(own_seg, viscosity, slabs, share)
    visc_share = exchange(visc_send)
    visc_in = [visc_share] + [around(visc_share, "seg", -i) for i in range(1, segs)]
    send_half, _ = to_chunks(start, slabs, outside[W], 2, [visc_send])
    main_half = exchange(send_half)
    mat_high, mat_low, adj_high, adj_low = split(inverse)
    frame = to_frame(own_seg, visc_in)
    send_other, ends = to_chunks(start, slabs, outside[U], 2, [frame, mat_high])
    main_other = exchange(send_other)
    forward = [(i, i + 1) for i in range(slabs - 1)]
    below = lax.ppermute(ends[1], "slab", forward)
    above = lax.ppermute(ends[0], "slab", [(i, j) for j, i in forward])

    own, outer, targets, later = [], [], [], (visc_share, visc_share)
    few = max(1, block // 4)
    own, targets, later = [], [], (visc_share,)
    for part, sizes in ((main_half, (block,)), (main_other, (few, block - few))):
        low_rows, high_rows = row_parts(outer_kernel, part, later, (2, 2), "outer_rows")
        low_in, high_in = around(high_rows, "slab", 1), around(low_rows, "slab", -1)
        own.append((low_in, part, high_in))
        parts = row_parts(pieces_kernel, part, (low_rows,), sizes, "pieces")
        targets.append([around(piece, "seg", -1) for piece in parts])
        later = (low_in, high_in)

    mats = mat_high, mat_low
    first_half = first_step(*own[0], frame, frame, *mats)
    out, low_edge, high_edge = second_step(
        first_half, first_half, frame, *mats, W, targets[0], (parts[0],)
    )
    out = after(out, (own[1][0], own[1][2], targets[1][0]))
    first_other = carried_step(own[1], own[0], out, frame, *mats)
    other, *more = second_step(
        first_other, first_half, frame, *mats, U, targets[1], (out,)
    )
    low_edges = [around(edge, "slab", 1) for edge in (high_edge, more[1])]
    high_edges = [around(edge, "slab", -1) for edge in (low_edge, more[0])]
    half = exchange(out)
    residual = (out, after(other, (*low_edges, *high_edges, half)))
    firsts = (first_half, first_other)
    pulled = adjoint_step(residual, low_edges, high_edges, firsts, frame, adj_high, adj_low)
    planes, other = to_planes((half, exchange(residual[1])), pulled)
    priors = [around(part, "seg", 1) for part in (half, other)]
    gradient = last_step(visc, below, above, exchange(pulled), (send_half, send_other), priors)
    shape = (1, fields, depth, rows, width)
    return (planes.reshape(shape), gradient.reshape(shape))


def solution(mesh):
    in_specs = (P("seg", None, "slab", None, None), P("slab", None, None), P())
    out_specs = (P("seg", None, "slab", None, None), P("seg", None, "slab", None, None))
    return jax.shard_map(local, mesh=mesh, in_specs=in_specs, out_specs=out_specs, check_vma=False)
```

```python
import functools

import jax
import jax.numpy as jnp
from jax import lax
from jax.experimental import pallas as pl
from jax.experimental.pallas import tpu as pltpu
from jax.sharding import PartitionSpec as P

time_step = 0.1
vmem_bytes = 56 * 1024 * 1024
f32, bf16 = jnp.float32, jnp.bfloat16
fields = 4
W, T, U, V = range(4)
outside = (2, 3, 0, 1)
pad = 8
tall = 32


def whole():
    return pl.BlockSpec(memory_space=pltpu.VMEM)


def anywhere():
    return pl.BlockSpec(memory_space=pl.ANY)


def scalars():
    return pl.BlockSpec(memory_space=pltpu.SMEM)


def vmem(*shape):
    return pltpu.VMEM(shape, f32)


def dmas(count):
    return pltpu.SemaphoreType.DMA((count,))


def call(kernel, ins, outs, scratch, flops, name, kind=f32, aliases=None):
    moved = sum(4 * x.size for x, _ in ins)
    return pl.pallas_call(
        kernel,
        in_specs=[spec for _, spec in ins],
        out_specs=tuple(spec for _, spec in outs),
        out_shape=tuple(jax.ShapeDtypeStruct(shape, kind) for shape, _ in outs),
        scratch_shapes=scratch,
        input_output_aliases=aliases or {},
        compiler_params=pltpu.CompilerParams(vmem_limit_bytes=vmem_bytes),
        cost_estimate=pl.CostEstimate(flops=flops, bytes_accessed=moved, transcendentals=0),
        name=name,
    )(*[x for x, _ in ins])


def start_all(pairs, sem):
    copies = [
        pltpu.make_async_copy(source, target, sem.at[i])
        for i, (source, target) in enumerate(pairs)
    ]
    for copy in copies:
        copy.start()
    return copies


def wait_all(copies):
    for copy in copies:
        copy.wait()


def spans(parts, axis=1):
    start = 0
    for part in parts:
        yield part, pl.ds(start, part.shape[axis])
        start += part.shape[axis]


def east(value):
    return pltpu.roll(value, value.shape[1] - 1, 1)


def west(value):
    return pltpu.roll(value, 1, 1)


def parts_of(value):
    high = value.astype(bf16)
    return high, (value - high.astype(f32)).astype(bf16)


def product(matrix_high, matrix_low, high, low):
    dot = functools.partial(jnp.dot, preferred_element_type=f32)
    return dot(matrix_high, high) + (dot(matrix_high, low) + dot(matrix_low, high))


def split_kernel(x_ref, high, low, adj_high, adj_low):
    for f in range(fields):
        high[f], low[f] = parts_of(x_ref[outside[f]])
        adj_high[f], adj_low[f] = parts_of(x_ref[outside[f]].T)


def split(inverse):
    return call(
        split_kernel,
        [(inverse, whole())],
        [(inverse.shape, whole())] * 4,
        [],
        0,
        "split",
        bf16,
    )


def visc_kernel(own, x_ref, visc, send):
    slabs, share = send.shape[:2]
    rows, depth, _ = visc.shape
    block = rows // slabs
    for y in range(rows):
        visc[y] = x_ref[pl.ds(y, depth, stride=rows), :]
    for p in range(slabs):
        for i in range(share):
            send[p, i] = visc[lax.rem(p * block - 2 + share * own[0] + i + rows, rows)]


def visc_chunks(own, viscosity, slabs, share):
    depth, rows, width = viscosity.shape
    return call(
        visc_kernel,
        [(own, scalars()), (viscosity.reshape(-1, width), whole())],
        [((rows, depth, width), whole()), ((slabs, share, depth, width), whole())],
        [],
        0,
        "visc_chunks",
    )


def frame_kernel(own, *refs):
    *shares, frame, sem = refs
    slabs, share, depth, _ = shares[0].shape
    pairs = []
    for i, part in enumerate(shares):
        start = lax.rem(own[0] + i, len(shares)) * share
        for p in range(slabs):
            pairs.append((part.at[p], frame.at[pl.ds(start, share), pl.ds(p * depth, depth)]))
    wait_all(start_all(pairs, sem))


def to_frame(own, shares):
    slabs, share, depth, width = shares[0].shape
    return call(
        frame_kernel,
        [(own, scalars())] + [(x, anywhere()) for x in shares],
        [((len(shares) * share, slabs * depth, width), whole())],
        [dmas(len(shares) * slabs)],
        0,
        "to_frame",
    )[0]


def chunks_kernel(start, x_ref, *refs):
    send, edges, planes, held, sem = refs[-5:]
    count, slabs, block, depth, _ = held.shape
    rows = slabs * block
    copies = start_all([(x_ref.at[start + f], planes.at[f]) for f in range(count)], sem)
    ends = [
        pltpu.make_async_copy(x_ref.at[:, pl.ds(z * rows, rows)], edges.at[i], sem.at[count + i])
        for i, z in enumerate((0, depth - 1))
    ]
    for copy in ends:
        copy.start()
    leaving = []
    for f in range(count):
        copies[f].wait()
        for y in range(rows):
            held[f, y // block, y % block] = planes[f, pl.ds(y, depth, stride=rows), :]
        copy = pltpu.make_async_copy(held.at[f], send.at[:, f], sem.at[f])
        copy.start()
        leaving.append(copy)
    wait_all(leaving + ends)


def to_chunks(states, slabs, start, count, later):
    _, depth, rows, width = states.shape
    block = rows // slabs
    return call(
        functools.partial(chunks_kernel, start),
        [(states.reshape(fields, -1, width), anywhere())]
        + [(x, anywhere()) for x in later],
        [
            ((slabs, count, block, depth, width), anywhere()),
            ((2, fields, rows, width), whole()),
        ],
        [
            vmem(count, depth * rows, width),
            vmem(count, slabs, block, depth, width),
            dmas(count + 2),
        ],
        0,
        "to_chunks",
    )


def planes_kernel(half, other, _, o_ref, again, held, sem):
    slabs, _, block, depth, _ = half.shape
    rows = slabs * block
    pairs = []
    for p in range(slabs):
        place = pl.ds(p * block, block)
        pairs.append((half.at[p], held.at[pl.ds(0, 2), place]))
        pairs.append((other.at[p], held.at[pl.ds(2, 2), place]))
    wait_all(start_all(pairs, sem))
    places = [held.at[pl.ds(2, 2), pl.ds(p * block, block)] for p in range(slabs)]
    copies = start_all([(places[p], again.at[p]) for p in range(slabs)], sem)

    def row(y, _):
        for f in range(fields):
            where = pl.ds(outside[f] * depth * rows + y, depth, stride=rows)
            o_ref[where, :] = held[f, y]
        return 0

    lax.fori_loop(0, rows, row, 0, unroll=4)
    wait_all(copies)


def to_planes(halves, later):
    slabs, _, block, depth, width = halves[0].shape
    return call(
        planes_kernel,
        [(x, anywhere()) for x in (*halves, later)],
        [
            ((fields * depth * slabs * block, width), whole()),
            (halves[1].shape, anywhere()),
        ],
        [vmem(fields, slabs * block, depth, width), dmas(2 * slabs)],
        0,
        "to_planes",
    )


def clear_pads(ref):
    edge = jnp.zeros(ref.shape[1:2] + (pad, ref.shape[3]), f32)
    for f in range(ref.shape[0]):
        ref[f, :, 0:pad] = edge
        ref[f, :, ref.shape[2] - pad :] = edge


def first_fluxes(state, visc, shift, carry):
    order = visc.shape[1]
    for z in range(0, order, tall):
        here, pads = pl.ds(z, tall), pl.ds(z + pad, tall)
        along_y = 0.5 * (visc[shift, here] + visc[shift + 1, here])
        for f in range(state.shape[0]):
            carry[f, here] = along_y * (state[f, 1, pads] - state[f, 0, pads])


def spread_of(state, f, j, value, here, pads, along_x, along_y, carry):
    flux_x = along_x * (east(value) - value)
    flux_y = along_y * (state[f, j + 1, pads] - value)
    spread = flux_x - west(flux_x) + (flux_y - carry[f, here])
    carry[f, here] = flux_y
    return spread


def advance_rows(state, speeds, shift, coupled, scratch, count, finish):
    visc, mat_high, mat_low, carry, high, low = scratch
    order, width = visc.shape[1:]
    first_fluxes(state, visc, shift, carry)

    def pair(k, _):
        for half in range(2):
            j = 2 * k + half + 1
            side = slice(half * width, (half + 1) * width)
            for z in range(0, order, tall):
                here, pads = pl.ds(z, tall), pl.ds(z + pad, tall)
                above, below = pl.ds(z + pad + 1, tall), pl.ds(z + pad - 1, tall)
                own = visc[j + shift, here]
                along_x = 0.5 * (own + east(own))
                along_y = 0.5 * (own + visc[j + shift + 1, here])
                speed = speeds[j, pads]
                for f in range(2):
                    value = state[f, j, pads]
                    rate = spread_of(state, f, j, value, here, pads, along_x, along_y, carry)
                    rate = rate - speed * (state[f, j, above] - state[f, j, below])
                    if coupled:
                        rate = rate + state[1 - f, j, pads]
                    high[f, here, side], low[f, here, side] = parts_of(value + time_step * rate)
        for f in range(2):
            out = product(mat_high[f], mat_low[f], high[f], low[f])
            finish(f, 2 * k, out[:, :width])
            finish(f, 2 * k + 1, out[:, width:])
        return 0

    lax.fori_loop(0, count // 2, pair, 0)


def step_scratch(order, width, count):
    return [
        vmem(count, order, width),
        pltpu.VMEM((count, order, 2 * width), bf16),
        pltpu.VMEM((count, order, 2 * width), bf16),
    ]


def two_scratch(frame):
    _, order, width = frame.shape
    matrix = pltpu.VMEM((2, order, order), bf16)
    return [vmem(*frame.shape), matrix, matrix] + step_scratch(order, width, 2)


def constants(base, sources, scratch):
    frame, mat_high, mat_low = sources
    two = pl.ds(base, 2)
    return [(frame, scratch[0]), (mat_high.at[two], scratch[1]), (mat_low.at[two], scratch[2])]


def rows_of(low_in, main, high_in, p, target):
    _, _, block, depth, _ = main.shape
    padded = pl.ds(p * depth + pad, depth)
    for row, count, part in ((0, 2, low_in), (2, block, main), (block + 2, 2, high_in)):
        yield part, target.at[:, pl.ds(row, count), padded]


def first_finish(first, order):
    def finish(f, row, piece):
        first[f, row, pl.ds(pad, order)] = piece

    return finish


def first_kernel(low_in, main, high_in, _, *refs):
    sources, (first, state, *scratch, sem) = refs[:3], refs[3:]
    slabs, _, block, depth, _ = main.shape
    pairs = constants(W, sources, scratch)
    for p in range(slabs):
        pairs += [(a.at[p], b) for a, b in rows_of(low_in, main, high_in, p, state)]
    copies = start_all(pairs, sem)
    clear_pads(state)
    clear_pads(first)
    wait_all(copies)
    finish = first_finish(first, slabs * depth)
    advance_rows(state, state.at[W], 0, True, scratch, block + 2, finish)


def first_step(low_in, main, high_in, later, frame, mat_high, mat_low):
    slabs, _, block, depth, width = main.shape
    order = slabs * depth
    volume = 2 * (block + 2) * order * width
    return call(
        first_kernel,
        [(x, anywhere()) for x in (low_in, main, high_in, later, frame, mat_high, mat_low)],
        [((2, block + 2, order + 2 * pad, width), whole())],
        [vmem(2, block + 4, order + 2 * pad, width)]
        + two_scratch(frame)
        + [dmas(3 * slabs + 3)],
        6 * order * volume,
        "first_step",
    )[0]


def carried_kernel(*refs):
    low_in, main, high_in, low_w, main_w, high_w, _ = refs[:7]
    sources, (first, state, speeds, *scratch, sem) = refs[7:10], refs[10:]
    slabs, _, block, depth, _ = main.shape
    pairs = constants(U, sources, scratch)
    for p in range(slabs):
        pairs += [(a.at[p], b) for a, b in rows_of(low_in, main, high_in, p, state)]
        w_rows = rows_of(low_w, main_w, high_w, p, speeds)
        pairs += [(a.at[p, pl.ds(W, 1)], b) for a, b in w_rows]
    copies = start_all(pairs, sem)
    clear_pads(state)
    clear_pads(first)
    wait_all(copies)
    finish = first_finish(first, slabs * depth)
    advance_rows(state, speeds.at[0], 0, False, scratch, block + 2, finish)


def carried_step(own, with_w, later, frame, mat_high, mat_low):
    slabs, _, block, depth, width = own[1].shape
    order = slabs * depth
    volume = 2 * (block + 2) * order * width
    return call(
        carried_kernel,
        [(x, anywhere()) for x in (*own, *with_w, later, frame, mat_high, mat_low)],
        [((2, block + 2, order + 2 * pad, width), whole())],
        [
            vmem(2, block + 4, order + 2 * pad, width),
            vmem(1, block + 4, order + 2 * pad, width),
        ]
        + two_scratch(frame)
        + [dmas(6 * slabs + 3)],
        6 * order * volume,
        "carried_step",
    )[0]


def second_kernel(base, count, first, with_w, *refs):
    sources, targets = refs[:3], refs[3 : 3 + count]
    out, low_edge, high_edge, state, speeds, *scratch, held, sem = refs[-13:]
    slabs, _, block, depth, _ = out.shape
    places = [held.at[:, :, pl.ds(p * depth, depth)] for p in range(slabs)]
    pairs = constants(base, sources, scratch) + [(first, state)]
    if base != W:
        pairs.append((with_w.at[W], speeds))
    for target, span in spans(targets, 2):
        for p in range(slabs):
            pairs.append((target.at[p], held.at[:, span, pl.ds(p * depth, depth)]))
    wait_all(start_all(pairs, sem))

    def finish(f, row, piece):
        held[f, row] = piece - held[f, row]

    speeds = state.at[W] if base == W else speeds
    advance_rows(state, speeds, 1, base == W, scratch, block, finish)
    copies = start_all([(places[p], out.at[p]) for p in range(slabs)], sem)
    low_edge[...] = held[:, 0]
    high_edge[...] = held[:, block - 1]
    wait_all(copies)


def second_step(first, with_w, frame, mat_high, mat_low, base, targets, later):
    _, order, width = frame.shape
    slabs, _, _, depth, _ = targets[0].shape
    block = sum(target.shape[2] for target in targets)
    operands = (first, with_w, frame, mat_high, mat_low, *targets, *later)
    return call(
        functools.partial(second_kernel, base, len(targets)),
        [(x, anywhere()) for x in operands],
        [((slabs, 2, block, depth, width), anywhere())] + [((2, order, width), whole())] * 2,
        [vmem(*first.shape), vmem(*first.shape[1:])]
        + two_scratch(frame)
        + [vmem(2, block, order, width), dmas(2 * slabs + 5)],
        6 * order * 2 * block * order * width,
        "second_step",
    )


def after_kernel(*refs):
    del refs


def after(value, later):
    return call(
        after_kernel,
        [(x, anywhere()) for x in (value, *later)],
        [(value.shape, anywhere())],
        [],
        0,
        "after",
        aliases={0: 0},
    )[0]


def outer_kernel(count, chunks, *refs):
    *outs, sem = refs[-count - 1 :]
    block = chunks.shape[2]
    low, high = chunks.at[:, :, pl.ds(0, 2)], chunks.at[:, :, pl.ds(block - 2, 2)]
    pairs = [(low, outs[0]), (high, outs[1])]
    pairs += [(chunks.at[:, :, span], part) for part, span in spans(outs[2:], 2)]
    wait_all(start_all(pairs, sem))


def pieces_kernel(count, chunks, *refs):
    *outs, sem = refs[-count - 1 :]
    wait_all(start_all([(chunks.at[:, :, span], part) for part, span in spans(outs, 2)], sem))


def row_parts(kernel, chunks, later, sizes, name):
    slabs, count, _, depth, width = chunks.shape
    return call(
        functools.partial(kernel, len(sizes)),
        [(chunks, anywhere())] + [(x, anywhere()) for x in later],
        [((slabs, count, size, depth, width), whole()) for size in sizes],
        [dmas(len(sizes))],
        0,
        name,
    )


def adjoint_kernel(*refs):
    halves, low_edges, high_edges = refs[0:2], refs[2:4], refs[4:6]
    firsts, (visc, mat_high, mat_low) = refs[6:8], refs[8:11]
    out, cot, pulled, ends, carry, high, low, sem = refs[11:]
    slabs, _, block, depth, width = halves[0].shape
    order = slabs * depth
    main = pl.ds(1, block)
    pairs = []
    for source, span in spans(halves):
        for p in range(slabs):
            pairs.append((source.at[p], cot.at[span, main, pl.ds(p * depth, depth)]))
    for i in range(2):
        pairs.append((low_edges[i], cot.at[pl.ds(2 * i, 2), 0]))
        pairs.append((high_edges[i], cot.at[pl.ds(2 * i, 2), block + 1]))
    copies = start_all(pairs, sem)
    clear_pads(pulled)
    wait_all(copies)

    def pull(k, _):
        for f in range(fields):
            pair = jnp.concatenate([cot[f, 2 * k], cot[f, 2 * k + 1]], axis=1)
            out = product(mat_high[f], mat_low[f], *parts_of(pair))
            pulled[f, 2 * k, pl.ds(pad, order)] = out[:, :width]
            pulled[f, 2 * k + 1, pl.ds(pad, order)] = out[:, width:]
        return 0

    lax.fori_loop(0, (block + 2) // 2, pull, 0)
    first_fluxes(pulled, visc, 1, carry)

    def rows(k, _):
        for half in range(2):
            j = 2 * k + half + 1
            side = slice(half * width, (half + 1) * width)
            for z in range(0, order, tall):
                here, pads = pl.ds(z, tall), pl.ds(z + pad, tall)
                above, below = pl.ds(z + pad + 1, tall), pl.ds(z + pad - 1, tall)
                own = visc[j + 1, here]
                along_x = 0.5 * (own + east(own))
                along_y = 0.5 * (own + visc[j + 2, here])
                speed_above, speed_below = firsts[0][W, j, above], firsts[0][W, j, below]
                coupling = pulled[T, j, pads]
                for f in (U, V, T, W):
                    value = pulled[f, j, pads]
                    rate = spread_of(pulled, f, j, value, here, pads, along_x, along_y, carry)
                    up, down = pulled[f, j, above], pulled[f, j, below]
                    rate = rate + (speed_above * up - speed_below * down)
                    if f == W:
                        slope = speed_above - speed_below
                    else:
                        ref, i = firsts[f // 2], f % 2
                        slope = ref[i, j, above] - ref[i, j, below]
                    coupling = coupling - value * slope
                    if f == T:
                        rate = rate + pulled[W, j, pads]
                    if f == W:
                        rate = rate + coupling
                    high[f, here, side], low[f, here, side] = parts_of(value + time_step * rate)
        for f in range(fields):
            out = product(mat_high[f], mat_low[f], high[f], low[f])
            cot[f, 2 * k + 1] = out[:, :width]
            cot[f, 2 * k + 2] = out[:, width:]
        return 0

    lax.fori_loop(0, block // 2, rows, 0)
    pairs = []
    for p in range(slabs):
        for f in range(fields):
            source = cot.at[f, main, pl.ds(p * depth, depth)]
            pairs.append((source, out.at[p, pl.ds(f * block, block)]))
    copies = start_all(pairs, sem)
    for p in range(slabs):
        for f in range(fields):
            for y in range(block):
                for side, z in ((0, p * depth - 1), (1, (p + 1) * depth)):
                    to = slice(f * block + y, f * block + y + 1)
                    if 0 <= z < order:
                        ends[p, side, to] = cot[f, y + 1, z : z + 1]
                    else:
                        ends[p, side, to] = jnp.zeros((1, width), f32)
    ends_copy = pltpu.make_async_copy(
        ends, out.at[:, pl.ds(fields * block, 2)], sem.at[len(pairs)]
    )
    ends_copy.start()
    wait_all(copies)
    ends_copy.wait()


def adjoint_step(halves, low_edges, high_edges, firsts, visc, mat_high, mat_low):
    slabs, _, block, depth, width = halves[0].shape
    order = slabs * depth
    volume = fields * (block + 1) * order * width
    return call(
        adjoint_kernel,
        [(x, anywhere()) for x in (*halves, *low_edges, *high_edges)]
        + [(x, whole()) for x in (*firsts, visc, mat_high, mat_low)],
        [((slabs, fields * block + 2, depth, width), anywhere())],
        [
            vmem(fields, block + 2, order, width),
            vmem(fields, block + 2, order + 2 * pad, width),
            vmem(slabs, 2, depth, width),
        ]
        + step_scratch(order, width, fields)
        + [dmas(slabs * fields + 1)],
        12 * order * volume,
        "adjoint_step",
    )[0]


def last_kernel(*refs):
    visc_in, edges_below, edges_above, chunks, *states, half, other, out = refs[:9]
    pulled, state, prior, planes, coupling, ends, visc, sem = refs[9:]
    slabs, block, depth, width = visc.shape
    rows, step = slabs * block, pulled.shape[3]
    main = pl.ds(pad, depth)
    above, below = pl.ds(pad + 1, depth), pl.ds(pad - 1, depth)

    def copy(source, target, which):
        return pltpu.make_async_copy(source, target, sem.at[which])

    arrive = {"visc": copy(visc_in, visc, 0)}
    arrive["ends"] = copy(chunks.at[:, pl.ds(fields * block, 2)], ends, 1)
    for f in range(fields):
        source = chunks.at[:, pl.ds(f * block, block)]
        arrive["pulled", f] = copy(source, pulled.at[f, :, :, main], 2 + f)
        source = states[f // 2].at[:, f % 2]
        arrive["state", f] = copy(source, state.at[f, :, :, main], 2 + fields + f)
        source = (half, other)[f // 2].at[:, f % 2]
        arrive["prior", f] = copy(source, prior.at[f], 2 + 2 * fields + f)
    order = ["visc", "ends", ("state", W)]
    order += [(which, f) for f in (U, V, T, W) for which in ("pulled", "state", "prior")]
    for which in dict.fromkeys(order):
        arrive[which].start()

    def ready(*which):
        for name in which:
            if name in arrive:
                arrive.pop(name).wait()

    flat = (fields * rows * step, width)
    state_rows, pulled_rows = state.reshape(flat), pulled.reshape(flat)
    first, last = pad - 1, pad + depth
    for f in range(fields):
        base = f * rows * step
        state_rows[pl.ds(base + first, rows, stride=step), :] = edges_below[outside[f]]
        state_rows[pl.ds(base + last, rows, stride=step), :] = edges_above[outside[f]]
    ready("visc", "ends")
    for f in range(fields):
        for p in range(slabs):
            base, part = (f * rows + p * block) * step, pl.ds(f * block, block)
            pulled_rows[pl.ds(base + first, block, stride=step), :] = ends[p, 0, part]
            pulled_rows[pl.ds(base + last, block, stride=step), :] = ends[p, 1, part]
    ready(("state", W))
    leaving = []
    for f in (U, V, T, W):
        ready(("pulled", f), ("state", f), ("prior", f))
        if f == T:
            ready(("pulled", W))
        along_y = 0.5 * (visc[slabs - 1, block - 1] + visc[0, 0])
        south = along_y * (pulled[f, 0, 0, main] - pulled[f, slabs - 1, block - 1, main])

        def group(p, south):
            after = lax.rem(p + 1, slabs)
            for i in range(block):
                n, m = (p, i + 1) if i + 1 < block else (after, 0)
                own = visc[p, i]
                along_x = 0.5 * (own + east(own))
                along_y = 0.5 * (own + visc[n, m])
                value = pulled[f, p, i, main]
                flux_x = along_x * (east(value) - value)
                flux_y = along_y * (pulled[f, n, m, main] - value)
                rate = flux_x - west(flux_x) + (flux_y - south)
                south = flux_y
                flow = state[W, p, i, above] * pulled[f, p, i, above]
                rate = rate + (flow - state[W, p, i, below] * pulled[f, p, i, below])
                lost = value * (state[f, p, i, above] - state[f, p, i, below])
                if f == U:
                    coupling[p, i] = lost
                elif f == V:
                    coupling[p, i] = coupling[p, i] + lost
                elif f == T:
                    coupling[p, i] = value - (coupling[p, i] + lost)
                    rate = rate + pulled[W, p, i, main]
                else:
                    rate = rate + (coupling[p, i] - lost)
                result = value + time_step * rate - prior[f, p, i]
                planes[f, pl.ds(p * block + i, depth, stride=rows), :] = result
            return south

        lax.fori_loop(0, slabs, group, south)
        leave = copy(planes.at[f], out.at[outside[f]], 2 + f)
        leave.start()
        leaving.append(leave)
    wait_all(leaving)


def last_step(visc, below, above, chunks, states, priors):
    rows, depth, width = visc.shape
    slabs = chunks.shape[0]
    block = rows // slabs
    padded = vmem(fields, slabs, block, depth + 2 * pad, width)
    one = (slabs, block, depth, width)
    return call(
        last_kernel,
        [(visc.reshape(one), anywhere()), (below, whole()), (above, whole())]
        + [(x, anywhere()) for x in (chunks, *states, *priors)],
        [((fields, depth * rows, width), anywhere())],
        [
            padded,
            padded,
            vmem(fields, *one),
            vmem(fields, depth * rows, width),
            vmem(*one),
            vmem(slabs, 2, depth, width),
            vmem(*one),
            dmas(2 + 3 * fields),
        ],
        30 * fields * rows * depth * width,
        "last_step",
    )[0]


def exchange(chunks):
    return lax.all_to_all(chunks, "slab", split_axis=0, concat_axis=0, tiled=True)


def around(value, axis, steps):
    count = lax.axis_size(axis)
    return lax.ppermute(value, axis, [(i, (i + steps) % count) for i in range(count)])


def local(states, viscosity, inverse):
    start = states[0]
    _, depth, rows, width = start.shape
    slabs, segs = lax.axis_size("slab"), lax.axis_size("seg")
    block = rows // slabs
    share = -(-(block + 4) // segs)

    own_seg = jnp.full((1,), lax.axis_index("seg"), jnp.int32)
    visc, visc_send = visc_chunks(own_seg, viscosity, slabs, share)
    visc_share = exchange(visc_send)
    visc_in = [visc_share] + [around(visc_share, "seg", -i) for i in range(1, segs)]
    send_half, _ = to_chunks(start, slabs, outside[W], 2, [visc_send])
    main_half = exchange(send_half)
    mat_high, mat_low, adj_high, adj_low = split(inverse)
    frame = to_frame(own_seg, visc_in)
    send_other, ends = to_chunks(start, slabs, outside[U], 2, [frame, mat_high])
    main_other = exchange(send_other)
    forward = [(i, i + 1) for i in range(slabs - 1)]
    below = lax.ppermute(ends[1], "slab", forward)
    above = lax.ppermute(ends[0], "slab", [(i, j) for j, i in forward])

    mats = mat_high, mat_low
    low_rows, high_rows, again = row_parts(
        outer_kernel, main_half, (visc_share,), (2, 2, block), "outer_rows"
    )
    own = [(around(high_rows, "slab", 1), main_half, around(low_rows, "slab", -1))]
    target = around(again, "seg", -1)
    first_half = first_step(*own[0], frame, frame, *mats)

    later = (own[0][0], own[0][2], first_half)
    low_rows, high_rows = row_parts(outer_kernel, main_other, later, (2, 2), "outer_rows")
    own.append((around(high_rows, "slab", 1), main_other, around(low_rows, "slab", -1)))
    few = max(1, block // 8)
    parts = row_parts(pieces_kernel, main_other, (low_rows,), (few, block - few), "pieces")
    targets = [[target], [around(part, "seg", -1) for part in parts]]

    out, low_edge, high_edge = second_step(
        first_half, first_half, frame, *mats, W, targets[0], (parts[0],)
    )
    out = after(out, (own[1][0], own[1][2], targets[1][0]))
    first_other = carried_step(own[1], own[0], out, frame, *mats)
    other, *more = second_step(
        first_other, first_half, frame, *mats, U, targets[1], (out,)
    )
    low_edges = [around(edge, "slab", 1) for edge in (high_edge, more[1])]
    high_edges = [around(edge, "slab", -1) for edge in (low_edge, more[0])]
    half = exchange(out)
    residual = (out, after(other, (*low_edges, *high_edges, half)))
    firsts = (first_half, first_other)
    pulled = adjoint_step(residual, low_edges, high_edges, firsts, frame, adj_high, adj_low)
    planes, other = to_planes((half, exchange(residual[1])), pulled)
    priors = [around(part, "seg", 1) for part in (half, other)]
    gradient = last_step(visc, below, above, exchange(pulled), (send_half, send_other), priors)
    shape = (1, fields, depth, rows, width)
    return (planes.reshape(shape), gradient.reshape(shape))


def solution(mesh):
    in_specs = (P("seg", None, "slab", None, None), P("slab", None, None), P())
    out_specs = (P("seg", None, "slab", None, None), P("seg", None, "slab", None, None))
    return jax.shard_map(local, mesh=mesh, in_specs=in_specs, out_specs=out_specs, check_vma=False)
```

```python
import functools

import jax
import jax.numpy as jnp
from jax import lax
from jax.experimental import pallas as pl
from jax.experimental.pallas import tpu as pltpu
from jax.sharding import PartitionSpec as P

time_step = 0.1
vmem_bytes = 56 * 1024 * 1024
f32, bf16 = jnp.float32, jnp.bfloat16
fields = 4
W, T, U, V = range(4)
outside = (2, 3, 0, 1)
pad = 8
tall = 32


def whole():
    return pl.BlockSpec(memory_space=pltpu.VMEM)


def anywhere():
    return pl.BlockSpec(memory_space=pl.ANY)


def scalars():
    return pl.BlockSpec(memory_space=pltpu.SMEM)


def vmem(*shape):
    return pltpu.VMEM(shape, f32)


def dmas(count):
    return pltpu.SemaphoreType.DMA((count,))


def call(kernel, ins, outs, scratch, flops, name, kind=f32, aliases=None):
    moved = sum(4 * x.size for x, _ in ins)
    return pl.pallas_call(
        kernel,
        in_specs=[spec for _, spec in ins],
        out_specs=tuple(spec for _, spec in outs),
        out_shape=tuple(jax.ShapeDtypeStruct(shape, kind) for shape, _ in outs),
        scratch_shapes=scratch,
        input_output_aliases=aliases or {},
        compiler_params=pltpu.CompilerParams(vmem_limit_bytes=vmem_bytes),
        cost_estimate=pl.CostEstimate(flops=flops, bytes_accessed=moved, transcendentals=0),
        name=name,
    )(*[x for x, _ in ins])


def start_all(pairs, sem):
    copies = [
        pltpu.make_async_copy(source, target, sem.at[i])
        for i, (source, target) in enumerate(pairs)
    ]
    for copy in copies:
        copy.start()
    return copies


def wait_all(copies):
    for copy in copies:
        copy.wait()


def spans(parts, axis=1):
    start = 0
    for part in parts:
        yield part, pl.ds(start, part.shape[axis])
        start += part.shape[axis]


def east(value):
    return pltpu.roll(value, value.shape[1] - 1, 1)


def west(value):
    return pltpu.roll(value, 1, 1)


def parts_of(value):
    high = value.astype(bf16)
    return high, (value - high.astype(f32)).astype(bf16)


def product(matrix_high, matrix_low, high, low):
    dot = functools.partial(jnp.dot, preferred_element_type=f32)
    return dot(matrix_high, high) + (dot(matrix_high, low) + dot(matrix_low, high))


def split_kernel(x_ref, high, low, adj_high, adj_low):
    for f in range(fields):
        high[f], low[f] = parts_of(x_ref[outside[f]])
        adj_high[f], adj_low[f] = parts_of(x_ref[outside[f]].T)


def split(inverse):
    return call(
        split_kernel,
        [(inverse, whole())],
        [(inverse.shape, whole())] * 4,
        [],
        0,
        "split",
        bf16,
    )


def visc_kernel(own, x_ref, visc, send):
    slabs, share = send.shape[:2]
    rows, depth, _ = visc.shape
    block = rows // slabs
    for y in range(rows):
        visc[y] = x_ref[pl.ds(y, depth, stride=rows), :]
    for p in range(slabs):
        for i in range(share):
            send[p, i] = visc[lax.rem(p * block - 2 + share * own[0] + i + rows, rows)]


def visc_chunks(own, viscosity, slabs, share):
    depth, rows, width = viscosity.shape
    return call(
        visc_kernel,
        [(own, scalars()), (viscosity.reshape(-1, width), whole())],
        [((rows, depth, width), whole()), ((slabs, share, depth, width), whole())],
        [],
        0,
        "visc_chunks",
    )


def frame_kernel(own, *refs):
    *shares, frame, sem = refs
    slabs, share, depth, _ = shares[0].shape
    pairs = []
    for i, part in enumerate(shares):
        start = lax.rem(own[0] + i, len(shares)) * share
        for p in range(slabs):
            pairs.append((part.at[p], frame.at[pl.ds(start, share), pl.ds(p * depth, depth)]))
    wait_all(start_all(pairs, sem))


def to_frame(own, shares):
    slabs, share, depth, width = shares[0].shape
    return call(
        frame_kernel,
        [(own, scalars())] + [(x, anywhere()) for x in shares],
        [((len(shares) * share, slabs * depth, width), whole())],
        [dmas(len(shares) * slabs)],
        0,
        "to_frame",
    )[0]


def chunks_kernel(start, x_ref, *refs):
    send, edges, planes, held, sem = refs[-5:]
    count, slabs, block, depth, _ = held.shape
    rows = slabs * block
    copies = start_all([(x_ref.at[start + f], planes.at[f]) for f in range(count)], sem)
    ends = [
        pltpu.make_async_copy(x_ref.at[:, pl.ds(z * rows, rows)], edges.at[i], sem.at[count + i])
        for i, z in enumerate((0, depth - 1))
    ]
    for copy in ends:
        copy.start()
    leaving = []
    for f in range(count):
        copies[f].wait()
        for y in range(rows):
            held[f, y // block, y % block] = planes[f, pl.ds(y, depth, stride=rows), :]
        copy = pltpu.make_async_copy(held.at[f], send.at[:, f], sem.at[f])
        copy.start()
        leaving.append(copy)
    wait_all(leaving + ends)


def to_chunks(states, slabs, start, count, later):
    _, depth, rows, width = states.shape
    block = rows // slabs
    return call(
        functools.partial(chunks_kernel, start),
        [(states.reshape(fields, -1, width), anywhere())]
        + [(x, anywhere()) for x in later],
        [
            ((slabs, count, block, depth, width), anywhere()),
            ((2, fields, rows, width), whole()),
        ],
        [
            vmem(count, depth * rows, width),
            vmem(count, slabs, block, depth, width),
            dmas(count + 2),
        ],
        0,
        "to_chunks",
    )


def planes_kernel(half, other, _, o_ref, again, held, sem):
    slabs, _, block, depth, _ = half.shape
    rows = slabs * block
    pairs = []
    for p in range(slabs):
        place = pl.ds(p * block, block)
        pairs.append((half.at[p], held.at[pl.ds(0, 2), place]))
        pairs.append((other.at[p], held.at[pl.ds(2, 2), place]))
    wait_all(start_all(pairs, sem))
    places = [held.at[pl.ds(2, 2), pl.ds(p * block, block)] for p in range(slabs)]
    copies = start_all([(places[p], again.at[p]) for p in range(slabs)], sem)

    def row(y, _):
        for f in range(fields):
            where = pl.ds(outside[f] * depth * rows + y, depth, stride=rows)
            o_ref[where, :] = held[f, y]
        return 0

    lax.fori_loop(0, rows, row, 0, unroll=4)
    wait_all(copies)


def to_planes(halves, later):
    slabs, _, block, depth, width = halves[0].shape
    return call(
        planes_kernel,
        [(x, anywhere()) for x in (*halves, later)],
        [
            ((fields * depth * slabs * block, width), whole()),
            (halves[1].shape, anywhere()),
        ],
        [vmem(fields, slabs * block, depth, width), dmas(2 * slabs)],
        0,
        "to_planes",
    )


def clear_pads(ref):
    edge = jnp.zeros(ref.shape[1:2] + (pad, ref.shape[3]), f32)
    for f in range(ref.shape[0]):
        ref[f, :, 0:pad] = edge
        ref[f, :, ref.shape[2] - pad :] = edge


def first_fluxes(state, visc, shift, carry):
    order = visc.shape[1]
    for z in range(0, order, tall):
        here, pads = pl.ds(z, tall), pl.ds(z + pad, tall)
        along_y = 0.5 * (visc[shift, here] + visc[shift + 1, here])
        for f in range(state.shape[0]):
            carry[f, here] = along_y * (state[f, 1, pads] - state[f, 0, pads])


def spread_of(state, f, j, value, here, pads, along_x, along_y, carry):
    flux_x = along_x * (east(value) - value)
    flux_y = along_y * (state[f, j + 1, pads] - value)
    spread = flux_x - west(flux_x) + (flux_y - carry[f, here])
    carry[f, here] = flux_y
    return spread


def advance_rows(state, speeds, shift, coupled, scratch, count, finish):
    visc, mat_high, mat_low, carry, high, low = scratch
    order, width = visc.shape[1:]
    first_fluxes(state, visc, shift, carry)

    def pair(k, _):
        for half in range(2):
            j = 2 * k + half + 1
            side = slice(half * width, (half + 1) * width)
            for z in range(0, order, tall):
                here, pads = pl.ds(z, tall), pl.ds(z + pad, tall)
                above, below = pl.ds(z + pad + 1, tall), pl.ds(z + pad - 1, tall)
                own = visc[j + shift, here]
                along_x = 0.5 * (own + east(own))
                along_y = 0.5 * (own + visc[j + shift + 1, here])
                speed = speeds[j, pads]
                for f in range(2):
                    value = state[f, j, pads]
                    rate = spread_of(state, f, j, value, here, pads, along_x, along_y, carry)
                    rate = rate - speed * (state[f, j, above] - state[f, j, below])
                    if coupled:
                        rate = rate + state[1 - f, j, pads]
                    high[f, here, side], low[f, here, side] = parts_of(value + time_step * rate)
        for f in range(2):
            out = product(mat_high[f], mat_low[f], high[f], low[f])
            finish(f, 2 * k, out[:, :width])
            finish(f, 2 * k + 1, out[:, width:])
        return 0

    lax.fori_loop(0, count // 2, pair, 0)


def step_scratch(order, width, count):
    return [
        vmem(count, order, width),
        pltpu.VMEM((count, order, 2 * width), bf16),
        pltpu.VMEM((count, order, 2 * width), bf16),
    ]


def two_scratch(frame):
    _, order, width = frame.shape
    matrix = pltpu.VMEM((2, order, order), bf16)
    return [vmem(*frame.shape), matrix, matrix] + step_scratch(order, width, 2)


def constants(base, sources, scratch):
    frame, mat_high, mat_low = sources
    two = pl.ds(base, 2)
    return [(frame, scratch[0]), (mat_high.at[two], scratch[1]), (mat_low.at[two], scratch[2])]


def rows_of(low_in, main, high_in, p, target):
    _, _, block, depth, _ = main.shape
    padded = pl.ds(p * depth + pad, depth)
    for row, count, part in ((0, 2, low_in), (2, block, main), (block + 2, 2, high_in)):
        yield part, target.at[:, pl.ds(row, count), padded]


def first_finish(first, order):
    def finish(f, row, piece):
        first[f, row, pl.ds(pad, order)] = piece

    return finish


def carried_kernel(*refs):
    low_in, main, high_in, low_w, main_w, high_w, _ = refs[:7]
    sources, (first, state, speeds, *scratch, sem) = refs[7:10], refs[10:]
    slabs, _, block, depth, _ = main.shape
    pairs = constants(U, sources, scratch)
    for p in range(slabs):
        pairs += [(a.at[p], b) for a, b in rows_of(low_in, main, high_in, p, state)]
        w_rows = rows_of(low_w, main_w, high_w, p, speeds)
        pairs += [(a.at[p, pl.ds(W, 1)], b) for a, b in w_rows]
    copies = start_all(pairs, sem)
    clear_pads(state)
    clear_pads(first)
    wait_all(copies)
    finish = first_finish(first, slabs * depth)
    advance_rows(state, speeds.at[0], 0, False, scratch, block + 2, finish)


def carried_step(own, with_w, later, frame, mat_high, mat_low):
    slabs, _, block, depth, width = own[1].shape
    order = slabs * depth
    volume = 2 * (block + 2) * order * width
    return call(
        carried_kernel,
        [(x, anywhere()) for x in (*own, *with_w, later, frame, mat_high, mat_low)],
        [((2, block + 2, order + 2 * pad, width), whole())],
        [
            vmem(2, block + 4, order + 2 * pad, width),
            vmem(1, block + 4, order + 2 * pad, width),
        ]
        + two_scratch(frame)
        + [dmas(6 * slabs + 3)],
        6 * order * volume,
        "carried_step",
    )[0]


def second_kernel(base, count, first, with_w, *refs):
    sources, targets = refs[:3], refs[3 : 3 + count]
    out, low_edge, high_edge, state, speeds, *scratch, held, sem = refs[-13:]
    slabs, _, block, depth, _ = out.shape
    places = [held.at[:, :, pl.ds(p * depth, depth)] for p in range(slabs)]
    pairs = constants(base, sources, scratch) + [(first, state)]
    if base != W:
        pairs.append((with_w.at[W], speeds))
    for target, span in spans(targets, 2):
        for p in range(slabs):
            pairs.append((target.at[p], held.at[:, span, pl.ds(p * depth, depth)]))
    wait_all(start_all(pairs, sem))

    def finish(f, row, piece):
        held[f, row] = piece - held[f, row]

    speeds = state.at[W] if base == W else speeds
    advance_rows(state, speeds, 1, base == W, scratch, block, finish)
    copies = start_all([(places[p], out.at[p]) for p in range(slabs)], sem)
    low_edge[...] = held[:, 0]
    high_edge[...] = held[:, block - 1]
    wait_all(copies)


def second_step(first, with_w, frame, mat_high, mat_low, base, targets, later):
    _, order, width = frame.shape
    slabs, _, _, depth, _ = targets[0].shape
    block = sum(target.shape[2] for target in targets)
    operands = (first, with_w, frame, mat_high, mat_low, *targets, *later)
    return call(
        functools.partial(second_kernel, base, len(targets)),
        [(x, anywhere()) for x in operands],
        [((slabs, 2, block, depth, width), anywhere())] + [((2, order, width), whole())] * 2,
        [vmem(*first.shape), vmem(*first.shape[1:])]
        + two_scratch(frame)
        + [vmem(2, block, order, width), dmas(2 * slabs + 5)],
        6 * order * 2 * block * order * width,
        "second_step",
    )


def two_steps_kernel(low_in, main, high_in, target, _, *refs):
    sources, (first, out, low_edge, high_edge), refs = refs[:3], refs[3:7], refs[7:]
    state, *scratch, held, sem = refs
    slabs, _, block, depth, _ = main.shape
    pairs = constants(W, sources, scratch)
    places = [held.at[:, :, pl.ds(p * depth, depth)] for p in range(slabs)]
    for p in range(slabs):
        pairs += [(a.at[p], b) for a, b in rows_of(low_in, main, high_in, p, state)]
        pairs.append((target.at[p], places[p]))
    copies = start_all(pairs, sem)
    clear_pads(state)
    clear_pads(first)
    wait_all(copies)
    finish = first_finish(first, slabs * depth)
    advance_rows(state, state.at[W], 0, True, scratch, block + 2, finish)

    def subtract(f, row, piece):
        held[f, row] = piece - held[f, row]

    advance_rows(first, first.at[W], 1, True, scratch, block, subtract)
    copies = start_all([(places[p], out.at[p]) for p in range(slabs)], sem)
    low_edge[...] = held[:, 0]
    high_edge[...] = held[:, block - 1]
    wait_all(copies)


def two_steps(low_in, main, high_in, target, later, frame, mat_high, mat_low):
    slabs, _, block, depth, width = main.shape
    order = slabs * depth
    volume = 2 * (block + 1) * order * width
    operands = (low_in, main, high_in, target, later, frame, mat_high, mat_low)
    return call(
        two_steps_kernel,
        [(x, anywhere()) for x in operands],
        [
            ((2, block + 2, order + 2 * pad, width), whole()),
            (main.shape, anywhere()),
            ((2, order, width), whole()),
            ((2, order, width), whole()),
        ],
        [vmem(2, block + 4, order + 2 * pad, width)]
        + two_scratch(frame)
        + [vmem(2, block, order, width), dmas(4 * slabs + 3)],
        12 * order * volume,
        "two_steps",
    )


def after_kernel(*refs):
    del refs


def after(value, later):
    return call(
        after_kernel,
        [(x, anywhere()) for x in (value, *later)],
        [(value.shape, anywhere())],
        [],
        0,
        "after",
        aliases={0: 0},
    )[0]


def outer_kernel(chunks, _before, _after, low_rows, high_rows, *refs):
    *again, sem = refs
    block = chunks.shape[2]
    low, high = chunks.at[:, :, pl.ds(0, 2)], chunks.at[:, :, pl.ds(block - 2, 2)]
    pairs = [(low, low_rows), (high, high_rows)]
    pairs += [(chunks.at[:, :, span], part) for part, span in spans(again, 2)]
    wait_all(start_all(pairs, sem))


def outer_rows(chunks, later, pieces):
    slabs, count, _, depth, width = chunks.shape
    rows = [((slabs, count, size, depth, width), whole()) for size in (2, 2, *pieces)]
    return call(
        outer_kernel,
        [(chunks, anywhere())] + [(x, anywhere()) for x in later],
        rows,
        [dmas(len(rows))],
        0,
        "outer_rows",
    )


def adjoint_kernel(*refs):
    halves, low_edges, high_edges = refs[0:2], refs[2:4], refs[4:6]
    firsts, (visc, mat_high, mat_low) = refs[6:8], refs[8:11]
    out, cot, pulled, ends, carry, high, low, sem = refs[11:]
    slabs, _, block, depth, width = halves[0].shape
    order = slabs * depth
    main = pl.ds(1, block)
    pairs = []
    for source, span in spans(halves):
        for p in range(slabs):
            pairs.append((source.at[p], cot.at[span, main, pl.ds(p * depth, depth)]))
    for i in range(2):
        pairs.append((low_edges[i], cot.at[pl.ds(2 * i, 2), 0]))
        pairs.append((high_edges[i], cot.at[pl.ds(2 * i, 2), block + 1]))
    copies = start_all(pairs, sem)
    clear_pads(pulled)
    wait_all(copies)

    def pull(k, _):
        for f in range(fields):
            pair = jnp.concatenate([cot[f, 2 * k], cot[f, 2 * k + 1]], axis=1)
            out = product(mat_high[f], mat_low[f], *parts_of(pair))
            pulled[f, 2 * k, pl.ds(pad, order)] = out[:, :width]
            pulled[f, 2 * k + 1, pl.ds(pad, order)] = out[:, width:]
        return 0

    lax.fori_loop(0, (block + 2) // 2, pull, 0)
    first_fluxes(pulled, visc, 1, carry)

    def rows(k, _):
        for half in range(2):
            j = 2 * k + half + 1
            side = slice(half * width, (half + 1) * width)
            for z in range(0, order, tall):
                here, pads = pl.ds(z, tall), pl.ds(z + pad, tall)
                above, below = pl.ds(z + pad + 1, tall), pl.ds(z + pad - 1, tall)
                own = visc[j + 1, here]
                along_x = 0.5 * (own + east(own))
                along_y = 0.5 * (own + visc[j + 2, here])
                speed_above, speed_below = firsts[0][W, j, above], firsts[0][W, j, below]
                coupling = pulled[T, j, pads]
                for f in (U, V, T, W):
                    value = pulled[f, j, pads]
                    rate = spread_of(pulled, f, j, value, here, pads, along_x, along_y, carry)
                    up, down = pulled[f, j, above], pulled[f, j, below]
                    rate = rate + (speed_above * up - speed_below * down)
                    if f == W:
                        slope = speed_above - speed_below
                    else:
                        ref, i = firsts[f // 2], f % 2
                        slope = ref[i, j, above] - ref[i, j, below]
                    coupling = coupling - value * slope
                    if f == T:
                        rate = rate + pulled[W, j, pads]
                    if f == W:
                        rate = rate + coupling
                    high[f, here, side], low[f, here, side] = parts_of(value + time_step * rate)
        for f in range(fields):
            out = product(mat_high[f], mat_low[f], high[f], low[f])
            cot[f, 2 * k + 1] = out[:, :width]
            cot[f, 2 * k + 2] = out[:, width:]
        return 0

    lax.fori_loop(0, block // 2, rows, 0)
    pairs = []
    for p in range(slabs):
        for f in range(fields):
            source = cot.at[f, main, pl.ds(p * depth, depth)]
            pairs.append((source, out.at[p, pl.ds(f * block, block)]))
    copies = start_all(pairs, sem)
    for p in range(slabs):
        for f in range(fields):
            for y in range(block):
                for side, z in ((0, p * depth - 1), (1, (p + 1) * depth)):
                    to = slice(f * block + y, f * block + y + 1)
                    if 0 <= z < order:
                        ends[p, side, to] = cot[f, y + 1, z : z + 1]
                    else:
                        ends[p, side, to] = jnp.zeros((1, width), f32)
    ends_copy = pltpu.make_async_copy(
        ends, out.at[:, pl.ds(fields * block, 2)], sem.at[len(pairs)]
    )
    ends_copy.start()
    wait_all(copies)
    ends_copy.wait()


def adjoint_step(halves, low_edges, high_edges, firsts, visc, mat_high, mat_low):
    slabs, _, block, depth, width = halves[0].shape
    order = slabs * depth
    volume = fields * (block + 1) * order * width
    return call(
        adjoint_kernel,
        [(x, anywhere()) for x in (*halves, *low_edges, *high_edges)]
        + [(x, whole()) for x in (*firsts, visc, mat_high, mat_low)],
        [((slabs, fields * block + 2, depth, width), anywhere())],
        [
            vmem(fields, block + 2, order, width),
            vmem(fields, block + 2, order + 2 * pad, width),
            vmem(slabs, 2, depth, width),
        ]
        + step_scratch(order, width, fields)
        + [dmas(slabs * fields + 1)],
        12 * order * volume,
        "adjoint_step",
    )[0]


def last_kernel(*refs):
    visc_in, edges_below, edges_above, chunks, *states, half, other, out = refs[:9]
    pulled, state, prior, planes, coupling, ends, visc, sem = refs[9:]
    slabs, block, depth, width = visc.shape
    rows, step = slabs * block, pulled.shape[3]
    main = pl.ds(pad, depth)
    above, below = pl.ds(pad + 1, depth), pl.ds(pad - 1, depth)

    def copy(source, target, which):
        return pltpu.make_async_copy(source, target, sem.at[which])

    arrive = {"visc": copy(visc_in, visc, 0)}
    arrive["ends"] = copy(chunks.at[:, pl.ds(fields * block, 2)], ends, 1)
    for f in range(fields):
        source = chunks.at[:, pl.ds(f * block, block)]
        arrive["pulled", f] = copy(source, pulled.at[f, :, :, main], 2 + f)
        source = states[f // 2].at[:, f % 2]
        arrive["state", f] = copy(source, state.at[f, :, :, main], 2 + fields + f)
        source = (half, other)[f // 2].at[:, f % 2]
        arrive["prior", f] = copy(source, prior.at[f], 2 + 2 * fields + f)
    order = ["visc", "ends", ("state", W)]
    order += [(which, f) for f in (U, V, T, W) for which in ("pulled", "state", "prior")]
    for which in dict.fromkeys(order):
        arrive[which].start()

    def ready(*which):
        for name in which:
            if name in arrive:
                arrive.pop(name).wait()

    flat = (fields * rows * step, width)
    state_rows, pulled_rows = state.reshape(flat), pulled.reshape(flat)
    first, last = pad - 1, pad + depth
    for f in range(fields):
        base = f * rows * step
        state_rows[pl.ds(base + first, rows, stride=step), :] = edges_below[outside[f]]
        state_rows[pl.ds(base + last, rows, stride=step), :] = edges_above[outside[f]]
    ready("visc", "ends")
    for f in range(fields):
        for p in range(slabs):
            base, part = (f * rows + p * block) * step, pl.ds(f * block, block)
            pulled_rows[pl.ds(base + first, block, stride=step), :] = ends[p, 0, part]
            pulled_rows[pl.ds(base + last, block, stride=step), :] = ends[p, 1, part]
    ready(("state", W))
    leaving = []
    for f in (U, V, T, W):
        ready(("pulled", f), ("state", f), ("prior", f))
        if f == T:
            ready(("pulled", W))
        along_y = 0.5 * (visc[slabs - 1, block - 1] + visc[0, 0])
        south = along_y * (pulled[f, 0, 0, main] - pulled[f, slabs - 1, block - 1, main])

        def group(p, south):
            after = lax.rem(p + 1, slabs)
            for i in range(block):
                n, m = (p, i + 1) if i + 1 < block else (after, 0)
                own = visc[p, i]
                along_x = 0.5 * (own + east(own))
                along_y = 0.5 * (own + visc[n, m])
                value = pulled[f, p, i, main]
                flux_x = along_x * (east(value) - value)
                flux_y = along_y * (pulled[f, n, m, main] - value)
                rate = flux_x - west(flux_x) + (flux_y - south)
                south = flux_y
                flow = state[W, p, i, above] * pulled[f, p, i, above]
                rate = rate + (flow - state[W, p, i, below] * pulled[f, p, i, below])
                lost = value * (state[f, p, i, above] - state[f, p, i, below])
                if f == U:
                    coupling[p, i] = lost
                elif f == V:
                    coupling[p, i] = coupling[p, i] + lost
                elif f == T:
                    coupling[p, i] = value - (coupling[p, i] + lost)
                    rate = rate + pulled[W, p, i, main]
                else:
                    rate = rate + (coupling[p, i] - lost)
                result = value + time_step * rate - prior[f, p, i]
                planes[f, pl.ds(p * block + i, depth, stride=rows), :] = result
            return south

        lax.fori_loop(0, slabs, group, south)
        leave = copy(planes.at[f], out.at[outside[f]], 2 + f)
        leave.start()
        leaving.append(leave)
    wait_all(leaving)


def last_step(visc, below, above, chunks, states, priors):
    rows, depth, width = visc.shape
    slabs = chunks.shape[0]
    block = rows // slabs
    padded = vmem(fields, slabs, block, depth + 2 * pad, width)
    one = (slabs, block, depth, width)
    return call(
        last_kernel,
        [(visc.reshape(one), anywhere()), (below, whole()), (above, whole())]
        + [(x, anywhere()) for x in (chunks, *states, *priors)],
        [((fields, depth * rows, width), anywhere())],
        [
            padded,
            padded,
            vmem(fields, *one),
            vmem(fields, depth * rows, width),
            vmem(*one),
            vmem(slabs, 2, depth, width),
            vmem(*one),
            dmas(2 + 3 * fields),
        ],
        30 * fields * rows * depth * width,
        "last_step",
    )[0]


def exchange(chunks):
    return lax.all_to_all(chunks, "slab", split_axis=0, concat_axis=0, tiled=True)


def around(value, axis, steps):
    count = lax.axis_size(axis)
    return lax.ppermute(value, axis, [(i, (i + steps) % count) for i in range(count)])


def local(states, viscosity, inverse):
    start = states[0]
    _, depth, rows, width = start.shape
    slabs, segs = lax.axis_size("slab"), lax.axis_size("seg")
    block = rows // slabs
    share = -(-(block + 4) // segs)

    own_seg = jnp.full((1,), lax.axis_index("seg"), jnp.int32)
    visc, visc_send = visc_chunks(own_seg, viscosity, slabs, share)
    visc_share = exchange(visc_send)
    visc_in = [visc_share] + [around(visc_share, "seg", -i) for i in range(1, segs)]
    send_half, _ = to_chunks(start, slabs, outside[W], 2, [visc_send])
    main_half = exchange(send_half)
    mat_high, mat_low, adj_high, adj_low = split(inverse)
    frame = to_frame(own_seg, visc_in)
    send_other, ends = to_chunks(start, slabs, outside[U], 2, [frame, mat_high])
    main_other = exchange(send_other)
    forward = [(i, i + 1) for i in range(slabs - 1)]
    below = lax.ppermute(ends[1], "slab", forward)
    above = lax.ppermute(ends[0], "slab", [(i, j) for j, i in forward])

    own, outer, targets, later = [], [], [], (visc_share, visc_share)
    few = max(1, 3 * block // 8)
    for part, pieces in ((main_half, (block,)), (main_other, (few, block - few))):
        low_rows, high_rows, *again = outer_rows(part, later, pieces)
        low_in = around(high_rows, "slab", 1)
        high_in = around(low_rows, "slab", -1)
        own.append((low_in, part, high_in))
        outer.append(low_rows)
        targets.append([around(piece, "seg", -1) for piece in again])
        later = (low_in, high_in)

    mats = mat_high, mat_low
    first_half, out, low_edge, high_edge = two_steps(
        *own[0], targets[0][0], outer[1], frame, *mats
    )
    out = after(out, (own[1][0], own[1][2], targets[1][0]))
    first_other = carried_step(own[1], own[0], out, frame, *mats)
    other, *more = second_step(
        first_other, first_half, frame, *mats, U, targets[1], (out,)
    )
    low_edges = [around(edge, "slab", 1) for edge in (high_edge, more[1])]
    high_edges = [around(edge, "slab", -1) for edge in (low_edge, more[0])]
    half = exchange(out)
    residual = (out, after(other, (*low_edges, *high_edges, half)))
    firsts = (first_half, first_other)
    pulled = adjoint_step(residual, low_edges, high_edges, firsts, frame, adj_high, adj_low)
    planes, other = to_planes((half, exchange(residual[1])), pulled)
    priors = [around(part, "seg", 1) for part in (half, other)]
    gradient = last_step(visc, below, above, exchange(pulled), (send_half, send_other), priors)
    shape = (1, fields, depth, rows, width)
    return (planes.reshape(shape), gradient.reshape(shape))


def solution(mesh):
    in_specs = (P("seg", None, "slab", None, None), P("slab", None, None), P())
    out_specs = (P("seg", None, "slab", None, None), P("seg", None, "slab", None, None))
    return jax.shard_map(local, mesh=mesh, in_specs=in_specs, out_specs=out_specs, check_vma=False)
```

```python
import functools

import jax
import jax.numpy as jnp
from jax import lax
from jax.experimental import pallas as pl
from jax.experimental.pallas import tpu as pltpu
from jax.sharding import PartitionSpec as P

time_step = 0.1
vmem_bytes = 56 * 1024 * 1024
f32, bf16 = jnp.float32, jnp.bfloat16
fields = 4
W, T, U, V = range(4)
outside = (2, 3, 0, 1)
pad = 8
tall = 32


def whole():
    return pl.BlockSpec(memory_space=pltpu.VMEM)


def anywhere():
    return pl.BlockSpec(memory_space=pl.ANY)


def scalars():
    return pl.BlockSpec(memory_space=pltpu.SMEM)


def vmem(*shape):
    return pltpu.VMEM(shape, f32)


def dmas(count):
    return pltpu.SemaphoreType.DMA((count,))


def call(kernel, ins, outs, scratch, flops, name, kind=f32, aliases=None):
    moved = sum(4 * x.size for x, _ in ins)
    return pl.pallas_call(
        kernel,
        in_specs=[spec for _, spec in ins],
        out_specs=tuple(spec for _, spec in outs),
        out_shape=tuple(jax.ShapeDtypeStruct(shape, kind) for shape, _ in outs),
        scratch_shapes=scratch,
        input_output_aliases=aliases or {},
        compiler_params=pltpu.CompilerParams(vmem_limit_bytes=vmem_bytes),
        cost_estimate=pl.CostEstimate(flops=flops, bytes_accessed=moved, transcendentals=0),
        name=name,
    )(*[x for x, _ in ins])


def start_all(pairs, sem):
    copies = [
        pltpu.make_async_copy(source, target, sem.at[i])
        for i, (source, target) in enumerate(pairs)
    ]
    for copy in copies:
        copy.start()
    return copies


def wait_all(copies):
    for copy in copies:
        copy.wait()


def spans(parts, axis=1):
    start = 0
    for part in parts:
        yield part, pl.ds(start, part.shape[axis])
        start += part.shape[axis]


def east(value):
    return pltpu.roll(value, value.shape[1] - 1, 1)


def west(value):
    return pltpu.roll(value, 1, 1)


def parts_of(value):
    high = value.astype(bf16)
    return high, (value - high.astype(f32)).astype(bf16)


def product(matrix_high, matrix_low, high, low):
    dot = functools.partial(jnp.dot, preferred_element_type=f32)
    return dot(matrix_high, high) + (dot(matrix_high, low) + dot(matrix_low, high))


def split_kernel(x_ref, high, low, adj_high, adj_low):
    for f in range(fields):
        high[f], low[f] = parts_of(x_ref[outside[f]])
        adj_high[f], adj_low[f] = parts_of(x_ref[outside[f]].T)


def split(inverse):
    return call(
        split_kernel,
        [(inverse, whole())],
        [(inverse.shape, whole())] * 4,
        [],
        0,
        "split",
        bf16,
    )


def visc_kernel(own, x_ref, visc, send):
    slabs, share = send.shape[:2]
    rows, depth, _ = visc.shape
    block = rows // slabs
    for y in range(rows):
        visc[y] = x_ref[pl.ds(y, depth, stride=rows), :]
    for p in range(slabs):
        for i in range(share):
            send[p, i] = visc[lax.rem(p * block - 2 + share * own[0] + i + rows, rows)]


def visc_chunks(own, viscosity, slabs, share):
    depth, rows, width = viscosity.shape
    return call(
        visc_kernel,
        [(own, scalars()), (viscosity.reshape(-1, width), whole())],
        [((rows, depth, width), whole()), ((slabs, share, depth, width), whole())],
        [],
        0,
        "visc_chunks",
    )


def frame_kernel(own, *refs):
    *shares, frame, sem = refs
    slabs, share, depth, _ = shares[0].shape
    pairs = []
    for i, part in enumerate(shares):
        start = lax.rem(own[0] + i, len(shares)) * share
        for p in range(slabs):
            pairs.append((part.at[p], frame.at[pl.ds(start, share), pl.ds(p * depth, depth)]))
    wait_all(start_all(pairs, sem))


def to_frame(own, shares):
    slabs, share, depth, width = shares[0].shape
    return call(
        frame_kernel,
        [(own, scalars())] + [(x, anywhere()) for x in shares],
        [((len(shares) * share, slabs * depth, width), whole())],
        [dmas(len(shares) * slabs)],
        0,
        "to_frame",
    )[0]


def chunks_kernel(start, x_ref, *refs):
    send, edges, planes, held, sem = refs[-5:]
    count, slabs, block, depth, _ = held.shape
    rows = slabs * block
    copies = start_all([(x_ref.at[start + f], planes.at[f]) for f in range(count)], sem)
    ends = [
        pltpu.make_async_copy(x_ref.at[:, pl.ds(z * rows, rows)], edges.at[i], sem.at[count + i])
        for i, z in enumerate((0, depth - 1))
    ]
    for copy in ends:
        copy.start()
    leaving = []
    for f in range(count):
        copies[f].wait()
        for y in range(rows):
            held[f, y // block, y % block] = planes[f, pl.ds(y, depth, stride=rows), :]
        copy = pltpu.make_async_copy(held.at[f], send.at[:, f], sem.at[f])
        copy.start()
        leaving.append(copy)
    wait_all(leaving + ends)


def to_chunks(states, slabs, start, count, later):
    _, depth, rows, width = states.shape
    block = rows // slabs
    return call(
        functools.partial(chunks_kernel, start),
        [(states.reshape(fields, -1, width), anywhere())]
        + [(x, anywhere()) for x in later],
        [
            ((slabs, count, block, depth, width), anywhere()),
            ((2, fields, rows, width), whole()),
        ],
        [
            vmem(count, depth * rows, width),
            vmem(count, slabs, block, depth, width),
            dmas(count + 2),
        ],
        0,
        "to_chunks",
    )


def planes_kernel(half, other, _, o_ref, again, held, sem):
    slabs, _, block, depth, _ = half.shape
    rows = slabs * block
    pairs = []
    for p in range(slabs):
        place = pl.ds(p * block, block)
        pairs.append((half.at[p], held.at[pl.ds(0, 2), place]))
        pairs.append((other.at[p], held.at[pl.ds(2, 2), place]))
    wait_all(start_all(pairs, sem))
    places = [held.at[pl.ds(2, 2), pl.ds(p * block, block)] for p in range(slabs)]
    copies = start_all([(places[p], again.at[p]) for p in range(slabs)], sem)

    def row(y, _):
        for f in range(fields):
            where = pl.ds(outside[f] * depth * rows + y, depth, stride=rows)
            o_ref[where, :] = held[f, y]
        return 0

    lax.fori_loop(0, rows, row, 0, unroll=4)
    wait_all(copies)


def to_planes(halves, later):
    slabs, _, block, depth, width = halves[0].shape
    return call(
        planes_kernel,
        [(x, anywhere()) for x in (*halves, later)],
        [
            ((fields * depth * slabs * block, width), whole()),
            (halves[1].shape, anywhere()),
        ],
        [vmem(fields, slabs * block, depth, width), dmas(2 * slabs)],
        0,
        "to_planes",
    )


def clear_pads(ref):
    edge = jnp.zeros(ref.shape[1:2] + (pad, ref.shape[3]), f32)
    for f in range(ref.shape[0]):
        ref[f, :, 0:pad] = edge
        ref[f, :, ref.shape[2] - pad :] = edge


def first_fluxes(state, visc, shift, carry):
    order = visc.shape[1]
    for z in range(0, order, tall):
        here, pads = pl.ds(z, tall), pl.ds(z + pad, tall)
        along_y = 0.5 * (visc[shift, here] + visc[shift + 1, here])
        for f in range(state.shape[0]):
            carry[f, here] = along_y * (state[f, 1, pads] - state[f, 0, pads])


def spread_of(state, f, j, value, here, pads, along_x, along_y, carry):
    flux_x = along_x * (east(value) - value)
    flux_y = along_y * (state[f, j + 1, pads] - value)
    spread = flux_x - west(flux_x) + (flux_y - carry[f, here])
    carry[f, here] = flux_y
    return spread


def advance_rows(state, speeds, shift, coupled, scratch, count, finish):
    visc, mat_high, mat_low, carry, high, low = scratch
    order, width = visc.shape[1:]
    first_fluxes(state, visc, shift, carry)

    def pair(k, _):
        for half in range(2):
            j = 2 * k + half + 1
            side = slice(half * width, (half + 1) * width)
            for z in range(0, order, tall):
                here, pads = pl.ds(z, tall), pl.ds(z + pad, tall)
                above, below = pl.ds(z + pad + 1, tall), pl.ds(z + pad - 1, tall)
                own = visc[j + shift, here]
                along_x = 0.5 * (own + east(own))
                along_y = 0.5 * (own + visc[j + shift + 1, here])
                speed = speeds[j, pads]
                for f in range(2):
                    value = state[f, j, pads]
                    rate = spread_of(state, f, j, value, here, pads, along_x, along_y, carry)
                    rate = rate - speed * (state[f, j, above] - state[f, j, below])
                    if coupled:
                        rate = rate + state[1 - f, j, pads]
                    high[f, here, side], low[f, here, side] = parts_of(value + time_step * rate)
        for f in range(2):
            out = product(mat_high[f], mat_low[f], high[f], low[f])
            finish(f, 2 * k, out[:, :width])
            finish(f, 2 * k + 1, out[:, width:])
        return 0

    lax.fori_loop(0, count // 2, pair, 0)


def step_scratch(order, width, count):
    return [
        vmem(count, order, width),
        pltpu.VMEM((count, order, 2 * width), bf16),
        pltpu.VMEM((count, order, 2 * width), bf16),
    ]


def two_scratch(frame):
    _, order, width = frame.shape
    matrix = pltpu.VMEM((2, order, order), bf16)
    return [vmem(*frame.shape), matrix, matrix] + step_scratch(order, width, 2)


def constants(base, sources, scratch):
    frame, mat_high, mat_low = sources
    two = pl.ds(base, 2)
    return [(frame, scratch[0]), (mat_high.at[two], scratch[1]), (mat_low.at[two], scratch[2])]


def rows_of(low_in, main, high_in, p, target):
    _, _, block, depth, _ = main.shape
    padded = pl.ds(p * depth + pad, depth)
    for row, count, part in ((0, 2, low_in), (2, block, main), (block + 2, 2, high_in)):
        yield part, target.at[:, pl.ds(row, count), padded]


def first_finish(first, order):
    def finish(f, row, piece):
        first[f, row, pl.ds(pad, order)] = piece

    return finish


def carried_kernel(*refs):
    low_in, main, high_in, low_w, main_w, high_w, _ = refs[:7]
    sources, (first, state, speeds, *scratch, sem) = refs[7:10], refs[10:]
    slabs, _, block, depth, _ = main.shape
    pairs = constants(U, sources, scratch)
    for p in range(slabs):
        pairs += [(a.at[p], b) for a, b in rows_of(low_in, main, high_in, p, state)]
        w_rows = rows_of(low_w, main_w, high_w, p, speeds)
        pairs += [(a.at[p, pl.ds(W, 1)], b) for a, b in w_rows]
    copies = start_all(pairs, sem)
    clear_pads(state)
    clear_pads(first)
    wait_all(copies)
    finish = first_finish(first, slabs * depth)
    advance_rows(state, speeds.at[0], 0, False, scratch, block + 2, finish)


def carried_step(own, with_w, later, frame, mat_high, mat_low):
    slabs, _, block, depth, width = own[1].shape
    order = slabs * depth
    volume = 2 * (block + 2) * order * width
    return call(
        carried_kernel,
        [(x, anywhere()) for x in (*own, *with_w, later, frame, mat_high, mat_low)],
        [((2, block + 2, order + 2 * pad, width), whole())],
        [
            vmem(2, block + 4, order + 2 * pad, width),
            vmem(1, block + 4, order + 2 * pad, width),
        ]
        + two_scratch(frame)
        + [dmas(6 * slabs + 3)],
        6 * order * volume,
        "carried_step",
    )[0]


def second_kernel(base, count, first, with_w, *refs):
    sources, targets = refs[:3], refs[3 : 3 + count]
    out, low_edge, high_edge, state, speeds, *scratch, held, sem = refs[-13:]
    slabs, _, block, depth, _ = out.shape
    places = [held.at[:, :, pl.ds(p * depth, depth)] for p in range(slabs)]
    pairs = constants(base, sources, scratch) + [(first, state)]
    if base != W:
        pairs.append((with_w.at[W], speeds))
    for target, span in spans(targets, 2):
        for p in range(slabs):
            pairs.append((target.at[p], held.at[:, span, pl.ds(p * depth, depth)]))
    wait_all(start_all(pairs, sem))

    def finish(f, row, piece):
        held[f, row] = piece - held[f, row]

    speeds = state.at[W] if base == W else speeds
    advance_rows(state, speeds, 1, base == W, scratch, block, finish)
    copies = start_all([(places[p], out.at[p]) for p in range(slabs)], sem)
    low_edge[...] = held[:, 0]
    high_edge[...] = held[:, block - 1]
    wait_all(copies)


def second_step(first, with_w, frame, mat_high, mat_low, base, targets, later):
    _, order, width = frame.shape
    slabs, _, _, depth, _ = targets[0].shape
    block = sum(target.shape[2] for target in targets)
    operands = (first, with_w, frame, mat_high, mat_low, *targets, *later)
    return call(
        functools.partial(second_kernel, base, len(targets)),
        [(x, anywhere()) for x in operands],
        [((slabs, 2, block, depth, width), anywhere())] + [((2, order, width), whole())] * 2,
        [vmem(*first.shape), vmem(*first.shape[1:])]
        + two_scratch(frame)
        + [vmem(2, block, order, width), dmas(2 * slabs + 5)],
        6 * order * 2 * block * order * width,
        "second_step",
    )


def two_steps_kernel(low_in, main, high_in, target, _, *refs):
    sources, (first, out, low_edge, high_edge), refs = refs[:3], refs[3:7], refs[7:]
    state, *scratch, held, sem = refs
    slabs, _, block, depth, _ = main.shape
    pairs = constants(W, sources, scratch)
    places = [held.at[:, :, pl.ds(p * depth, depth)] for p in range(slabs)]
    for p in range(slabs):
        pairs += [(a.at[p], b) for a, b in rows_of(low_in, main, high_in, p, state)]
        pairs.append((target.at[p], places[p]))
    copies = start_all(pairs, sem)
    clear_pads(state)
    clear_pads(first)
    wait_all(copies)
    finish = first_finish(first, slabs * depth)
    advance_rows(state, state.at[W], 0, True, scratch, block + 2, finish)

    def subtract(f, row, piece):
        held[f, row] = piece - held[f, row]

    advance_rows(first, first.at[W], 1, True, scratch, block, subtract)
    copies = start_all([(places[p], out.at[p]) for p in range(slabs)], sem)
    low_edge[...] = held[:, 0]
    high_edge[...] = held[:, block - 1]
    wait_all(copies)


def two_steps(low_in, main, high_in, target, later, frame, mat_high, mat_low):
    slabs, _, block, depth, width = main.shape
    order = slabs * depth
    volume = 2 * (block + 1) * order * width
    operands = [(x, anywhere()) for x in (low_in, main, high_in)] + [(target, whole())]
    operands += [(x, anywhere()) for x in (later, frame, mat_high, mat_low)]
    return call(
        two_steps_kernel,
        operands,
        [
            ((2, block + 2, order + 2 * pad, width), whole()),
            (main.shape, anywhere()),
            ((2, order, width), whole()),
            ((2, order, width), whole()),
        ],
        [vmem(2, block + 4, order + 2 * pad, width)]
        + two_scratch(frame)
        + [vmem(2, block, order, width), dmas(4 * slabs + 3)],
        12 * order * volume,
        "two_steps",
    )


def after_kernel(*refs):
    del refs


def after(value, later):
    return call(
        after_kernel,
        [(x, anywhere()) for x in (value, *later)],
        [(value.shape, anywhere())],
        [],
        0,
        "after",
        aliases={0: 0},
    )[0]


def outer_kernel(chunks, _before, _after, low_rows, high_rows, *refs):
    *again, sem = refs
    block = chunks.shape[2]
    low, high = chunks.at[:, :, pl.ds(0, 2)], chunks.at[:, :, pl.ds(block - 2, 2)]
    pairs = [(low, low_rows), (high, high_rows)]
    pairs += [(chunks.at[:, :, span], part) for part, span in spans(again, 2)]
    wait_all(start_all(pairs, sem))


def outer_rows(chunks, later, pieces):
    slabs, count, _, depth, width = chunks.shape
    rows = [((slabs, count, size, depth, width), whole()) for size in (2, 2, *pieces)]
    return call(
        outer_kernel,
        [(chunks, anywhere())] + [(x, anywhere()) for x in later],
        rows,
        [dmas(len(rows))],
        0,
        "outer_rows",
    )


def adjoint_kernel(*refs):
    halves, low_edges, high_edges = refs[0:2], refs[2:4], refs[4:6]
    firsts, (visc, mat_high, mat_low) = refs[6:8], refs[8:11]
    out, cot, pulled, ends, carry, high, low, sem = refs[11:]
    slabs, _, block, depth, width = halves[0].shape
    order = slabs * depth
    main = pl.ds(1, block)
    pairs = []
    for source, span in spans(halves):
        for p in range(slabs):
            pairs.append((source.at[p], cot.at[span, main, pl.ds(p * depth, depth)]))
    for i in range(2):
        pairs.append((low_edges[i], cot.at[pl.ds(2 * i, 2), 0]))
        pairs.append((high_edges[i], cot.at[pl.ds(2 * i, 2), block + 1]))
    copies = start_all(pairs, sem)
    clear_pads(pulled)
    wait_all(copies)

    def pull(k, _):
        for f in range(fields):
            pair = jnp.concatenate([cot[f, 2 * k], cot[f, 2 * k + 1]], axis=1)
            out = product(mat_high[f], mat_low[f], *parts_of(pair))
            pulled[f, 2 * k, pl.ds(pad, order)] = out[:, :width]
            pulled[f, 2 * k + 1, pl.ds(pad, order)] = out[:, width:]
        return 0

    lax.fori_loop(0, (block + 2) // 2, pull, 0)
    first_fluxes(pulled, visc, 1, carry)

    def rows(k, _):
        for half in range(2):
            j = 2 * k + half + 1
            side = slice(half * width, (half + 1) * width)
            for z in range(0, order, tall):
                here, pads = pl.ds(z, tall), pl.ds(z + pad, tall)
                above, below = pl.ds(z + pad + 1, tall), pl.ds(z + pad - 1, tall)
                own = visc[j + 1, here]
                along_x = 0.5 * (own + east(own))
                along_y = 0.5 * (own + visc[j + 2, here])
                speed_above, speed_below = firsts[0][W, j, above], firsts[0][W, j, below]
                coupling = pulled[T, j, pads]
                for f in (U, V, T, W):
                    value = pulled[f, j, pads]
                    rate = spread_of(pulled, f, j, value, here, pads, along_x, along_y, carry)
                    up, down = pulled[f, j, above], pulled[f, j, below]
                    rate = rate + (speed_above * up - speed_below * down)
                    if f == W:
                        slope = speed_above - speed_below
                    else:
                        ref, i = firsts[f // 2], f % 2
                        slope = ref[i, j, above] - ref[i, j, below]
                    coupling = coupling - value * slope
                    if f == T:
                        rate = rate + pulled[W, j, pads]
                    if f == W:
                        rate = rate + coupling
                    high[f, here, side], low[f, here, side] = parts_of(value + time_step * rate)
        for f in range(fields):
            out = product(mat_high[f], mat_low[f], high[f], low[f])
            cot[f, 2 * k + 1] = out[:, :width]
            cot[f, 2 * k + 2] = out[:, width:]
        return 0

    lax.fori_loop(0, block // 2, rows, 0)
    pairs = []
    for p in range(slabs):
        for f in range(fields):
            source = cot.at[f, main, pl.ds(p * depth, depth)]
            pairs.append((source, out.at[p, pl.ds(f * block, block)]))
    copies = start_all(pairs, sem)
    for p in range(slabs):
        for f in range(fields):
            for y in range(block):
                for side, z in ((0, p * depth - 1), (1, (p + 1) * depth)):
                    to = slice(f * block + y, f * block + y + 1)
                    if 0 <= z < order:
                        ends[p, side, to] = cot[f, y + 1, z : z + 1]
                    else:
                        ends[p, side, to] = jnp.zeros((1, width), f32)
    ends_copy = pltpu.make_async_copy(
        ends, out.at[:, pl.ds(fields * block, 2)], sem.at[len(pairs)]
    )
    ends_copy.start()
    wait_all(copies)
    ends_copy.wait()


def adjoint_step(halves, low_edges, high_edges, firsts, visc, mat_high, mat_low):
    slabs, _, block, depth, width = halves[0].shape
    order = slabs * depth
    volume = fields * (block + 1) * order * width
    return call(
        adjoint_kernel,
        [(x, anywhere()) for x in (*halves, *low_edges, *high_edges)]
        + [(x, whole()) for x in (*firsts, visc, mat_high, mat_low)],
        [((slabs, fields * block + 2, depth, width), anywhere())],
        [
            vmem(fields, block + 2, order, width),
            vmem(fields, block + 2, order + 2 * pad, width),
            vmem(slabs, 2, depth, width),
        ]
        + step_scratch(order, width, fields)
        + [dmas(slabs * fields + 1)],
        12 * order * volume,
        "adjoint_step",
    )[0]


def last_kernel(*refs):
    visc_in, edges_below, edges_above, chunks, *states, half, other, out = refs[:9]
    pulled, state, prior, planes, coupling, ends, visc, sem = refs[9:]
    slabs, block, depth, width = visc.shape
    rows, step = slabs * block, pulled.shape[3]
    main = pl.ds(pad, depth)
    above, below = pl.ds(pad + 1, depth), pl.ds(pad - 1, depth)

    def copy(source, target, which):
        return pltpu.make_async_copy(source, target, sem.at[which])

    arrive = {"visc": copy(visc_in, visc, 0)}
    arrive["ends"] = copy(chunks.at[:, pl.ds(fields * block, 2)], ends, 1)
    for f in range(fields):
        source = chunks.at[:, pl.ds(f * block, block)]
        arrive["pulled", f] = copy(source, pulled.at[f, :, :, main], 2 + f)
        source = states[f // 2].at[:, f % 2]
        arrive["state", f] = copy(source, state.at[f, :, :, main], 2 + fields + f)
        source = (half, other)[f // 2].at[:, f % 2]
        arrive["prior", f] = copy(source, prior.at[f], 2 + 2 * fields + f)
    order = ["visc", "ends", ("state", W)]
    order += [(which, f) for f in (U, V, T, W) for which in ("pulled", "state", "prior")]
    for which in dict.fromkeys(order):
        arrive[which].start()

    def ready(*which):
        for name in which:
            if name in arrive:
                arrive.pop(name).wait()

    flat = (fields * rows * step, width)
    state_rows, pulled_rows = state.reshape(flat), pulled.reshape(flat)
    first, last = pad - 1, pad + depth
    for f in range(fields):
        base = f * rows * step
        state_rows[pl.ds(base + first, rows, stride=step), :] = edges_below[outside[f]]
        state_rows[pl.ds(base + last, rows, stride=step), :] = edges_above[outside[f]]
    ready("visc", "ends")
    for f in range(fields):
        for p in range(slabs):
            base, part = (f * rows + p * block) * step, pl.ds(f * block, block)
            pulled_rows[pl.ds(base + first, block, stride=step), :] = ends[p, 0, part]
            pulled_rows[pl.ds(base + last, block, stride=step), :] = ends[p, 1, part]
    ready(("state", W))
    leaving = []
    for f in (U, V, T, W):
        ready(("pulled", f), ("state", f), ("prior", f))
        if f == T:
            ready(("pulled", W))
        along_y = 0.5 * (visc[slabs - 1, block - 1] + visc[0, 0])
        south = along_y * (pulled[f, 0, 0, main] - pulled[f, slabs - 1, block - 1, main])

        def group(p, south):
            after = lax.rem(p + 1, slabs)
            for i in range(block):
                n, m = (p, i + 1) if i + 1 < block else (after, 0)
                own = visc[p, i]
                along_x = 0.5 * (own + east(own))
                along_y = 0.5 * (own + visc[n, m])
                value = pulled[f, p, i, main]
                flux_x = along_x * (east(value) - value)
                flux_y = along_y * (pulled[f, n, m, main] - value)
                rate = flux_x - west(flux_x) + (flux_y - south)
                south = flux_y
                flow = state[W, p, i, above] * pulled[f, p, i, above]
                rate = rate + (flow - state[W, p, i, below] * pulled[f, p, i, below])
                lost = value * (state[f, p, i, above] - state[f, p, i, below])
                if f == U:
                    coupling[p, i] = lost
                elif f == V:
                    coupling[p, i] = coupling[p, i] + lost
                elif f == T:
                    coupling[p, i] = value - (coupling[p, i] + lost)
                    rate = rate + pulled[W, p, i, main]
                else:
                    rate = rate + (coupling[p, i] - lost)
                result = value + time_step * rate - prior[f, p, i]
                planes[f, pl.ds(p * block + i, depth, stride=rows), :] = result
            return south

        lax.fori_loop(0, slabs, group, south)
        leave = copy(planes.at[f], out.at[outside[f]], 2 + f)
        leave.start()
        leaving.append(leave)
    wait_all(leaving)


def last_step(visc, below, above, chunks, states, priors):
    rows, depth, width = visc.shape
    slabs = chunks.shape[0]
    block = rows // slabs
    padded = vmem(fields, slabs, block, depth + 2 * pad, width)
    one = (slabs, block, depth, width)
    return call(
        last_kernel,
        [(visc.reshape(one), anywhere()), (below, whole()), (above, whole())]
        + [(x, anywhere()) for x in (chunks, *states, *priors)],
        [((fields, depth * rows, width), anywhere())],
        [
            padded,
            padded,
            vmem(fields, *one),
            vmem(fields, depth * rows, width),
            vmem(*one),
            vmem(slabs, 2, depth, width),
            vmem(*one),
            dmas(2 + 3 * fields),
        ],
        30 * fields * rows * depth * width,
        "last_step",
    )[0]


def exchange(chunks):
    return lax.all_to_all(chunks, "slab", split_axis=0, concat_axis=0, tiled=True)


def around(value, axis, steps):
    count = lax.axis_size(axis)
    return lax.ppermute(value, axis, [(i, (i + steps) % count) for i in range(count)])


def local(states, viscosity, inverse):
    start = states[0]
    _, depth, rows, width = start.shape
    slabs, segs = lax.axis_size("slab"), lax.axis_size("seg")
    block = rows // slabs
    share = -(-(block + 4) // segs)

    own_seg = jnp.full((1,), lax.axis_index("seg"), jnp.int32)
    visc, visc_send = visc_chunks(own_seg, viscosity, slabs, share)
    visc_share = exchange(visc_send)
    visc_in = [visc_share] + [around(visc_share, "seg", -i) for i in range(1, segs)]
    send_half, _ = to_chunks(start, slabs, outside[W], 2, [visc_send])
    main_half = exchange(send_half)
    mat_high, mat_low, adj_high, adj_low = split(inverse)
    frame = to_frame(own_seg, visc_in)
    send_other, ends = to_chunks(start, slabs, outside[U], 2, [frame, mat_high])
    main_other = exchange(send_other)
    forward = [(i, i + 1) for i in range(slabs - 1)]
    below = lax.ppermute(ends[1], "slab", forward)
    above = lax.ppermute(ends[0], "slab", [(i, j) for j, i in forward])

    own, outer, targets, later = [], [], [], (visc_share, visc_share)
    few = max(1, 3 * block // 8)
    for part, pieces in ((main_half, (block,)), (main_other, (few, block - few))):
        low_rows, high_rows, *again = outer_rows(part, later, pieces)
        low_in = around(high_rows, "slab", 1)
        high_in = around(low_rows, "slab", -1)
        own.append((low_in, part, high_in))
        outer.append(low_rows)
        targets.append([around(piece, "seg", -1) for piece in again])
        later = (low_in, high_in)

    mats = mat_high, mat_low
    first_half, out, low_edge, high_edge = two_steps(
        *own[0], targets[0][0], outer[1], frame, *mats
    )
    out = after(out, (own[1][0], own[1][2], targets[1][0]))
    first_other = carried_step(own[1], own[0], out, frame, *mats)
    other, *more = second_step(
        first_other, first_half, frame, *mats, U, targets[1], (out,)
    )
    low_edges = [around(edge, "slab", 1) for edge in (high_edge, more[1])]
    high_edges = [around(edge, "slab", -1) for edge in (low_edge, more[0])]
    half = exchange(out)
    residual = (out, after(other, (*low_edges, *high_edges, half)))
    firsts = (first_half, first_other)
    pulled = adjoint_step(residual, low_edges, high_edges, firsts, frame, adj_high, adj_low)
    planes, other = to_planes((half, exchange(residual[1])), pulled)
    priors = [around(part, "seg", 1) for part in (half, other)]
    gradient = last_step(visc, below, above, exchange(pulled), (send_half, send_other), priors)
    shape = (1, fields, depth, rows, width)
    return (planes.reshape(shape), gradient.reshape(shape))


def solution(mesh):
    in_specs = (P("seg", None, "slab", None, None), P("slab", None, None), P())
    out_specs = (P("seg", None, "slab", None, None), P("seg", None, "slab", None, None))
    return jax.shard_map(local, mesh=mesh, in_specs=in_specs, out_specs=out_specs, check_vma=False)
```
